32 devices in a mesh: wide: 8 (over y, x, core), narrow: 4 (over z).
Axes of the slice: x: 2, y: 2, z: 4, core: 2. Of those that a mesh axis runs over, the one named last changes fastest.
Arguments:
- latents: bfloat16 [32, 1024, 768], P(('wide', 'narrow')), may hold values from -6 to 6
- condition: bfloat16 [32, 768], P(('wide', 'narrow')), may hold values from -6 to 6
- valid_mask: int32 [32, 1024], P(('wide', 'narrow')), may hold values from 0 to 1, as said below
- ada_weight: bfloat16 [768, 4608], P(('wide', 'narrow')), may hold values from -0.21875 to 0.21875
- ada_bias: bfloat16 [4608], P(('wide', 'narrow')), may hold values from -3 to 3
- dw1_kernel: bfloat16 [9, 768], P(None, ('wide', 'narrow')), may hold values from -2 to 2
- dw1_bias: bfloat16 [768], P(('wide', 'narrow')), may hold values from -3 to 3
- qkv_weight: bfloat16 [768, 2304], P(('wide', 'narrow')), may hold values from -0.21875 to 0.21875
- proj_weight: bfloat16 [768, 768], P(('wide', 'narrow')), may hold values from -1.25 to 1.25
- proj_bias: bfloat16 [768], P(('wide', 'narrow')), may hold values from -3 to 3
- fc1_weight: bfloat16 [768, 3072], P(('wide', 'narrow')), may hold values from -0.21875 to 0.21875
- fc1_bias: bfloat16 [3072], P(('wide', 'narrow')), may hold values from -3 to 3
- dw2_kernel: bfloat16 [9, 3072], P(None, ('wide', 'narrow')), may hold values from -2 to 2
- dw2_bias: bfloat16 [3072], P(('wide', 'narrow')), may hold values from -3 to 3
- fc2_weight: bfloat16 [3072, 768], P(('wide', 'narrow')), may hold values from -0.109375 to 0.109375
- fc2_bias: bfloat16 [768], P(('wide', 'narrow')), may hold values from -3 to 3
- out_cotangent: bfloat16 [32, 1024, 768], P(('wide', 'narrow')), may hold values from -6 to 6
Outputs:
- block_out: bfloat16 [32, 1024, 768], P(('wide', 'narrow'))
- input_grad: bfloat16 [32, 1024, 768], P(('wide', 'narrow'))
- cond_grad: float32 [32, 768], P(('wide', 'narrow'))
- ada_wgrad: float32 [768, 4608], P(('wide', 'narrow'))
- ada_bgrad: float32 [4608], P(('wide', 'narrow'))
- dw1_kgrad: float32 [9, 768], P(None, ('wide', 'narrow'))
- dw1_bgrad: float32 [768], P(('wide', 'narrow'))
- qkv_grad: float32 [768, 2304], P(('wide', 'narrow'))
- proj_wgrad: float32 [768, 768], P(('wide', 'narrow'))
- proj_bgrad: float32 [768], P(('wide', 'narrow'))
- fc1_wgrad: float32 [768, 3072], P(('wide', 'narrow'))
- fc1_bgrad: float32 [3072], P(('wide', 'narrow'))
- dw2_kgrad: float32 [9, 3072], P(None, ('wide', 'narrow'))
- dw2_bgrad: float32 [3072], P(('wide', 'narrow'))
- fc2_wgrad: float32 [3072, 768], P(('wide', 'narrow'))
- fc2_bgrad: float32 [768], P(('wide', 'narrow'))
The draws below stay inside these ranges and needn't reach their ends.
Inputs may be any that keep to these rules, and one draw needn't show every extreme that they name: `valid_mask`: in each latent the valid tokens are those of the first h rows and first w columns of its 32 x 32 grid, h and w even and at least 16; at least one latent of every draw is wholly valid.
All inputs are finite; a program needn't handle non-finite values.
Results may differ from the reference program's by a relative error of at most 0.014.
The reference program's roundings to bfloat16 on the way count: a program that leaves them out, or rounds other values in their place, can miss the bound.
Values may be sent and summed in bfloat16 or wider, within the bound.
A program may use at most 384 MiB of HBM per device.

```python
import jax
import jax.numpy as jnp
from jax import lax

D = 768
HEADS = 12
HEAD = 64
FF = 3072
GRID = 32
SEQ = 1024
BATCH = 32


def draw_valid_mask(key, part):
    key = jax.random.fold_in(key, 7)
    key_rows, key_cols, key_full = jax.random.split(key, 3)
    heights = 2 * jax.random.randint(key_rows, (BATCH,), GRID // 4, GRID // 2 + 1)
    widths = 2 * jax.random.randint(key_cols, (BATCH,), GRID // 4, GRID // 2 + 1)
    full_index = jax.random.randint(key_full, (), 0, BATCH)
    chosen = jnp.arange(BATCH) == full_index
    heights = jnp.where(chosen, GRID, heights)
    widths = jnp.where(chosen, GRID, widths)
    positions = jnp.arange(GRID)
    inside = (positions[None, :, None] < heights[:, None, None]) & (positions[None, None, :] < widths[:, None, None])
    return inside.reshape(BATCH, GRID * GRID).astype(jnp.int32)


def strengthened(values, key, source, target, blocks, factor):
    owner, partner = [(jnp.arange(values.shape[dim]) // (values.shape[dim] // blocks)).reshape([-1 if axis == dim else 1 for axis in range(values.ndim)]) for dim in (source, target)]
    chosen = jax.random.permutation(key, blocks)[partner]
    strong = (owner == chosen) | (owner == (partner + blocks // 2) % blocks)
    return jnp.where(strong, factor * values, values)


def block_scale(stream_key, extent, cuts, low, high):
    def one(position, parts):
        steps = jax.random.uniform(jax.random.fold_in(jax.random.fold_in(stream_key, 6), position), (parts,), jnp.float32, low / len(cuts), high / len(cuts))
        return jnp.repeat(jnp.exp(steps), extent[position] // parts).reshape((-1,) + (1,) * (len(extent) - position - 1))

    level = one(*cuts[0])
    for cut in cuts[1:]:
        level = level * one(*cut)
    return level


def centred(key, shape, width, most, cuts=(), dtype=jnp.bfloat16):
    factor_of = block_scale(key, shape, cuts, -0.22, 0.18) if cuts else 1.0
    values = jax.random.normal(key, shape, jnp.float32) * width * factor_of
    return jnp.minimum(jnp.maximum(values, -most), most).astype(dtype)


def heavy_noise(key, dims, scale, reach, pieces, heavy, dtype=jnp.bfloat16):
    values = scale * jax.random.normal(key, dims, jnp.float32)
    if pieces:
        values = values * block_scale(key, dims, pieces, -0.22, 0.18)
    return jnp.clip(strengthened(values, jax.random.fold_in(key, 3), *heavy), -reach, reach).astype(dtype)


def setup_inputs(seed: int = 0) -> dict:
    seeds = jax.random.split(jax.random.key(seed), 18)
    return {
        "latents": centred(seeds[0], (BATCH, SEQ, D), 1.0, 6.0, ((0, 32),)),
        "condition": centred(seeds[1], (BATCH, D), 1.0, 6.0, ((0, 32),)),
        "valid_mask": draw_valid_mask(jax.random.fold_in(seeds[17], 71), 0),
        "ada_weight": centred(seeds[3], (D, 6 * D), D ** -0.5, 0.21875, ((0, 32),)),
        "ada_bias": centred(seeds[4], (6 * D,), 0.5, 3.0, ((0, 32),)),
        "dw1_kernel": centred(seeds[5], (9, D), 0.35, 2.0, ((1, 32),)),
        "dw1_bias": centred(seeds[6], (D,), 0.5, 3.0, ((0, 32),)),
        "qkv_weight": centred(seeds[7], (D, 3 * D), D ** -0.5, 0.21875, ((0, 32),)),
        "proj_weight": centred(seeds[8], (D, D), (D // 32) ** -0.5, 1.25, ((0, 32),)),
        "proj_bias": centred(seeds[9], (D,), 0.5, 3.0, ((0, 32),)),
        "fc1_weight": centred(seeds[10], (D, FF), D ** -0.5, 0.21875, ((0, 32),)),
        "fc1_bias": centred(seeds[11], (FF,), 0.5, 3.0, ((0, 32),)),
        "dw2_kernel": centred(seeds[12], (9, FF), 0.35, 2.0, ((1, 32),)),
        "dw2_bias": centred(seeds[13], (FF,), 0.5, 3.0, ((0, 32),)),
        "fc2_weight": centred(seeds[14], (FF, D), FF ** -0.5, 0.109375, ((0, 32),)),
        "fc2_bias": centred(seeds[15], (D,), 0.5, 3.0, ((0, 32),)),
        "out_cotangent": heavy_noise(seeds[16], (BATCH, SEQ, D), 1.0, 6.0, ((0, 32),), (0, 2, 32, 2.75)),
    }


@jax.custom_vjp
def low(v):
    return lax.optimization_barrier(v.astype(jnp.bfloat16)).astype(jnp.float32)

@jax.custom_vjp
def low_back(v):
    return v

def low_keep(v):
    return (low(v), None)

def low_pass(kept, grad):
    return (grad,)

def back_keep(v):
    return (v, None)

def back_low(kept, grad):
    return (low(grad),)
low.defvjp(low_keep, low_pass)
low_back.defvjp(back_keep, back_low)
HIGH = lax.Precision.HIGHEST

def smooth_gate(values):
    return values * jax.nn.sigmoid(values)

def gelu_tanh(values):
    return 0.5 * values * (1.0 + jnp.tanh(0.7978845608028654 * (values + 0.044715 * values * values * values)))

def modulate(values, offsets, scales):
    centered = values - lax.optimization_barrier(jnp.mean(values, axis=-1, keepdims=True))
    spread = lax.optimization_barrier(jnp.mean(centered * centered, axis=-1, keepdims=True))
    return centered * lax.rsqrt(spread + 1e-06) * (1.0 + scales) + offsets

def depthwise(source, kernel, offsets):
    channels = source.shape[-1]
    square = source.reshape(GRID, GRID, channels)
    padded = jnp.pad(square, ((1, 1), (1, 1), (0, 0)))
    result = jnp.zeros_like(square) + offsets
    for offset_index in range(9):
        row_shift = offset_index // 3
        col_shift = offset_index % 3
        result = result + kernel[offset_index] * padded[row_shift:row_shift + GRID, col_shift:col_shift + GRID]
    return result.reshape(GRID * GRID, channels)

def regroup(tokens):
    channels = tokens.shape[-1]
    half_side = GRID // 2
    grid_view = tokens.reshape(half_side, 2, half_side, 2, channels).transpose(1, 3, 0, 2, 4)
    return grid_view.reshape(4, half_side * half_side, channels)

def ungroup(groups):
    channels = groups.shape[-1]
    half_side = GRID // 2
    grid_view = groups.reshape(2, 2, half_side, half_side, channels).transpose(2, 0, 3, 1, 4)
    return grid_view.reshape(GRID * GRID, channels)

def latent_pass(tokens, cond_row, validity, params):
    ada_weight, ada_bias, dw1_kernel, dw1_bias, qkv_weight, proj_weight, proj_bias, fc1_weight, fc1_bias, dw2_kernel, dw2_bias, fc2_weight, fc2_bias = params
    model_width = tokens.shape[1]
    silu_low = low(smooth_gate(cond_row))
    modulation = low_back(jnp.dot(silu_low[None, :], ada_weight, precision=HIGH))[0] + ada_bias
    shifts = jnp.split(modulation, 6)
    normed = modulate(tokens, shifts[0], shifts[1])
    mixed_rows = low(depthwise(normed, dw1_kernel, dw1_bias))
    triple = low(low_back(jnp.dot(mixed_rows, qkv_weight, precision=HIGH)))
    grouped = regroup(triple)
    queries = grouped[:, :, :model_width].reshape(4, -1, HEADS, HEAD)
    key_rows = grouped[:, :, model_width:2 * model_width].reshape(4, -1, HEADS, HEAD)
    values = grouped[:, :, 2 * model_width:].reshape(4, -1, HEADS, HEAD)
    key_keep = regroup(validity[:, None])[:, :, 0]
    scores = low_back(jnp.einsum('gqhd,gkhd->hgqk', queries, key_rows, precision=HIGH) * 0.125)
    scores = jnp.where(key_keep[None, :, None, :] > 0.5, scores, -1e+30)
    largest = lax.optimization_barrier(jnp.max(scores, axis=-1, keepdims=True))
    exponent = jnp.exp(scores - largest)
    attention = low(exponent / lax.optimization_barrier(jnp.sum(exponent, axis=-1, keepdims=True)))
    attended = low(low_back(jnp.einsum('hgqk,gkhd->gqhd', attention, values, precision=HIGH)))
    attended = ungroup(attended.reshape(4, -1, model_width))
    branch = low_back(jnp.dot(attended, proj_weight, precision=HIGH)) + proj_bias
    middle = tokens + shifts[2] * branch
    normed_two = low(modulate(middle, shifts[3], shifts[4]))
    hidden = low_back(jnp.dot(normed_two, fc1_weight, precision=HIGH)) + fc1_bias
    activated = low(gelu_tanh(depthwise(hidden, dw2_kernel, dw2_bias)))
    branch_two = low_back(jnp.dot(activated, fc2_weight, precision=HIGH)) + fc2_bias
    return middle + shifts[5] * branch_two

def reference(latents, condition, valid_mask, ada_weight, ada_bias, dw1_kernel, dw1_bias, qkv_weight, proj_weight, proj_bias, fc1_weight, fc1_bias, dw2_kernel, dw2_bias, fc2_weight, fc2_bias, out_cotangent):
    params = tuple((member.astype(jnp.float32) for member in (ada_weight, ada_bias, dw1_kernel, dw1_bias, qkv_weight, proj_weight, proj_bias, fc1_weight, fc1_bias, dw2_kernel, dw2_bias, fc2_weight, fc2_bias)))
    validity = valid_mask.astype(jnp.float32)
    tokens = latents.astype(jnp.float32)
    cond_rows = condition.astype(jnp.float32)
    checked = jax.checkpoint(latent_pass)

    def batch_pass(token_set, cond_set, param_set):
        return lax.map(lambda sample: checked(sample[0], sample[1], sample[2], param_set), (token_set, cond_set, validity))
    result, pullback = jax.vjp(batch_pass, tokens, cond_rows, params)
    cotangent = out_cotangent.astype(jnp.float32) * validity[:, :, None]
    token_grad, cond_grad, param_grads = pullback(cotangent)
    return (result.astype(jnp.bfloat16), token_grad.astype(jnp.bfloat16), cond_grad, param_grads[0], param_grads[1], param_grads[2], param_grads[3], param_grads[4], param_grads[5], param_grads[6], param_grads[7], param_grads[8], param_grads[9], param_grads[10], param_grads[11], param_grads[12])
```

```python
import functools

import jax
import jax.numpy as jnp
from jax import lax
from jax.experimental import pallas as pl
from jax.experimental.pallas import tpu as pltpu
from jax.sharding import PartitionSpec as P

HEAD = 64
GRID = 32
HALF = 16
GROUP = 256
TOKENS = 1024
C0 = 0.7978845608028654
C1 = 0.044715
EPS = 1e-06
MIB = 1 << 20
AXES = ("wide", "narrow")
F32, BF16 = jnp.float32, jnp.bfloat16


def dot_nn(a, b):
    return lax.dot_general(a, b, (((1,), (0,)), ((), ())), preferred_element_type=F32)


def dot_nt(a, b):
    return lax.dot_general(a, b, (((1,), (1,)), ((), ())), preferred_element_type=F32)


def dot_tn(a, b):
    return lax.dot_general(a, b, (((0,), (0,)), ((), ())), preferred_element_type=F32)


def whole(shape):
    return pl.BlockSpec(shape, lambda *_: (0,) * len(shape))


def once(shape):
    return pl.BlockSpec(shape, lambda *_: (0,) * len(shape), pipeline_mode=pl.Buffered(1))


def like(shape, dtype):
    return jax.ShapeDtypeStruct(shape, dtype)


def shift_pair(pair, parity, first, last):
    low, high = pair
    zero = jnp.zeros_like(low)
    if parity == 0:
        low, high = pltpu.roll(low, 1, 0), pltpu.roll(high, 1, 0)
        return jnp.where(first, zero, low), jnp.where(first, low, high)
    low, high = pltpu.roll(low, 7, 0), pltpu.roll(high, 7, 0)
    return jnp.where(last, high, low), jnp.where(last, zero, high)


def row_sources(gi, r):
    if gi == 0:
        return ((1, r - 1), (0, r), (1, r))
    return ((0, r), (1, r), (0, r + 1))


def load_pair(ref, slab, gi, gj, r):
    tile = 2 + 2 * r
    group = 2 * gi + gj
    return ref[slab, group, tile], ref[slab, group, tile + 1]


def store_pair(ref, slab, gi, gj, r, pair):
    tile = 2 + 2 * r
    group = 2 * gi + gj
    ref[slab, group, tile] = pair[0]
    ref[slab, group, tile + 1] = pair[1]


def edge_masks():
    sub = lax.broadcasted_iota(jnp.int32, (8, 128), 0)
    return sub == 0, sub == 7


def clear_edges(ref):
    slabs = ref.shape[0]
    ref[:, :, 0:2] = jnp.zeros((slabs, 4, 2, 8, 128), F32)
    ref[:, :, 34:36] = jnp.zeros((slabs, 4, 2, 8, 128), F32)


def conv_cell(src, slab, gi, gj, r, k, bias, masks):
    sources = row_sources(gi, r)
    other = 1 - gj
    near = 2 if gj == 0 else 0
    far = 2 - near
    same = [load_pair(src, slab, p, gj, rr) for p, rr in sources]
    cross = [load_pair(src, slab, p, other, rr) for p, rr in sources]
    straight, moved = [], []
    for h in (0, 1):
        acc, off = bias, None
        for a in range(3):
            acc = acc + k[3 * a + 1] * same[a][h] + k[3 * a + near] * cross[a][h]
            term = k[3 * a + far] * cross[a][h]
            off = term if off is None else off + term
        straight.append(acc)
        moved.append(off)
    moved = shift_pair(moved, gj, *masks)
    return straight[0] + moved[0], straight[1] + moved[1]


def conv_back(slab, k, src, grad, grad_moved, put):
    def body(r, carry):
        kg, total = list(carry[:9]), carry[9]
        for gi in (0, 1):
            sources = row_sources(gi, r)
            for gj in (0, 1):
                other = 1 - gj
                near = 2 if gj == 0 else 0
                here = load_pair(src, slab, gi, gj, r)
                out = [None, None]
                for a in range(3):
                    p, rr = sources[2 - a]
                    trio = {
                        1: load_pair(grad, slab, p, gj, rr),
                        2 - near: load_pair(grad, slab, p, other, rr),
                        near: load_pair(grad_moved, slab, p, other, rr),
                    }
                    for b in range(3):
                        n = 3 * a + b
                        for h in (0, 1):
                            term = k[n] * trio[b][h]
                            out[h] = term if out[h] is None else out[h] + term
                            kg[n] = kg[n] + here[h] * trio[b][h]
                total = total + out[0] + out[1]
                put(gi, gj, r, out)
        return tuple(kg) + (total,)

    zero = jnp.zeros((8, 128), F32)
    return lax.fori_loop(0, HALF, body, (zero,) * 10)


def group_rows(gi, gj, r):
    return pl.ds(pl.multiple_of((2 * gi + gj) * GROUP + r * HALF, HALF), HALF)


def row_sum(values):
    rows, columns = values.shape
    return jnp.sum(values.reshape(rows // 8, 8, columns), axis=0)


def unit_rows(values):
    model = values.shape[-1]
    centered = values - jnp.sum(values, axis=-1, keepdims=True) * (1.0 / model)
    spread = jnp.sum(centered * centered, axis=-1, keepdims=True) * (1.0 / model)
    scale = lax.rsqrt(spread + EPS)
    return centered * scale, scale


def unit_back(grad, unit, scale):
    model = grad.shape[-1]
    mean = jnp.sum(grad, axis=-1, keepdims=True) * (1.0 / model)
    tilt = jnp.sum(grad * unit, axis=-1, keepdims=True) * (1.0 / model)
    return scale * (grad - mean - unit * tilt)


def order_matrix():
    d = jnp.arange(GROUP)
    group, position, column = d // 64, (d % 64) // HALF, d % HALF
    source = (2 * position + group // 2) * GRID + 2 * column + group % 2
    return (source[:, None] == jnp.arange(GROUP)[None, :]).astype(BF16)


def pre_kernel(x_ref, cot_ref, mask_ref, order_ref, mod_ref, kern_ref, bias_ref,
               lat_ref, gout_ref, g2_ref, normed_ref, mixed_ref, keep_ref, fc2b_ref):
    model = x_ref.shape[1]
    slabs = model // 128
    clear_edges(normed_ref)
    shift, scale, gate = mod_ref[0:1, :], mod_ref[1:2, :], mod_ref[5:6, :]
    total = jnp.zeros((8, model), F32)
    for t in range(4):
        rows = pl.ds(t * GROUP, GROUP)
        tokens = dot_nn(order_ref[...], x_ref[rows, :])
        unit, _ = unit_rows(tokens)
        normed = unit * (1.0 + scale) + shift
        kept = dot_nn(order_ref[...], mask_ref[rows, :])
        spread = jnp.concatenate([kept] * slabs, axis=1)
        gout = dot_nn(order_ref[...], cot_ref[rows, :]) * spread
        two = gout * gate
        total = total + row_sum(two)
        for g in range(4):
            src = slice(64 * g, 64 * g + 64)
            dst = pl.ds(g * GROUP + 64 * t, 64)
            lat_ref[dst, :] = tokens[src].astype(BF16)
            gout_ref[dst, :] = gout[src].astype(BF16)
            g2_ref[dst, :] = two[src].astype(BF16)
            keep_ref[dst, :] = (kept[src] - 1.0) * 1e30
            for s in range(slabs):
                tile = normed[src, s * 128 : s * 128 + 128].reshape(8, 8, 128)
                normed_ref[s, g, 2 + 8 * t : 10 + 8 * t] = tile
    fc2b_ref[...] = total
    masks = edge_masks()
    for s in range(slabs):
        lanes = pl.ds(s * 128, 128)
        k = [kern_ref[n, :, lanes] for n in range(9)]
        bias = bias_ref[:, lanes]

        def body(r, carry):
            for gi in (0, 1):
                for gj in (0, 1):
                    pair = conv_cell(normed_ref, s, gi, gj, r, k, bias, masks)
                    mixed_ref[group_rows(gi, gj, r), lanes] = jnp.concatenate(pair, 0).astype(BF16)
            return carry

        lax.fori_loop(0, HALF, body, 0)


def pre(x, cot, mask, order, mod, kern, bias):
    tokens, model = x.shape
    slabs = model // 128
    mask = jnp.broadcast_to(mask.astype(BF16)[:, None], (tokens, 128))
    kern = jnp.broadcast_to(kern.astype(F32)[:, None, :], (9, 8, model))
    bias = jnp.broadcast_to(bias.astype(F32)[None, :], (8, model))
    return pl.pallas_call(
        pre_kernel,
        out_shape=[
            like((tokens, model), BF16), like((tokens, model), BF16), like((tokens, model), BF16),
            like((slabs, 4, 36, 8, 128), F32), like((tokens, model), BF16),
            like((tokens, 128), F32), like((8, model), F32),
        ],
        compiler_params=pltpu.CompilerParams(vmem_limit_bytes=56 * MIB),
        name="norm_and_mix",
    )(x, cot, mask, order, mod, kern, bias)


def attend_kernel(mixed_ref, lat_ref, keep_ref, mod_ref, qkv_ref, proj_ref, projb_ref,
                  triple_ref, probs_ref, att_ref, branch_ref, middle_ref, n2_ref):
    model = lat_ref.shape[1]
    slabs = model // 128
    triple_ref[...] = dot_nn(mixed_ref[...], qkv_ref[...]).astype(BF16)
    lane = lax.broadcasted_iota(jnp.int32, (GROUP, 128), 1)
    left = lane < HEAD
    keep = jnp.concatenate([keep_ref[...]] * 2, axis=1)
    for s in range(slabs):
        q = triple_ref[:, s * 128 : s * 128 + 128]
        k = triple_ref[:, model + s * 128 : model + s * 128 + 128] * jnp.asarray(0.125, BF16)
        v = triple_ref[:, 2 * model + s * 128 : 2 * model + s * 128 + 128]
        outs = []
        for h in (0, 1):
            own = left if h == 0 else jnp.logical_not(left)
            scores = dot_nt(jnp.where(own, k, jnp.zeros_like(k)), q) + keep
            e = jnp.exp(scores - jnp.max(scores, axis=0, keepdims=True))
            p = (e * (1.0 / jnp.sum(e, axis=0, keepdims=True))).astype(BF16)
            probs_ref[2 * s + h] = p
            outs.append(dot_tn(p, v))
        att_ref[:, s * 128 : s * 128 + 128] = jnp.where(left, outs[0], outs[1]).astype(BF16)
    branch = dot_nn(att_ref[...], proj_ref[...]) + projb_ref[...]
    middle = lat_ref[...].astype(F32) + mod_ref[2:3, :] * branch
    unit, _ = unit_rows(middle)
    branch_ref[...] = branch
    middle_ref[...] = middle
    n2_ref[...] = (unit * (1.0 + mod_ref[4:5, :]) + mod_ref[3:4, :]).astype(BF16)


def attend(mixed, lat, keep, mod, qkv, proj, projb):
    tokens, model = lat.shape
    heads = model // HEAD
    by_group = lambda columns: pl.BlockSpec((GROUP, columns), lambda g: (g, 0))
    return pl.pallas_call(
        attend_kernel,
        grid=(4,),
        in_specs=[
            by_group(model), by_group(model), by_group(128), whole(mod.shape),
            once(qkv.shape), once(proj.shape), whole((1, model)),
        ],
        out_specs=[
            by_group(3 * model), pl.BlockSpec((heads, GROUP, GROUP), lambda g: (g, 0, 0)),
            by_group(model), by_group(model), by_group(model), by_group(model),
        ],
        out_shape=[
            like((tokens, 3 * model), BF16), like((4 * heads, GROUP, GROUP), BF16),
            like((tokens, model), BF16), like((tokens, model), F32),
            like((tokens, model), F32), like((tokens, model), BF16),
        ],
        compiler_params=pltpu.CompilerParams(vmem_limit_bytes=56 * MIB),
        name="attend",
    )(mixed, lat, keep, mod, qkv, proj, projb.astype(F32)[None, :])


def ff_kernel(n2_ref, n2t_ref, g2_ref, fc1_ref, fc1b_ref, kern_ref, dwb_ref, fc2_ref,
              branch_ref, gn2_ref, w1g_ref, w2g_ref, kg_ref, dwbg_ref, fc1bg_ref,
              hid, ga, gc, gcs, act, ghl):
    step = pl.program_id(0)
    slabs = hid.shape[0]

    @pl.when(step == 0)
    def _():
        branch_ref[...] = jnp.zeros_like(branch_ref)
        gn2_ref[...] = jnp.zeros_like(gn2_ref)
        for ref in (hid, gc, gcs):
            clear_edges(ref)

    for g in range(4):
        rows = pl.ds(g * GROUP, GROUP)
        full = dot_nn(n2_ref[rows, :], fc1_ref[...]) + fc1b_ref[...]
        back = dot_nt(g2_ref[rows, :], fc2_ref[...])
        for slab in range(slabs):
            lanes = slice(slab * 128, slab * 128 + 128)
            hid[slab, g, 2:34] = full[:, lanes].reshape(32, 8, 128)
            ga[slab, g] = back[:, lanes].reshape(32, 8, 128)

    masks = edge_masks()
    for slab in range(slabs):
        lanes = pl.ds(slab * 128, 128)
        k = [kern_ref[n, :, lanes] for n in range(9)]
        bias = dwb_ref[:, lanes]

        def forward(r, total):
            for gi in (0, 1):
                for gj in (0, 1):
                    pair = conv_cell(hid, slab, gi, gj, r, k, bias, masks)
                    acts, grads = [], []
                    for h in (0, 1):
                        x = pair[h]
                        x2 = x * x
                        half = 0.5 * jnp.tanh(x * (C0 + (C0 * C1) * x2)) + 0.5
                        value = x * half
                        slope = half + (value - value * half) * (2.0 * C0 + (6.0 * C0 * C1) * x2)
                        acts.append(value)
                        grads.append(ga[slab, 2 * gi + gj, 2 * r + h] * slope)
                        total = total + grads[-1]
                    act[group_rows(gi, gj, r), lanes] = jnp.concatenate(acts, 0).astype(BF16)
                    store_pair(gc, slab, gi, gj, r, grads)
                    store_pair(gcs, slab, gi, gj, r, shift_pair(grads, 1 - gj, *masks))
            return total

        dwbg_ref[:, lanes] = lax.fori_loop(0, HALF, forward, jnp.zeros((8, 128), F32))

        def put(gi, gj, r, pair):
            ghl[group_rows(gi, gj, r), lanes] = jnp.concatenate(pair, 0).astype(BF16)

        sums = conv_back(slab, k, hid, gc, gcs, put)
        for n in range(9):
            kg_ref[n, :, lanes] = sums[n]
        fc1bg_ref[:, lanes] = sums[9]

    branch_ref[...] += dot_nn(act[...], fc2_ref[...])
    gn2_ref[...] += dot_nt(ghl[...], fc1_ref[...])
    w2g_ref[...] = dot_tn(act[...], g2_ref[...]).astype(w2g_ref.dtype)
    w1g_ref[...] = dot_nn(n2t_ref[...], ghl[...]).astype(w1g_ref.dtype)


def feed_forward(n2, g2, fc1, fc1_bias, kern, dw_bias, fc2, width=256):
    tokens, model = n2.shape
    hidden = fc1.shape[1]
    slabs = width // 128
    fc1b = fc1_bias.astype(F32)[None, :]
    kern8 = jnp.broadcast_to(kern.astype(F32)[:, None, :], (9, 8, hidden))
    dwb8 = jnp.broadcast_to(dw_bias.astype(F32)[None, :], (8, hidden))
    padded = pltpu.VMEM((slabs, 4, 36, 8, 128), F32)
    columns = lambda rows: pl.BlockSpec((rows, width), lambda s: (0, s))
    out = pl.pallas_call(
        ff_kernel,
        grid=(hidden // width,),
        in_specs=[
            once((tokens, model)), once((model, tokens)), once((tokens, model)),
            columns(model), columns(1), pl.BlockSpec((9, 8, width), lambda s: (0, 0, s)),
            columns(8), pl.BlockSpec((width, model), lambda s: (s, 0)),
        ],
        out_specs=[
            whole((tokens, model)), whole((tokens, model)), columns(model),
            pl.BlockSpec((width, model), lambda s: (s, 0)),
            pl.BlockSpec((9, 8, width), lambda s: (0, 0, s)), columns(8), columns(8),
        ],
        out_shape=[
            like((tokens, model), F32), like((tokens, model), F32),
            like((model, hidden), BF16), like((hidden, model), BF16),
            like((9, 8, hidden), F32), like((8, hidden), F32), like((8, hidden), F32),
        ],
        scratch_shapes=[
            padded, pltpu.VMEM((slabs, 4, 32, 8, 128), F32), padded, padded,
            pltpu.VMEM((tokens, width), BF16), pltpu.VMEM((tokens, width), BF16),
        ],
        compiler_params=pltpu.CompilerParams(vmem_limit_bytes=56 * MIB),
        name="feed_forward",
    )(n2, n2.T, g2, fc1, fc1b, kern8, dwb8, fc2)
    branch, gn2, w1g, w2g, kg, dwbg, fc1bg = out
    return branch, gn2, w1g, w2g, kg.sum(1), dwbg.sum(0), fc1bg.sum(0)


def post_kernel(gn2_ref, two_ref, middle_ref, branch_ref, gout_ref, att_ref, triple_ref, probs_ref,
                mixed_ref, lat_ref, mod_ref, fc2b_ref, proj_ref, qkv_ref, normed_ref, kern_ref,
                order_ref,
                out_ref, xg_ref, sums_ref, qkvg_ref, projg_ref, kg_ref,
                gmid, gmix, gmoved, gnorm, out_rows, ga, gt, qkv_sum, proj_sum):
    step = pl.program_id(0)
    model = lat_ref.shape[1]
    slabs = model // 128

    @pl.when(step == 0)
    def _():
        clear_edges(gmix)
        clear_edges(gmoved)
        sums_ref[...] = jnp.zeros_like(sums_ref)
        qkv_sum[...] = jnp.zeros_like(qkv_sum)
        proj_sum[...] = jnp.zeros_like(proj_sum)

    @pl.when(step < 4)
    def _():
        rows = pl.ds(pl.multiple_of(step * GROUP, GROUP), GROUP)
        middle = middle_ref[...]
        two = two_ref[...] + fc2b_ref[...]
        gout = gout_ref[...].astype(F32)
        out_rows[rows, :] = (middle + mod_ref[5:6, :] * two).astype(BF16)
        sums_ref[5] += row_sum(gout * two)
        unit, scale = unit_rows(middle)
        gn2 = gn2_ref[...]
        sums_ref[3] += row_sum(gn2)
        sums_ref[4] += row_sum(gn2 * unit)
        gm = gout + unit_back(gn2 * (1.0 + mod_ref[4:5, :]), unit, scale)
        gmid[rows, :] = gm
        sums_ref[2] += row_sum(gm * branch_ref[...])
        gb = gm * mod_ref[2:3, :]
        sums_ref[6] += row_sum(gb)
        gbl = gb.astype(BF16)
        proj_sum[...] += dot_tn(att_ref[...], gbl)
        ga[...] = dot_nt(gbl, proj_ref[...]).astype(BF16)
        lane = lax.broadcasted_iota(jnp.int32, (GROUP, 128), 1)
        left = lane < HEAD
        for s in range(slabs):
            lanes = slice(s * 128, s * 128 + 128)
            q = triple_ref[:, s * 128 : s * 128 + 128] * jnp.asarray(0.125, BF16)
            k = triple_ref[:, model + s * 128 : model + s * 128 + 128] * jnp.asarray(0.125, BF16)
            v = triple_ref[:, 2 * model + s * 128 : 2 * model + s * 128 + 128]
            g = ga[:, lanes]
            gq = gk = gv = None
            for h in (0, 1):
                own = left if h == 0 else jnp.logical_not(left)
                mine = lambda value: jnp.where(own, value, jnp.zeros_like(value))
                p_low = probs_ref[2 * s + h]
                p = p_low.astype(F32)
                gh = mine(g)
                gp = dot_nt(v, gh)
                inner = jnp.sum(p * gp, axis=0, keepdims=True)
                gs = (p * (gp - inner)).astype(BF16)
                parts = (dot_tn(gs, mine(k)), dot_nn(gs, mine(q)), dot_nn(p_low, gh))
                if h == 0:
                    gq, gk, gv = parts
                else:
                    gq, gk, gv = gq + parts[0], gk + parts[1], gv + parts[2]
            gt[:, s * 128 : s * 128 + 128] = gq.astype(BF16)
            gt[:, model + s * 128 : model + s * 128 + 128] = gk.astype(BF16)
            gt[:, 2 * model + s * 128 : 2 * model + s * 128 + 128] = gv.astype(BF16)
        qkv_sum[...] += dot_tn(mixed_ref[...], gt[...])
        gmixed = dot_nt(gt[...], qkv_ref[...])
        for s in range(slabs):
            gmix[s, step, 2:34] = gmixed[:, s * 128 : s * 128 + 128].reshape(32, 8, 128)

    @pl.when(step == 4)
    def _():
        qkvg_ref[...] = qkv_sum[...].astype(BF16)
        projg_ref[...] = proj_sum[...].astype(BF16)
        masks = edge_masks()
        for s in range(slabs):
            lanes = pl.ds(s * 128, 128)
            k = [kern_ref[n, :, lanes] for n in range(9)]

            def move(r, total):
                for gi in (0, 1):
                    for gj in (0, 1):
                        pair = load_pair(gmix, s, gi, gj, r)
                        total = total + pair[0] + pair[1]
                        store_pair(gmoved, s, gi, gj, r, shift_pair(pair, 1 - gj, *masks))
                return total

            sums_ref[7, :, lanes] = lax.fori_loop(0, HALF, move, jnp.zeros((8, 128), F32))

            def put(gi, gj, r, pair):
                gnorm[group_rows(gi, gj, r), lanes] = jnp.concatenate(pair, 0)

            sums = conv_back(s, k, normed_ref, gmix, gmoved, put)
            for n in range(9):
                kg_ref[n, :, lanes] = sums[n]
            sums_ref[0, :, lanes] = sums[9]
        scale_sum = jnp.zeros((8, model), F32)
        for g in range(4):
            rows = pl.ds(g * GROUP, GROUP)
            unit, scale = unit_rows(lat_ref[rows, :].astype(F32))
            gn = gnorm[rows, :]
            scale_sum = scale_sum + row_sum(gn * unit)
            grad = gmid[rows, :] + unit_back(gn * (1.0 + mod_ref[1:2, :]), unit, scale)
            gnorm[rows, :] = grad
        sums_ref[1] = scale_sum
        for t in range(4):
            parts = [pl.ds(g * GROUP + 64 * t, 64) for g in range(4)]
            block = jnp.concatenate([out_rows[p, :] for p in parts], axis=0)
            out_ref[t * GROUP : t * GROUP + GROUP, :] = dot_tn(order_ref[...], block).astype(BF16)
            block = jnp.concatenate([gnorm[p, :].astype(BF16) for p in parts], axis=0)
            xg_ref[t * GROUP : t * GROUP + GROUP, :] = dot_tn(order_ref[...], block).astype(BF16)


def post(gn2, two, middle, branch, gout, att, triple, probs, mixed, lat, mod, fc2b, proj, qkv,
         normed, kern, order):
    tokens, model = lat.shape
    heads, slabs = model // HEAD, model // 128
    kern = jnp.broadcast_to(kern.astype(F32)[:, None, :], (9, 8, model))
    at = lambda g: jnp.minimum(g, 3)
    by_group = lambda columns: pl.BlockSpec((GROUP, columns), lambda g: (at(g), 0))
    padded = pltpu.VMEM((slabs, 4, 36, 8, 128), F32)
    return pl.pallas_call(
        post_kernel,
        grid=(5,),
        in_specs=[
            by_group(model), by_group(model), by_group(model), by_group(model), by_group(model),
            by_group(model), by_group(3 * model),
            pl.BlockSpec((heads, GROUP, GROUP), lambda g: (at(g), 0, 0)),
            by_group(model), once((tokens, model)), once(mod.shape), once((1, model)),
            once(proj.shape), once(qkv.shape), once(normed.shape), once(kern.shape),
            once(order.shape),
        ],
        out_specs=[
            once((tokens, model)), once((tokens, model)), once((8, 8, model)),
            once(qkv.shape), once(proj.shape), once(kern.shape),
        ],
        out_shape=[
            like((tokens, model), BF16), like((tokens, model), BF16), like((8, 8, model), F32),
            like(qkv.shape, BF16), like(proj.shape, BF16), like(kern.shape, F32),
        ],
        scratch_shapes=[
            pltpu.VMEM((tokens, model), F32), padded, padded, pltpu.VMEM((tokens, model), F32),
            pltpu.VMEM((tokens, model), BF16), pltpu.VMEM((GROUP, model), BF16),
            pltpu.VMEM((GROUP, 3 * model), BF16), pltpu.VMEM(qkv.shape, F32),
            pltpu.VMEM(proj.shape, F32),
        ],
        compiler_params=pltpu.CompilerParams(vmem_limit_bytes=62 * MIB),
        name="attend_back",
    )(gn2, two, middle, branch, gout, att, triple, probs, mixed, lat, mod,
      fc2b.astype(F32)[None, :], proj, qkv, normed, kern, order)


def flip(index, bit):
    return index + bit - 2 * bit * lax.rem(index // bit, 2)


def bits_of(count):
    return [1 << b for b in range(count.bit_length() - 1)]


def at(w, n):
    return {"wide": w, "narrow": n}


def greet(places):
    barrier = pltpu.get_barrier_semaphore()
    for place in places:
        pl.semaphore_signal(barrier, inc=1, device_id=place, device_id_type=pl.DeviceIdType.MESH)
    pl.semaphore_wait(barrier, len(places))


def greet_all(me, total, narrow):
    barrier = pltpu.get_barrier_semaphore()

    def body(k, carry):
        d = lax.rem(me + k, total)
        pl.semaphore_signal(
            barrier, inc=1, device_id=at(d // narrow, lax.rem(d, narrow)),
            device_id_type=pl.DeviceIdType.MESH,
        )
        return carry

    lax.fori_loop(1, total, body, 0)
    pl.semaphore_wait(barrier, total - 1)


def remote(src, dst, send_sem, recv_sem, place):
    return pltpu.make_async_remote_copy(
        src_ref=src, dst_ref=dst, send_sem=send_sem, recv_sem=recv_sem, device_id=place,
        device_id_type=pl.DeviceIdType.MESH,
    )


def sends_to_all(me, total, narrow, src_of, dst, send_sems, recv_sems):
    def copy(k):
        d = lax.rem(me + k, total)
        return remote(src_of(d), dst.at[me], send_sems.at[k], recv_sems.at[k],
                      at(d // narrow, lax.rem(d, narrow)))

    def start(k, carry):
        copy(k).start()
        return carry

    def wait(k, carry):
        copy(k).wait()
        return carry

    lax.fori_loop(1, total, start, 0)
    return lambda: lax.fori_loop(1, total, wait, 0)


def modulation_kernel(wide, narrow, sil_ref, weight_ref, bias_ref, mod_ref, sils_ref,
                      got, part, rows, send_a, recv_a, send_b, recv_b):
    total = wide * narrow
    me = lax.axis_index("wide") * narrow + lax.axis_index("narrow")
    greet_all(me, total, narrow)
    got[me] = sil_ref[me]
    sends_to_all(me, total, narrow, lambda d: sil_ref.at[d], got, send_a, recv_a)()
    sil = got[...].reshape(total, 128)
    sils_ref[...] = sil
    product = dot_nn(sil.astype(BF16), weight_ref[...]) + bias_ref[...]
    for d in range(total):
        part[d] = product[d : d + 1, :]
    rows[me] = part[me]
    sends_to_all(me, total, narrow, lambda d: part.at[d], rows, send_b, recv_b)()
    mod_ref[...] = jnp.sum(rows[...], axis=0)


def modulation(wide, narrow, sil, weight, bias):
    total, columns = wide * narrow, weight.shape[1]
    sems = pltpu.SemaphoreType.DMA((total,))
    return pl.pallas_call(
        functools.partial(modulation_kernel, wide, narrow),
        out_shape=[like((1, columns), F32), like((total, 128), F32)],
        scratch_shapes=[
            pltpu.VMEM((total, 1, 128), F32), pltpu.VMEM((total, 1, columns), F32),
            pltpu.VMEM((total, 1, columns), F32), sems, sems, sems, sems,
        ],
        compiler_params=pltpu.CompilerParams(
            vmem_limit_bytes=56 * MIB, collective_id=0, has_side_effects=True
        ),
        name="modulation",
    )(sil, weight, bias)


def modulation_back_kernel(wide, narrow, grad_ref, small_ref, sils_ref, weight_ref,
                           wgrad_ref, bgrad_ref, cond_ref, small_out,
                           rows, part, smalls, send_a, recv_a, send_b, recv_b, send_c, recv_c):
    total = wide * narrow
    me = lax.axis_index("wide") * narrow + lax.axis_index("narrow")
    greet_all(me, total, narrow)
    rows[me] = grad_ref[0]
    smalls[me] = small_ref[me]
    wait = sends_to_all(me, total, narrow, lambda d: grad_ref.at[0], rows, send_a, recv_a)
    wait_small = sends_to_all(me, total, narrow, lambda d: small_ref.at[d], smalls, send_c, recv_c)
    wait()
    grads = rows[...]
    bgrad_ref[...] = jnp.sum(grads, axis=0)
    low = grads.reshape(total, grads.shape[2]).astype(BF16)
    cond = dot_nt(low, weight_ref[...])
    for d in range(total):
        part[d] = cond[d : d + 1, :]
    cond_ref[me] = part[me]
    wait = sends_to_all(me, total, narrow, lambda d: part.at[d], cond_ref, send_b, recv_b)
    wgrad_ref[...] = dot_tn(sils_ref[...].astype(BF16), low)[: wgrad_ref.shape[0]]
    wait_small()
    small_out[...] = jnp.sum(smalls[...], axis=0)
    wait()


def modulation_back(wide, narrow, grad, small, sils, weight, owned):
    total, columns = wide * narrow, weight.shape[1]
    sems = pltpu.SemaphoreType.DMA((total,))
    return pl.pallas_call(
        functools.partial(modulation_back_kernel, wide, narrow),
        out_shape=[
            like((owned, columns), F32), like((1, columns), F32), like((total, 1, 128), F32),
            like(small.shape[1:], F32),
        ],
        scratch_shapes=[
            pltpu.VMEM((total, 1, columns), F32), pltpu.VMEM((total, 1, 128), F32),
            pltpu.VMEM(small.shape, F32), sems, sems, sems, sems, sems, sems,
        ],
        compiler_params=pltpu.CompilerParams(
            vmem_limit_bytes=56 * MIB, collective_id=1, has_side_effects=True
        ),
        name="modulation_back",
    )(grad, small, sils, weight)


def partners(wide, narrow, w, n):
    places = [at(w, lax.rem(n + k, narrow)) for k in range(1, narrow)]
    return places + [at(flip(w, bit), n) for bit in bits_of(wide)]


class Gather:
    def __init__(self, wide, narrow, src, dst, sends, recvs, chunk, turn, columns):
        self.w, self.n = lax.axis_index("wide"), lax.axis_index("narrow")
        self.wide, self.narrow = wide, narrow
        self.src, self.dst = src, dst
        self.sends, self.recvs, self.chunk = sends, recvs, chunk
        self.columns = columns
        far = bits_of(wide)[1:]
        cut = turn % len(far) if far else 0
        self.order = far[cut:] + far[:cut] + bits_of(wide)[:1]
        self.stages = 1 + len(self.order)

    def copies(self, stage):
        place = lambda ref, *index: ref.at[(*index, slice(None), self.columns)]
        if stage == 0:
            return [
                remote(place(self.src), place(self.dst, self.w, self.n),
                       self.sends.at[self.chunk, k - 1], self.recvs.at[self.chunk, k - 1],
                       at(self.w, lax.rem(self.n + k, self.narrow)))
                for k in range(1, self.narrow)
            ]
        held = [self.w]
        for bit in self.order[: stage - 1]:
            held = held + [flip(h, bit) for h in held]
        base = self.narrow - 2 + len(held)
        place = lambda h: self.dst.at[h, :, :, self.columns]
        return [
            remote(place(h), place(h), self.sends.at[self.chunk, base + i],
                   self.recvs.at[self.chunk, base + i], at(flip(self.w, self.order[stage - 1]), self.n))
            for i, h in enumerate(held)
        ]

    def start(self, stage):
        for copy in self.copies(stage):
            copy.start()

    def wait(self, stage):
        for copy in self.copies(stage):
            copy.wait_recv()

    def finish(self):
        for stage in range(self.stages):
            for copy in self.copies(stage):
                copy.wait_send()


def gather_kernel(wide, narrow, chunks, count, *refs):
    srcs, dsts = refs[:count], refs[count : 2 * count]
    sends, recvs, locals_ = refs[2 * count :]
    w, n = lax.axis_index("wide"), lax.axis_index("narrow")
    own = [pltpu.make_async_copy(srcs[i], dsts[i].at[w, n], locals_.at[i]) for i in range(count)]
    for copy in own:
        copy.start()
    greet(partners(wide, narrow, w, n))
    jobs = [
        Gather(wide, narrow, srcs[i], dsts[i], sends, recvs, c, c, pl.ds(at_, size))
        for c, (i, at_, size) in enumerate(chunks)
    ]
    stages = jobs[0].stages
    for wave in range(len(jobs) + stages):
        for c, job in enumerate(jobs):
            stage = wave - c
            if stage == 1 and c == 0:
                for copy in own:
                    copy.wait()
            if 1 <= stage <= stages:
                job.wait(stage - 1)
            if 0 <= stage < stages:
                job.start(stage)
    for job in jobs:
        job.finish()


def gather(wide, narrow, blocks, chunks):
    count = len(blocks)
    sems = pltpu.SemaphoreType.DMA((len(chunks), narrow + wide - 2))
    anywhere = pl.BlockSpec(memory_space=pl.ANY)
    return pl.pallas_call(
        functools.partial(gather_kernel, wide, narrow, chunks, count),
        in_specs=[anywhere] * count,
        out_specs=[anywhere] * count,
        out_shape=[like((wide, narrow) + b.shape, b.dtype) for b in blocks],
        scratch_shapes=[sems, sems, pltpu.SemaphoreType.DMA((count,))],
        compiler_params=pltpu.CompilerParams(collective_id=2, has_side_effects=True),
        name="gather",
    )(*blocks)


def insert_bit(index, position, value):
    low = index % (1 << position)
    return ((index // (1 << position)) * 2 + value) * (1 << position) + low


class Scatter:
    def __init__(self, wide, narrow, src, halves, line, got, sends, recvs, chunk, turn, columns):
        self.w, self.n = lax.axis_index("wide"), lax.axis_index("narrow")
        self.wide, self.narrow = wide, narrow
        self.src, self.halves, self.line, self.got = src, halves, line, got
        self.sends, self.recvs, self.chunk = sends, recvs, chunk
        self.columns = columns
        far = bits_of(wide)[1:]
        cut = turn % len(far) if far else 0
        self.order = bits_of(wide)[:1] + far[cut:] + far[:cut]
        self.stages = 1 + len(self.order)
        self.rows = line.shape[1]

    def level(self, stage):
        source = self.src if stage == 0 else self.halves[stage - 1]
        bit = self.order[stage]
        position = sum(1 for b in bits_of(self.wide) if b < bit and b not in self.order[:stage])
        return source, bit, position, self.wide >> (stage + 1)

    def copies(self, stage):
        if stage == len(self.order):
            base = self.wide - 1
            return [
                remote(self.line.at[lax.rem(self.n + k, self.narrow), :, self.columns],
                       self.got.at[k - 1, :, self.columns],
                       self.sends.at[self.chunk, base + k - 1], self.recvs.at[self.chunk, base + k - 1],
                       at(self.w, lax.rem(self.n + k, self.narrow)))
                for k in range(1, self.narrow)
            ]
        source, bit, position, size = self.level(stage)
        theirs = 1 - lax.rem(self.w // bit, 2)
        base = self.wide - 2 * size
        return [
            remote(source.at[insert_bit(j, position, theirs), :, self.columns],
                   self.halves[stage].at[j, :, self.columns],
                   self.sends.at[self.chunk, base + j], self.recvs.at[self.chunk, base + j],
                   at(flip(self.w, bit), self.n))
            for j in range(size)
        ]

    def start(self, stage):
        for copy in self.copies(stage):
            copy.start()

    def wait(self, stage):
        for copy in self.copies(stage):
            copy.wait()

    def add(self, stage):
        if stage == len(self.order):
            return
        source, bit, position, size = self.level(stage)
        mine = lax.rem(self.w // bit, 2)
        into = self.halves[stage]
        last = stage == len(self.order) - 1
        for j in range(size):
            index = insert_bit(j, position, mine)
            if last:
                both = (source[index, :, self.columns].astype(F32)
                        + into[j, :, self.columns].astype(F32))
                for m in range(self.narrow):
                    self.line[m, :, self.columns] = both[m * self.rows : (m + 1) * self.rows].astype(BF16)
            else:
                def body(i, carry):
                    rows = pl.ds(pl.multiple_of(i * 16, 16), 16)
                    into[j, rows, self.columns] = (
                        source[index, rows, self.columns].astype(F32)
                        + into[j, rows, self.columns].astype(F32)
                    ).astype(BF16)
                    return carry

                lax.fori_loop(0, into.shape[1] // 16, body, 0)

    def result(self, out):
        value = self.line[self.n, :, self.columns].astype(F32)
        for k in range(1, self.narrow):
            value = value + self.got[k - 1, :, self.columns].astype(F32)
        out[:, self.columns] = value


def scatter_kernel(wide, narrow, chunks, count, levels, *refs):
    srcs, outs = refs[:count], refs[count : 2 * count]
    rest = refs[2 * count :]
    sends, recvs = rest[-2:]
    per = levels + 2
    w, n = lax.axis_index("wide"), lax.axis_index("narrow")
    greet(partners(wide, narrow, w, n))
    jobs = []
    for c, (i, start, size) in enumerate(chunks):
        own = rest[i * per : (i + 1) * per]
        jobs.append(Scatter(wide, narrow, srcs[i], own[:levels], own[levels], own[levels + 1],
                            sends, recvs, c, c, pl.ds(start, size)))
    stages = jobs[0].stages
    for wave in range(len(jobs) + stages):
        for c, job in enumerate(jobs):
            stage = wave - c
            if 1 <= stage <= stages:
                job.wait(stage - 1)
                job.add(stage - 1)
            if 0 <= stage < stages:
                job.start(stage)
            if stage == stages:
                job.result(outs[chunks[c][0]])


def scatter(wide, narrow, arrays, chunks):
    count, levels = len(arrays), len(bits_of(wide))
    sems = pltpu.SemaphoreType.DMA((len(chunks), narrow + wide - 2))
    scratch, outs = [], []
    for a in arrays:
        _, height, columns = a.shape
        rows = height // narrow
        for stage in range(levels):
            scratch.append(pltpu.VMEM((wide >> (stage + 1), height, columns), BF16))
        scratch.append(pltpu.VMEM((narrow, rows, columns), BF16))
        scratch.append(pltpu.VMEM((narrow - 1, rows, columns), BF16))
        outs.append(like((rows, columns), F32))
    return pl.pallas_call(
        functools.partial(scatter_kernel, wide, narrow, chunks, count, levels),
        out_shape=outs,
        scratch_shapes=scratch + [sems, sems],
        compiler_params=pltpu.CompilerParams(
            vmem_limit_bytes=60 * MIB, collective_id=3, has_side_effects=True
        ),
        name="scatter",
    )(*arrays)


def smooth_gate(values):
    return values * jax.nn.sigmoid(values)


def on_device(wide, narrow, latents, condition, valid_mask, ada_weight, ada_bias, dw1_kernel, dw1_bias,
              qkv_weight, proj_weight, proj_bias, fc1_weight, fc1_bias, dw2_kernel, dw2_bias,
              fc2_weight, fc2_bias, out_cotangent):
    total = wide * narrow
    me = lax.axis_index("wide") * narrow + lax.axis_index("narrow")
    model = latents.shape[2]
    hidden = fc1_weight.shape[1]
    own, own_ff = model // total, hidden // total

    sil, silu_back = jax.vjp(smooth_gate, condition[0].astype(F32))
    sil = sil.astype(BF16).astype(F32).reshape(total, 1, own)
    sil = jnp.pad(sil, ((0, 0), (0, 0), (0, 128 - own)))
    ada_rows = jnp.pad(ada_weight, ((0, 128 - own), (0, 0)))
    bias_at = lax.dynamic_update_slice(
        jnp.zeros((1, 6 * model), F32), ada_bias.astype(F32)[None, :], (0, me * ada_bias.shape[0])
    )
    mod, sils = modulation(wide, narrow, sil, ada_rows, bias_at)
    mod = mod.reshape(6, model)

    small = jnp.concatenate([
        jnp.concatenate([dw1_kernel, dw1_bias[None], proj_bias[None], fc2_bias[None]]).reshape(-1),
        jnp.concatenate([dw2_kernel, dw2_bias[None], fc1_bias[None]]).reshape(-1),
    ])
    lines = -(-small.shape[0] // 2048) * 16
    small = jnp.pad(small, (0, lines * 128 - small.shape[0])).reshape(lines, 128)
    blocks = [small, qkv_weight, proj_weight, fc1_weight, fc2_weight]
    chunks = [(0, 0, 128), (1, 0, 1152), (1, 1152, 1152), (2, 0, 768), (3, 0, 1536), (4, 0, 384),
              (3, 1536, 1536), (4, 384, 384)]
    small, qkv, proj, fc1, fc2 = gather(wide, narrow, blocks, chunks)
    qkv, proj = qkv.reshape(model, 3 * model), proj.reshape(model, model)
    fc1, fc2 = fc1.reshape(model, hidden), fc2.reshape(hidden, model)
    small = small.reshape(total, lines * 128)
    narrow_part = small[:, : 12 * own].reshape(total, 12, own).transpose(1, 0, 2).reshape(12, model)
    wide_part = small[:, 12 * own : 12 * own + 11 * own_ff]
    wide_part = wide_part.reshape(total, 11, own_ff).transpose(1, 0, 2).reshape(11, hidden)
    dw1k, dw1b, projb, fc2b = narrow_part[:9], narrow_part[9], narrow_part[10], narrow_part[11]
    dw2k, dw2b, fc1b = wide_part[:9], wide_part[9], wide_part[10]

    order = order_matrix()
    lat, gout, g2, normed, mixed, keep, fc2bg = pre(
        latents[0], out_cotangent[0], valid_mask[0], order, mod, dw1k, dw1b
    )
    triple, probs, att, branch, middle, n2 = attend(mixed, lat, keep, mod, qkv, proj, projb)
    two, gn2, w1g, w2g, kg2, dwb2, fc1bg = feed_forward(n2, g2, fc1, fc1b, dw2k, dw2b, fc2)
    out, xg, sums, qkvg, projg, kg1 = post(
        gn2, two, middle, branch, gout, att, triple, probs, mixed, lat, mod, fc2b, proj, qkv,
        normed, dw1k, order
    )
    sums = sums.sum(1)
    grad_mod = sums[:6].reshape(1, 1, 6 * model)
    narrow_part = jnp.concatenate([kg1.sum(1), sums[7][None], sums[6][None], fc2bg.sum(0)[None]])
    wide_part = jnp.concatenate([kg2, dwb2[None], fc1bg[None]])
    small = jnp.concatenate([
        narrow_part.reshape(12, total, own).transpose(1, 0, 2).reshape(total, 12 * own),
        wide_part.reshape(11, total, own_ff).transpose(1, 0, 2).reshape(total, 11 * own_ff),
    ], axis=1)
    small = jnp.pad(small, ((0, 0), (0, -small.shape[1] % 128)))
    ada_wgrad, ada_bsum, cond, small = modulation_back(
        wide, narrow, grad_mod, small[:, None], sils, ada_rows, own
    )
    ada_bgrad = lax.dynamic_slice(ada_bsum[0], (me * ada_bias.shape[0],), ada_bias.shape)
    (cond_grad,) = silu_back(cond[:, 0, :own].reshape(model))

    narrow_part = small[0, : 12 * own].reshape(12, own)
    wide_part = small[0, 12 * own : 12 * own + 11 * own_ff].reshape(11, own_ff)

    as_lines = lambda grad: grad.reshape(wide, grad.shape[0] // wide, grad.shape[1])
    chunks = [(0, 0, 384), (1, 0, 1536), (0, 384, 384), (1, 1536, 1536), (3, 0, 768), (2, 0, 1152),
              (2, 1152, 1152)]
    fc2g, fc1g, qkvg, projg = scatter(
        wide, narrow, [as_lines(w2g), as_lines(w1g), as_lines(qkvg), as_lines(projg)], chunks
    )
    return (
        out[None], xg[None], cond_grad[None], ada_wgrad, ada_bgrad,
        narrow_part[:9], narrow_part[9], qkvg, projg, narrow_part[10], fc1g, wide_part[10],
        wide_part[:9], wide_part[9], fc2g, narrow_part[11],
    )


def solution(mesh):
    wide, narrow = mesh.shape["wide"], mesh.shape["narrow"]
    rows = lambda rank: P(AXES, *(None,) * (rank - 1))
    lanes = P(None, AXES)
    in_specs = (
        rows(3), rows(2), rows(2), rows(2), rows(1), lanes, rows(1), rows(2), rows(2), rows(1),
        rows(2), rows(1), lanes, rows(1), rows(2), rows(1), rows(3),
    )
    out_specs = (
        rows(3), rows(3), rows(2), rows(2), rows(1), lanes, rows(1), rows(2), rows(2), rows(1),
        rows(2), rows(1), lanes, rows(1), rows(2), rows(1),
    )
    return jax.shard_map(
        functools.partial(on_device, wide, narrow), mesh=mesh, in_specs=in_specs,
        out_specs=out_specs, check_vma=False,
    )
```

```python
import functools

import jax
import jax.numpy as jnp
from jax import lax
from jax.experimental import pallas as pl
from jax.experimental.pallas import tpu as pltpu
from jax.sharding import PartitionSpec as P

HEAD = 64
GRID = 32
HALF = 16
GROUP = 256
TOKENS = 1024
C0 = 0.7978845608028654
C1 = 0.044715
EPS = 1e-06
MIB = 1 << 20
AXES = ("wide", "narrow")
F32, BF16 = jnp.float32, jnp.bfloat16


def dot_nn(a, b):
    return lax.dot_general(a, b, (((1,), (0,)), ((), ())), preferred_element_type=F32)


def dot_nt(a, b):
    return lax.dot_general(a, b, (((1,), (1,)), ((), ())), preferred_element_type=F32)


def dot_tn(a, b):
    return lax.dot_general(a, b, (((0,), (0,)), ((), ())), preferred_element_type=F32)


def whole(shape):
    return pl.BlockSpec(shape, lambda *_: (0,) * len(shape))


def once(shape):
    return pl.BlockSpec(shape, lambda *_: (0,) * len(shape), pipeline_mode=pl.Buffered(1))


def like(shape, dtype):
    return jax.ShapeDtypeStruct(shape, dtype)


def shift_pair(pair, parity, first, last):
    low, high = pair
    zero = jnp.zeros_like(low)
    if parity == 0:
        low, high = pltpu.roll(low, 1, 0), pltpu.roll(high, 1, 0)
        return jnp.where(first, zero, low), jnp.where(first, low, high)
    low, high = pltpu.roll(low, 7, 0), pltpu.roll(high, 7, 0)
    return jnp.where(last, high, low), jnp.where(last, zero, high)


def row_sources(gi, r):
    if gi == 0:
        return ((1, r - 1), (0, r), (1, r))
    return ((0, r), (1, r), (0, r + 1))


def load_pair(ref, slab, gi, gj, r):
    tile = 2 + 2 * r
    group = 2 * gi + gj
    return ref[slab, group, tile], ref[slab, group, tile + 1]


def store_pair(ref, slab, gi, gj, r, pair):
    tile = 2 + 2 * r
    group = 2 * gi + gj
    ref[slab, group, tile] = pair[0]
    ref[slab, group, tile + 1] = pair[1]


def edge_masks():
    sub = lax.broadcasted_iota(jnp.int32, (8, 128), 0)
    return sub == 0, sub == 7


def clear_edges(ref):
    slabs = ref.shape[0]
    ref[:, :, 0:2] = jnp.zeros((slabs, 4, 2, 8, 128), F32)
    ref[:, :, 34:36] = jnp.zeros((slabs, 4, 2, 8, 128), F32)


def conv_cell(src, slab, gi, gj, r, k, bias, masks):
    sources = row_sources(gi, r)
    other = 1 - gj
    near = 2 if gj == 0 else 0
    far = 2 - near
    same = [load_pair(src, slab, p, gj, rr) for p, rr in sources]
    cross = [load_pair(src, slab, p, other, rr) for p, rr in sources]
    straight, moved = [], []
    for h in (0, 1):
        acc, off = bias, None
        for a in range(3):
            acc = acc + k[3 * a + 1] * same[a][h] + k[3 * a + near] * cross[a][h]
            term = k[3 * a + far] * cross[a][h]
            off = term if off is None else off + term
        straight.append(acc)
        moved.append(off)
    moved = shift_pair(moved, gj, *masks)
    return straight[0] + moved[0], straight[1] + moved[1]


def conv_back_row(slab, k, src, grad, grad_moved, put, r, carry):
    kg, total = list(carry[:9]), carry[9]
    for gi in (0, 1):
        sources = row_sources(gi, r)
        for gj in (0, 1):
            other = 1 - gj
            near = 2 if gj == 0 else 0
            here = load_pair(src, slab, gi, gj, r)
            out = [None, None]
            for a in range(3):
                p, rr = sources[2 - a]
                trio = {
                    1: load_pair(grad, slab, p, gj, rr),
                    2 - near: load_pair(grad, slab, p, other, rr),
                    near: load_pair(grad_moved, slab, p, other, rr),
                }
                for b in range(3):
                    n = 3 * a + b
                    for h in (0, 1):
                        term = k[n] * trio[b][h]
                        out[h] = term if out[h] is None else out[h] + term
                        kg[n] = kg[n] + here[h] * trio[b][h]
            total = total + out[0] + out[1]
            put(gi, gj, r, out)
    return tuple(kg) + (total,)


def conv_back(slab, k, src, grad, grad_moved, put):
    body = lambda r, carry: conv_back_row(slab, k, src, grad, grad_moved, put, r, carry)
    return lax.fori_loop(0, HALF, body, (jnp.zeros((8, 128), F32),) * 10)


def group_rows(gi, gj, r):
    return pl.ds(pl.multiple_of((2 * gi + gj) * GROUP + r * HALF, HALF), HALF)


def row_sum(values):
    rows, columns = values.shape
    return jnp.sum(values.reshape(rows // 8, 8, columns), axis=0)


def unit_rows(values):
    model = values.shape[-1]
    centered = values - jnp.sum(values, axis=-1, keepdims=True) * (1.0 / model)
    spread = jnp.sum(centered * centered, axis=-1, keepdims=True) * (1.0 / model)
    scale = lax.rsqrt(spread + EPS)
    return centered * scale, scale


def unit_back(grad, unit, scale):
    model = grad.shape[-1]
    mean = jnp.sum(grad, axis=-1, keepdims=True) * (1.0 / model)
    tilt = jnp.sum(grad * unit, axis=-1, keepdims=True) * (1.0 / model)
    return scale * (grad - mean - unit * tilt)


def order_matrix():
    d = jnp.arange(GROUP)
    group, position, column = d // 64, (d % 64) // HALF, d % HALF
    source = (2 * position + group // 2) * GRID + 2 * column + group % 2
    return (source[:, None] == jnp.arange(GROUP)[None, :]).astype(BF16)


def ff_kernel(n2_ref, n2t_ref, g2_ref, fc1_ref, small_ref, fc2_ref,
              branch_ref, gn2_ref, w1g_ref, w2g_ref, sums_ref,
              hid, ga, gc, gcs, act, ghl):
    step = pl.program_id(0)
    slabs = hid.shape[0]

    @pl.when(step == 0)
    def _():
        branch_ref[...] = jnp.zeros_like(branch_ref)
        gn2_ref[...] = jnp.zeros_like(gn2_ref)
        for ref in (hid, gc, gcs):
            clear_edges(ref)

    for g in range(4):
        rows = pl.ds(g * GROUP, GROUP)
        full = dot_nn(n2_ref[rows, :], fc1_ref[...]) + small_ref[10:11, :]
        back = dot_nt(g2_ref[rows, :], fc2_ref[...])
        for slab in range(slabs):
            lanes = slice(slab * 128, slab * 128 + 128)
            hid[slab, g, 2:34] = full[:, lanes].reshape(32, 8, 128)
            ga[slab, g] = back[:, lanes].reshape(32, 8, 128)

    masks = edge_masks()
    for slab in range(slabs):
        lanes = pl.ds(slab * 128, 128)
        k = [jnp.broadcast_to(small_ref[n : n + 1, lanes], (8, 128)) for n in range(9)]
        bias = jnp.broadcast_to(small_ref[9:10, lanes], (8, 128))

        def forward(r, total):
            for gi in (0, 1):
                for gj in (0, 1):
                    pair = conv_cell(hid, slab, gi, gj, r, k, bias, masks)
                    acts, grads = [], []
                    for h in (0, 1):
                        x = pair[h]
                        x2 = x * x
                        half = 0.5 * jnp.tanh(x * (C0 + (C0 * C1) * x2)) + 0.5
                        value = x * half
                        slope = half + (value - value * half) * (2.0 * C0 + (6.0 * C0 * C1) * x2)
                        acts.append(value)
                        grads.append(ga[slab, 2 * gi + gj, 2 * r + h] * slope)
                        total = total + grads[-1]
                    act[group_rows(gi, gj, r), lanes] = jnp.concatenate(acts, 0).astype(BF16)
                    store_pair(gc, slab, gi, gj, r, grads)
                    store_pair(gcs, slab, gi, gj, r, shift_pair(grads, 1 - gj, *masks))
            return total

        total = lax.fori_loop(0, HALF, forward, jnp.zeros((8, 128), F32))

        def put(gi, gj, r, pair):
            ghl[group_rows(gi, gj, r), lanes] = jnp.concatenate(pair, 0).astype(BF16)

        sums = conv_back(slab, k, hid, gc, gcs, put)
        for n, value in enumerate([*sums[:9], total, sums[9]]):
            sums_ref[n : n + 1, lanes] = jnp.sum(value, axis=0, keepdims=True)
        sums_ref[11:16, lanes] = jnp.zeros((5, 128), F32)

    branch_ref[...] += dot_nn(act[...], fc2_ref[...])
    gn2_ref[...] += dot_nt(ghl[...], fc1_ref[...])
    w2g_ref[...] = dot_tn(act[...], g2_ref[...]).astype(w2g_ref.dtype)
    w1g_ref[...] = dot_nn(n2t_ref[...], ghl[...]).astype(w1g_ref.dtype)


def feed_forward(n2, g2, fc1, small, fc2, width=256):
    tokens, model = n2.shape
    hidden = fc1.shape[1]
    slabs = width // 128
    padded = pltpu.VMEM((slabs, 4, 36, 8, 128), F32)
    columns = lambda rows: pl.BlockSpec((rows, width), lambda s: (0, s))
    lines = pl.BlockSpec((width, model), lambda s: (s, 0))
    return pl.pallas_call(
        ff_kernel,
        grid=(hidden // width,),
        in_specs=[
            once((tokens, model)), once((model, tokens)), once((tokens, model)),
            columns(model), columns(16), lines,
        ],
        out_specs=[whole((tokens, model)), whole((tokens, model)), columns(model), lines, columns(16)],
        out_shape=[
            like((tokens, model), F32), like((tokens, model), F32),
            like((model, hidden), BF16), like((hidden, model), BF16), like((16, hidden), F32),
        ],
        scratch_shapes=[
            padded, pltpu.VMEM((slabs, 4, 32, 8, 128), F32), padded, padded,
            pltpu.VMEM((tokens, width), BF16), pltpu.VMEM((tokens, width), BF16),
        ],
        compiler_params=pltpu.CompilerParams(vmem_limit_bytes=56 * MIB),
        name="feed_forward",
    )(n2, n2.T, g2, fc1, small, fc2)


def flip(index, bit):
    return index + bit - 2 * bit * lax.rem(index // bit, 2)


def bits_of(count):
    return [1 << b for b in range(count.bit_length() - 1)]


def at(w, n):
    return {"wide": w, "narrow": n}


def greet(places):
    barrier = pltpu.get_barrier_semaphore()
    for place in places:
        pl.semaphore_signal(barrier, inc=1, device_id=place, device_id_type=pl.DeviceIdType.MESH)
    pl.semaphore_wait(barrier, len(places))


def greet_all(place):
    barrier = pltpu.get_barrier_semaphore()
    total = place.total

    def body(k, carry):
        pl.semaphore_signal(
            barrier, inc=1, device_id=place.device(lax.rem(place.sid + k, total)),
            device_id_type=pl.DeviceIdType.MESH,
        )
        return carry

    lax.fori_loop(1, total, body, 0)
    pl.semaphore_wait(barrier, total - 1)


def remote(src, dst, send_sem, recv_sem, place):
    return pltpu.make_async_remote_copy(
        src_ref=src, dst_ref=dst, send_sem=send_sem, recv_sem=recv_sem, device_id=place,
        device_id_type=pl.DeviceIdType.MESH,
    )


class Place:
    def __init__(self, wide, narrow):
        self.wide, self.narrow = wide, narrow
        self.w, self.n = lax.axis_index("wide"), lax.axis_index("narrow")
        self.total, self.half = wide * narrow, wide * narrow // 2
        self.me = self.w * narrow + self.n
        self.core = lax.rem(self.w, 2)
        self.slot = (self.w // 2) * narrow + self.n
        self.sid = self.core * self.half + self.slot
        self.sibling = at(flip(self.w, 1), self.n)

    def device(self, sid):
        core, slot = sid // self.half, lax.rem(sid, self.half)
        return at(2 * (slot // self.narrow) + core, lax.rem(slot, self.narrow))

    def partners(self):
        places = [at(self.w, lax.rem(self.n + k, self.narrow)) for k in range(1, self.narrow)]
        return places + [at(flip(self.w, bit), self.n) for bit in bits_of(self.wide)]

    def to_all(self, src_of, dst, sends, recvs):
        def copy(k):
            sid = lax.rem(self.sid + k, self.total)
            return remote(src_of(sid), dst, sends.at[k], recvs.at[k], self.device(sid))

        return exchange(copy, self.total)

    def to_kin(self, src_of, dst, sends, recvs):
        def copy(k):
            slot = lax.rem(self.slot + k, self.half)
            return remote(src_of(slot), dst, sends.at[k], recvs.at[k],
                          self.device(self.core * self.half + slot))

        return exchange(copy, self.half)


def exchange(copy, count):
    def start(k, carry):
        copy(k).start()
        return carry

    def wait(k, carry):
        copy(k).wait()
        return carry

    lax.fori_loop(1, count, start, 0)
    return lambda: lax.fori_loop(1, count, wait, 0)


class Gather:
    def __init__(self, place, src, dst, sends, recvs, chunk, turn, columns):
        self.p = place
        self.src, self.dst = src, dst
        self.sends, self.recvs, self.chunk = sends, recvs, chunk
        self.columns = columns
        far = bits_of(place.wide)[1:]
        cut = turn % len(far) if far else 0
        self.order = far[cut:] + far[:cut] + bits_of(place.wide)[:1]
        self.stages = 1 + len(self.order)

    def copies(self, stage):
        w, n, narrow = self.p.w, self.p.n, self.p.narrow
        if stage == 0:
            return [
                remote(self.src.at[:, self.columns], self.dst.at[w, n, :, self.columns],
                       self.sends.at[self.chunk, k - 1], self.recvs.at[self.chunk, k - 1],
                       at(w, lax.rem(n + k, narrow)))
                for k in range(1, narrow)
            ]
        held = [w]
        for bit in self.order[: stage - 1]:
            held = held + [flip(h, bit) for h in held]
        base = narrow - 2 + len(held)
        part = lambda h: self.dst.at[h, :, :, self.columns]
        return [
            remote(part(h), part(h), self.sends.at[self.chunk, base + i],
                   self.recvs.at[self.chunk, base + i], at(flip(w, self.order[stage - 1]), n))
            for i, h in enumerate(held)
        ]

    def start(self, stage):
        for copy in self.copies(stage):
            copy.start()

    def wait(self, stage):
        for copy in self.copies(stage):
            copy.wait_recv()

    def finish(self):
        for stage in range(self.stages):
            for copy in self.copies(stage):
                copy.wait_send()


class Waves:
    def __init__(self, chunks):
        self.chunks, self.wave = chunks, 0
        self.stages = chunks[0][0].stages
        self.count = len(chunks) + self.stages

    def run(self, wave):
        for c, jobs in enumerate(self.chunks):
            stage = wave - c
            for job in jobs:
                if 1 <= stage <= self.stages:
                    job.wait(stage - 1)
                if 0 <= stage < self.stages:
                    job.start(stage)

    def tick(self, times=1):
        for _ in range(times):
            if self.wave < self.count:
                self.run(self.wave)
                self.wave += 1

    def at_hook(self, hook, hooks):
        left = self.count - 1
        for wave in range(1 + hook * left // hooks, 1 + (hook + 1) * left // hooks):
            self.run(wave)

    def finish(self):
        for jobs in self.chunks:
            for job in jobs:
                job.finish()

    def end(self):
        self.tick(self.count)
        self.finish()


def slots_of(chunks):
    return sum(len(chunk) for chunk in chunks)


def job_sems(wide, narrow, chunks):
    return [pltpu.SemaphoreType.DMA((slots_of(chunks), narrow + wide - 2))] * 2


def gather_jobs(place, srcs, dsts, sends, recvs, chunks):
    jobs, slot = [], 0
    for chunk in chunks:
        jobs.append([])
        for i, start, size, turn in chunk:
            jobs[-1].append(
                Gather(place, srcs[i], dsts[i], sends, recvs, slot, turn, pl.ds(start, size))
            )
            slot += 1
    return Waves(jobs)


def both(i, start, size):
    return [(i, start + turn * (size // 2), size // 2, turn) for turn in (0, 1)]


def insert_bit(index, position, value):
    low = index % (1 << position)
    return ((index // (1 << position)) * 2 + value) * (1 << position) + low


class Scatter:
    def __init__(self, place, src, buffers, out, sends, recvs, chunk, turn, columns):
        self.p = place
        self.src, self.out = src, out
        self.halves, self.line, self.got = buffers[:-2], buffers[-2], buffers[-1]
        self.sends, self.recvs, self.chunk = sends, recvs, chunk
        self.columns = columns
        far = bits_of(place.wide)[1:]
        cut = turn % len(far) if far else 0
        self.order = bits_of(place.wide)[:1] + far[cut:] + far[:cut]
        self.stages = 1 + len(self.order)
        self.rows = self.line.shape[1]

    def level(self, stage):
        source = self.src if stage == 0 else self.halves[stage - 1]
        bit = self.order[stage]
        wide = self.p.wide
        position = sum(1 for b in bits_of(wide) if b < bit and b not in self.order[:stage])
        return source, bit, position, wide >> (stage + 1)

    def copies(self, stage):
        w, n, narrow = self.p.w, self.p.n, self.p.narrow
        if stage == len(self.order):
            base = self.p.wide - 1
            return [
                remote(self.line.at[lax.rem(n + k, narrow), :, self.columns],
                       self.got.at[k - 1, :, self.columns],
                       self.sends.at[self.chunk, base + k - 1], self.recvs.at[self.chunk, base + k - 1],
                       at(w, lax.rem(n + k, narrow)))
                for k in range(1, narrow)
            ]
        source, bit, position, size = self.level(stage)
        theirs = 1 - lax.rem(w // bit, 2)
        base = self.p.wide - 2 * size
        return [
            remote(source.at[insert_bit(j, position, theirs), :, self.columns],
                   self.halves[stage].at[j, :, self.columns],
                   self.sends.at[self.chunk, base + j], self.recvs.at[self.chunk, base + j],
                   at(flip(w, bit), n))
            for j in range(size)
        ]

    def start(self, stage):
        for copy in self.copies(stage):
            copy.start()

    def wait(self, stage):
        for copy in self.copies(stage):
            copy.wait()
        if stage == len(self.order):
            value = self.line[self.p.n, :, self.columns].astype(F32)
            for k in range(1, self.p.narrow):
                value = value + self.got[k - 1, :, self.columns].astype(F32)
            self.out[:, self.columns] = value
        else:
            self.add(stage)

    def add(self, stage):
        source, bit, position, size = self.level(stage)
        mine = lax.rem(self.p.w // bit, 2)
        into = self.halves[stage]
        for j in range(size):
            index = insert_bit(j, position, mine)
            if stage == len(self.order) - 1:
                total = (source[index, :, self.columns].astype(F32)
                         + into[j, :, self.columns].astype(F32))
                for m in range(self.p.narrow):
                    rows = slice(m * self.rows, (m + 1) * self.rows)
                    self.line[m, :, self.columns] = total[rows].astype(BF16)
                continue

            def body(i, carry):
                rows = pl.ds(pl.multiple_of(i * 16, 16), 16)
                into[j, rows, self.columns] = (
                    source[index, rows, self.columns].astype(F32)
                    + into[j, rows, self.columns].astype(F32)
                ).astype(BF16)
                return carry

            lax.fori_loop(0, into.shape[1] // 16, body, 0)

    def finish(self):
        pass


def scatter_scratch(wide, narrow, shapes):
    scratch = []
    for _, height, columns in shapes:
        for stage in range(len(bits_of(wide))):
            scratch.append(pltpu.VMEM((wide >> (stage + 1), height, columns), BF16))
        scratch.append(pltpu.VMEM((narrow, height // narrow, columns), BF16))
        scratch.append(pltpu.VMEM((narrow - 1, height // narrow, columns), BF16))
    return scratch


def scatter_jobs(place, srcs, outs, buffers, sends, recvs, chunks):
    per = len(buffers) // len(srcs)
    jobs, slot = [], 0
    for chunk in chunks:
        jobs.append([])
        for i, start, size, turn in chunk:
            own = buffers[i * per : (i + 1) * per]
            jobs[-1].append(
                Scatter(place, srcs[i], own, outs[i], sends, recvs, slot, turn, pl.ds(start, size))
            )
            slot += 1
    return Waves(jobs)


def owned_shape(shape, narrow):
    return like((shape[1] // narrow, shape[2]), F32)


def spread_pieces(pieces, own):
    total, rows, _ = pieces.shape
    used = lax.broadcasted_iota(jnp.int32, (rows, 128), 1) < own
    tiles = [None] * (total * own // 128 + 1)
    for d in range(total):
        piece = jnp.where(used, pieces[d], 0.0)
        tile, shift = divmod(d * own, 128)
        if shift:
            piece = pltpu.roll(piece, shift, 1)
        lane = lax.broadcasted_iota(jnp.int32, (rows, 128), 1)
        parts = [(tile, jnp.where(lane >= shift, piece, 0.0))]
        if shift + own > 128:
            parts.append((tile + 1, jnp.where(lane < shift, piece, 0.0)))
        for t, part in parts:
            tiles[t] = part if tiles[t] is None else tiles[t] + part
    return jnp.concatenate(tiles[: total * own // 128], axis=1)


def cut_piece(values, d, own):
    tile, shift = divmod(d * own, 128)
    piece = values[:, tile * 128 : tile * 128 + 128]
    if not shift:
        return piece
    piece = pltpu.roll(piece, 128 - shift, 1)
    if shift + own > 128:
        after = pltpu.roll(values[:, tile * 128 + 128 : tile * 128 + 256], 128 - shift, 1)
        lane = lax.broadcasted_iota(jnp.int32, piece.shape, 1)
        piece = jnp.where(lane < 128 - shift, piece, after)
    return piece


def front_kernel(wide, narrow, chunks, count, own, own_ff, *refs):
    (x_ref, cot_ref, mask_ref, order_ref, sil_ref, ada_ref, bias_ref, small_ref) = refs[:8]
    srcs = refs[8 : 8 + count]
    (mod_ref, sils_ref, model_ref, hidden_ref, lat_ref, gout_ref, g2_ref, normed_ref, mixed_ref,
     keep_ref, fc2b_ref) = refs[8 + count : 19 + count]
    dsts = refs[19 + count : 19 + 2 * count]
    (got, part, sib, rows_in, smalls, send_a, recv_a, send_b, recv_b, send_c, recv_c,
     sends, recvs, local) = refs[19 + 2 * count :]
    p = Place(wide, narrow)
    model = x_ref.shape[1]
    slabs = model // 128
    own_copies = [
        pltpu.make_async_copy(srcs[i], dsts[i].at[p.w, p.n], local.at[i]) for i in range(count)
    ]
    for copy in own_copies:
        copy.start()
    smalls[p.w, p.n] = small_ref[...]
    greet_all(p)
    got[p.sid] = sil_ref[p.sid]
    wait_sil = p.to_all(lambda sid: sil_ref.at[sid], got.at[p.sid], send_a, recv_a)
    waves = gather_jobs(p, [small_ref, *srcs], [smalls, *dsts], sends, recvs, chunks)
    waves.tick()

    clear_edges(normed_ref)

    def arrange(t):
        rows = pl.ds(t * GROUP, GROUP)
        tokens = dot_nn(order_ref[...], x_ref[rows, :])
        unit, _ = unit_rows(tokens)
        kept = dot_nn(order_ref[...], mask_ref[rows, :])
        gout = dot_nn(order_ref[...], cot_ref[rows, :]) * jnp.concatenate([kept] * slabs, axis=1)
        for g in range(4):
            src = slice(64 * g, 64 * g + 64)
            dst = pl.ds(g * GROUP + 64 * t, 64)
            lat_ref[dst, :] = tokens[src].astype(BF16)
            gout_ref[dst, :] = gout[src].astype(BF16)
            keep_ref[dst, :] = (kept[src] - 1.0) * 1e30
            for s in range(slabs):
                tile = unit[src, s * 128 : s * 128 + 128].reshape(8, 8, 128)
                normed_ref[s, g, 2 + 8 * t : 10 + 8 * t] = tile

    arrange(0)
    for copy in own_copies:
        copy.wait()
    waves.tick()
    wait_sil()
    sil = got[...].reshape(p.total, 128)
    sils_ref[...] = sil
    product = dot_nn(sil[:, :own].astype(BF16), ada_ref[...]) + bias_ref[...]
    for d in range(p.total):
        part[d // p.half, d % p.half] = product[d : d + 1, :]
    to_sibling = remote(part.at[1 - p.core], sib, send_b, recv_b, p.sibling)
    to_sibling.start()
    arrange(1)
    to_sibling.wait()
    part[p.core] = part[p.core] + sib[...]
    rows_in[p.slot] = part[p.core, p.slot]
    wait_rows = p.to_kin(lambda slot: part.at[p.core, slot], rows_in.at[p.slot], send_c, recv_c)
    waves.tick()
    arrange(2)
    waves.tick()
    arrange(3)
    waves.tick()
    small = smalls[...].reshape(p.total, 32, 128).astype(F32)
    model_ref[...] = spread_pieces(small[:, :16], own)
    hidden_ref[...] = spread_pieces(small[:, 16:], own_ff)
    wait_rows()
    mod = jnp.sum(rows_in[...], axis=0)
    for i in range(6):
        mod_ref[i : i + 1, :] = mod[:, i * model : (i + 1) * model]
    waves.tick()

    shift, scale, gate = mod_ref[0:1, :], mod_ref[1:2, :], mod_ref[5:6, :]
    total = jnp.zeros((8, model), F32)
    for g in range(4):
        rows = pl.ds(g * GROUP, GROUP)
        two = gout_ref[rows, :].astype(F32) * gate
        total = total + row_sum(two)
        g2_ref[rows, :] = two.astype(BF16)
    fc2b_ref[...] = total
    masks = edge_masks()
    for s in range(slabs):
        lanes = pl.ds(s * 128, 128)
        at_s = slice(s * 128, s * 128 + 128)
        shift8 = jnp.broadcast_to(shift[:, at_s], (8, 128))
        scale8 = jnp.broadcast_to(1.0 + scale[:, at_s], (8, 128))
        normed_ref[s, :, 2:34] = normed_ref[s, :, 2:34] * scale8 + shift8
        k = [jnp.broadcast_to(model_ref[n : n + 1, at_s], (8, 128)) for n in range(9)]
        bias = jnp.broadcast_to(model_ref[9:10, at_s], (8, 128))

        def body(r, carry):
            for gi in (0, 1):
                for gj in (0, 1):
                    pair = conv_cell(normed_ref, s, gi, gj, r, k, bias, masks)
                    mixed_ref[group_rows(gi, gj, r), lanes] = jnp.concatenate(pair, 0).astype(BF16)
            return carry

        lax.fori_loop(0, HALF, body, 0)
        waves.tick()
    waves.end()


def front(wide, narrow, x, cot, mask, order, sil, ada, bias, small, blocks, chunks, hidden):
    total = wide * narrow
    tokens, model = x.shape
    slabs, count, columns = model // 128, len(blocks), ada.shape[1]
    own, own_ff = model // total, hidden // total
    inside = pl.BlockSpec(memory_space=pltpu.VMEM)
    anywhere = pl.BlockSpec(memory_space=pl.ANY)
    all_sems = pltpu.SemaphoreType.DMA((total,))
    one_sem = pltpu.SemaphoreType.DMA
    kin_sems = pltpu.SemaphoreType.DMA((total // 2,))
    return pl.pallas_call(
        functools.partial(front_kernel, wide, narrow, chunks, count, own, own_ff),
        in_specs=[inside] * 8 + [anywhere] * count,
        out_specs=[inside] * 11 + [anywhere] * count,
        out_shape=[
            like((8, model), F32), like((total, 128), F32), like((16, model), F32),
            like((16, hidden), F32), like((tokens, model), BF16), like((tokens, model), BF16),
            like((tokens, model), BF16), like((slabs, 4, 36, 8, 128), F32),
            like((tokens, model), BF16), like((tokens, 128), F32), like((8, model), F32),
        ] + [like((wide, narrow) + b.shape, BF16) for b in blocks],
        scratch_shapes=[
            pltpu.VMEM((total, 1, 128), F32), pltpu.VMEM((2, total // 2, 1, columns), F32),
            pltpu.VMEM((total // 2, 1, columns), F32), pltpu.VMEM((total // 2, 1, columns), F32),
            pltpu.VMEM((wide, narrow, 32, 128), BF16),
            all_sems, all_sems, one_sem, one_sem, kin_sems, kin_sems,
            *job_sems(wide, narrow, chunks), pltpu.SemaphoreType.DMA((count,)),
        ],
        compiler_params=pltpu.CompilerParams(
            vmem_limit_bytes=56 * MIB, collective_id=0, has_side_effects=True
        ),
        name="front",
    )(x, cot, mask, order, sil, ada, bias, small, *blocks)


def attend_kernel(wide, narrow, chunks, count, *refs):
    mixed_ref, lat_ref, keep_ref, mod_ref, small_ref, qkv_ref, proj_ref = refs[:7]
    srcs = refs[7 : 7 + count]
    triple_ref, probs_ref, att_ref, branch_ref, middle_ref, n2_ref = refs[7 + count : 13 + count]
    dsts = refs[13 + count : 13 + 2 * count]
    sends, recvs, local = refs[13 + 2 * count :]
    step = pl.program_id(0)
    p = Place(wide, narrow)
    waves = gather_jobs(p, srcs, dsts, sends, recvs, chunks)
    own_copies = [
        pltpu.make_async_copy(srcs[i], dsts[i].at[p.w, p.n], local.at[i]) for i in range(count)
    ]

    def on(when, work):
        pl.when(step == when)(work)

    def first():
        for copy in own_copies:
            copy.start()
        greet(p.partners())
        waves.run(0)
        for copy in own_copies:
            copy.wait()

    def hook(position):
        for when in range(4):
            on(when, lambda: waves.at_hook(2 * when + position, 8))

    on(0, first)
    model = lat_ref.shape[1]
    slabs = model // 128
    triple_ref[...] = dot_nn(mixed_ref[...], qkv_ref[...]).astype(BF16)
    lane = lax.broadcasted_iota(jnp.int32, (GROUP, 128), 1)
    left = lane < HEAD
    keep = jnp.concatenate([keep_ref[...]] * 2, axis=1)
    for s in range(slabs):
        q = triple_ref[:, s * 128 : s * 128 + 128]
        k = triple_ref[:, model + s * 128 : model + s * 128 + 128] * jnp.asarray(0.125, BF16)
        v = triple_ref[:, 2 * model + s * 128 : 2 * model + s * 128 + 128]
        outs = []
        for h in (0, 1):
            mine = left if h == 0 else jnp.logical_not(left)
            scores = dot_nt(jnp.where(mine, k, jnp.zeros_like(k)), q) + keep
            e = jnp.exp(scores - jnp.max(scores, axis=0, keepdims=True))
            prob = (e * (1.0 / jnp.sum(e, axis=0, keepdims=True))).astype(BF16)
            probs_ref[2 * s + h] = prob
            outs.append(dot_tn(prob, v))
        att_ref[:, s * 128 : s * 128 + 128] = jnp.where(left, outs[0], outs[1]).astype(BF16)
        if s == slabs // 2 - 1:
            hook(0)
    branch = dot_nn(att_ref[...], proj_ref[...]) + small_ref[10:11, :]
    middle = lat_ref[...].astype(F32) + mod_ref[2:3, :] * branch
    unit, _ = unit_rows(middle)
    branch_ref[...] = branch
    middle_ref[...] = middle
    n2_ref[...] = (unit * (1.0 + mod_ref[4:5, :]) + mod_ref[3:4, :]).astype(BF16)
    hook(1)
    on(3, waves.finish)


def attend(wide, narrow, mixed, lat, keep, mod, small, qkv, proj, blocks, chunks):
    tokens, model = lat.shape
    heads, count = model // HEAD, len(blocks)
    by_group = lambda columns: pl.BlockSpec((GROUP, columns), lambda g: (g, 0))
    anywhere = pl.BlockSpec(memory_space=pl.ANY)
    return pl.pallas_call(
        functools.partial(attend_kernel, wide, narrow, chunks, count),
        grid=(4,),
        in_specs=[
            by_group(model), by_group(model), by_group(128), whole(mod.shape),
            whole(small.shape), once(qkv.shape), once(proj.shape),
        ] + [anywhere] * count,
        out_specs=[
            by_group(3 * model), pl.BlockSpec((heads, GROUP, GROUP), lambda g: (g, 0, 0)),
            by_group(model), by_group(model), by_group(model), by_group(model),
        ] + [anywhere] * count,
        out_shape=[
            like((tokens, 3 * model), BF16), like((4 * heads, GROUP, GROUP), BF16),
            like((tokens, model), BF16), like((tokens, model), F32),
            like((tokens, model), F32), like((tokens, model), BF16),
        ] + [like((wide, narrow) + b.shape, BF16) for b in blocks],
        scratch_shapes=[*job_sems(wide, narrow, chunks), pltpu.SemaphoreType.DMA((count,))],
        compiler_params=pltpu.CompilerParams(
            vmem_limit_bytes=56 * MIB, collective_id=1, has_side_effects=True
        ),
        name="attend",
    )(mixed, lat, keep, mod, small, qkv, proj, *blocks)


def back_kernel(wide, narrow, chunks, count, *refs):
    (gn2_ref, two_ref, middle_ref, branch_ref, gout_ref, att_ref, triple_ref, probs_ref, mixed_ref,
     mod_ref, small_ref, proj_ref, qkv_ref) = refs[:13]
    srcs = refs[13 : 13 + count]
    out_ref, gmid_ref, gmix_ref, sums_ref, qkvg_ref, projg_ref = refs[13 + count : 19 + count]
    outs = refs[19 + count : 19 + 2 * count]
    ga, gt, qkv_sum, proj_sum = refs[19 + 2 * count : 23 + 2 * count]
    buffers, (sends, recvs) = refs[23 + 2 * count : -2], refs[-2:]
    step = pl.program_id(0)
    model = gn2_ref.shape[1]
    slabs = model // 128
    p = Place(wide, narrow)
    waves = scatter_jobs(p, srcs, outs, buffers, sends, recvs, chunks)

    def hook(position):
        for when in range(4):
            pl.when(step == when)(lambda: waves.at_hook(4 * when + position, 16))

    @pl.when(step == 0)
    def _():
        greet(p.partners())
        waves.run(0)
        sums_ref[...] = jnp.zeros_like(sums_ref)
        qkv_sum[...] = jnp.zeros_like(qkv_sum)
        proj_sum[...] = jnp.zeros_like(proj_sum)

    middle = middle_ref[...]
    two = two_ref[...] + small_ref[11:12, :]
    gout = gout_ref[...].astype(F32)
    out_ref[...] = (middle + mod_ref[5:6, :] * two).astype(BF16)
    sums_ref[3] += row_sum(gout * two)
    unit, scale = unit_rows(middle)
    gn2 = gn2_ref[...]
    sums_ref[1] += row_sum(gn2)
    sums_ref[2] += row_sum(gn2 * unit)
    gm = gout + unit_back(gn2 * (1.0 + mod_ref[4:5, :]), unit, scale)
    gmid_ref[...] = gm
    sums_ref[0] += row_sum(gm * branch_ref[...])
    gb = gm * mod_ref[2:3, :]
    sums_ref[4] += row_sum(gb)
    gbl = gb.astype(BF16)
    proj_sum[...] += dot_tn(att_ref[...], gbl)
    ga[...] = dot_nt(gbl, proj_ref[...]).astype(BF16)
    hook(0)
    lane = lax.broadcasted_iota(jnp.int32, (GROUP, 128), 1)
    left = lane < HEAD
    for s in range(slabs):
        lanes = slice(s * 128, s * 128 + 128)
        q = triple_ref[:, s * 128 : s * 128 + 128] * jnp.asarray(0.125, BF16)
        k = triple_ref[:, model + s * 128 : model + s * 128 + 128] * jnp.asarray(0.125, BF16)
        v = triple_ref[:, 2 * model + s * 128 : 2 * model + s * 128 + 128]
        g = ga[:, lanes]
        gq = gk = gv = None
        for h in (0, 1):
            own = left if h == 0 else jnp.logical_not(left)
            mine = lambda value: jnp.where(own, value, jnp.zeros_like(value))
            p_low = probs_ref[2 * s + h]
            prob = p_low.astype(F32)
            gh = mine(g)
            gp = dot_nt(v, gh)
            inner = jnp.sum(prob * gp, axis=0, keepdims=True)
            gs = (prob * (gp - inner)).astype(BF16)
            parts = (dot_tn(gs, mine(k)), dot_nn(gs, mine(q)), dot_nn(p_low, gh))
            if h == 0:
                gq, gk, gv = parts
            else:
                gq, gk, gv = gq + parts[0], gk + parts[1], gv + parts[2]
        gt[:, s * 128 : s * 128 + 128] = gq.astype(BF16)
        gt[:, model + s * 128 : model + s * 128 + 128] = gk.astype(BF16)
        gt[:, 2 * model + s * 128 : 2 * model + s * 128 + 128] = gv.astype(BF16)
        if s in (1, 3):
            hook(1 + s // 2)
    qkv_sum[...] += dot_tn(mixed_ref[...], gt[...])
    gmixed = dot_nt(gt[...], qkv_ref[...])
    zero = jnp.zeros((slabs, 1, 2, 8, 128), F32)
    gmix_ref[:, :, 0:2] = zero
    gmix_ref[:, :, 34:36] = zero
    for s in range(slabs):
        gmix_ref[s, 0, 2:34] = gmixed[:, s * 128 : s * 128 + 128].reshape(32, 8, 128)
    hook(3)

    @pl.when(step == 3)
    def _():
        qkvg_ref[...] = qkv_sum[...].astype(BF16)
        projg_ref[...] = proj_sum[...].astype(BF16)
        waves.finish()


def back(wide, narrow, gn2, two, middle, branch, gout, att, triple, probs, mixed, mod, small, proj,
         qkv, arrays, chunks):
    tokens, model = middle.shape
    heads, slabs, count = model // HEAD, model // 128, len(arrays)
    by_group = lambda columns: pl.BlockSpec((GROUP, columns), lambda g: (g, 0))
    shapes = [a.shape for a in arrays]
    return pl.pallas_call(
        functools.partial(back_kernel, wide, narrow, chunks, count),
        grid=(4,),
        in_specs=[by_group(model)] * 6 + [
            by_group(3 * model), pl.BlockSpec((heads, GROUP, GROUP), lambda g: (g, 0, 0)),
            by_group(model), once(mod.shape), once(small.shape), once(proj.shape), once(qkv.shape),
        ] + [once(s) for s in shapes],
        out_specs=[
            by_group(model), by_group(model),
            pl.BlockSpec((slabs, 1, 36, 8, 128), lambda g: (0, g, 0, 0, 0)), once((5, 8, model)),
            once(qkv.shape), once(proj.shape),
        ] + [once(owned_shape(s, narrow).shape) for s in shapes],
        out_shape=[
            like((tokens, model), BF16), like((tokens, model), F32),
            like((slabs, 4, 36, 8, 128), F32), like((5, 8, model), F32),
            like(qkv.shape, BF16), like(proj.shape, BF16),
        ] + [owned_shape(s, narrow) for s in shapes],
        scratch_shapes=[
            pltpu.VMEM((GROUP, model), BF16), pltpu.VMEM((GROUP, 3 * model), BF16),
            pltpu.VMEM(qkv.shape, F32), pltpu.VMEM(proj.shape, F32),
            *scatter_scratch(wide, narrow, shapes), *job_sems(wide, narrow, chunks),
        ],
        compiler_params=pltpu.CompilerParams(
            vmem_limit_bytes=62 * MIB, collective_id=2, has_side_effects=True
        ),
        name="attend_back",
    )(gn2, two, middle, branch, gout, att, triple, probs, mixed, mod, small, proj, qkv, *arrays)


def tail_kernel(wide, narrow, chunks, count, own, own_ff, *refs):
    (lat_ref, gmid_ref, rows_ref, gmix_ref, normed_ref, mod_ref, small_ref, sums_ref, fc2b_ref,
     hidden_ref, sils_ref, ada_ref, order_ref) = refs[:13]
    srcs = refs[13 : 13 + count]
    out_ref, xg_ref, wgrad_ref, bgrad_ref, cond_ref, small_out = refs[13 + count : 19 + count]
    outs = refs[19 + count : 19 + 2 * count]
    (gmoved, gnorm, early, late, cuts, cuts_in, part, send_a, recv_a, send_b, recv_b, send_c, recv_c,
     send_d, recv_d, send_e, recv_e, send_f, recv_f) = refs[19 + 2 * count : 38 + 2 * count]
    buffers, (sends, recvs) = refs[38 + 2 * count : -2], refs[-2:]
    p = Place(wide, narrow)
    model = lat_ref.shape[1]
    slabs = model // 128
    greet_all(p)
    waves = scatter_jobs(p, srcs, outs, buffers, sends, recvs, chunks)
    waves.tick()

    gates = jnp.sum(sums_ref[...], axis=1)
    for i, row in enumerate((0, 1, 2, 3)):
        early[p.core, p.slot, :, i * model : (i + 1) * model] = gates[row : row + 1]
    mine = lambda ref: ref.at[p.core, p.slot]
    wait_early = p.to_kin(lambda slot: mine(early), mine(early), send_a, recv_a)

    clear_edges(gmoved)
    masks = edge_masks()
    rows_out = []
    for s in range(slabs):
        lanes = pl.ds(s * 128, 128)
        at_s = slice(s * 128, s * 128 + 128)
        k = [jnp.broadcast_to(small_ref[n : n + 1, at_s], (8, 128)) for n in range(9)]

        def move(r, total):
            for gi in (0, 1):
                for gj in (0, 1):
                    pair = load_pair(gmix_ref, s, gi, gj, r)
                    total = total + pair[0] + pair[1]
                    store_pair(gmoved, s, gi, gj, r, shift_pair(pair, 1 - gj, *masks))
            return total

        total = lax.fori_loop(0, HALF, move, jnp.zeros((8, 128), F32))

        def put(gi, gj, r, pair):
            gnorm[group_rows(gi, gj, r), lanes] = jnp.concatenate(pair, 0)

        sums = conv_back(s, k, normed_ref, gmix_ref, gmoved, put)
        late[p.core, p.slot, :, at_s] = jnp.sum(sums[9], axis=0, keepdims=True)
        column = [jnp.sum(v, axis=0, keepdims=True) for v in (*sums[:9], total)]
        column.append(jnp.sum(sums_ref[4, :, at_s], axis=0, keepdims=True))
        column.append(jnp.sum(fc2b_ref[:, at_s], axis=0, keepdims=True))
        rows_out.append(jnp.concatenate(column + [jnp.zeros((4, 128), F32)], axis=0))
        if s % 2:
            waves.tick()
    narrow_rows = jnp.concatenate(rows_out, axis=1)
    for sid in range(p.total):
        core, slot = divmod(sid, p.half)
        d = (2 * (slot // narrow) + core) * narrow + slot % narrow
        cuts[sid, :16] = cut_piece(narrow_rows, d, own)
        cuts[sid, 16:] = cut_piece(hidden_ref[...], d, own_ff)
    cuts_in[p.sid] = cuts[p.sid]
    wait_cuts = p.to_all(lambda sid: cuts.at[sid], cuts_in.at[p.sid], send_b, recv_b)
    waves.tick()
    scale_sum = jnp.zeros((8, model), F32)
    for g in range(4):
        rows = pl.ds(g * GROUP, GROUP)
        unit, scale = unit_rows(lat_ref[rows, :].astype(F32))
        gn = gnorm[rows, :]
        scale_sum = scale_sum + row_sum(gn * unit)
        grad = gmid_ref[rows, :] + unit_back(gn * (1.0 + mod_ref[1:2, :]), unit, scale)
        gnorm[rows, :] = grad
    late[p.core, p.slot, :, model:] = jnp.sum(scale_sum, axis=0, keepdims=True)
    wait_late = p.to_kin(lambda slot: mine(late), mine(late), send_c, recv_c)
    wait_early()
    swap_early = remote(early.at[p.core], early.at[p.core], send_d, recv_d, p.sibling)
    swap_early.start()
    waves.tick()
    for t in range(4):
        parts = [pl.ds(g * GROUP + 64 * t, 64) for g in range(4)]
        block = jnp.concatenate([rows_ref[q, :] for q in parts], axis=0)
        out_ref[t * GROUP : t * GROUP + GROUP, :] = dot_tn(order_ref[...], block).astype(BF16)
        block = jnp.concatenate([gnorm[q, :].astype(BF16) for q in parts], axis=0)
        xg_ref[t * GROUP : t * GROUP + GROUP, :] = dot_tn(order_ref[...], block).astype(BF16)
    wait_late()
    swap_late = remote(late.at[p.core], late.at[p.core], send_e, recv_e, p.sibling)
    swap_late.start()
    waves.tick()
    swap_early.wait()
    swap_late.wait()
    sil = sils_ref[:, :own].astype(BF16)
    cond = None
    for ref, start in ((late, 0), (early, 2 * model)):
        size = ref.shape[-1]
        span = slice(start, start + size)
        grads = ref[...].reshape(p.total, size)
        bgrad_ref[:, span] = jnp.sum(grads, axis=0, keepdims=True)
        low = grads.astype(BF16)
        wgrad_ref[:, span] = dot_tn(sil, low)
        term = dot_nt(low, ada_ref[:, span])
        cond = term if cond is None else cond + term
    cond = jnp.concatenate([cond, jnp.zeros((p.total, 128 - own), F32)], axis=1)
    for sid in range(p.total):
        part[sid] = cond[sid : sid + 1, :]
    cond_ref[p.me] = part[p.sid]
    wait_cond = p.to_all(lambda sid: part.at[sid], cond_ref.at[p.me], send_f, recv_f)
    wait_cuts()
    small_out[...] = jnp.sum(cuts_in[...], axis=0)
    waves.end()
    wait_cond()


def tail(wide, narrow, lat, gmid, rows, gmix, normed, mod, small, sums, fc2b, hidden_sums, sils, ada,
         order, arrays, chunks):
    total = wide * narrow
    tokens, model = lat.shape
    slabs, count, columns = model // 128, len(arrays), ada.shape[1]
    own, own_ff = ada.shape[0], hidden_sums.shape[1] // total
    shapes = [a.shape for a in arrays]
    all_sems, kin_sems = (pltpu.SemaphoreType.DMA((n,)) for n in (total, total // 2))
    one_sem = pltpu.SemaphoreType.DMA
    return pl.pallas_call(
        functools.partial(tail_kernel, wide, narrow, chunks, count, own, own_ff),
        out_shape=[
            like((tokens, model), BF16), like((tokens, model), BF16), like((own, columns), F32),
            like((1, columns), F32), like((total, 1, 128), F32), like((32, 128), F32),
        ] + [owned_shape(s, narrow) for s in shapes],
        scratch_shapes=[
            pltpu.VMEM((slabs, 4, 36, 8, 128), F32), pltpu.VMEM((tokens, model), F32),
            pltpu.VMEM((2, total // 2, 1, 4 * model), F32),
            pltpu.VMEM((2, total // 2, 1, 2 * model), F32),
            pltpu.VMEM((total, 32, 128), F32), pltpu.VMEM((total, 32, 128), F32),
            pltpu.VMEM((total, 1, 128), F32),
            kin_sems, kin_sems, all_sems, all_sems, kin_sems, kin_sems, one_sem, one_sem,
            one_sem, one_sem, all_sems, all_sems,
            *scatter_scratch(wide, narrow, shapes), *job_sems(wide, narrow, chunks),
        ],
        compiler_params=pltpu.CompilerParams(
            vmem_limit_bytes=60 * MIB, collective_id=3, has_side_effects=True
        ),
        name="tail",
    )(lat, gmid, rows, gmix, normed, mod, small, sums, fc2b, hidden_sums, sils, ada, order, *arrays)


def smooth_gate(values):
    return values * jax.nn.sigmoid(values)


def on_device(wide, narrow, latents, condition, valid_mask, ada_weight, ada_bias, dw1_kernel, dw1_bias,
              qkv_weight, proj_weight, proj_bias, fc1_weight, fc1_bias, dw2_kernel, dw2_bias,
              fc2_weight, fc2_bias, out_cotangent):
    total = wide * narrow
    w, n = lax.axis_index("wide"), lax.axis_index("narrow")
    me = w * narrow + n
    model, hidden = latents.shape[2], fc1_weight.shape[1]
    own, own_ff = model // total, hidden // total

    sil, silu_back = jax.vjp(smooth_gate, condition[0].astype(F32))
    sil = sil.astype(BF16).astype(F32).reshape(wide // 2, 2, narrow, 1, own)
    sil = jnp.pad(sil.transpose(1, 0, 2, 3, 4).reshape(total, 1, own), ((0, 0), (0, 0), (0, 128 - own)))
    bias_at = lax.dynamic_update_slice(
        jnp.zeros((1, 6 * model), F32), ada_bias.astype(F32)[None, :], (0, me * ada_bias.shape[0])
    )
    lanes = lambda rows: jnp.pad(rows, ((0, 0), (0, 128 - rows.shape[1])))
    small = jnp.concatenate([
        lanes(dw1_kernel), lanes(dw1_bias[None]), lanes(proj_bias[None]), lanes(fc2_bias[None]),
        jnp.zeros((4, 128), BF16), lanes(dw2_kernel), lanes(dw2_bias[None]), lanes(fc1_bias[None]),
        jnp.zeros((5, 128), BF16),
    ])
    mask = jnp.broadcast_to(valid_mask[0].astype(BF16)[:, None], (latents.shape[1], 128))
    order = order_matrix()

    chunks = [[(0, 0, 128, 0)], both(1, 0, 3 * model), both(2, 0, model)]
    (mod, sils, model_small, hidden_small, lat, gout, g2, normed, mixed, keep, fc2b, qkv, proj) = front(
        wide, narrow, latents[0], out_cotangent[0], mask, order, sil, ada_weight, bias_at, small,
        [qkv_weight, proj_weight], chunks, hidden,
    )
    qkv, proj = qkv.reshape(model, 3 * model), proj.reshape(model, model)
    chunks = [both(0, 0, hidden), both(1, 0, model)]
    triple, probs, att, branch, middle, n2, fc1, fc2 = attend(
        wide, narrow, mixed, lat, keep, mod, model_small, qkv, proj, [fc1_weight, fc2_weight], chunks
    )
    fc1, fc2 = fc1.reshape(model, hidden), fc2.reshape(hidden, model)
    two, gn2, fc1g, fc2g, hidden_sums = feed_forward(n2, g2, fc1, hidden_small, fc2)
    as_lines = lambda grad: grad.reshape(wide, grad.shape[0] // wide, grad.shape[1])
    chunks = [both(0, 0, hidden), both(1, 0, model)]
    rows, gmid, gmix, sums, qkvg, projg, fc1g, fc2g = back(
        wide, narrow, gn2, two, middle, branch, gout, att, triple, probs, mixed, mod, model_small,
        proj, qkv, [as_lines(fc1g), as_lines(fc2g)], chunks,
    )
    chunks = [both(1, 0, model), both(0, 0, 3 * model)]
    out, xg, ada_wgrad, ada_bsum, cond, small, qkvg, projg = tail(
        wide, narrow, lat, gmid, rows, gmix, normed, mod, model_small, sums, fc2b, hidden_sums, sils,
        ada_weight, order, [as_lines(qkvg), as_lines(projg)], chunks,
    )
    ada_bgrad = lax.dynamic_slice(ada_bsum[0], (me * ada_bias.shape[0],), ada_bias.shape)
    (cond_grad,) = silu_back(cond[:, 0, :own].reshape(model))
    return (
        out[None], xg[None], cond_grad[None], ada_wgrad, ada_bgrad,
        small[:9, :own], small[9, :own], qkvg, projg, small[10, :own], fc1g, small[26, :own_ff],
        small[16:25, :own_ff], small[25, :own_ff], fc2g, small[11, :own],
    )


def solution(mesh):
    wide, narrow = mesh.shape["wide"], mesh.shape["narrow"]
    rows = lambda rank: P(AXES, *(None,) * (rank - 1))
    lanes = P(None, AXES)
    in_specs = (
        rows(3), rows(2), rows(2), rows(2), rows(1), lanes, rows(1), rows(2), rows(2), rows(1),
        rows(2), rows(1), lanes, rows(1), rows(2), rows(1), rows(3),
    )
    out_specs = (
        rows(3), rows(3), rows(2), rows(2), rows(1), lanes, rows(1), rows(2), rows(2), rows(1),
        rows(2), rows(1), lanes, rows(1), rows(2), rows(1),
    )
    return jax.shard_map(
        functools.partial(on_device, wide, narrow), mesh=mesh, in_specs=in_specs,
        out_specs=out_specs, check_vma=False,
    )
```

```python
import functools

import jax
import jax.numpy as jnp
from jax import lax
from jax.experimental import pallas as pl
from jax.experimental.pallas import tpu as pltpu
from jax.sharding import PartitionSpec as P

HEAD = 64
GRID = 32
HALF = 16
GROUP = 256
TOKENS = 1024
C0 = 0.7978845608028654
C1 = 0.044715
EPS = 1e-06
MIB = 1 << 20
AXES = ("wide", "narrow")
F32, BF16 = jnp.float32, jnp.bfloat16


def dot_nn(a, b):
    return lax.dot_general(a, b, (((1,), (0,)), ((), ())), preferred_element_type=F32)


def dot_nt(a, b):
    return lax.dot_general(a, b, (((1,), (1,)), ((), ())), preferred_element_type=F32)


def dot_tn(a, b):
    return lax.dot_general(a, b, (((0,), (0,)), ((), ())), preferred_element_type=F32)


def whole(shape):
    return pl.BlockSpec(shape, lambda *_: (0,) * len(shape))


def once(shape):
    return pl.BlockSpec(shape, lambda *_: (0,) * len(shape), pipeline_mode=pl.Buffered(1))


def like(shape, dtype):
    return jax.ShapeDtypeStruct(shape, dtype)


def shift_pair(pair, parity, first, last):
    low, high = pair
    zero = jnp.zeros_like(low)
    if parity == 0:
        low, high = pltpu.roll(low, 1, 0), pltpu.roll(high, 1, 0)
        return jnp.where(first, zero, low), jnp.where(first, low, high)
    low, high = pltpu.roll(low, 7, 0), pltpu.roll(high, 7, 0)
    return jnp.where(last, high, low), jnp.where(last, zero, high)


def row_sources(gi, r):
    if gi == 0:
        return ((1, r - 1), (0, r), (1, r))
    return ((0, r), (1, r), (0, r + 1))


def load_pair(ref, slab, gi, gj, r):
    tile = 2 + 2 * r
    group = 2 * gi + gj
    return ref[slab, group, tile], ref[slab, group, tile + 1]


def store_pair(ref, slab, gi, gj, r, pair):
    tile = 2 + 2 * r
    group = 2 * gi + gj
    ref[slab, group, tile] = pair[0]
    ref[slab, group, tile + 1] = pair[1]


def edge_masks():
    sub = lax.broadcasted_iota(jnp.int32, (8, 128), 0)
    return sub == 0, sub == 7


def clear_edges(ref):
    slabs = ref.shape[0]
    ref[:, :, 0:2] = jnp.zeros((slabs, 4, 2, 8, 128), F32)
    ref[:, :, 34:36] = jnp.zeros((slabs, 4, 2, 8, 128), F32)


def conv_cell(src, slab, gi, gj, r, k, bias, masks):
    sources = row_sources(gi, r)
    other = 1 - gj
    near = 2 if gj == 0 else 0
    far = 2 - near
    same = [load_pair(src, slab, p, gj, rr) for p, rr in sources]
    cross = [load_pair(src, slab, p, other, rr) for p, rr in sources]
    straight, moved = [], []
    for h in (0, 1):
        acc, off = bias, None
        for a in range(3):
            acc = acc + k[3 * a + 1] * same[a][h] + k[3 * a + near] * cross[a][h]
            term = k[3 * a + far] * cross[a][h]
            off = term if off is None else off + term
        straight.append(acc)
        moved.append(off)
    moved = shift_pair(moved, gj, *masks)
    return straight[0] + moved[0], straight[1] + moved[1]


def conv_back_row(slab, k, src, grad, grad_moved, put, r, carry):
    kg, total = list(carry[:9]), carry[9]
    for gi in (0, 1):
        sources = row_sources(gi, r)
        for gj in (0, 1):
            other = 1 - gj
            near = 2 if gj == 0 else 0
            here = load_pair(src, slab, gi, gj, r)
            out = [None, None]
            for a in range(3):
                p, rr = sources[2 - a]
                trio = {
                    1: load_pair(grad, slab, p, gj, rr),
                    2 - near: load_pair(grad, slab, p, other, rr),
                    near: load_pair(grad_moved, slab, p, other, rr),
                }
                for b in range(3):
                    n = 3 * a + b
                    for h in (0, 1):
                        term = k[n] * trio[b][h]
                        out[h] = term if out[h] is None else out[h] + term
                        kg[n] = kg[n] + here[h] * trio[b][h]
            total = total + out[0] + out[1]
            put(gi, gj, r, out)
    return tuple(kg) + (total,)


def conv_back(slab, k, src, grad, grad_moved, put):
    body = lambda r, carry: conv_back_row(slab, k, src, grad, grad_moved, put, r, carry)
    return lax.fori_loop(0, HALF, body, (jnp.zeros((8, 128), F32),) * 10)


def group_rows(gi, gj, r):
    return pl.ds(pl.multiple_of((2 * gi + gj) * GROUP + r * HALF, HALF), HALF)


def row_sum(values):
    rows, columns = values.shape
    return jnp.sum(values.reshape(rows // 8, 8, columns), axis=0)


def unit_rows(values):
    model = values.shape[-1]
    centered = values - jnp.sum(values, axis=-1, keepdims=True) * (1.0 / model)
    spread = jnp.sum(centered * centered, axis=-1, keepdims=True) * (1.0 / model)
    scale = lax.rsqrt(spread + EPS)
    return centered * scale, scale


def unit_back(grad, unit, scale):
    model = grad.shape[-1]
    mean = jnp.sum(grad, axis=-1, keepdims=True) * (1.0 / model)
    tilt = jnp.sum(grad * unit, axis=-1, keepdims=True) * (1.0 / model)
    return scale * (grad - mean - unit * tilt)


def order_matrix():
    d = jnp.arange(GROUP)
    group, position, column = d // 64, (d % 64) // HALF, d % HALF
    source = (2 * position + group // 2) * GRID + 2 * column + group % 2
    return (source[:, None] == jnp.arange(GROUP)[None, :]).astype(BF16)


def ff_kernel(wide, narrow, chunks, count, steps, sums_over, *refs):
    n2_ref, n2t_ref, g2_ref, fc1_ref, small_ref, fc2_ref = refs[:6]
    srcs = refs[6 : 6 + count]
    branch_ref, gn2_ref, w1g_ref, w2g_ref, sums_ref = refs[6 + count : 11 + count]
    dsts = refs[11 + count : 11 + 2 * count]
    hid, ga, gc, gcs, act, ghl = refs[11 + 2 * count : 17 + 2 * count]
    step = pl.program_id(0)
    slabs = hid.shape[0]
    p = Place(wide, narrow)
    if sums_over:
        buffers, (sends, recvs) = refs[17 + 2 * count : -2], refs[-2:]
        waves = scatter_jobs(p, srcs, dsts, buffers, sends, recvs, chunks)
        own_copies = []
    else:
        sends, recvs, local = refs[17 + 2 * count :]
        waves = gather_jobs(p, srcs, dsts, sends, recvs, chunks)
        own_copies = [
            pltpu.make_async_copy(
                srcs[i], dsts[i].at[(*digits_of(p.w, wide), p.n)], local.at[i]
            )
            for i in range(count)
        ]

    def hook(position):
        for when in range(steps):
            pl.when(step == when)(lambda: waves.at_hook(3 * when + position, 3 * steps))

    @pl.when(step == 0)
    def _():
        for copy in own_copies:
            copy.start()
        greet(p.partners())
        waves.run(0)
        for copy in own_copies:
            copy.wait()
        branch_ref[...] = jnp.zeros_like(branch_ref)
        gn2_ref[...] = jnp.zeros_like(gn2_ref)
        for ref in (hid, gc, gcs):
            clear_edges(ref)

    for g in range(4):
        rows = pl.ds(g * GROUP, GROUP)
        full = dot_nn(n2_ref[rows, :], fc1_ref[...]) + small_ref[10:11, :]
        back = dot_nt(g2_ref[rows, :], fc2_ref[...])
        for slab in range(slabs):
            lanes = slice(slab * 128, slab * 128 + 128)
            hid[slab, g, 2:34] = full[:, lanes].reshape(32, 8, 128)
            ga[slab, g] = back[:, lanes].reshape(32, 8, 128)

    hook(0)
    masks = edge_masks()
    for slab in range(slabs):
        lanes = pl.ds(slab * 128, 128)
        k = [jnp.broadcast_to(small_ref[n : n + 1, lanes], (8, 128)) for n in range(9)]
        bias = jnp.broadcast_to(small_ref[9:10, lanes], (8, 128))

        def forward(r, total):
            for gi in (0, 1):
                for gj in (0, 1):
                    pair = conv_cell(hid, slab, gi, gj, r, k, bias, masks)
                    acts, grads = [], []
                    for h in (0, 1):
                        x = pair[h]
                        x2 = x * x
                        half = 0.5 * jnp.tanh(x * (C0 + (C0 * C1) * x2)) + 0.5
                        value = x * half
                        slope = half + (value - value * half) * (2.0 * C0 + (6.0 * C0 * C1) * x2)
                        acts.append(value)
                        grads.append(ga[slab, 2 * gi + gj, 2 * r + h] * slope)
                        total = total + grads[-1]
                    act[group_rows(gi, gj, r), lanes] = jnp.concatenate(acts, 0).astype(BF16)
                    store_pair(gc, slab, gi, gj, r, grads)
                    store_pair(gcs, slab, gi, gj, r, shift_pair(grads, 1 - gj, *masks))
            return total

        total = lax.fori_loop(0, HALF, forward, jnp.zeros((8, 128), F32))

        def put(gi, gj, r, pair):
            ghl[group_rows(gi, gj, r), lanes] = jnp.concatenate(pair, 0).astype(BF16)

        sums = conv_back(slab, k, hid, gc, gcs, put)
        for n, value in enumerate([*sums[:9], total, sums[9]]):
            sums_ref[n : n + 1, lanes] = jnp.sum(value, axis=0, keepdims=True)
        sums_ref[11:16, lanes] = jnp.zeros((5, 128), F32)
        if slab == 0:
            hook(1)

    branch_ref[...] += dot_nn(act[...], fc2_ref[...])
    gn2_ref[...] += dot_nt(ghl[...], fc1_ref[...])
    w2g_ref[...] = dot_tn(act[...], g2_ref[...]).astype(w2g_ref.dtype)
    w1g_ref[...] = dot_nn(n2t_ref[...], ghl[...]).astype(w1g_ref.dtype)
    hook(2)

    @pl.when(step == steps - 1)
    def _():
        waves.finish()


def feed_forward(wide, narrow, n2, n2t, g2, fc1, small, part, fc2, arrays, chunks, sums_over,
                 width=256):
    tokens, model = n2.shape
    hidden = fc1.shape[1]
    slabs, steps, count = width // 128, hidden // width, len(arrays)
    padded = pltpu.VMEM((slabs, 4, 36, 8, 128), F32)
    columns = lambda rows: pl.BlockSpec((rows, width), lambda s: (0, s))
    lines = pl.BlockSpec((width, model), lambda s: (s, 0))
    anywhere = pl.BlockSpec(memory_space=pl.ANY)
    if sums_over:
        shapes = [a.shape for a in arrays]
        moved = [owned_shape(s, narrow) for s in shapes]
        extra = scatter_scratch(wide, narrow, shapes) + job_sems(wide, narrow, chunks)
        in_moved, out_moved = [once(s) for s in shapes], [once(m.shape) for m in moved]
    else:
        moved = [gathered_shape(wide, narrow, a.shape) for a in arrays]
        extra = job_sems(wide, narrow, chunks) + [pltpu.SemaphoreType.DMA((count,))]
        in_moved = out_moved = [anywhere] * count
    return pl.pallas_call(
        functools.partial(ff_kernel, wide, narrow, chunks, count, steps, sums_over),
        grid=(steps,),
        in_specs=[
            once((tokens, model)), once((model, tokens)), once((tokens, model)),
            columns(model), pl.BlockSpec((16, width), lambda s: (0, part * steps + s)), lines,
        ] + in_moved,
        out_specs=[
            once((tokens, model)), once((tokens, model)), columns(model), lines, columns(16)
        ] + out_moved,
        out_shape=[
            like((tokens, model), F32), like((tokens, model), F32),
            like((model, hidden), BF16), like((hidden, model), BF16), like((16, hidden), F32),
        ] + moved,
        scratch_shapes=[
            padded, pltpu.VMEM((slabs, 4, 32, 8, 128), F32), padded, padded,
            pltpu.VMEM((tokens, width), BF16), pltpu.VMEM((tokens, width), BF16),
        ] + extra,
        compiler_params=pltpu.CompilerParams(
            vmem_limit_bytes=56 * MIB, collective_id=4 if sums_over else 3, has_side_effects=True
        ),
        name="feed_forward",
    )(n2, n2t, g2, fc1, small, fc2, *arrays)


def flip(index, bit):
    return index + bit - 2 * bit * lax.rem(index // bit, 2)


def bits_of(count):
    return [1 << b for b in range(count.bit_length() - 1)]


def digits_of(index, wide):
    levels = wide.bit_length() - 1
    return [lax.rem(index // (1 << (levels - 1 - i)), 2) for i in range(levels)]


def static_digits(index, wide):
    levels = wide.bit_length() - 1
    return [(index >> (levels - 1 - i)) & 1 for i in range(levels)]


def at(w, n):
    return {"wide": w, "narrow": n}


def greet(places):
    barrier = pltpu.get_barrier_semaphore()
    for place in places:
        pl.semaphore_signal(barrier, inc=1, device_id=place, device_id_type=pl.DeviceIdType.MESH)
    pl.semaphore_wait(barrier, len(places))


def greet_all(place):
    barrier = pltpu.get_barrier_semaphore()
    total = place.total

    def body(k, carry):
        pl.semaphore_signal(
            barrier, inc=1, device_id=place.device(lax.rem(place.sid + k, total)),
            device_id_type=pl.DeviceIdType.MESH,
        )
        return carry

    lax.fori_loop(1, total, body, 0)
    pl.semaphore_wait(barrier, total - 1)


def remote(src, dst, send_sem, recv_sem, place):
    return pltpu.make_async_remote_copy(
        src_ref=src, dst_ref=dst, send_sem=send_sem, recv_sem=recv_sem, device_id=place,
        device_id_type=pl.DeviceIdType.MESH,
    )


class Place:
    def __init__(self, wide, narrow):
        self.wide, self.narrow = wide, narrow
        self.w, self.n = lax.axis_index("wide"), lax.axis_index("narrow")
        self.total, self.half = wide * narrow, wide * narrow // 2
        self.me = self.w * narrow + self.n
        self.core = lax.rem(self.w, 2)
        self.slot = (self.w // 2) * narrow + self.n
        self.sid = self.core * self.half + self.slot
        self.sibling = at(flip(self.w, 1), self.n)

    def device(self, sid):
        core, slot = sid // self.half, lax.rem(sid, self.half)
        return at(2 * (slot // self.narrow) + core, lax.rem(slot, self.narrow))

    def order_of(self, sid):
        core, slot = divmod(sid, self.half)
        return (2 * (slot // self.narrow) + core) * self.narrow + slot % self.narrow

    def partners(self):
        places = [at(self.w, lax.rem(self.n + k, self.narrow)) for k in range(1, self.narrow)]
        return places + [at(flip(self.w, bit), self.n) for bit in bits_of(self.wide)]

    def all_copies(self, src_of, dst, sends, recvs):
        def copy(k):
            sid = lax.rem(self.sid + k, self.total)
            return remote(src_of(sid), dst, sends.at[k], recvs.at[k], self.device(sid))

        return Exchange(copy, self.total)

    def kin_copies(self, src_of, dst, sends, recvs):
        def copy(k):
            slot = lax.rem(self.slot + k, self.half)
            return remote(src_of(slot), dst, sends.at[k], recvs.at[k],
                          self.device(self.core * self.half + slot))

        return Exchange(copy, self.half)

    def to_all(self, *refs):
        return self.all_copies(*refs).start()

    def to_kin(self, *refs):
        return self.kin_copies(*refs).start()

    def to_all_wait(self, *refs):
        self.all_copies(*refs).wait()

    def to_kin_wait(self, *refs):
        self.kin_copies(*refs).wait()


class Exchange:
    def __init__(self, copy, count):
        self.copy, self.count = copy, count

    def start(self):
        def body(k, carry):
            self.copy(k).start()
            return carry

        lax.fori_loop(1, self.count, body, 0)
        return self.wait

    def wait(self):
        def body(k, carry):
            self.copy(k).wait()
            return carry

        lax.fori_loop(1, self.count, body, 0)


def bit_sizes(wide):
    return (2,) * (wide.bit_length() - 1)


class Transfer:
    def __init__(self, place, sends, recvs, chunk, columns):
        self.p, self.sends, self.recvs, self.chunk = place, sends, recvs, chunk
        start, size = columns
        self.all = pl.ds(start, size)
        levels = len(bit_sizes(place.wide))
        far = list(range(levels - 1))
        if size % 256:
            self.parts = [(self.all, far)]
        else:
            self.parts = [(pl.ds(start, size // 2), far), (pl.ds(start + size // 2, size // 2), far[::-1])]
        self.stages = levels + 1
        self.bits = digits_of(place.w, place.wide)
        self.count = 0

    def copy(self, src, dst, place):
        slot = self.count
        self.count += 1
        return remote(src, dst, self.sends.at[self.chunk, slot], self.recvs.at[self.chunk, slot], place)

    def along(self, level):
        return at(flip(self.p.w, 1 << (len(self.bits) - 1 - level)), self.p.n)

    def in_line(self, k):
        return at(self.p.w, lax.rem(self.p.n + k, self.p.narrow))

    def copies(self, stage):
        self.count = 0
        for before in range(stage):
            self.count += len(self.make(before, True))
        return self.make(stage, False)

    def start(self, stage):
        for copy in self.copies(stage):
            copy.start()

    def finish(self):
        pass


class Gather(Transfer):
    def __init__(self, place, src, dst, sends, recvs, chunk, columns):
        super().__init__(place, sends, recvs, chunk, columns)
        self.src, self.dst = src, dst

    def make(self, stage, count_only):
        levels = len(self.bits)
        if stage == 0:
            ks = range(1, self.p.narrow)
            if count_only:
                return list(ks)
            return [
                self.copy(self.src.at[:, self.all],
                          self.dst.at[(*self.bits, self.p.n, slice(None), self.all)], self.in_line(k))
                for k in ks
            ]
        if stage == levels:
            parts = [(self.all, list(range(levels)))]
        else:
            parts = self.parts
        if count_only:
            return list(parts)
        found = []
        for columns, order in parts:
            index = list(self.bits)
            for level in order[: stage - 1]:
                index[level] = slice(None)
            part = self.dst.at[(*index, slice(None), slice(None), columns)]
            found.append(self.copy(part, part, self.along(order[stage - 1])))
        return found

    def wait(self, stage):
        for copy in self.copies(stage):
            copy.wait_recv()

    def finish(self):
        for stage in range(self.stages):
            for copy in self.copies(stage):
                copy.wait_send()


class Waves:
    def __init__(self, chunks, lag=2):
        self.chunks, self.wave, self.lag = chunks, 0, lag
        self.stages = chunks[0][0].stages
        self.count = len(chunks) + lag * self.stages

    def run(self, wave):
        for c, jobs in enumerate(self.chunks):
            stage, rest = divmod(wave - c, self.lag)
            if rest:
                continue
            for job in jobs:
                if 1 <= stage <= self.stages:
                    job.wait(stage - 1)
                if 0 <= stage < self.stages:
                    job.start(stage)

    def tick(self, times=1):
        for _ in range(times):
            if self.wave < self.count:
                self.run(self.wave)
                self.wave += 1

    def through(self, chunk):
        while self.wave <= chunk + self.lag * self.stages:
            self.tick()

    def at_hook(self, hook, hooks):
        left = self.count - 1
        for wave in range(1 + hook * left // hooks, 1 + (hook + 1) * left // hooks):
            self.run(wave)

    def finish(self):
        for jobs in self.chunks:
            for job in jobs:
                job.finish()

    def end(self):
        self.tick(self.count)
        self.finish()


def job_sems(wide, narrow, chunks):
    per = narrow - 1 + 2 * (wide.bit_length() - 1)
    return [pltpu.SemaphoreType.DMA((len(chunks), per))] * 2


def gather_jobs(place, srcs, dsts, sends, recvs, chunks, lag=2):
    return Waves([
        [Gather(place, srcs[i], dsts[i], sends, recvs, c, columns)]
        for c, (i, *columns) in enumerate(chunks)
    ], lag)


def gathered_shape(wide, narrow, shape):
    return like((*bit_sizes(wide), narrow, *shape), BF16)


def thirds(i, size):
    return [(i, t * (size // 3), size // 3) for t in range(3)]


class Scatter(Transfer):
    def __init__(self, place, src, buffers, out, sends, recvs, chunk, columns):
        super().__init__(place, sends, recvs, chunk, columns)
        self.src, self.out = src, out
        self.halves, self.line, self.got = buffers[:-2], buffers[-2], buffers[-1]
        self.rows = self.line.shape[1]
        core = len(self.bits) - 1
        self.parts = [(columns, [core] + order) for columns, order in self.parts]

    def make(self, stage, count_only):
        levels = len(self.bits)
        if stage == levels:
            ks = range(1, self.p.narrow)
            if count_only:
                return list(ks)
            return [
                self.copy(self.line.at[lax.rem(self.p.n + k, self.p.narrow), :, self.all],
                          self.got.at[k - 1, :, self.all], self.in_line(k))
                for k in ks
            ]
        parts = self.parts if stage else [(self.all, self.parts[0][1])]
        if count_only:
            return list(parts)
        found = []
        for columns, order in parts:
            source, index, kept = self.level(order, stage, True)
            into = self.halves[stage].at[(*kept, slice(None), columns)]
            found.append(self.copy(source.at[(*index, slice(None), columns)], into, self.along(order[stage])))
        return found

    def level(self, order, stage, theirs):
        source = self.src if stage == 0 else self.halves[stage - 1]
        left = [level for level in range(len(self.bits)) if level not in order[:stage]]
        bit = self.bits[order[stage]]
        bit = 1 - bit if theirs else bit
        index = [bit if level == order[stage] else slice(None) for level in left]
        return source, index, [slice(None)] * (len(left) - 1)

    def wait(self, stage):
        for copy in self.copies(stage):
            copy.wait()
        levels = len(self.bits)
        if stage == levels:
            value = self.line[self.p.n, :, self.all].astype(F32)
            for k in range(1, self.p.narrow):
                value = value + self.got[k - 1, :, self.all].astype(F32)
            self.out[:, self.all] = value
            return
        for columns, order in self.parts:
            source, index, kept = self.level(order, stage, False)
            into = self.halves[stage]
            for j in range(1 << len(kept)):
                digits = [(j >> i) & 1 for i in range(len(kept))]
                mine = [v if not isinstance(v, slice) else None for v in index]
                rest = iter(digits)
                mine = [next(rest) if v is None else v for v in mine]
                self.add(source, tuple(mine), into, tuple(digits), columns, stage == levels - 1)

    def add(self, source, mine, into, arrived, columns, last):
        if last:
            total = source[(*mine, slice(None), columns)].astype(F32) + into[
                (*arrived, slice(None), columns)
            ].astype(F32)
            for m in range(self.p.narrow):
                rows = slice(m * self.rows, (m + 1) * self.rows)
                self.line[m, :, columns] = total[rows].astype(BF16)
            return

        def body(i, carry):
            rows = pl.ds(pl.multiple_of(i * 16, 16), 16)
            into[(*arrived, rows, columns)] = (
                source[(*mine, rows, columns)].astype(F32) + into[(*arrived, rows, columns)].astype(F32)
            ).astype(BF16)
            return carry

        lax.fori_loop(0, into.shape[-2] // 16, body, 0)


def scatter_scratch(wide, narrow, shapes):
    scratch = []
    for *_, height, columns in shapes:
        for stage in range(wide.bit_length() - 1):
            scratch.append(pltpu.VMEM((*bit_sizes(wide)[stage + 1 :], height, columns), BF16))
        scratch.append(pltpu.VMEM((narrow, height // narrow, columns), BF16))
        scratch.append(pltpu.VMEM((narrow - 1, height // narrow, columns), BF16))
    return scratch


def scatter_jobs(place, srcs, outs, buffers, sends, recvs, chunks, lag=2):
    per = len(buffers) // len(srcs)
    return Waves([
        [Scatter(place, srcs[i], buffers[i * per : (i + 1) * per], outs[i], sends, recvs, c, columns)]
        for c, (i, *columns) in enumerate(chunks)
    ], lag)


def owned_shape(shape, narrow):
    return like((shape[-2] // narrow, shape[-1]), F32)


def move_lanes(tiles, moves, count):
    rows = tiles[0].shape[0]
    lane = lax.broadcasted_iota(jnp.int32, (rows, 128), 1)
    out = [jnp.zeros((rows, 128), F32) for _ in range(count)]
    for start, to, length in moves:
        while length:
            size = min(length, 128 - start % 128, 128 - to % 128)
            tile = tiles[start // 128]
            turn = (to - start) % 128
            if turn:
                tile = pltpu.roll(tile, turn, 1)
            inside = (lane >= to % 128) & (lane < to % 128 + size)
            out[to // 128] = jnp.where(inside, tile, out[to // 128])
            start, to, length = start + size, to + size, length - size
    return out


def tiles_of(values):
    return [values[:, i : i + 128] for i in range(0, values.shape[1], 128)]


def front_kernel(wide, narrow, chunks, count, own, own_ff, *refs):
    (x_ref, cot_ref, mask_ref, order_ref, cond_ref, ada_ref, bias_ref, small_ref, fc1_ref) = refs[:9]
    srcs = refs[9 : 9 + count]
    (mod_ref, sils_ref, model_ref, hidden_ref, lat_ref, gout_ref, g2_ref, normed_ref, mixed_ref,
     keep_ref, fc2b_ref, fc1b_ref) = refs[9 + count : 21 + count]
    dsts = refs[21 + count : 22 + 2 * count]
    (fc1a_ref, sil_out, got, part, sib, rows_in, smalls, send_a, recv_a, send_b, recv_b, send_c, recv_c,
     sends, recvs, local) = refs[22 + 2 * count :]
    p = Place(wide, narrow)
    mine = digits_of(p.w, wide)
    model = x_ref.shape[1]
    slabs = model // 128
    own_copies = [
        pltpu.make_async_copy(srcs[i], dsts[1 + i].at[(*mine, p.n)], local.at[i]) for i in range(count)
    ]
    for copy in own_copies:
        copy.start()
    waves = gather_jobs(p, [small_ref, fc1a_ref, *srcs], [smalls, *dsts], sends, recvs, chunks)
    cond = cond_ref[...].astype(F32)
    sil = (cond * jax.nn.sigmoid(cond)).astype(BF16).astype(F32)
    tiles = tiles_of(sil)
    for sid in range(p.total):
        d = p.order_of(sid)
        sil_out[sid] = move_lanes(tiles, [(own * d, 0, own)], 1)[0]
    greet_all(p)
    waves.tick(2)
    got[p.sid] = sil_out[p.sid]
    wait_sil = p.to_all(lambda sid: sil_out.at[sid], got.at[p.sid], send_a, recv_a)

    def arrange(t):
        rows = pl.ds(t * GROUP, GROUP)
        tokens = dot_nn(order_ref[...], x_ref[rows, :])
        unit, _ = unit_rows(tokens)
        kept = dot_nn(order_ref[...], mask_ref[rows, :])
        gout = dot_nn(order_ref[...], cot_ref[rows, :]) * jnp.concatenate([kept] * slabs, axis=1)
        for g in range(4):
            src = slice(64 * g, 64 * g + 64)
            dst = pl.ds(g * GROUP + 64 * t, 64)
            lat_ref[dst, :] = tokens[src].astype(BF16)
            gout_ref[dst, :] = gout[src].astype(BF16)
            keep_ref[dst, :] = (kept[src] - 1.0) * 1e30
            for s in range(slabs):
                tile = unit[src, s * 128 : s * 128 + 128].reshape(8, 8, 128)
                normed_ref[s, g, 2 + 8 * t : 10 + 8 * t] = tile

    arrange(0)
    wait_sil()
    sil = got[...].reshape(p.total, 128)
    sils_ref[...] = sil
    product = dot_nn(sil[:, :own].astype(BF16), ada_ref[...]) + bias_ref[...]
    for d in range(p.total):
        part[d // p.half, d % p.half] = product[d : d + 1, :]
    to_sibling = remote(part.at[1 - p.core], sib, send_b, recv_b, p.sibling)
    to_sibling.start()
    for copy in own_copies:
        copy.wait()
    smalls[(*mine, p.n)] = small_ref[...]
    waves.tick()
    arrange(1)
    to_sibling.wait()
    part[p.core] = part[p.core] + sib[...]
    rows_in[p.slot] = part[p.core, p.slot]
    wait_rows = p.to_kin(lambda slot: part.at[p.core, slot], rows_in.at[p.slot], send_c, recv_c)
    waves.tick()
    arrange(2)
    columns = tiles_of(fc1_ref[...].astype(F32))
    for h, ref in enumerate((fc1a_ref, fc1b_ref)):
        moves = [
            (own_ff * d + own_ff // 2 * h, own_ff // 2 * d, own_ff // 2) for d in range(p.total)
        ]
        ref[...] = jnp.concatenate(move_lanes(columns, moves, len(columns) // 2), axis=1).astype(BF16)
    own_fc1 = pltpu.make_async_copy(fc1a_ref, dsts[0].at[(*mine, p.n)], local.at[count])
    own_fc1.start()
    waves.tick()
    arrange(3)
    clear_edges(normed_ref)
    waves.tick()
    wait_rows()
    mod = jnp.sum(rows_in[...], axis=0)
    for i in range(6):
        mod_ref[i : i + 1, :] = mod[:, i * model : (i + 1) * model]
    own_fc1.wait()
    waves.through(0)
    pieces = [smalls[(*static_digits(d // narrow, wide), d % narrow)].astype(F32) for d in range(p.total)]
    moves = [(128 * d, own * d, own) for d in range(p.total)]
    model_ref[...] = jnp.concatenate(move_lanes([q[:16] for q in pieces], moves, slabs), axis=1)
    half, hidden = own_ff // 2, fc1_ref.shape[1]
    moves = [
        (128 * d + half * h, hidden // 2 * h + half * d, half) for d in range(p.total) for h in (0, 1)
    ]
    hidden_ref[...] = jnp.concatenate(
        move_lanes([q[16:] for q in pieces], moves, hidden // 128), axis=1
    )
    waves.tick()

    shift, scale, gate = mod_ref[0:1, :], mod_ref[1:2, :], mod_ref[5:6, :]
    total = jnp.zeros((8, model), F32)
    for g in range(4):
        rows = pl.ds(g * GROUP, GROUP)
        two = gout_ref[rows, :].astype(F32) * gate
        total = total + row_sum(two)
        g2_ref[rows, :] = two.astype(BF16)
    fc2b_ref[...] = total
    masks = edge_masks()
    for s in range(slabs):
        lanes = pl.ds(s * 128, 128)
        at_s = slice(s * 128, s * 128 + 128)
        shift8 = jnp.broadcast_to(shift[:, at_s], (8, 128))
        scale8 = jnp.broadcast_to(1.0 + scale[:, at_s], (8, 128))
        normed_ref[s, :, 2:34] = normed_ref[s, :, 2:34] * scale8 + shift8
        k = [jnp.broadcast_to(model_ref[n : n + 1, at_s], (8, 128)) for n in range(9)]
        bias = jnp.broadcast_to(model_ref[9:10, at_s], (8, 128))

        def body(r, carry):
            for gi in (0, 1):
                for gj in (0, 1):
                    pair = conv_cell(normed_ref, s, gi, gj, r, k, bias, masks)
                    mixed_ref[group_rows(gi, gj, r), lanes] = jnp.concatenate(pair, 0).astype(BF16)
            return carry

        lax.fori_loop(0, HALF, body, 0)
        waves.tick()
    waves.end()


def front(wide, narrow, x, cot, mask, order, cond, ada, bias, small, fc1, blocks, chunks):
    total = wide * narrow
    tokens, model = x.shape
    slabs, count, columns = model // 128, len(blocks), ada.shape[1]
    hidden = fc1.shape[1]
    own, own_ff = model // total, hidden // total
    inside = pl.BlockSpec(memory_space=pltpu.VMEM)
    anywhere = pl.BlockSpec(memory_space=pl.ANY)
    all_sems = pltpu.SemaphoreType.DMA((total,))
    one_sem = pltpu.SemaphoreType.DMA
    kin_sems = pltpu.SemaphoreType.DMA((total // 2,))
    return pl.pallas_call(
        functools.partial(front_kernel, wide, narrow, chunks, count, own, own_ff),
        in_specs=[inside] * 9 + [anywhere] * count,
        out_specs=[inside] * 12 + [anywhere] * (count + 1),
        out_shape=[
            like((8, model), F32), like((total, 128), F32), like((16, model), F32),
            like((16, hidden), F32), like((tokens, model), BF16), like((tokens, model), BF16),
            like((tokens, model), BF16), like((slabs, 4, 36, 8, 128), F32),
            like((tokens, model), BF16), like((tokens, 128), F32), like((8, model), F32),
            like((own, hidden // 2), BF16),
            gathered_shape(wide, narrow, (own, hidden // 2)),
        ] + [gathered_shape(wide, narrow, b.shape) for b in blocks],
        scratch_shapes=[
            pltpu.VMEM((own, hidden // 2), BF16), pltpu.VMEM((total, 1, 128), F32),
            pltpu.VMEM((total, 1, 128), F32), pltpu.VMEM((2, total // 2, 1, columns), F32),
            pltpu.VMEM((total // 2, 1, columns), F32), pltpu.VMEM((total // 2, 1, columns), F32),
            pltpu.VMEM((*bit_sizes(wide), narrow, 32, 128), BF16),
            all_sems, all_sems, one_sem, one_sem, kin_sems, kin_sems,
            *job_sems(wide, narrow, chunks), pltpu.SemaphoreType.DMA((count + 1,)),
        ],
        compiler_params=pltpu.CompilerParams(
            vmem_limit_bytes=56 * MIB, collective_id=0, has_side_effects=True
        ),
        name="front",
    )(x, cot, mask, order, cond, ada, bias, small, fc1, *blocks)


def attend_kernel(wide, narrow, chunks, count, *refs):
    mixed_ref, lat_ref, keep_ref, mod_ref, small_ref, qkv_ref, proj_ref = refs[:7]
    srcs = refs[7 : 7 + count]
    (triple_ref, probs_ref, att_ref, branch_ref, middle_ref, n2_ref,
     n2t_ref) = refs[7 + count : 14 + count]
    dsts = refs[14 + count : 14 + 2 * count]
    sends, recvs, local = refs[14 + 2 * count :]
    step = pl.program_id(0)
    p = Place(wide, narrow)
    waves = gather_jobs(p, srcs, dsts, sends, recvs, chunks)
    own_copies = [
        pltpu.make_async_copy(
            srcs[i], dsts[i].at[(*digits_of(p.w, wide), p.n)], local.at[i]
        ) for i in range(count)
    ]

    def on(when, work):
        pl.when(step == when)(work)

    def first():
        for copy in own_copies:
            copy.start()
        greet(p.partners())
        waves.run(0)
        for copy in own_copies:
            copy.wait()

    def hook(position):
        for when in range(4):
            on(when, lambda: waves.at_hook(2 * when + position, 8))

    on(0, first)
    model = lat_ref.shape[1]
    slabs = model // 128
    triple_ref[...] = dot_nn(mixed_ref[...], qkv_ref[...]).astype(BF16)
    lane = lax.broadcasted_iota(jnp.int32, (GROUP, 128), 1)
    left = lane < HEAD
    keep = jnp.concatenate([keep_ref[...]] * 2, axis=1)
    for s in range(slabs):
        q = triple_ref[:, s * 128 : s * 128 + 128]
        k = triple_ref[:, model + s * 128 : model + s * 128 + 128] * jnp.asarray(0.125, BF16)
        v = triple_ref[:, 2 * model + s * 128 : 2 * model + s * 128 + 128]
        outs = []
        for h in (0, 1):
            mine = left if h == 0 else jnp.logical_not(left)
            scores = dot_nt(jnp.where(mine, k, jnp.zeros_like(k)), q) + keep
            e = jnp.exp(scores - jnp.max(scores, axis=0, keepdims=True))
            prob = (e * (1.0 / jnp.sum(e, axis=0, keepdims=True))).astype(BF16)
            probs_ref[2 * s + h, 0] = prob
            outs.append(dot_tn(prob, v))
        att_ref[:, s * 128 : s * 128 + 128] = jnp.where(left, outs[0], outs[1]).astype(BF16)
        if s == slabs // 2 - 1:
            hook(0)
    branch = dot_nn(att_ref[...], proj_ref[...]) + small_ref[10:11, :]
    middle = lat_ref[...].astype(F32) + mod_ref[2:3, :] * branch
    unit, _ = unit_rows(middle)
    branch_ref[...] = branch
    middle_ref[...] = middle
    n2 = unit * (1.0 + mod_ref[4:5, :]) + mod_ref[3:4, :]
    n2_ref[...] = n2.astype(BF16)
    n2t_ref[...] = n2.T.astype(BF16)
    hook(1)
    on(3, waves.finish)


def attend(wide, narrow, mixed, lat, keep, mod, small, qkv, proj, blocks, chunks):
    tokens, model = lat.shape
    heads, count = model // HEAD, len(blocks)
    by_group = lambda columns: pl.BlockSpec((GROUP, columns), lambda g: (g, 0))
    anywhere = pl.BlockSpec(memory_space=pl.ANY)
    return pl.pallas_call(
        functools.partial(attend_kernel, wide, narrow, chunks, count),
        grid=(4,),
        in_specs=[
            by_group(model), by_group(model), by_group(128), whole(mod.shape),
            whole(small.shape), once(qkv.shape), once(proj.shape),
        ] + [anywhere] * count,
        out_specs=[
            by_group(3 * model), pl.BlockSpec((heads, 1, GROUP, GROUP), lambda g: (0, g, 0, 0)),
            by_group(model), by_group(model), by_group(model), by_group(model),
            pl.BlockSpec((model, GROUP), lambda g: (0, g)),
        ] + [anywhere] * count,
        out_shape=[
            like((tokens, 3 * model), BF16), like((heads, 4, GROUP, GROUP), BF16),
            like((tokens, model), BF16), like((tokens, model), F32),
            like((tokens, model), F32), like((tokens, model), BF16), like((model, tokens), BF16),
        ] + [gathered_shape(wide, narrow, b.shape) for b in blocks],
        scratch_shapes=[*job_sems(wide, narrow, chunks), pltpu.SemaphoreType.DMA((count,))],
        compiler_params=pltpu.CompilerParams(
            vmem_limit_bytes=56 * MIB, collective_id=1, has_side_effects=True
        ),
        name="attend",
    )(mixed, lat, keep, mod, small, qkv, proj, *blocks)


def back_kernel(wide, narrow, chunks, own, own_ff, *refs):
    (gn2a_ref, gn2b_ref, twoa_ref, twob_ref, middle_ref, branch_ref, gout_ref, att_ref, mixed_ref,
     q_ref, k_ref, v_ref, probs_ref, mod_ref, small_ref, proj_ref, wq_ref, wk_ref, wv_ref,
     lat_ref, normed_ref, fc2b_ref, hida_ref, hidb_ref, sils_ref, ada_ref, fc1s_ref,
     fc2s_ref) = refs[:28]
    (rows_ref, xg_ref, wgrad_ref, cond_ref, small_out, qkvg_ref, projg_ref, fc1g_ref,
     fc2g_ref) = refs[28:37]
    (ga, gmid, gmix, gmoved, sums, proj_src, qkv_src, early, late, cuts_in, hcuts, hcuts_in, part, cond_in,
     send_a, recv_a, send_b, recv_b, send_c, recv_c, send_d, recv_d, send_e, recv_e, send_f, recv_f,
     send_g, recv_g) = refs[37:65]
    buffers, (sends, recvs) = refs[65:-2], refs[-2:]
    step = pl.program_id(0)
    model = lat_ref.shape[1]
    slabs = model // 128
    last = 3 + slabs
    p = Place(wide, narrow)
    half, hidden = own_ff // 2, 2 * hida_ref.shape[1]
    waves = scatter_jobs(p, [fc1s_ref, fc2s_ref, proj_src, qkv_src],
                         [fc1g_ref, fc2g_ref, projg_ref, qkvg_ref], buffers, sends, recvs, chunks)
    gbl = xg_ref
    mine = lambda ref: ref.at[p.core, p.slot]

    @pl.when(step == 0)
    def _():
        greet_all(p)
        waves.run(0)
        waves.run(1)
        sums[...] = jnp.zeros_like(sums)
        gmix[...] = jnp.zeros_like(gmix)
        clear_edges(gmoved)
        tiles = tiles_of(hida_ref[...]) + tiles_of(hidb_ref[...])
        for sid in range(p.total):
            d = p.order_of(sid)
            moves = [(half * d, 0, half), (hidden // 2 + half * d, half, half)]
            hcuts[sid] = move_lanes(tiles, moves, 1)[0]
        hcuts_in[p.sid] = hcuts[p.sid]
        p.to_all(lambda sid: hcuts.at[sid], hcuts_in.at[p.sid], send_g, recv_g)

    @pl.when(step < 4)
    def _():
        rows = pl.ds(pl.multiple_of(step * GROUP, GROUP), GROUP)
        middle = middle_ref[...]
        two = twoa_ref[...] + twob_ref[...] + small_ref[11:12, :]
        gout = gout_ref[...].astype(F32)
        rows_ref[...] = (middle + mod_ref[5:6, :] * two).astype(BF16)
        sums[3] += row_sum(gout * two)
        unit, scale = unit_rows(middle)
        gn2 = gn2a_ref[...] + gn2b_ref[...]
        sums[1] += row_sum(gn2)
        sums[2] += row_sum(gn2 * unit)
        gm = gout + unit_back(gn2 * (1.0 + mod_ref[4:5, :]), unit, scale)
        gmid[rows, :] = gm
        sums[0] += row_sum(gm * branch_ref[...])
        gb = gm * mod_ref[2:3, :]
        sums[4] += row_sum(gb)
        low = gb.astype(BF16)
        gbl[rows, :] = low
        ga[rows, :] = dot_nt(low, proj_ref[...]).astype(BF16)

    for when, wave in ((1, 2), (1, 3), (2, 4), (3, 5)):
        pl.when(step == when)(lambda: waves.run(wave))

    @pl.when(step == 3)
    def _():
        proj_src[...] = dot_tn(att_ref[...], gbl[...]).astype(BF16).reshape(proj_src.shape)
        waves.run(6)
        for i in range(4):
            early[p.core, p.slot, :, i * model : (i + 1) * model] = jnp.sum(
                sums[i], axis=0, keepdims=True
            )
        p.to_kin(lambda slot: mine(early), mine(early), send_a, recv_a)

    @pl.when(step >= 4)
    def _():
        s = step - 4
        lane = lax.broadcasted_iota(jnp.int32, (GROUP, 128), 1)
        left = lane < HEAD
        eighth = jnp.asarray(0.125, BF16)
        lanes = pl.ds(pl.multiple_of(s * 128, 128), 128)
        weight = jnp.concatenate([wq_ref[...], wk_ref[...], wv_ref[...]], axis=1)
        grads = []
        for g in range(4):
            rows = slice(g * GROUP, (g + 1) * GROUP)
            q, k, v = q_ref[rows, :] * eighth, k_ref[rows, :] * eighth, v_ref[rows, :]
            grad = ga[rows, lanes]
            gq = gk = gv = None
            for h in (0, 1):
                keep = left if h == 0 else jnp.logical_not(left)
                only = lambda value: jnp.where(keep, value, jnp.zeros_like(value))
                p_low = probs_ref[h, g]
                prob = p_low.astype(F32)
                gh = only(grad)
                gp = dot_nt(v, gh)
                inner = jnp.sum(prob * gp, axis=0, keepdims=True)
                gs = (prob * (gp - inner)).astype(BF16)
                terms = (dot_tn(gs, only(k)), dot_nn(gs, only(q)), dot_nn(p_low, gh))
                if h == 0:
                    gq, gk, gv = terms
                else:
                    gq, gk, gv = gq + terms[0], gk + terms[1], gv + terms[2]
            grads.append(jnp.concatenate([gq, gk, gv], axis=1).astype(BF16))
            gmixed = dot_nt(grads[-1], weight)
            for t in range(slabs):
                gmix[t + 1, g, 2:34] += gmixed[:, t * 128 : t * 128 + 128].reshape(32, 8, 128)
        grad = jnp.concatenate(grads, axis=0)
        columns = pl.ds(pl.multiple_of(s * 384, 128), 384)
        found = dot_tn(mixed_ref[...], grad).astype(BF16)
        qkv_src[..., columns] = found.reshape(*qkv_src.shape[:-1], 384)

    for s in range(slabs):
        pl.when(step == 4 + s)(lambda: waves.run(7 + s))

    @pl.when(step == 6)
    def _():
        p.to_kin_wait(lambda slot: mine(early), mine(early), send_a, recv_a)
        remote(early.at[p.core], early.at[p.core], send_d, recv_d, p.sibling).start()

    @pl.when(step == last)
    def _():
        waves.wave = 7 + slabs
        masks = edge_masks()
        rows_out = []
        for s in range(slabs):
            at_s = slice(s * 128, s * 128 + 128)
            k = [jnp.broadcast_to(small_ref[n : n + 1, at_s], (8, 128)) for n in range(9)]

            def move(r, total):
                for gi in (0, 1):
                    for gj in (0, 1):
                        pair = load_pair(gmix, s + 1, gi, gj, r)
                        total = total + pair[0] + pair[1]
                        store_pair(gmoved, 0, gi, gj, r, shift_pair(pair, 1 - gj, *masks))
                return total

            total = lax.fori_loop(0, HALF, move, jnp.zeros((8, 128), F32))

            def put(gi, gj, r, pair):
                store_pair(gmix, s, gi, gj, r, pair)

            found = conv_back(0, k, normed_ref.at[s : s + 1], gmix.at[s + 1 : s + 2], gmoved, put)
            late[p.core, p.slot, :, at_s] = jnp.sum(found[9], axis=0, keepdims=True)
            column = [jnp.sum(v, axis=0, keepdims=True) for v in (*found[:9], total)]
            column.append(jnp.sum(sums[4, :, at_s], axis=0, keepdims=True))
            column.append(jnp.sum(fc2b_ref[:, at_s], axis=0, keepdims=True))
            rows_out.append(jnp.concatenate(column + [jnp.zeros((4, 128), F32)], axis=0))
            if s % 2:
                waves.tick()
        scale_sum = jnp.zeros((8, model), F32)
        for g in range(4):
            rows = pl.ds(g * GROUP, GROUP)
            unit, scale = unit_rows(lat_ref[rows, :].astype(F32))
            gn = jnp.concatenate(
                [gmix[s, g, 2:34].reshape(GROUP, 128) for s in range(slabs)], axis=1
            )
            scale_sum = scale_sum + row_sum(gn * unit)
            gmid[rows, :] = gmid[rows, :] + unit_back(gn * (1.0 + mod_ref[1:2, :]), unit, scale)
        late[p.core, p.slot, :, model:] = jnp.sum(scale_sum, axis=0, keepdims=True)
        wait_late = p.to_kin(lambda slot: mine(late), mine(late), send_c, recv_c)
        waves.tick()
        p.to_all_wait(lambda sid: hcuts.at[sid], hcuts_in.at[p.sid], send_g, recv_g)
        small_out[16:, :] = jnp.sum(hcuts_in[...], axis=0)
        cuts = hcuts
        modulation = tiles_of(late[p.core, p.slot]) + tiles_of(early[p.core, p.slot])
        share = 6 * own
        for sid in range(p.total):
            d = p.order_of(sid)
            piece = move_lanes(rows_out, [(own * d, 0, own)], 1)[0][:12]
            bias = move_lanes(modulation, [(share * d, 0, share)], -(-share // 128))
            rest = [jnp.zeros((4 - len(bias), 128), F32)]
            cuts[sid] = jnp.concatenate([piece, *bias, *rest], axis=0)
        cuts_in[p.sid] = cuts[p.sid]
        wait_cuts = p.to_all(lambda sid: cuts.at[sid], cuts_in.at[p.sid], send_b, recv_b)
        xg_ref[...] = gmid[...].astype(BF16)
        wait_late()
        swap_late = remote(late.at[p.core], late.at[p.core], send_e, recv_e, p.sibling)
        swap_late.start()
        waves.tick()
        remote(early.at[p.core], early.at[p.core], send_d, recv_d, p.sibling).wait()
        swap_late.wait()
        sil = sils_ref[:, :own].astype(BF16)
        cond = None
        for ref, start in ((late, 0), (early, 2 * model)):
            size = ref.shape[-1]
            span = slice(start, start + size)
            found = ref[...].reshape(p.total, size)
            low = found.astype(BF16)
            wgrad_ref[:, span] = dot_tn(sil, low)
            term = dot_nt(low, ada_ref[:, span])
            cond = term if cond is None else cond + term
        cond = jnp.concatenate([cond, jnp.zeros((p.total, 128 - own), F32)], axis=1)
        for sid in range(p.total):
            part[sid] = cond[sid : sid + 1, :]
        cond_in[p.me] = part[p.sid]
        wait_cond = p.to_all(lambda sid: part.at[sid], cond_in.at[p.me], send_f, recv_f)
        waves.end()
        wait_cuts()
        small_out[:16, :] = jnp.sum(cuts_in[...], axis=0)
        wait_cond()
        cond_ref[...] = cond_in[...]


def back(wide, narrow, gn2, two, middle, branch, gout, att, mixed, triple, probs, mod, small, proj, qkv,
         lat, normed, fc2b, hidden_sums, sils, ada, fc1s, fc2s):
    total = wide * narrow
    tokens, model = lat.shape
    slabs, columns = model // 128, ada.shape[1]
    hidden = 2 * hidden_sums[0].shape[1]
    own, own_ff = ada.shape[0], hidden // total
    by_group = pl.BlockSpec((GROUP, model), lambda t: (jnp.minimum(t, 3), 0))
    slab = lambda t: jnp.clip(t - 4, 0, slabs - 1)
    third = lambda rows, i: pl.BlockSpec((rows, 128), lambda t: (0, i * slabs + slab(t)))
    all_sems, kin_sems = (pltpu.SemaphoreType.DMA((n,)) for n in (total, total // 2))
    one_sem = pltpu.SemaphoreType.DMA
    padded = lambda count: pltpu.VMEM((count, 4, 36, 8, 128), F32)
    height = model // wide
    bits = bit_sizes(wide)
    shapes = [fc1s.shape, fc2s.shape, (*bits, height, model), (*bits, height, 3 * model)]
    chunks = thirds(0, hidden // 2) + thirds(1, model) + [(2, 0, model)]
    chunks += [(3, 384 * s, 384) for s in range(slabs)]
    full = lambda a: once(a.shape)
    outs = [
        like((tokens, model), BF16), like((tokens, model), BF16), like((own, columns), F32),
        like((total, 1, 128), F32), like((32, 128), F32), like((own, 3 * model), F32),
        like((own, model), F32), like((own, hidden // 2), F32), like((own_ff // 2, model), F32),
    ]
    return pl.pallas_call(
        functools.partial(back_kernel, wide, narrow, chunks, own, own_ff),
        grid=(4 + slabs,),
        in_specs=[by_group] * 7 + [full(att), full(mixed)] + [third(tokens, i) for i in range(3)] + [
            pl.BlockSpec((2, 4, GROUP, GROUP), lambda t: (slab(t), 0, 0, 0)),
            full(mod), full(small), full(proj), third(model, 0), third(model, 1), third(model, 2),
            full(lat), full(normed), full(fc2b), full(hidden_sums[0]), full(hidden_sums[1]),
            full(sils), full(ada), full(fc1s), full(fc2s),
        ],
        out_specs=[by_group] + [once(o.shape) for o in outs[1:]],
        out_shape=outs,
        scratch_shapes=[
            pltpu.VMEM((tokens, model), BF16), pltpu.VMEM((tokens, model), F32),
            padded(slabs + 1), padded(1), pltpu.VMEM((5, 8, model), F32),
            pltpu.VMEM(shapes[2], BF16), pltpu.VMEM(shapes[3], BF16),
            pltpu.VMEM((2, total // 2, 1, 4 * model), F32),
            pltpu.VMEM((2, total // 2, 1, 2 * model), F32),
            pltpu.VMEM((total, 16, 128), F32), pltpu.VMEM((total, 16, 128), F32),
            pltpu.VMEM((total, 16, 128), F32),
            pltpu.VMEM((total, 1, 128), F32), pltpu.VMEM((total, 1, 128), F32),
            kin_sems, kin_sems, all_sems, all_sems, kin_sems, kin_sems, one_sem, one_sem,
            one_sem, one_sem, all_sems, all_sems, all_sems, all_sems,
            *scatter_scratch(wide, narrow, shapes), *job_sems(wide, narrow, chunks),
        ],
        compiler_params=pltpu.CompilerParams(
            vmem_limit_bytes=63 * MIB, collective_id=2, has_side_effects=True
        ),
        name="attend_back",
    )(*gn2, *two, middle, branch, gout, att, mixed, triple, triple, triple, probs, mod,
      small, proj, qkv, qkv, qkv, lat, normed, fc2b, *hidden_sums, sils, ada, fc1s,
      fc2s)


def finish_kernel(own, own_ff, order_ref, rows_ref, grads_ref, wgrad_ref, qkvg_ref, projg_ref, fc1a_ref,
                  fc1b_ref, fc2a_ref, fc2b_ref, small_ref, cond_ref, pieces_ref,
                  out_ref, xg_ref, wgrad_out, qkv_out, proj_out, fc1_out, fc2_out, condg_out, adab_out,
                  dw1k_out, dw1b_out, projb_out, fc2b_out, dw2k_out, dw2b_out, fc1b_out):
    model = out_ref.shape[1]
    for src, dst in ((rows_ref, out_ref), (grads_ref, xg_ref)):
        block = src[...].reshape(GROUP, model)
        dst[...] = dot_tn(order_ref[...], block).astype(BF16)

    @pl.when(pl.program_id(0) == 0)
    def _():
        half, hidden, total = own_ff // 2, fc1_out.shape[1], pieces_ref.shape[0]
        wgrad_out[...] = wgrad_ref[...]
        proj_out[...] = projg_ref[...]
        for s in range(model // 128):
            for i in range(3):
                to = i * model + s * 128
                qkv_out[:, to : to + 128] = qkvg_ref[:, s * 384 + i * 128 : s * 384 + i * 128 + 128]
        moves = [
            (hidden // 2 * h + half * d, own_ff * d + half * h, half)
            for d in range(total) for h in (0, 1)
        ]
        tiles = tiles_of(fc1a_ref[...]) + tiles_of(fc1b_ref[...])
        for i, tile in enumerate(move_lanes(tiles, moves, hidden // 128)):
            fc1_out[:, i * 128 : i * 128 + 128] = tile
        fc2_out[:half, :] = fc2a_ref[...]
        fc2_out[half:, :] = fc2b_ref[...]
        tiles = [pieces_ref[d] for d in range(total)]
        moves = [(128 * d, own * d, own) for d in range(total)]
        grad = jnp.concatenate(move_lanes(tiles, moves, model // 128), axis=1)
        cond = cond_ref[...].astype(F32)
        gate = jax.nn.sigmoid(cond)
        condg_out[...] = grad * (gate + cond * gate * (1.0 - gate))
        dw1k_out[...] = small_ref[0:9, :own]
        dw2k_out[...] = small_ref[16:25, :own_ff]
        rows = ((dw1b_out, 9), (projb_out, 10), (fc2b_out, 11), (dw2b_out, 25), (fc1b_out, 26))
        for ref, row in rows:
            ref[...] = small_ref[row : row + 1, : ref.shape[1]]
        for start in range(0, 6 * own, 128):
            size = min(128, 6 * own - start)
            row = 12 + start // 128
            adab_out[:, start : start + size] = small_ref[row : row + 1, :size]


def finish(order, rows, grads, wgrad, qkvg, projg, fc1, fc2, small, cond, pieces):
    tokens, model = rows.shape
    own, hidden, own_ff = wgrad.shape[0], 2 * fc1[0].shape[1], 2 * fc2[0].shape[0]
    split = lambda value: value.reshape(4, 4, 64, model)
    block = pl.BlockSpec((4, 1, 64, model), lambda t: (0, t, 0, 0))
    lines = pl.BlockSpec((GROUP, model), lambda t: (t, 0))
    rest = [wgrad, qkvg, projg, *fc1, *fc2, small, cond, pieces]
    outs = [
        like((tokens, model), BF16), like((tokens, model), BF16), like(wgrad.shape, F32),
        like(qkvg.shape, F32), like(projg.shape, F32), like((own, hidden), F32),
        like((own_ff, model), F32), like((1, model), F32), like((1, 6 * own), F32),
        like((9, own), F32), like((1, own), F32), like((1, own), F32), like((1, own), F32),
        like((9, own_ff), F32), like((1, own_ff), F32), like((1, own_ff), F32),
    ]
    return pl.pallas_call(
        functools.partial(finish_kernel, own, own_ff),
        grid=(4,),
        in_specs=[once(order.shape), block, block] + [once(a.shape) for a in rest],
        out_specs=[lines, lines] + [once(o.shape) for o in outs[2:]],
        out_shape=outs,
        compiler_params=pltpu.CompilerParams(vmem_limit_bytes=60 * MIB),
        name="finish",
    )(order, split(rows), split(grads), *rest)


def on_device(wide, narrow, latents, condition, valid_mask, ada_weight, ada_bias, dw1_kernel, dw1_bias,
              qkv_weight, proj_weight, proj_bias, fc1_weight, fc1_bias, dw2_kernel, dw2_bias,
              fc2_weight, fc2_bias, out_cotangent):
    total = wide * narrow
    w, n = lax.axis_index("wide"), lax.axis_index("narrow")
    me = w * narrow + n
    model, hidden = latents.shape[2], fc1_weight.shape[1]
    own, own_ff = model // total, hidden // total

    bias_at = lax.dynamic_update_slice(
        jnp.zeros((1, 6 * model), F32), ada_bias.astype(F32)[None, :], (0, me * ada_bias.shape[0])
    )
    parts = [(0, dw1_kernel), (9, dw1_bias[None]), (10, proj_bias[None]), (11, fc2_bias[None]),
             (16, dw2_kernel), (25, dw2_bias[None]), (26, fc1_bias[None])]
    small = sum(
        jnp.pad(v, ((row, 32 - row - v.shape[0]), (0, 128 - v.shape[1]))) for row, v in parts
    )
    mask = jnp.broadcast_to(valid_mask[0].astype(BF16)[:, None], (latents.shape[1], 128))
    order = order_matrix()

    chunks = [(0, 0, 128)] + thirds(2, 3 * model) + [(3, 0, model)] + thirds(1, hidden // 2)
    (mod, sils, model_small, hidden_small, lat, gout, g2, normed, mixed, keep, fc2b, fc1b, fc1_one, qkv,
     proj) = front(
        wide, narrow, latents[0], out_cotangent[0], mask, order, condition, ada_weight, bias_at, small,
        fc1_weight, [qkv_weight, proj_weight], chunks,
    )
    qkv, proj = qkv.reshape(model, 3 * model), proj.reshape(model, model)
    fc2a, fc2b_rows = fc2_weight[: own_ff // 2], fc2_weight[own_ff // 2 :]
    triple, probs, att, branch, middle, n2, n2t, fc2_one = attend(
        wide, narrow, mixed, lat, keep, mod, model_small, qkv, proj, [fc2a], thirds(0, model)
    )
    chunks = thirds(0, hidden // 2) + thirds(1, model)
    as_fc1 = lambda rows: rows.reshape(model, hidden // 2)
    as_fc2 = lambda rows: rows.reshape(hidden // 2, model)
    as_lines = lambda grad: grad.reshape(*bit_sizes(wide), grad.shape[0] // wide, grad.shape[1])
    two_a, gn2_a, fc1g, fc2g, sums_a, fc1_two, fc2_two = feed_forward(
        wide, narrow, n2, n2t, g2, as_fc1(fc1_one), hidden_small, 0, as_fc2(fc2_one),
        [fc1b, fc2b_rows], chunks, False,
    )
    two_b, gn2_b, fc1h, fc2h, sums_b, fc1o, fc2o = feed_forward(
        wide, narrow, n2, n2t, g2, as_fc1(fc1_two), hidden_small, 1, as_fc2(fc2_two),
        [as_lines(fc1g), as_lines(fc2g)], chunks, True,
    )
    rows, grads, ada_wgrad, pieces, small, qkvg, projg, fc1p, fc2p = back(
        wide, narrow, (gn2_a, gn2_b), (two_a, two_b), middle, branch, gout, att, mixed, triple, probs,
        mod, model_small, proj, qkv, lat, normed, fc2b, (sums_a, sums_b), sils, ada_weight,
        as_lines(fc1h), as_lines(fc2h),
    )
    (out, xg, ada_wgrad, qkvg, projg, fc1g, fc2g, cond_grad, ada_bgrad, dw1k, dw1b, projb, fc2bg, dw2k,
     dw2b, fc1bg) = finish(
        order, rows, grads, ada_wgrad, qkvg, projg, (fc1o, fc1p), (fc2o, fc2p), small, condition, pieces
    )
    return (
        out[None], xg[None], cond_grad, ada_wgrad, ada_bgrad[0], dw1k, dw1b[0], qkvg, projg, projb[0],
        fc1g, fc1bg[0], dw2k, dw2b[0], fc2g, fc2bg[0],
    )


def solution(mesh):
    wide, narrow = mesh.shape["wide"], mesh.shape["narrow"]
    rows = lambda rank: P(AXES, *(None,) * (rank - 1))
    lanes = P(None, AXES)
    in_specs = (
        rows(3), rows(2), rows(2), rows(2), rows(1), lanes, rows(1), rows(2), rows(2), rows(1),
        rows(2), rows(1), lanes, rows(1), rows(2), rows(1), rows(3),
    )
    out_specs = (
        rows(3), rows(3), rows(2), rows(2), rows(1), lanes, rows(1), rows(2), rows(2), rows(1),
        rows(2), rows(1), lanes, rows(1), rows(2), rows(1),
    )
    return jax.shard_map(
        functools.partial(on_device, wide, narrow), mesh=mesh, in_specs=in_specs,
        out_specs=out_specs, check_vma=False,
    )
```

```python
import functools

import jax
import jax.numpy as jnp
from jax import lax
from jax.experimental import pallas as pl
from jax.experimental.pallas import tpu as pltpu
from jax.sharding import PartitionSpec as P

HEAD = 64
GRID = 32
HALF = 16
GROUP = 256
TOKENS = 1024
C0 = 0.7978845608028654
C1 = 0.044715
EPS = 1e-06
MIB = 1 << 20
AXES = ("wide", "narrow")
F32, BF16 = jnp.float32, jnp.bfloat16


def dot_nn(a, b):
    return lax.dot_general(a, b, (((1,), (0,)), ((), ())), preferred_element_type=F32)


def dot_nt(a, b):
    return lax.dot_general(a, b, (((1,), (1,)), ((), ())), preferred_element_type=F32)


def dot_tn(a, b):
    return lax.dot_general(a, b, (((0,), (0,)), ((), ())), preferred_element_type=F32)


def whole(shape):
    return pl.BlockSpec(shape, lambda *_: (0,) * len(shape))


def once(shape):
    return pl.BlockSpec(shape, lambda *_: (0,) * len(shape), pipeline_mode=pl.Buffered(1))


def like(shape, dtype):
    return jax.ShapeDtypeStruct(shape, dtype)


def shift_pair(pair, parity, first, last):
    low, high = pair
    zero = jnp.zeros_like(low)
    if parity == 0:
        low, high = pltpu.roll(low, 1, 0), pltpu.roll(high, 1, 0)
        return jnp.where(first, zero, low), jnp.where(first, low, high)
    low, high = pltpu.roll(low, 7, 0), pltpu.roll(high, 7, 0)
    return jnp.where(last, high, low), jnp.where(last, zero, high)


def row_sources(gi, r):
    if gi == 0:
        return ((1, r - 1), (0, r), (1, r))
    return ((0, r), (1, r), (0, r + 1))


def load_pair(ref, slab, gi, gj, r):
    tile = 2 + 2 * r
    group = 2 * gi + gj
    return ref[slab, group, tile], ref[slab, group, tile + 1]


def store_pair(ref, slab, gi, gj, r, pair):
    tile = 2 + 2 * r
    group = 2 * gi + gj
    ref[slab, group, tile] = pair[0]
    ref[slab, group, tile + 1] = pair[1]


def edge_masks():
    sub = lax.broadcasted_iota(jnp.int32, (8, 128), 0)
    return sub == 0, sub == 7


def clear_edges(ref):
    slabs = ref.shape[0]
    ref[:, :, 0:2] = jnp.zeros((slabs, 4, 2, 8, 128), F32)
    ref[:, :, 34:36] = jnp.zeros((slabs, 4, 2, 8, 128), F32)


def conv_cell(src, slab, gi, gj, r, k, bias, masks):
    sources = row_sources(gi, r)
    other = 1 - gj
    near = 2 if gj == 0 else 0
    far = 2 - near
    same = [load_pair(src, slab, p, gj, rr) for p, rr in sources]
    cross = [load_pair(src, slab, p, other, rr) for p, rr in sources]
    straight, moved = [], []
    for h in (0, 1):
        acc, off = bias, None
        for a in range(3):
            acc = acc + k[3 * a + 1] * same[a][h] + k[3 * a + near] * cross[a][h]
            term = k[3 * a + far] * cross[a][h]
            off = term if off is None else off + term
        straight.append(acc)
        moved.append(off)
    moved = shift_pair(moved, gj, *masks)
    return straight[0] + moved[0], straight[1] + moved[1]


def conv_back_row(slab, k, src, grad, grad_moved, put, r, carry):
    kg, total = list(carry[:9]), carry[9]
    for gi in (0, 1):
        sources = row_sources(gi, r)
        for gj in (0, 1):
            other = 1 - gj
            near = 2 if gj == 0 else 0
            here = load_pair(src, slab, gi, gj, r)
            out = [None, None]
            for a in range(3):
                p, rr = sources[2 - a]
                trio = {
                    1: load_pair(grad, slab, p, gj, rr),
                    2 - near: load_pair(grad, slab, p, other, rr),
                    near: load_pair(grad_moved, slab, p, other, rr),
                }
                for b in range(3):
                    n = 3 * a + b
                    for h in (0, 1):
                        term = k[n] * trio[b][h]
                        out[h] = term if out[h] is None else out[h] + term
                        kg[n] = kg[n] + here[h] * trio[b][h]
            total = total + out[0] + out[1]
            put(gi, gj, r, out)
    return tuple(kg) + (total,)


def conv_back(slab, k, src, grad, grad_moved, put):
    body = lambda r, carry: conv_back_row(slab, k, src, grad, grad_moved, put, r, carry)
    return lax.fori_loop(0, HALF, body, (jnp.zeros((8, 128), F32),) * 10)


def group_rows(gi, gj, r):
    return pl.ds(pl.multiple_of((2 * gi + gj) * GROUP + r * HALF, HALF), HALF)


def row_sum(values):
    rows, columns = values.shape
    return jnp.sum(values.reshape(rows // 8, 8, columns), axis=0)


def unit_rows(values):
    model = values.shape[-1]
    centered = values - jnp.sum(values, axis=-1, keepdims=True) * (1.0 / model)
    spread = jnp.sum(centered * centered, axis=-1, keepdims=True) * (1.0 / model)
    scale = lax.rsqrt(spread + EPS)
    return centered * scale, scale


def unit_back(grad, unit, scale):
    model = grad.shape[-1]
    mean = jnp.sum(grad, axis=-1, keepdims=True) * (1.0 / model)
    tilt = jnp.sum(grad * unit, axis=-1, keepdims=True) * (1.0 / model)
    return scale * (grad - mean - unit * tilt)


def order_matrix():
    d = jnp.arange(GROUP)
    group, position, column = d // 64, (d % 64) // HALF, d % HALF
    source = (2 * position + group // 2) * GRID + 2 * column + group % 2
    return (source[:, None] == jnp.arange(GROUP)[None, :]).astype(BF16)


def ff_kernel(wide, narrow, chunks, count, steps, sums_over, *refs):
    n2_ref, n2t_ref, g2_ref, fc1_ref, small_ref, fc2_ref = refs[:6]
    so_far, refs = refs[6 : 6 + 2 * sums_over], refs[6 + 2 * sums_over :]
    srcs = refs[:count]
    branch_out, gn2_out, w1g_ref, w2g_ref, sums_ref = refs[count : 5 + count]
    dsts, refs = refs[5 + count : 5 + 2 * count], refs[5 + 2 * count :]
    hid, ga, gc, gcs, act, ghl, branch_ref, gn2_ref, held = refs[:9]
    totals = (branch_ref, gn2_ref)
    step = pl.program_id(0)
    slabs = hid.shape[0]
    p = Place(wide, narrow)
    if sums_over:
        buffers, (sends, recvs) = refs[9:-2], refs[-2:]
        waves = scatter_jobs(p, srcs, dsts, buffers, sends, recvs, chunks)
        own_copies = []
    else:
        sends, recvs, local = refs[9:]
        waves = gather_jobs(p, srcs, dsts, sends, recvs, chunks)
        own_copies = [
            pltpu.make_async_copy(
                srcs[i], dsts[i].at[(*digits_of(p.w, wide), p.n)], local.at[i]
            )
            for i in range(count)
        ]

    def hook(position):
        for when in range(steps):
            pl.when(step == when)(lambda: waves.at_hook(3 * when + position, 3 * steps))

    @pl.when(step == 0)
    def _():
        greet(p.partners())
        for copy in own_copies:
            copy.start()
        for i, ref in enumerate(totals):
            if sums_over:
                pltpu.make_async_copy(so_far[i], ref, held.at[i]).start()
            else:
                ref[...] = jnp.zeros_like(ref)
        for ref in (hid, gc, gcs):
            clear_edges(ref)

    for g in range(4):
        rows = pl.ds(g * GROUP, GROUP)
        full = dot_nn(n2_ref[rows, :], fc1_ref[...]) + small_ref[10:11, :]
        back = dot_nt(g2_ref[rows, :], fc2_ref[...])
        for slab in range(slabs):
            lanes = slice(slab * 128, slab * 128 + 128)
            hid[slab, g, 2:34] = full[:, lanes].reshape(32, 8, 128)
            ga[slab, g] = back[:, lanes].reshape(32, 8, 128)

    @pl.when(step == 0)
    def _():
        met(len(p.partners()))
        waves.run(0)
        waves.run(1)
        for copy in own_copies:
            copy.wait()

    hook(0)
    masks = edge_masks()
    for slab in range(slabs):
        lanes = pl.ds(slab * 128, 128)
        k = [jnp.broadcast_to(small_ref[n : n + 1, lanes], (8, 128)) for n in range(9)]
        bias = jnp.broadcast_to(small_ref[9:10, lanes], (8, 128))

        def forward(r, total):
            for gi in (0, 1):
                for gj in (0, 1):
                    pair = conv_cell(hid, slab, gi, gj, r, k, bias, masks)
                    acts, grads = [], []
                    for h in (0, 1):
                        x = pair[h]
                        x2 = x * x
                        half = 0.5 * jnp.tanh(x * (C0 + (C0 * C1) * x2)) + 0.5
                        value = x * half
                        slope = half + (value - value * half) * (2.0 * C0 + (6.0 * C0 * C1) * x2)
                        acts.append(value)
                        grads.append(ga[slab, 2 * gi + gj, 2 * r + h] * slope)
                        total = total + grads[-1]
                    act[group_rows(gi, gj, r), lanes] = jnp.concatenate(acts, 0).astype(BF16)
                    store_pair(gc, slab, gi, gj, r, grads)
                    store_pair(gcs, slab, gi, gj, r, shift_pair(grads, 1 - gj, *masks))
            return total

        total = lax.fori_loop(0, HALF, forward, jnp.zeros((8, 128), F32))

        def put(gi, gj, r, pair):
            ghl[group_rows(gi, gj, r), lanes] = jnp.concatenate(pair, 0).astype(BF16)

        sums = conv_back(slab, k, hid, gc, gcs, put)
        for n, value in enumerate([*sums[:9], total, sums[9]]):
            sums_ref[n : n + 1, lanes] = jnp.sum(value, axis=0, keepdims=True)
        sums_ref[11:16, lanes] = jnp.zeros((5, 128), F32)
        if slab == 0:
            hook(1)

    if sums_over:
        @pl.when(step == 0)
        def _():
            for i, ref in enumerate(totals):
                pltpu.make_async_copy(so_far[i], ref, held.at[i]).wait()

    branch_ref[...] += dot_nn(act[...], fc2_ref[...])
    gn2_ref[...] += dot_nt(ghl[...], fc1_ref[...])

    @pl.when(step == steps - 1)
    def _():
        for i, out in enumerate((branch_out, gn2_out)):
            pltpu.make_async_copy(totals[i], out, held.at[i]).start()

    w2g_ref[...] = dot_tn(act[...], g2_ref[...]).astype(w2g_ref.dtype)
    w1g_ref[...] = dot_nn(n2t_ref[...], ghl[...]).astype(w1g_ref.dtype)
    hook(2)

    @pl.when(step == steps - 1)
    def _():
        waves.finish()
        for i, out in enumerate((branch_out, gn2_out)):
            pltpu.make_async_copy(totals[i], out, held.at[i]).wait()


def feed_forward(wide, narrow, n2, n2t, g2, fc1, small, part, fc2, arrays, chunks, so_far=(),
                 width=256):
    sums_over = bool(so_far)
    tokens, model = n2.shape
    hidden = fc1.shape[1]
    slabs, steps, count = width // 128, hidden // width, len(arrays)
    padded = pltpu.VMEM((slabs, 4, 36, 8, 128), F32)
    columns = lambda rows: pl.BlockSpec((rows, width), lambda s: (0, s))
    lines = pl.BlockSpec((width, model), lambda s: (s, 0))
    anywhere = pl.BlockSpec(memory_space=pl.ANY)
    if sums_over:
        shapes = [a.shape for a in arrays]
        moved = [owned_shape(s, narrow) for s in shapes]
        extra = scatter_scratch(wide, narrow, shapes) + job_sems(wide, narrow, chunks)
        in_moved, out_moved = [once(s) for s in shapes], [once(m.shape) for m in moved]
    else:
        moved = [gathered_shape(wide, narrow, a.shape) for a in arrays]
        extra = job_sems(wide, narrow, chunks) + [pltpu.SemaphoreType.DMA((count,))]
        in_moved = out_moved = [anywhere] * count
    return pl.pallas_call(
        functools.partial(ff_kernel, wide, narrow, chunks, count, steps, sums_over),
        grid=(steps,),
        in_specs=[
            once((tokens, model)), once((model, tokens)), once((tokens, model)),
            columns(model), pl.BlockSpec((16, width), lambda s: (0, part * steps + s)), lines,
        ] + [anywhere] * len(so_far) + in_moved,
        out_specs=[
            anywhere, anywhere, columns(model), lines, columns(16)
        ] + out_moved,
        out_shape=[
            like((tokens, model), F32), like((tokens, model), F32),
            like((model, hidden), BF16), like((hidden, model), BF16), like((16, hidden), F32),
        ] + moved,
        scratch_shapes=[
            padded, pltpu.VMEM((slabs, 4, 32, 8, 128), F32), padded, padded,
            pltpu.VMEM((tokens, width), BF16), pltpu.VMEM((tokens, width), BF16),
            pltpu.VMEM((tokens, model), F32), pltpu.VMEM((tokens, model), F32),
            pltpu.SemaphoreType.DMA((2,)),
        ] + extra,
        compiler_params=pltpu.CompilerParams(
            vmem_limit_bytes=56 * MIB, collective_id=4 if sums_over else 3, has_side_effects=True
        ),
        name="feed_forward",
    )(n2, n2t, g2, fc1, small, fc2, *so_far, *arrays)


def flip(index, bit):
    return index + bit - 2 * bit * lax.rem(index // bit, 2)


def bits_of(count):
    return [1 << b for b in range(count.bit_length() - 1)]


def digits_of(index, wide):
    levels = wide.bit_length() - 1
    return [lax.rem(index // (1 << (levels - 1 - i)), 2) for i in range(levels)]


def static_digits(index, wide):
    levels = wide.bit_length() - 1
    return [(index >> (levels - 1 - i)) & 1 for i in range(levels)]


def at(w, n):
    return {"wide": w, "narrow": n}


def greet(places):
    barrier = pltpu.get_barrier_semaphore()
    for place in places:
        pl.semaphore_signal(barrier, inc=1, device_id=place, device_id_type=pl.DeviceIdType.MESH)


def met(count):
    pl.semaphore_wait(pltpu.get_barrier_semaphore(), count)


def greet_all(place):
    barrier = pltpu.get_barrier_semaphore()
    total = place.total

    def body(k, carry):
        pl.semaphore_signal(
            barrier, inc=1, device_id=place.device(lax.rem(place.sid + k, total)),
            device_id_type=pl.DeviceIdType.MESH,
        )
        return carry

    lax.fori_loop(1, total, body, 0)


def remote(src, dst, send_sem, recv_sem, place):
    return pltpu.make_async_remote_copy(
        src_ref=src, dst_ref=dst, send_sem=send_sem, recv_sem=recv_sem, device_id=place,
        device_id_type=pl.DeviceIdType.MESH,
    )


class Place:
    def __init__(self, wide, narrow):
        self.wide, self.narrow = wide, narrow
        self.w, self.n = lax.axis_index("wide"), lax.axis_index("narrow")
        self.total, self.half = wide * narrow, wide * narrow // 2
        self.me = self.w * narrow + self.n
        self.core = lax.rem(self.w, 2)
        self.slot = (self.w // 2) * narrow + self.n
        self.sid = self.core * self.half + self.slot
        self.sibling = at(flip(self.w, 1), self.n)

    def device(self, sid):
        core, slot = sid // self.half, lax.rem(sid, self.half)
        return at(2 * (slot // self.narrow) + core, lax.rem(slot, self.narrow))

    def order_of(self, sid):
        core, slot = divmod(sid, self.half)
        return (2 * (slot // self.narrow) + core) * self.narrow + slot % self.narrow

    def partners(self):
        places = [at(self.w, lax.rem(self.n + k, self.narrow)) for k in range(1, self.narrow)]
        return places + [at(flip(self.w, bit), self.n) for bit in bits_of(self.wide)]

    def all_copies(self, src_of, dst, sends, recvs):
        def copy(k):
            sid = lax.rem(self.sid + k, self.total)
            return remote(src_of(sid), dst, sends.at[k], recvs.at[k], self.device(sid))

        return Exchange(copy, self.total)

    def kin_copies(self, src_of, dst, sends, recvs):
        def copy(k):
            slot = lax.rem(self.slot + k, self.half)
            return remote(src_of(slot), dst, sends.at[k], recvs.at[k],
                          self.device(self.core * self.half + slot))

        return Exchange(copy, self.half)

    def to_all(self, *refs):
        return self.all_copies(*refs).start()

    def to_kin(self, *refs):
        return self.kin_copies(*refs).start()

    def to_all_wait(self, *refs):
        self.all_copies(*refs).wait()

    def to_kin_wait(self, *refs):
        self.kin_copies(*refs).wait()


class Exchange:
    def __init__(self, copy, count):
        self.copy, self.count = copy, count

    def start(self):
        def body(k, carry):
            self.copy(k).start()
            return carry

        lax.fori_loop(1, self.count, body, 0)
        return self.wait

    def wait(self):
        def body(k, carry):
            self.copy(k).wait()
            return carry

        lax.fori_loop(1, self.count, body, 0)


def bit_sizes(wide):
    return (2,) * (wide.bit_length() - 1)


class Transfer:
    def __init__(self, place, sends, recvs, chunk, columns, turn):
        self.p, self.sends, self.recvs, self.chunk = place, sends, recvs, chunk
        start, size = columns
        self.all = pl.ds(start, size)
        levels = len(bit_sizes(place.wide))
        far = list(range(levels - 1))
        half = size // 256 * 128
        if turn % 2:
            far = far[::-1]
        self.parts = [(pl.ds(start, size - half), far)]
        if half:
            self.parts.append((pl.ds(start + size - half, half), far[::-1]))
        self.stages = levels + 1
        self.bits = digits_of(place.w, place.wide)
        self.count = 0

    def copy(self, src, dst, place):
        slot = self.count
        self.count += 1
        return remote(src, dst, self.sends.at[self.chunk, slot], self.recvs.at[self.chunk, slot], place)

    def along(self, level):
        return at(flip(self.p.w, 1 << (len(self.bits) - 1 - level)), self.p.n)

    def in_line(self, k):
        return at(self.p.w, lax.rem(self.p.n + k, self.p.narrow))

    def copies(self, stage):
        self.count = 0
        for before in range(stage):
            self.count += len(self.make(before, True))
        return self.make(stage, False)

    def start(self, stage):
        for copy in self.copies(stage):
            copy.start()

    def finish(self, stages):
        pass


class Gather(Transfer):
    def __init__(self, place, src, dst, sends, recvs, chunk, columns, turn):
        super().__init__(place, sends, recvs, chunk, columns, turn)
        self.src, self.dst = src, dst

    def make(self, stage, count_only):
        levels = len(self.bits)
        if stage == 0:
            ks = range(1, self.p.narrow)
            if count_only:
                return list(ks)
            return [
                self.copy(self.src.at[:, self.all],
                          self.dst.at[(*self.bits, self.p.n, slice(None), self.all)], self.in_line(k))
                for k in ks
            ]
        if stage == levels:
            parts = [(self.all, list(range(levels)))]
        else:
            parts = self.parts
        if count_only:
            return list(parts)
        found = []
        for columns, order in parts:
            index = list(self.bits)
            for level in order[: stage - 1]:
                index[level] = slice(None)
            part = self.dst.at[(*index, slice(None), slice(None), columns)]
            found.append(self.copy(part, part, self.along(order[stage - 1])))
        return found

    def wait(self, stage):
        for copy in self.copies(stage):
            copy.wait_recv()

    def finish(self, stages):
        for stage in stages:
            for copy in self.copies(stage):
                copy.wait_send()


def steady(first, stages, lag=2):
    return [first + lag * s for s in range(stages + 1)]


class Waves:
    def __init__(self, jobs, plan, resume=-1):
        self.jobs, self.resume = jobs, resume
        self.stages = jobs[0].stages
        self.plan = plan or [steady(c, self.stages) for c in range(len(jobs))]
        self.wave = resume + 1
        self.last = max(waves[-1] for waves in self.plan)

    def run(self, wave):
        for job, waves in zip(self.jobs, self.plan):
            for stage, when in enumerate(waves):
                if when != wave:
                    continue
                if stage and waves[stage - 1] > self.resume:
                    job.wait(stage - 1)
                if stage < self.stages:
                    job.start(stage)

    def tick(self, times=1):
        for _ in range(times):
            if self.wave <= self.last:
                self.run(self.wave)
                self.wave += 1

    def through(self, wave):
        while self.wave <= min(wave, self.last):
            self.tick()

    def at_hook(self, hook, hooks):
        first = self.resume + 3
        left = self.last + 1 - first
        for wave in range(first + hook * left // hooks, first + (hook + 1) * left // hooks):
            self.run(wave)

    def finish(self, last=None):
        last = self.last if last is None else last
        for job, waves in zip(self.jobs, self.plan):
            here = [s for s in range(self.stages) if self.resume < waves[s] <= last]
            for stage in here:
                if waves[stage + 1] > last:
                    job.wait(stage)
            job.finish(here)

    def end(self, last=None):
        last = self.last if last is None else last
        self.through(last)
        self.finish(last)


def job_sems(wide, narrow, chunks):
    per = narrow - 1 + 2 * (wide.bit_length() - 1)
    return [pltpu.SemaphoreType.DMA((len(chunks), per))] * 2


def gather_jobs(place, srcs, dsts, sends, recvs, chunks, plan=None, resume=-1, shift=0):
    jobs = [
        Gather(place, srcs[i], dsts[i], sends, recvs, c, columns, c + shift)
        for c, (i, *columns) in enumerate(chunks)
    ]
    return Waves(jobs, plan, resume)


def gathered_shape(wide, narrow, shape):
    return like((*bit_sizes(wide), narrow, *shape), BF16)


def thirds(i, size):
    return [(i, t * (size // 3), size // 3) for t in range(3)]


class Scatter(Transfer):
    def __init__(self, place, src, buffers, out, sends, recvs, chunk, columns):
        super().__init__(place, sends, recvs, chunk, columns, chunk)
        self.src, self.out = src, out
        self.halves, self.line, self.got = buffers[:-2], buffers[-2], buffers[-1]
        self.rows = self.line.shape[1]
        core = len(self.bits) - 1
        self.parts = [(columns, [core] + order) for columns, order in self.parts]

    def make(self, stage, count_only):
        levels = len(self.bits)
        if stage == levels:
            ks = range(1, self.p.narrow)
            if count_only:
                return list(ks)
            return [
                self.copy(self.line.at[lax.rem(self.p.n + k, self.p.narrow), :, self.all],
                          self.got.at[k - 1, :, self.all], self.in_line(k))
                for k in ks
            ]
        parts = self.parts if stage else [(self.all, self.parts[0][1])]
        if count_only:
            return list(parts)
        found = []
        for columns, order in parts:
            source, index, kept = self.level(order, stage, True)
            into = self.halves[stage].at[(*kept, slice(None), columns)]
            found.append(self.copy(source.at[(*index, slice(None), columns)], into, self.along(order[stage])))
        return found

    def level(self, order, stage, theirs):
        source = self.src if stage == 0 else self.halves[stage - 1]
        left = [level for level in range(len(self.bits)) if level not in order[:stage]]
        bit = self.bits[order[stage]]
        bit = 1 - bit if theirs else bit
        index = [bit if level == order[stage] else slice(None) for level in left]
        return source, index, [slice(None)] * (len(left) - 1)

    def wait(self, stage):
        for copy in self.copies(stage):
            copy.wait()
        levels = len(self.bits)
        if stage == levels:
            value = self.line[self.p.n, :, self.all].astype(F32)
            for k in range(1, self.p.narrow):
                value = value + self.got[k - 1, :, self.all].astype(F32)
            self.out[:, self.all] = value
            return
        for columns, order in self.parts:
            source, index, kept = self.level(order, stage, False)
            into = self.halves[stage]
            for j in range(1 << len(kept)):
                digits = [(j >> i) & 1 for i in range(len(kept))]
                mine = [v if not isinstance(v, slice) else None for v in index]
                rest = iter(digits)
                mine = [next(rest) if v is None else v for v in mine]
                self.add(source, tuple(mine), into, tuple(digits), columns, stage == levels - 1)

    def add(self, source, mine, into, arrived, columns, last):
        if last:
            total = source[(*mine, slice(None), columns)].astype(F32) + into[
                (*arrived, slice(None), columns)
            ].astype(F32)
            for m in range(self.p.narrow):
                rows = slice(m * self.rows, (m + 1) * self.rows)
                self.line[m, :, columns] = total[rows].astype(BF16)
            return

        into[(*arrived, slice(None), columns)] = (
            source[(*mine, slice(None), columns)] + into[(*arrived, slice(None), columns)]
        )


def scatter_scratch(wide, narrow, shapes):
    scratch = []
    for *_, height, columns in shapes:
        for stage in range(wide.bit_length() - 1):
            scratch.append(pltpu.VMEM((*bit_sizes(wide)[stage + 1 :], height, columns), BF16))
        scratch.append(pltpu.VMEM((narrow, height // narrow, columns), BF16))
        scratch.append(pltpu.VMEM((narrow - 1, height // narrow, columns), BF16))
    return scratch


def scatter_jobs(place, srcs, outs, buffers, sends, recvs, chunks, plan=None):
    per = len(buffers) // len(srcs)
    jobs = [
        Scatter(place, srcs[i], buffers[i * per : (i + 1) * per], outs[i], sends, recvs, c, columns)
        for c, (i, *columns) in enumerate(chunks)
    ]
    return Waves(jobs, plan)


def owned_shape(shape, narrow):
    return like((shape[-2] // narrow, shape[-1]), F32)


def move_lanes(tiles, moves, count):
    rows = tiles[0].shape[0]
    lane = lax.broadcasted_iota(jnp.int32, (rows, 128), 1)
    out = [jnp.zeros((rows, 128), F32) for _ in range(count)]
    for start, to, length in moves:
        while length:
            size = min(length, 128 - start % 128, 128 - to % 128)
            tile = tiles[start // 128]
            turn = (to - start) % 128
            if turn:
                tile = pltpu.roll(tile, turn, 1)
            inside = (lane >= to % 128) & (lane < to % 128 + size)
            out[to // 128] = jnp.where(inside, tile, out[to // 128])
            start, to, length = start + size, to + size, length - size
    return out


def tiles_of(values):
    return [values[:, i : i + 128] for i in range(0, values.shape[1], 128)]


def front_kernel(wide, narrow, chunks, plan, count, own, own_ff, *refs):
    (x_ref, cot_ref, mask_ref, order_ref, cond_ref, ada_ref, bias_ref, small_ref, fc1_ref) = refs[:9]
    srcs = refs[9 : 9 + count]
    (mod_ref, sils_ref, model_ref, hidden_ref, lat_ref, gout_ref, g2_ref, normed_ref, mixed_ref,
     keep_ref, fc2b_ref, fc1b_ref) = refs[9 + count : 21 + count]
    dsts = refs[21 + count : 22 + 2 * count]
    (fc1a_ref, sil_out, got, part, sib, rows_in, smalls, send_a, recv_a, send_b, recv_b, send_c, recv_c,
     sends, recvs, local) = refs[22 + 2 * count :]
    p = Place(wide, narrow)
    mine = digits_of(p.w, wide)
    model = x_ref.shape[1]
    slabs = model // 128
    own_copies = [
        pltpu.make_async_copy(srcs[i], dsts[1 + i].at[(*mine, p.n)], local.at[i]) for i in range(count)
    ]
    for copy in own_copies:
        copy.start()
    greet_all(p)
    waves = gather_jobs(p, [small_ref, fc1a_ref, *srcs], [smalls, *dsts], sends, recvs, chunks, plan)
    last = waves.plan[chunks.index((3, 0, model))][-1]
    cond = cond_ref[...].astype(F32)
    sil = (cond * jax.nn.sigmoid(cond)).astype(BF16).astype(F32)
    tiles = tiles_of(sil)
    for sid in range(p.total):
        d = p.order_of(sid)
        sil_out[sid] = move_lanes(tiles, [(own * d, 0, own)], 1)[0]
    got[p.sid] = sil_out[p.sid]
    smalls[(*mine, p.n)] = small_ref[...]

    def arrange(t):
        rows = pl.ds(t * GROUP, GROUP)
        tokens = dot_nn(order_ref[...], x_ref[rows, :])
        unit, _ = unit_rows(tokens)
        kept = dot_nn(order_ref[...], mask_ref[rows, :])
        gout = dot_nn(order_ref[...], cot_ref[rows, :]) * jnp.concatenate([kept] * slabs, axis=1)
        for g in range(4):
            src = slice(64 * g, 64 * g + 64)
            dst = pl.ds(g * GROUP + 64 * t, 64)
            lat_ref[dst, :] = tokens[src].astype(BF16)
            gout_ref[dst, :] = gout[src].astype(BF16)
            keep_ref[dst, :] = (kept[src] - 1.0) * 1e30
            for s in range(slabs):
                tile = unit[src, s * 128 : s * 128 + 128].reshape(8, 8, 128)
                normed_ref[s, g, 2 + 8 * t : 10 + 8 * t] = tile

    met(p.total - 1)
    wait_sil = p.to_all(lambda sid: sil_out.at[sid], got.at[p.sid], send_a, recv_a)
    waves.tick(2)
    arrange(0)
    for copy in own_copies:
        copy.wait()
    waves.tick()
    arrange(1)
    wait_sil()
    sil = got[...].reshape(p.total, 128)
    sils_ref[...] = sil
    product = dot_nn(sil[:, :own].astype(BF16), ada_ref[...]) + bias_ref[...]
    for d in range(p.total):
        part[d // p.half, d % p.half] = product[d : d + 1, :]
    to_sibling = remote(part.at[1 - p.core], sib, send_b, recv_b, p.sibling)
    to_sibling.start()
    waves.tick()
    arrange(2)
    to_sibling.wait()
    part[p.core] = part[p.core] + sib[...]
    rows_in[p.slot] = part[p.core, p.slot]
    wait_rows = p.to_kin(lambda slot: part.at[p.core, slot], rows_in.at[p.slot], send_c, recv_c)
    waves.tick()
    arrange(3)
    clear_edges(normed_ref)
    waves.tick()
    columns = tiles_of(fc1_ref[...].astype(F32))
    for h, ref in enumerate((fc1a_ref, fc1b_ref)):
        moves = [
            (own_ff * d + own_ff // 2 * h, own_ff // 2 * d, own_ff // 2) for d in range(p.total)
        ]
        ref[...] = jnp.concatenate(move_lanes(columns, moves, len(columns) // 2), axis=1).astype(BF16)
    own_fc1 = pltpu.make_async_copy(fc1a_ref, dsts[0].at[(*mine, p.n)], local.at[count])
    own_fc1.start()
    waves.through(waves.plan[0][-1])
    pieces = [smalls[(*static_digits(d // narrow, wide), d % narrow)].astype(F32) for d in range(p.total)]
    moves = [(128 * d, own * d, own) for d in range(p.total)]
    model_ref[...] = jnp.concatenate(move_lanes([q[:16] for q in pieces], moves, slabs), axis=1)
    half, hidden = own_ff // 2, fc1_ref.shape[1]
    moves = [
        (128 * d + half * h, hidden // 2 * h + half * d, half) for d in range(p.total) for h in (0, 1)
    ]
    hidden_ref[...] = jnp.concatenate(
        move_lanes([q[16:] for q in pieces], moves, hidden // 128), axis=1
    )
    own_fc1.wait()
    wait_rows()
    mod = jnp.sum(rows_in[...], axis=0)
    for i in range(6):
        mod_ref[i : i + 1, :] = mod[:, i * model : (i + 1) * model]

    shift, scale, gate = mod_ref[0:1, :], mod_ref[1:2, :], mod_ref[5:6, :]
    total = jnp.zeros((8, model), F32)
    for g in range(4):
        rows = pl.ds(g * GROUP, GROUP)
        two = gout_ref[rows, :].astype(F32) * gate
        total = total + row_sum(two)
        g2_ref[rows, :] = two.astype(BF16)
    fc2b_ref[...] = total
    masks = edge_masks()
    for s in range(slabs):
        lanes = pl.ds(s * 128, 128)
        at_s = slice(s * 128, s * 128 + 128)
        shift8 = jnp.broadcast_to(shift[:, at_s], (8, 128))
        scale8 = jnp.broadcast_to(1.0 + scale[:, at_s], (8, 128))
        normed_ref[s, :, 2:34] = normed_ref[s, :, 2:34] * scale8 + shift8
        k = [jnp.broadcast_to(model_ref[n : n + 1, at_s], (8, 128)) for n in range(9)]
        bias = jnp.broadcast_to(model_ref[9:10, at_s], (8, 128))

        def body(r, carry):
            for gi in (0, 1):
                for gj in (0, 1):
                    pair = conv_cell(normed_ref, s, gi, gj, r, k, bias, masks)
                    mixed_ref[group_rows(gi, gj, r), lanes] = jnp.concatenate(pair, 0).astype(BF16)
            return carry

        lax.fori_loop(0, HALF, body, 0)
        waves.through(min(waves.wave, last))
    waves.end(last)


def front(wide, narrow, x, cot, mask, order, cond, ada, bias, small, fc1, blocks, chunks, plan):
    total = wide * narrow
    tokens, model = x.shape
    slabs, count, columns = model // 128, len(blocks), ada.shape[1]
    hidden = fc1.shape[1]
    own, own_ff = model // total, hidden // total
    inside = pl.BlockSpec(memory_space=pltpu.VMEM)
    anywhere = pl.BlockSpec(memory_space=pl.ANY)
    all_sems = pltpu.SemaphoreType.DMA((total,))
    one_sem = pltpu.SemaphoreType.DMA
    kin_sems = pltpu.SemaphoreType.DMA((total // 2,))
    return pl.pallas_call(
        functools.partial(front_kernel, wide, narrow, chunks, plan, count, own, own_ff),
        in_specs=[inside] * 9 + [anywhere] * count,
        out_specs=[inside] * 12 + [anywhere] * (count + 1),
        out_shape=[
            like((8, model), F32), like((total, 128), F32), like((16, model), F32),
            like((16, hidden), F32), like((tokens, model), BF16), like((tokens, model), BF16),
            like((tokens, model), BF16), like((slabs, 4, 36, 8, 128), F32),
            like((tokens, model), BF16), like((tokens, 128), F32), like((8, model), F32),
            like((own, hidden // 2), BF16),
            gathered_shape(wide, narrow, (own, hidden // 2)),
        ] + [gathered_shape(wide, narrow, b.shape) for b in blocks],
        scratch_shapes=[
            pltpu.VMEM((own, hidden // 2), BF16), pltpu.VMEM((total, 1, 128), F32),
            pltpu.VMEM((total, 1, 128), F32), pltpu.VMEM((2, total // 2, 1, columns), F32),
            pltpu.VMEM((total // 2, 1, columns), F32), pltpu.VMEM((total // 2, 1, columns), F32),
            pltpu.VMEM((*bit_sizes(wide), narrow, 32, 128), BF16),
            all_sems, all_sems, one_sem, one_sem, kin_sems, kin_sems,
            *job_sems(wide, narrow, chunks), pltpu.SemaphoreType.DMA((count + 1,)),
        ],
        compiler_params=pltpu.CompilerParams(
            vmem_limit_bytes=56 * MIB, collective_id=0, has_side_effects=True
        ),
        name="front",
    )(x, cot, mask, order, cond, ada, bias, small, fc1, *blocks)


def attend_kernel(wide, narrow, chunks, plan, resume, shift, *refs):
    mixed_ref, lat_ref, keep_ref, mod_ref, small_ref, qkv_ref, proj_ref, fc1_in, fc2_in = refs[:9]
    triple_ref, probs_ref, att_ref, branch_ref, n2_ref, n2t_ref, fc1_ref, fc2_ref = refs[9:17]
    sends, recvs = refs[17:]
    step = pl.program_id(0)
    p = Place(wide, narrow)
    waves = gather_jobs(p, [fc1_in, fc2_in], [fc1_ref, fc2_ref], sends, recvs, chunks, plan, resume,
                        shift)

    def on(when, work):
        pl.when(step == when)(work)

    def hook(position):
        for when in range(4):
            on(when, lambda: waves.at_hook(2 * when + position, 8))

    def first():
        met(len(p.partners()))
        waves.run(resume + 1)
        waves.run(resume + 2)

    on(0, lambda: greet(p.partners()))
    model = lat_ref.shape[1]
    slabs = model // 128
    triple_ref[...] = dot_nn(mixed_ref[...], qkv_ref[...]).astype(BF16)
    on(0, first)
    lane = lax.broadcasted_iota(jnp.int32, (GROUP, 128), 1)
    left = lane < HEAD
    keep = jnp.concatenate([keep_ref[...]] * 2, axis=1)
    for s in range(slabs):
        q = triple_ref[:, s * 128 : s * 128 + 128]
        k = triple_ref[:, model + s * 128 : model + s * 128 + 128] * jnp.asarray(0.125, BF16)
        v = triple_ref[:, 2 * model + s * 128 : 2 * model + s * 128 + 128]
        outs = []
        for h in (0, 1):
            mine = left if h == 0 else jnp.logical_not(left)
            scores = dot_nt(jnp.where(mine, k, jnp.zeros_like(k)), q) + keep
            e = jnp.exp(scores - jnp.max(scores, axis=0, keepdims=True))
            prob = (e * (1.0 / jnp.sum(e, axis=0, keepdims=True))).astype(BF16)
            probs_ref[2 * s + h, 0] = prob
            outs.append(dot_tn(prob, v))
        att_ref[:, s * 128 : s * 128 + 128] = jnp.where(left, outs[0], outs[1]).astype(BF16)
        if s == slabs // 2 - 1:
            hook(0)
    branch = dot_nn(att_ref[...], proj_ref[...]) + small_ref[10:11, :]
    middle = lat_ref[...].astype(F32) + mod_ref[2:3, :] * branch
    unit, _ = unit_rows(middle)
    branch_ref[...] = branch
    n2 = unit * (1.0 + mod_ref[4:5, :]) + mod_ref[3:4, :]
    n2_ref[...] = n2.astype(BF16)
    n2t_ref[...] = n2.T.astype(BF16)
    hook(1)
    on(3, waves.finish)


def attend(wide, narrow, mixed, lat, keep, mod, small, qkv, proj, fc1, fc2, chunks, plan, resume, shift):
    tokens, model = lat.shape
    heads = model // HEAD
    by_group = lambda columns: pl.BlockSpec((GROUP, columns), lambda g: (g, 0))
    anywhere = pl.BlockSpec(memory_space=pl.ANY)
    return pl.pallas_call(
        functools.partial(attend_kernel, wide, narrow, chunks, plan, resume, shift),
        grid=(4,),
        in_specs=[
            by_group(model), by_group(model), by_group(128), whole(mod.shape),
            whole(small.shape), once(qkv.shape), once(proj.shape), anywhere, anywhere,
        ],
        out_specs=[
            by_group(3 * model), pl.BlockSpec((heads, 1, GROUP, GROUP), lambda g: (0, g, 0, 0)),
            by_group(model), by_group(model), by_group(model),
            pl.BlockSpec((model, GROUP), lambda g: (0, g)), anywhere, anywhere,
        ],
        out_shape=[
            like((tokens, 3 * model), BF16), like((heads, 4, GROUP, GROUP), BF16),
            like((tokens, model), BF16), like((tokens, model), F32),
            like((tokens, model), BF16), like((model, tokens), BF16),
            like(fc1.shape, BF16), like(fc2.shape, BF16),
        ],
        input_output_aliases={7: 6, 8: 7},
        scratch_shapes=job_sems(wide, narrow, chunks),
        compiler_params=pltpu.CompilerParams(
            vmem_limit_bytes=56 * MIB, collective_id=1, has_side_effects=True
        ),
        name="attend",
    )(mixed, lat, keep, mod, small, qkv, proj, fc1, fc2)


def back_kernel(wide, narrow, chunks, plan, own, own_ff, *refs):
    (gn2_ref, two_ref, branch_ref, gout_ref, att_ref, mixed_ref,
     q_ref, k_ref, v_ref, probs_ref, mod_ref, small_ref, proj_ref, wq_ref, wk_ref, wv_ref,
     lat_ref, normed_hbm, fc2b_ref, hida_ref, hidb_ref, sils_ref, ada_ref, fc1s_ref,
     fc2s_ref) = refs[:25]
    (rows_ref, xg_ref, wgrad_ref, cond_ref, small_out, qkvg_ref, projg_ref, fc1g_ref,
     fc2g_ref) = refs[25:34]
    (ga, gmid, gmix, gmoved, sums, proj_src, qkv_src, early, late, cuts_in, hcuts, hcuts_in, part, cond_in,
     gt, normed_ref, held,
     send_a, recv_a, send_b, recv_b, send_c, recv_c, send_d, recv_d, send_e, recv_e, send_f, recv_f,
     send_g, recv_g) = refs[34:65]
    buffers, (sends, recvs) = refs[65:-2], refs[-2:]
    step = pl.program_id(0)
    model = lat_ref.shape[1]
    slabs = model // 128
    last = 3 + slabs
    p = Place(wide, narrow)
    half, hidden = own_ff // 2, 2 * hida_ref.shape[1]
    waves = scatter_jobs(p, [fc1s_ref, fc2s_ref, proj_src, qkv_src],
                         [fc1g_ref, fc2g_ref, projg_ref, qkvg_ref], buffers, sends, recvs, chunks,
                         plan)
    gbl = xg_ref
    mine = lambda ref: ref.at[p.core, p.slot]

    @pl.when(step == 0)
    def _():
        greet_all(p)
        pltpu.make_async_copy(normed_hbm, normed_ref, held).start()
        sums[...] = jnp.zeros_like(sums)
        gmix[...] = jnp.zeros_like(gmix)
        clear_edges(gmoved)
        tiles = tiles_of(hida_ref[...]) + tiles_of(hidb_ref[...])
        for sid in range(p.total):
            d = p.order_of(sid)
            moves = [(half * d, 0, half), (hidden // 2 + half * d, half, half)]
            hcuts[sid] = move_lanes(tiles, moves, 1)[0]
        hcuts_in[p.sid] = hcuts[p.sid]

    @pl.when(step < 4)
    def _():
        rows = pl.ds(pl.multiple_of(step * GROUP, GROUP), GROUP)
        branch = branch_ref[...]
        middle = lat_ref[rows, :].astype(F32) + mod_ref[2:3, :] * branch
        two = two_ref[...] + small_ref[11:12, :]
        gout = gout_ref[...].astype(F32)
        rows_ref[...] = (middle + mod_ref[5:6, :] * two).astype(BF16)
        sums[3] += row_sum(gout * two)
        unit, scale = unit_rows(middle)
        gn2 = gn2_ref[...]
        sums[1] += row_sum(gn2)
        sums[2] += row_sum(gn2 * unit)
        gm = gout + unit_back(gn2 * (1.0 + mod_ref[4:5, :]), unit, scale)
        gmid[rows, :] = gm
        sums[0] += row_sum(gm * branch)
        gb = gm * mod_ref[2:3, :]
        sums[4] += row_sum(gb)
        low = gb.astype(BF16)
        gbl[rows, :] = low
        ga[rows, :] = dot_nt(low, proj_ref[...]).astype(BF16)

    @pl.when(step == 0)
    def _():
        met(p.total - 1)
        waves.run(0)
        waves.run(1)
        p.to_all(lambda sid: hcuts.at[sid], hcuts_in.at[p.sid], send_g, recv_g)

    for when in (1, 2):
        pl.when(step == when)(lambda: waves.run(when + 1))

    @pl.when(step == 3)
    def _():
        proj_src[...] = dot_tn(att_ref[...], gbl[...]).astype(BF16).reshape(proj_src.shape)
        waves.run(4)
        for i in range(4):
            early[p.core, p.slot, :, i * model : (i + 1) * model] = jnp.sum(
                sums[i], axis=0, keepdims=True
            )
        p.to_kin(lambda slot: mine(early), mine(early), send_a, recv_a)

    def attention(groups):
        s = step - 4
        lane = lax.broadcasted_iota(jnp.int32, (GROUP, 128), 1)
        left = lane < HEAD
        eighth = jnp.asarray(0.125, BF16)
        lanes = pl.ds(pl.multiple_of(s * 128, 128), 128)
        weight = jnp.concatenate([wq_ref[...], wk_ref[...], wv_ref[...]], axis=1)
        for g in groups:
            rows = slice(g * GROUP, (g + 1) * GROUP)
            q, k, v = q_ref[rows, :] * eighth, k_ref[rows, :] * eighth, v_ref[rows, :]
            grad = ga[rows, lanes]
            gq = gk = gv = None
            for h in (0, 1):
                keep = left if h == 0 else jnp.logical_not(left)
                only = lambda value: jnp.where(keep, value, jnp.zeros_like(value))
                p_low = probs_ref[h, g]
                prob = p_low.astype(F32)
                gh = only(grad)
                gp = dot_nt(v, gh)
                inner = jnp.sum(prob * gp, axis=0, keepdims=True)
                gs = (prob * (gp - inner)).astype(BF16)
                terms = (dot_tn(gs, only(k)), dot_nn(gs, only(q)), dot_nn(p_low, gh))
                if h == 0:
                    gq, gk, gv = terms
                else:
                    gq, gk, gv = gq + terms[0], gk + terms[1], gv + terms[2]
            found = jnp.concatenate([gq, gk, gv], axis=1).astype(BF16)
            gt[rows, :] = found
            gmixed = dot_nt(found, weight)
            for t in range(slabs):
                gmix[t + 1, g, 2:34] += gmixed[:, t * 128 : t * 128 + 128].reshape(32, 8, 128)

    pl.when(step >= 4)(lambda: attention((0, 1)))
    for s in range(slabs):
        pl.when(step == 4 + s)(lambda: waves.run(5 + 2 * s))

    @pl.when(step >= 4)
    def _():
        attention((2, 3))
        columns = pl.ds(pl.multiple_of((step - 4) * 384, 128), 384)
        found = dot_tn(mixed_ref[...], gt[...]).astype(BF16)
        qkv_src[..., columns] = found.reshape(*qkv_src.shape[:-1], 384)

    for s in range(slabs):
        pl.when(step == 4 + s)(lambda: waves.run(6 + 2 * s))

    @pl.when(step == 6)
    def _():
        p.to_kin_wait(lambda slot: mine(early), mine(early), send_a, recv_a)
        remote(early.at[p.core], early.at[p.core], send_d, recv_d, p.sibling).start()

    @pl.when(step == last)
    def _():
        waves.wave = 5 + 2 * slabs
        pltpu.make_async_copy(normed_hbm, normed_ref, held).wait()
        masks = edge_masks()
        rows_out = []
        for s in range(slabs):
            at_s = slice(s * 128, s * 128 + 128)
            k = [jnp.broadcast_to(small_ref[n : n + 1, at_s], (8, 128)) for n in range(9)]

            def move(r, total):
                for gi in (0, 1):
                    for gj in (0, 1):
                        pair = load_pair(gmix, s + 1, gi, gj, r)
                        total = total + pair[0] + pair[1]
                        store_pair(gmoved, 0, gi, gj, r, shift_pair(pair, 1 - gj, *masks))
                return total

            total = lax.fori_loop(0, HALF, move, jnp.zeros((8, 128), F32))

            def put(gi, gj, r, pair):
                store_pair(gmix, s, gi, gj, r, pair)

            found = conv_back(0, k, normed_ref.at[s : s + 1], gmix.at[s + 1 : s + 2], gmoved, put)
            late[p.core, p.slot, :, at_s] = jnp.sum(found[9], axis=0, keepdims=True)
            column = [jnp.sum(v, axis=0, keepdims=True) for v in (*found[:9], total)]
            column.append(jnp.sum(sums[4, :, at_s], axis=0, keepdims=True))
            column.append(jnp.sum(fc2b_ref[:, at_s], axis=0, keepdims=True))
            rows_out.append(jnp.concatenate(column + [jnp.zeros((4, 128), F32)], axis=0))
            if s % 2:
                waves.tick()
        scale_sum = jnp.zeros((8, model), F32)
        for g in range(4):
            rows = pl.ds(g * GROUP, GROUP)
            unit, scale = unit_rows(lat_ref[rows, :].astype(F32))
            gn = jnp.concatenate(
                [gmix[s, g, 2:34].reshape(GROUP, 128) for s in range(slabs)], axis=1
            )
            scale_sum = scale_sum + row_sum(gn * unit)
            gmid[rows, :] = gmid[rows, :] + unit_back(gn * (1.0 + mod_ref[1:2, :]), unit, scale)
        late[p.core, p.slot, :, model:] = jnp.sum(scale_sum, axis=0, keepdims=True)
        wait_late = p.to_kin(lambda slot: mine(late), mine(late), send_c, recv_c)
        waves.tick()
        p.to_all_wait(lambda sid: hcuts.at[sid], hcuts_in.at[p.sid], send_g, recv_g)
        small_out[16:, :] = jnp.sum(hcuts_in[...], axis=0)
        cuts = hcuts
        modulation = tiles_of(late[p.core, p.slot]) + tiles_of(early[p.core, p.slot])
        share = 6 * own
        for sid in range(p.total):
            d = p.order_of(sid)
            piece = move_lanes(rows_out, [(own * d, 0, own)], 1)[0][:12]
            bias = move_lanes(modulation, [(share * d, 0, share)], -(-share // 128))
            rest = [jnp.zeros((4 - len(bias), 128), F32)]
            cuts[sid] = jnp.concatenate([piece, *bias, *rest], axis=0)
        cuts_in[p.sid] = cuts[p.sid]
        wait_cuts = p.to_all(lambda sid: cuts.at[sid], cuts_in.at[p.sid], send_b, recv_b)
        xg_ref[...] = gmid[...].astype(BF16)
        wait_late()
        swap_late = remote(late.at[p.core], late.at[p.core], send_e, recv_e, p.sibling)
        swap_late.start()
        waves.tick()
        remote(early.at[p.core], early.at[p.core], send_d, recv_d, p.sibling).wait()
        swap_late.wait()
        sil = sils_ref[:, :own].astype(BF16)
        cond = None
        for ref, start in ((late, 0), (early, 2 * model)):
            size = ref.shape[-1]
            span = slice(start, start + size)
            found = ref[...].reshape(p.total, size)
            low = found.astype(BF16)
            wgrad_ref[:, span] = dot_tn(sil, low)
            term = dot_nt(low, ada_ref[:, span])
            cond = term if cond is None else cond + term
        cond = jnp.concatenate([cond, jnp.zeros((p.total, 128 - own), F32)], axis=1)
        for sid in range(p.total):
            part[sid] = cond[sid : sid + 1, :]
        cond_in[p.me] = part[p.sid]
        wait_cond = p.to_all(lambda sid: part.at[sid], cond_in.at[p.me], send_f, recv_f)
        waves.end()
        wait_cuts()
        small_out[:16, :] = jnp.sum(cuts_in[...], axis=0)
        wait_cond()
        cond_ref[...] = cond_in[...]


def back(wide, narrow, gn2, two, branch, gout, att, mixed, triple, probs, mod, small, proj, qkv,
         lat, normed, fc2b, hidden_sums, sils, ada, fc1s, fc2s):
    total = wide * narrow
    tokens, model = lat.shape
    slabs, columns = model // 128, ada.shape[1]
    hidden = 2 * hidden_sums[0].shape[1]
    own, own_ff = ada.shape[0], hidden // total
    by_group = pl.BlockSpec((GROUP, model), lambda t: (jnp.minimum(t, 3), 0))
    slab = lambda t: jnp.clip(t - 4, 0, slabs - 1)
    third = lambda rows, i: pl.BlockSpec((rows, 128), lambda t: (0, i * slabs + slab(t)))
    all_sems, kin_sems = (pltpu.SemaphoreType.DMA((n,)) for n in (total, total // 2))
    one_sem = pltpu.SemaphoreType.DMA
    padded = lambda count: pltpu.VMEM((count, 4, 36, 8, 128), F32)
    height = model // wide
    bits = bit_sizes(wide)
    shapes = [fc1s.shape, fc2s.shape, (*bits, height, model), (*bits, height, 3 * model)]
    chunks = thirds(0, hidden // 2) + thirds(1, model) + [(2, 0, model)]
    chunks += [(3, 384 * s, 384) for s in range(slabs)]
    starts = [0, 1, 2, 3, 5, 7, 4] + [6 + 2 * s for s in range(slabs)]
    plan = [steady(c, wide.bit_length()) for c in starts]
    full = lambda a: once(a.shape)
    outs = [
        like((tokens, model), BF16), like((tokens, model), BF16), like((own, columns), F32),
        like((total, 1, 128), F32), like((32, 128), F32), like((own, 3 * model), F32),
        like((own, model), F32), like((own, hidden // 2), F32), like((own_ff // 2, model), F32),
    ]
    return pl.pallas_call(
        functools.partial(back_kernel, wide, narrow, chunks, plan, own, own_ff),
        grid=(4 + slabs,),
        in_specs=[by_group] * 4 + [full(att), full(mixed)] + [third(tokens, i) for i in range(3)] + [
            pl.BlockSpec((2, 4, GROUP, GROUP), lambda t: (slab(t), 0, 0, 0)),
            full(mod), full(small), full(proj), third(model, 0), third(model, 1), third(model, 2),
            full(lat), pl.BlockSpec(memory_space=pl.ANY), full(fc2b), full(hidden_sums[0]), full(hidden_sums[1]),
            full(sils), full(ada), full(fc1s), full(fc2s),
        ],
        out_specs=[by_group] + [once(o.shape) for o in outs[1:]],
        out_shape=outs,
        scratch_shapes=[
            pltpu.VMEM((tokens, model), BF16), pltpu.VMEM((tokens, model), F32),
            padded(slabs + 1), padded(1), pltpu.VMEM((5, 8, model), F32),
            pltpu.VMEM(shapes[2], BF16), pltpu.VMEM(shapes[3], BF16),
            pltpu.VMEM((2, total // 2, 1, 4 * model), F32),
            pltpu.VMEM((2, total // 2, 1, 2 * model), F32),
            pltpu.VMEM((total, 16, 128), F32), pltpu.VMEM((total, 16, 128), F32),
            pltpu.VMEM((total, 16, 128), F32),
            pltpu.VMEM((total, 1, 128), F32), pltpu.VMEM((total, 1, 128), F32),
            pltpu.VMEM((tokens, 384), BF16), padded(slabs), one_sem,
            kin_sems, kin_sems, all_sems, all_sems, kin_sems, kin_sems, one_sem, one_sem,
            one_sem, one_sem, all_sems, all_sems, all_sems, all_sems,
            *scatter_scratch(wide, narrow, shapes), *job_sems(wide, narrow, chunks),
        ],
        compiler_params=pltpu.CompilerParams(
            vmem_limit_bytes=63 * MIB, collective_id=2, has_side_effects=True
        ),
        name="attend_back",
    )(gn2, two, branch, gout, att, mixed, triple, triple, triple, probs, mod,
      small, proj, qkv, qkv, qkv, lat, normed, fc2b, *hidden_sums, sils, ada, fc1s,
      fc2s)


def finish_kernel(own, own_ff, order_ref, rows_ref, grads_ref, wgrad_ref, qkvg_ref, projg_ref, fc1a_ref,
                  fc1b_ref, fc2a_ref, fc2b_ref, small_ref, cond_ref, pieces_ref,
                  out_ref, xg_ref, wgrad_out, qkv_out, proj_out, fc1_out, fc2_out, condg_out, adab_out,
                  dw1k_out, dw1b_out, projb_out, fc2b_out, dw2k_out, dw2b_out, fc1b_out):
    model = out_ref.shape[1]
    for src, dst in ((rows_ref, out_ref), (grads_ref, xg_ref)):
        block = src[...].reshape(GROUP, model)
        dst[...] = dot_tn(order_ref[...], block).astype(BF16)

    @pl.when(pl.program_id(0) == 0)
    def _():
        half, hidden, total = own_ff // 2, fc1_out.shape[1], pieces_ref.shape[0]
        wgrad_out[...] = wgrad_ref[...]
        proj_out[...] = projg_ref[...]
        for s in range(model // 128):
            for i in range(3):
                to = i * model + s * 128
                qkv_out[:, to : to + 128] = qkvg_ref[:, s * 384 + i * 128 : s * 384 + i * 128 + 128]
        moves = [
            (hidden // 2 * h + half * d, own_ff * d + half * h, half)
            for d in range(total) for h in (0, 1)
        ]
        tiles = tiles_of(fc1a_ref[...]) + tiles_of(fc1b_ref[...])
        for i, tile in enumerate(move_lanes(tiles, moves, hidden // 128)):
            fc1_out[:, i * 128 : i * 128 + 128] = tile
        fc2_out[:half, :] = fc2a_ref[...]
        fc2_out[half:, :] = fc2b_ref[...]
        tiles = [pieces_ref[d] for d in range(total)]
        moves = [(128 * d, own * d, own) for d in range(total)]
        grad = jnp.concatenate(move_lanes(tiles, moves, model // 128), axis=1)
        cond = cond_ref[...].astype(F32)
        gate = jax.nn.sigmoid(cond)
        condg_out[...] = grad * (gate + cond * gate * (1.0 - gate))
        dw1k_out[...] = small_ref[0:9, :own]
        dw2k_out[...] = small_ref[16:25, :own_ff]
        rows = ((dw1b_out, 9), (projb_out, 10), (fc2b_out, 11), (dw2b_out, 25), (fc1b_out, 26))
        for ref, row in rows:
            ref[...] = small_ref[row : row + 1, : ref.shape[1]]
        for start in range(0, 6 * own, 128):
            size = min(128, 6 * own - start)
            row = 12 + start // 128
            adab_out[:, start : start + size] = small_ref[row : row + 1, :size]


def finish(order, rows, grads, wgrad, qkvg, projg, fc1, fc2, small, cond, pieces):
    tokens, model = rows.shape
    own, hidden, own_ff = wgrad.shape[0], 2 * fc1[0].shape[1], 2 * fc2[0].shape[0]
    split = lambda value: value.reshape(4, 4, 64, model)
    block = pl.BlockSpec((4, 1, 64, model), lambda t: (0, t, 0, 0))
    lines = pl.BlockSpec((GROUP, model), lambda t: (t, 0))
    rest = [wgrad, qkvg, projg, *fc1, *fc2, small, cond, pieces]
    outs = [
        like((tokens, model), BF16), like((tokens, model), BF16), like(wgrad.shape, F32),
        like(qkvg.shape, F32), like(projg.shape, F32), like((own, hidden), F32),
        like((own_ff, model), F32), like((1, model), F32), like((1, 6 * own), F32),
        like((9, own), F32), like((1, own), F32), like((1, own), F32), like((1, own), F32),
        like((9, own_ff), F32), like((1, own_ff), F32), like((1, own_ff), F32),
    ]
    return pl.pallas_call(
        functools.partial(finish_kernel, own, own_ff),
        grid=(4,),
        in_specs=[once(order.shape), block, block] + [once(a.shape) for a in rest],
        out_specs=[lines, lines] + [once(o.shape) for o in outs[2:]],
        out_shape=outs,
        compiler_params=pltpu.CompilerParams(vmem_limit_bytes=60 * MIB),
        name="finish",
    )(order, split(rows), split(grads), *rest)


def on_device(wide, narrow, latents, condition, valid_mask, ada_weight, ada_bias, dw1_kernel, dw1_bias,
              qkv_weight, proj_weight, proj_bias, fc1_weight, fc1_bias, dw2_kernel, dw2_bias,
              fc2_weight, fc2_bias, out_cotangent):
    total = wide * narrow
    w, n = lax.axis_index("wide"), lax.axis_index("narrow")
    me = w * narrow + n
    model, hidden = latents.shape[2], fc1_weight.shape[1]
    own, own_ff = model // total, hidden // total

    bias_at = lax.dynamic_update_slice(
        jnp.zeros((1, 6 * model), F32), ada_bias.astype(F32)[None, :], (0, me * ada_bias.shape[0])
    )
    parts = [(0, dw1_kernel), (9, dw1_bias[None]), (10, proj_bias[None]), (11, fc2_bias[None]),
             (16, dw2_kernel), (25, dw2_bias[None]), (26, fc1_bias[None])]
    small = sum(
        jnp.pad(v, ((row, 32 - row - v.shape[0]), (0, 128 - v.shape[1]))) for row, v in parts
    )
    mask = jnp.broadcast_to(valid_mask[0].astype(BF16)[:, None], (latents.shape[1], 128))
    order = order_matrix()

    fc2a, fc2b_rows = fc2_weight[: own_ff // 2], fc2_weight[own_ff // 2 :]
    chunks = [(0, 0, 128)] + thirds(2, 3 * model) + [(3, 0, model)]
    stages = wide.bit_length()
    plan = [steady(c, stages) for c in range(5)]
    needed = plan[4][-1]
    chunks += thirds(1, hidden // 2) + thirds(4, model)
    plan += [[6 + c] + steady(needed + 1 + c, stages - 1) for c in range(6)]
    (mod, sils, model_small, hidden_small, lat, gout, g2, normed, mixed, keep, fc2b, fc1b, fc1_one, qkv,
     proj, fc2_one) = front(
        wide, narrow, latents[0], out_cotangent[0], mask, order, condition, ada_weight, bias_at, small,
        fc1_weight, [qkv_weight, proj_weight, fc2a], chunks, plan,
    )
    qkv, proj = qkv.reshape(model, 3 * model), proj.reshape(model, model)
    triple, probs, att, branch, n2, n2t, fc1_one, fc2_one = attend(
        wide, narrow, mixed, lat, keep, mod, model_small, qkv, proj, fc1_one, fc2_one,
        thirds(0, hidden // 2) + thirds(1, model), plan[5:], needed, 5,
    )
    chunks = thirds(0, hidden // 2) + thirds(1, model)
    as_fc1 = lambda rows: rows.reshape(model, hidden // 2)
    as_fc2 = lambda rows: rows.reshape(hidden // 2, model)
    as_lines = lambda grad: grad.reshape(*bit_sizes(wide), grad.shape[0] // wide, grad.shape[1])
    two, gn2, fc1g, fc2g, sums_a, fc1_two, fc2_two = feed_forward(
        wide, narrow, n2, n2t, g2, as_fc1(fc1_one), hidden_small, 0, as_fc2(fc2_one),
        [fc1b, fc2b_rows], chunks,
    )
    two, gn2, fc1h, fc2h, sums_b, fc1o, fc2o = feed_forward(
        wide, narrow, n2, n2t, g2, as_fc1(fc1_two), hidden_small, 1, as_fc2(fc2_two),
        [as_lines(fc1g), as_lines(fc2g)], chunks, (two, gn2),
    )
    rows, grads, ada_wgrad, pieces, small, qkvg, projg, fc1p, fc2p = back(
        wide, narrow, gn2, two, branch, gout, att, mixed, triple, probs,
        mod, model_small, proj, qkv, lat, normed, fc2b, (sums_a, sums_b), sils, ada_weight,
        as_lines(fc1h), as_lines(fc2h),
    )
    (out, xg, ada_wgrad, qkvg, projg, fc1g, fc2g, cond_grad, ada_bgrad, dw1k, dw1b, projb, fc2bg, dw2k,
     dw2b, fc1bg) = finish(
        order, rows, grads, ada_wgrad, qkvg, projg, (fc1o, fc1p), (fc2o, fc2p), small, condition, pieces
    )
    return (
        out[None], xg[None], cond_grad, ada_wgrad, ada_bgrad[0], dw1k, dw1b[0], qkvg, projg, projb[0],
        fc1g, fc1bg[0], dw2k, dw2b[0], fc2g, fc2bg[0],
    )


def solution(mesh):
    wide, narrow = mesh.shape["wide"], mesh.shape["narrow"]
    rows = lambda rank: P(AXES, *(None,) * (rank - 1))
    lanes = P(None, AXES)
    in_specs = (
        rows(3), rows(2), rows(2), rows(2), rows(1), lanes, rows(1), rows(2), rows(2), rows(1),
        rows(2), rows(1), lanes, rows(1), rows(2), rows(1), rows(3),
    )
    out_specs = (
        rows(3), rows(3), rows(2), rows(2), rows(1), lanes, rows(1), rows(2), rows(2), rows(1),
        rows(2), rows(1), lanes, rows(1), rows(2), rows(1),
    )
    return jax.shard_map(
        functools.partial(on_device, wide, narrow), mesh=mesh, in_specs=in_specs,
        out_specs=out_specs, check_vma=False,
    )
```

```python
import functools

import jax
import jax.numpy as jnp
from jax import lax
from jax.experimental import pallas as pl
from jax.experimental.pallas import tpu as pltpu
from jax.sharding import PartitionSpec as P

HEAD = 64
GRID = 32
HALF = 16
GROUP = 256
TOKENS = 1024
C0 = 0.7978845608028654
C1 = 0.044715
EPS = 1e-06
MIB = 1 << 20
AXES = ("wide", "narrow")
F32, BF16 = jnp.float32, jnp.bfloat16


def dot_nn(a, b):
    return lax.dot_general(a, b, (((1,), (0,)), ((), ())), preferred_element_type=F32)


def dot_nt(a, b):
    return lax.dot_general(a, b, (((1,), (1,)), ((), ())), preferred_element_type=F32)


def dot_tn(a, b):
    return lax.dot_general(a, b, (((0,), (0,)), ((), ())), preferred_element_type=F32)


def whole(shape):
    return pl.BlockSpec(shape, lambda *_: (0,) * len(shape))


def once(shape):
    return pl.BlockSpec(shape, lambda *_: (0,) * len(shape), pipeline_mode=pl.Buffered(1))


def like(shape, dtype):
    return jax.ShapeDtypeStruct(shape, dtype)


def shift_pair(pair, parity, first, last):
    low, high = pair
    zero = jnp.zeros_like(low)
    if parity == 0:
        low, high = pltpu.roll(low, 1, 0), pltpu.roll(high, 1, 0)
        return jnp.where(first, zero, low), jnp.where(first, low, high)
    low, high = pltpu.roll(low, 7, 0), pltpu.roll(high, 7, 0)
    return jnp.where(last, high, low), jnp.where(last, zero, high)


def row_sources(gi, r):
    if gi == 0:
        return ((1, r - 1), (0, r), (1, r))
    return ((0, r), (1, r), (0, r + 1))


def load_pair(ref, slab, gi, gj, r):
    tile = 2 + 2 * r
    group = 2 * gi + gj
    return ref[slab, group, tile], ref[slab, group, tile + 1]


def store_pair(ref, slab, gi, gj, r, pair):
    tile = 2 + 2 * r
    group = 2 * gi + gj
    ref[slab, group, tile] = pair[0]
    ref[slab, group, tile + 1] = pair[1]


def edge_masks():
    sub = lax.broadcasted_iota(jnp.int32, (8, 128), 0)
    return sub == 0, sub == 7


def clear_edges(ref):
    slabs = ref.shape[0]
    ref[:, :, 0:2] = jnp.zeros((slabs, 4, 2, 8, 128), F32)
    ref[:, :, 34:36] = jnp.zeros((slabs, 4, 2, 8, 128), F32)


def conv_cell(src, slab, gi, gj, r, k, bias, masks):
    sources = row_sources(gi, r)
    other = 1 - gj
    near = 2 if gj == 0 else 0
    far = 2 - near
    same = [load_pair(src, slab, p, gj, rr) for p, rr in sources]
    cross = [load_pair(src, slab, p, other, rr) for p, rr in sources]
    straight, moved = [], []
    for h in (0, 1):
        acc, off = bias, None
        for a in range(3):
            acc = acc + k[3 * a + 1] * same[a][h] + k[3 * a + near] * cross[a][h]
            term = k[3 * a + far] * cross[a][h]
            off = term if off is None else off + term
        straight.append(acc)
        moved.append(off)
    moved = shift_pair(moved, gj, *masks)
    return straight[0] + moved[0], straight[1] + moved[1]


def conv_back_row(slab, k, src, grad, grad_moved, put, r, carry):
    kg, total = list(carry[:9]), carry[9]
    for gi in (0, 1):
        sources = row_sources(gi, r)
        for gj in (0, 1):
            other = 1 - gj
            near = 2 if gj == 0 else 0
            here = load_pair(src, slab, gi, gj, r)
            out = [None, None]
            for a in range(3):
                p, rr = sources[2 - a]
                trio = {
                    1: load_pair(grad, slab, p, gj, rr),
                    2 - near: load_pair(grad, slab, p, other, rr),
                    near: load_pair(grad_moved, slab, p, other, rr),
                }
                for b in range(3):
                    n = 3 * a + b
                    for h in (0, 1):
                        term = k[n] * trio[b][h]
                        out[h] = term if out[h] is None else out[h] + term
                        kg[n] = kg[n] + here[h] * trio[b][h]
            total = total + out[0] + out[1]
            put(gi, gj, r, out)
    return tuple(kg) + (total,)


def conv_back(slab, k, src, grad, grad_moved, put):
    body = lambda r, carry: conv_back_row(slab, k, src, grad, grad_moved, put, r, carry)
    return lax.fori_loop(0, HALF, body, (jnp.zeros((8, 128), F32),) * 10)


def group_rows(gi, gj, r):
    return pl.ds(pl.multiple_of((2 * gi + gj) * GROUP + r * HALF, HALF), HALF)


def row_sum(values):
    rows, columns = values.shape
    return jnp.sum(values.reshape(rows // 8, 8, columns), axis=0)


def unit_rows(values):
    model = values.shape[-1]
    centered = values - jnp.sum(values, axis=-1, keepdims=True) * (1.0 / model)
    spread = jnp.sum(centered * centered, axis=-1, keepdims=True) * (1.0 / model)
    scale = lax.rsqrt(spread + EPS)
    return centered * scale, scale


def unit_back(grad, unit, scale):
    model = grad.shape[-1]
    mean = jnp.sum(grad, axis=-1, keepdims=True) * (1.0 / model)
    tilt = jnp.sum(grad * unit, axis=-1, keepdims=True) * (1.0 / model)
    return scale * (grad - mean - unit * tilt)


def order_matrix():
    d = lax.broadcasted_iota(jnp.int32, (GROUP, GROUP), 0)
    column = lax.broadcasted_iota(jnp.int32, (GROUP, GROUP), 1)
    group, position = d >> 6, (d >> 4) & 3
    source = (2 * position + (group >> 1)) * GRID + 2 * (d & 15) + (group & 1)
    return jnp.where(source == column, 1.0, 0.0).astype(BF16)


def part_of(ref, span):
    return ref if span is None else ref.at[pl.ds(*span)]


def span_shape(array, span):
    return array.shape if span is None else (span[1], *array.shape[1:])


def ff_kernel(wide, narrow, chunks, spans, steps, sums_over, *refs):
    count = len(spans)
    n2_ref, n2t_ref, g2_ref, fc1_ref, small_ref, fc2_ref = refs[:6]
    so_far, refs = refs[6 : 6 + 2 * sums_over], refs[6 + 2 * sums_over :]
    srcs = [part_of(ref, span) for ref, span in zip(refs, spans)]
    branch_out, gn2_out, w1g_ref, w2g_ref, sums_ref = refs[count : 5 + count]
    dsts, refs = refs[5 + count : 5 + 2 * count], refs[5 + 2 * count :]
    hid, ga, gc, gcs, act, ghl, branch_ref, gn2_ref, held = refs[:9]
    totals = (branch_ref, gn2_ref)
    step = pl.program_id(0)
    slabs = hid.shape[0]
    p = Place(wide, narrow)
    if sums_over:
        buffers, (sends, recvs) = refs[9:-2], refs[-2:]
        waves = scatter_jobs(p, srcs, dsts, buffers, sends, recvs, chunks)
        own_copies = []
    else:
        sends, recvs, local = refs[9:]
        waves = gather_jobs(p, srcs, dsts, sends, recvs, chunks)
        own_copies = [
            pltpu.make_async_copy(
                srcs[i], dsts[i].at[(*digits_of(p.w, wide), p.n)], local.at[i]
            )
            for i in range(count)
        ]

    def hook(position):
        for when in range(steps):
            pl.when(step == when)(lambda: waves.at_hook(3 * when + position, 3 * steps))

    @pl.when(step == 0)
    def _():
        greet(p.partners())
        for copy in own_copies:
            copy.start()
        for i, ref in enumerate(totals):
            if sums_over:
                pltpu.make_async_copy(so_far[i], ref, held.at[i]).start()
            else:
                ref[...] = jnp.zeros_like(ref)
        for ref in (hid, gc, gcs):
            clear_edges(ref)

    for g in range(4):
        rows = pl.ds(g * GROUP, GROUP)
        full = dot_nn(n2_ref[rows, :], fc1_ref[...]) + small_ref[10:11, :]
        back = dot_nt(g2_ref[rows, :], fc2_ref[...])
        for slab in range(slabs):
            lanes = slice(slab * 128, slab * 128 + 128)
            hid[slab, g, 2:34] = full[:, lanes].reshape(32, 8, 128)
            ga[slab, g] = back[:, lanes].reshape(32, 8, 128)

    @pl.when(step == 0)
    def _():
        met(len(p.partners()))
        waves.run(0)
        waves.run(1)
        for copy in own_copies:
            copy.wait()

    hook(0)
    masks = edge_masks()
    for slab in range(slabs):
        lanes = pl.ds(slab * 128, 128)
        k = [jnp.broadcast_to(small_ref[n : n + 1, lanes], (8, 128)) for n in range(9)]
        bias = jnp.broadcast_to(small_ref[9:10, lanes], (8, 128))

        def forward(r, total):
            for gi in (0, 1):
                for gj in (0, 1):
                    pair = conv_cell(hid, slab, gi, gj, r, k, bias, masks)
                    acts, grads = [], []
                    for h in (0, 1):
                        x = pair[h]
                        x2 = x * x
                        half = 0.5 * jnp.tanh(x * (C0 + (C0 * C1) * x2)) + 0.5
                        value = x * half
                        slope = half + (value - value * half) * (2.0 * C0 + (6.0 * C0 * C1) * x2)
                        acts.append(value)
                        grads.append(ga[slab, 2 * gi + gj, 2 * r + h] * slope)
                        total = total + grads[-1]
                    act[group_rows(gi, gj, r), lanes] = jnp.concatenate(acts, 0).astype(BF16)
                    store_pair(gc, slab, gi, gj, r, grads)
                    store_pair(gcs, slab, gi, gj, r, shift_pair(grads, 1 - gj, *masks))
            return total

        total = lax.fori_loop(0, HALF, forward, jnp.zeros((8, 128), F32))

        def put(gi, gj, r, pair):
            ghl[group_rows(gi, gj, r), lanes] = jnp.concatenate(pair, 0).astype(BF16)

        sums = conv_back(slab, k, hid, gc, gcs, put)
        for n, value in enumerate([*sums[:9], total, sums[9]]):
            sums_ref[n : n + 1, lanes] = jnp.sum(value, axis=0, keepdims=True)
        sums_ref[11:16, lanes] = jnp.zeros((5, 128), F32)
        if slab == 0:
            hook(1)

    if sums_over:
        @pl.when(step == 0)
        def _():
            for i, ref in enumerate(totals):
                pltpu.make_async_copy(so_far[i], ref, held.at[i]).wait()

    branch_ref[...] += dot_nn(act[...], fc2_ref[...])
    gn2_ref[...] += dot_nt(ghl[...], fc1_ref[...])

    @pl.when(step == steps - 1)
    def _():
        for i, out in enumerate((branch_out, gn2_out)):
            pltpu.make_async_copy(totals[i], out, held.at[i]).start()

    w2g_ref[...] = dot_tn(act[...], g2_ref[...]).astype(w2g_ref.dtype)
    w1g_ref[...] = dot_nn(n2t_ref[...], ghl[...]).astype(w1g_ref.dtype)
    hook(2)

    @pl.when(step == steps - 1)
    def _():
        waves.finish()
        for i, out in enumerate((branch_out, gn2_out)):
            pltpu.make_async_copy(totals[i], out, held.at[i]).wait()


def feed_forward(wide, narrow, n2, n2t, g2, fc1, small, part, fc2, arrays, spans, chunks, so_far=(),
                 width=256):
    sums_over = bool(so_far)
    tokens, model = n2.shape
    hidden = fc1.shape[1]
    slabs, steps, count = width // 128, hidden // width, len(arrays)
    padded = pltpu.VMEM((slabs, 4, 36, 8, 128), F32)
    columns = lambda rows: pl.BlockSpec((rows, width), lambda s: (0, s))
    lines = pl.BlockSpec((width, model), lambda s: (s, 0))
    anywhere = pl.BlockSpec(memory_space=pl.ANY)
    if sums_over:
        shapes = [a.shape for a in arrays]
        moved = [owned_shape(s, narrow) for s in shapes]
        extra = scatter_scratch(wide, narrow, shapes) + job_sems(wide, narrow, chunks)
        in_moved, out_moved = [once(s) for s in shapes], [once(m.shape) for m in moved]
    else:
        moved = [gathered_shape(wide, narrow, span_shape(a, s)) for a, s in zip(arrays, spans)]
        extra = job_sems(wide, narrow, chunks) + [pltpu.SemaphoreType.DMA((count,))]
        in_moved = out_moved = [anywhere] * count
    return pl.pallas_call(
        functools.partial(ff_kernel, wide, narrow, chunks, spans, steps, sums_over),
        grid=(steps,),
        in_specs=[
            once((tokens, model)), once((model, tokens)), once((tokens, model)),
            columns(model), pl.BlockSpec((16, width), lambda s: (0, part * steps + s)), lines,
        ] + [anywhere] * len(so_far) + in_moved,
        out_specs=[
            anywhere, anywhere, columns(model), lines, columns(16)
        ] + out_moved,
        out_shape=[
            like((tokens, model), F32), like((tokens, model), F32),
            like((model, hidden), BF16), like((hidden, model), BF16), like((16, hidden), F32),
        ] + moved,
        scratch_shapes=[
            padded, pltpu.VMEM((slabs, 4, 32, 8, 128), F32), padded, padded,
            pltpu.VMEM((tokens, width), BF16), pltpu.VMEM((tokens, width), BF16),
            pltpu.VMEM((tokens, model), F32), pltpu.VMEM((tokens, model), F32),
            pltpu.SemaphoreType.DMA((2,)),
        ] + extra,
        compiler_params=pltpu.CompilerParams(
            vmem_limit_bytes=56 * MIB, collective_id=4 if sums_over else 3, has_side_effects=True
        ),
        name="feed_forward",
    )(n2, n2t, g2, fc1, small, fc2, *so_far, *arrays)


def flip(index, bit):
    return index + bit - 2 * bit * lax.rem(index // bit, 2)


def bits_of(count):
    return [1 << b for b in range(count.bit_length() - 1)]


def digits_of(index, wide):
    levels = wide.bit_length() - 1
    return [lax.rem(index // (1 << (levels - 1 - i)), 2) for i in range(levels)]


def static_digits(index, wide):
    levels = wide.bit_length() - 1
    return [(index >> (levels - 1 - i)) & 1 for i in range(levels)]


def at(w, n):
    return {"wide": w, "narrow": n}


def greet(places):
    barrier = pltpu.get_barrier_semaphore()
    for place in places:
        pl.semaphore_signal(barrier, inc=1, device_id=place, device_id_type=pl.DeviceIdType.MESH)


def met(count):
    pl.semaphore_wait(pltpu.get_barrier_semaphore(), count)


def greet_all(place):
    barrier = pltpu.get_barrier_semaphore()
    total = place.total

    def body(k, carry):
        pl.semaphore_signal(
            barrier, inc=1, device_id=place.device(lax.rem(place.sid + k, total)),
            device_id_type=pl.DeviceIdType.MESH,
        )
        return carry

    lax.fori_loop(1, total, body, 0)


def remote(src, dst, send_sem, recv_sem, place):
    return pltpu.make_async_remote_copy(
        src_ref=src, dst_ref=dst, send_sem=send_sem, recv_sem=recv_sem, device_id=place,
        device_id_type=pl.DeviceIdType.MESH,
    )


class Place:
    def __init__(self, wide, narrow):
        self.wide, self.narrow = wide, narrow
        self.w, self.n = lax.axis_index("wide"), lax.axis_index("narrow")
        self.total, self.half = wide * narrow, wide * narrow // 2
        self.me = self.w * narrow + self.n
        self.core = lax.rem(self.w, 2)
        self.slot = (self.w // 2) * narrow + self.n
        self.sid = self.core * self.half + self.slot
        self.sibling = at(flip(self.w, 1), self.n)

    def device(self, sid):
        core, slot = sid // self.half, lax.rem(sid, self.half)
        return at(2 * (slot // self.narrow) + core, lax.rem(slot, self.narrow))

    def order_of(self, sid):
        core, slot = divmod(sid, self.half)
        return (2 * (slot // self.narrow) + core) * self.narrow + slot % self.narrow

    def partners(self):
        places = [at(self.w, lax.rem(self.n + k, self.narrow)) for k in range(1, self.narrow)]
        return places + [at(flip(self.w, bit), self.n) for bit in bits_of(self.wide)]

    def all_copies(self, src_of, dst, sends, recvs):
        def copy(k):
            sid = lax.rem(self.sid + k, self.total)
            return remote(src_of(sid), dst, sends.at[k], recvs.at[k], self.device(sid))

        return Exchange(copy, self.total)

    def kin_copies(self, src_of, dst, sends, recvs):
        def copy(k):
            slot = lax.rem(self.slot + k, self.half)
            return remote(src_of(slot), dst, sends.at[k], recvs.at[k],
                          self.device(self.core * self.half + slot))

        return Exchange(copy, self.half)

    def to_all(self, *refs):
        return self.all_copies(*refs).start()

    def to_kin(self, *refs):
        return self.kin_copies(*refs).start()

    def to_all_wait(self, *refs):
        self.all_copies(*refs).wait()

    def to_kin_wait(self, *refs):
        self.kin_copies(*refs).wait()


class Exchange:
    def __init__(self, copy, count):
        self.copy, self.count = copy, count

    def start(self):
        def body(k, carry):
            self.copy(k).start()
            return carry

        lax.fori_loop(1, self.count, body, 0)
        return self.wait

    def wait(self):
        def body(k, carry):
            self.copy(k).wait()
            return carry

        lax.fori_loop(1, self.count, body, 0)


def bit_sizes(wide):
    return (2,) * (wide.bit_length() - 1)


class Transfer:
    def __init__(self, place, sends, recvs, chunk, columns, turn):
        self.p, self.sends, self.recvs, self.chunk = place, sends, recvs, chunk
        start, size = columns
        self.all = pl.ds(start, size)
        levels = len(bit_sizes(place.wide))
        far = list(range(levels - 1))
        half = size // 256 * 128
        if turn % 2:
            far = far[::-1]
        self.parts = [(pl.ds(start, size - half), far)]
        if half:
            self.parts.append((pl.ds(start + size - half, half), far[::-1]))
        self.stages = levels + 1
        self.bits = digits_of(place.w, place.wide)
        self.count = 0

    def copy(self, src, dst, place):
        slot = self.count
        self.count += 1
        return remote(src, dst, self.sends.at[self.chunk, slot], self.recvs.at[self.chunk, slot], place)

    def along(self, level):
        return at(flip(self.p.w, 1 << (len(self.bits) - 1 - level)), self.p.n)

    def in_line(self, k):
        return at(self.p.w, lax.rem(self.p.n + k, self.p.narrow))

    def copies(self, stage):
        self.count = 0
        for before in range(stage):
            self.count += len(self.make(before, True))
        return self.make(stage, False)

    def start(self, stage):
        for copy in self.copies(stage):
            copy.start()

    def finish(self, stages):
        pass


class Gather(Transfer):
    def __init__(self, place, src, dst, sends, recvs, chunk, columns, turn):
        super().__init__(place, sends, recvs, chunk, columns, turn)
        self.src, self.dst = src, dst

    def make(self, stage, count_only):
        levels = len(self.bits)
        if stage == 0:
            ks = range(1, self.p.narrow)
            if count_only:
                return list(ks)
            return [
                self.copy(self.src.at[:, self.all],
                          self.dst.at[(*self.bits, self.p.n, slice(None), self.all)], self.in_line(k))
                for k in ks
            ]
        if stage == levels:
            parts = [(self.all, list(range(levels)))]
        else:
            parts = self.parts
        if count_only:
            return list(parts)
        found = []
        for columns, order in parts:
            index = list(self.bits)
            for level in order[: stage - 1]:
                index[level] = slice(None)
            part = self.dst.at[(*index, slice(None), slice(None), columns)]
            found.append(self.copy(part, part, self.along(order[stage - 1])))
        return found

    def wait(self, stage):
        for copy in self.copies(stage):
            copy.wait_recv()

    def finish(self, stages):
        for stage in stages:
            for copy in self.copies(stage):
                copy.wait_send()


def steady(first, stages, lag=2):
    return [first + lag * s for s in range(stages + 1)]


class Waves:
    def __init__(self, jobs, plan, resume=-1):
        self.jobs, self.resume = jobs, resume
        self.stages = jobs[0].stages
        self.plan = plan or [steady(c, self.stages) for c in range(len(jobs))]
        self.wave = resume + 1
        self.last = max(waves[-1] for waves in self.plan)

    def run(self, wave):
        for job, waves in zip(self.jobs, self.plan):
            for stage, when in enumerate(waves):
                if when != wave:
                    continue
                if stage and waves[stage - 1] > self.resume:
                    job.wait(stage - 1)
                if stage < self.stages:
                    job.start(stage)

    def tick(self, times=1):
        for _ in range(times):
            if self.wave <= self.last:
                self.run(self.wave)
                self.wave += 1

    def through(self, wave):
        while self.wave <= min(wave, self.last):
            self.tick()

    def at_hook(self, hook, hooks):
        first = self.resume + 3
        left = self.last + 1 - first
        for wave in range(first + hook * left // hooks, first + (hook + 1) * left // hooks):
            self.run(wave)

    def finish(self, last=None):
        last = self.last if last is None else last
        for job, waves in zip(self.jobs, self.plan):
            here = [s for s in range(self.stages) if self.resume < waves[s] <= last]
            for stage in here:
                if waves[stage + 1] > last:
                    job.wait(stage)
            job.finish(here)

    def end(self, last=None):
        last = self.last if last is None else last
        self.through(last)
        self.finish(last)


def job_sems(wide, narrow, chunks):
    per = narrow - 1 + 2 * (wide.bit_length() - 1)
    return [pltpu.SemaphoreType.DMA((len(chunks), per))] * 2


def gather_jobs(place, srcs, dsts, sends, recvs, chunks, plan=None, resume=-1, shift=0):
    jobs = [
        Gather(place, srcs[i], dsts[i], sends, recvs, c, columns, c + shift)
        for c, (i, *columns) in enumerate(chunks)
    ]
    return Waves(jobs, plan, resume)


def gathered_shape(wide, narrow, shape):
    return like((*bit_sizes(wide), narrow, *shape), BF16)


def thirds(i, size):
    return [(i, t * (size // 3), size // 3) for t in range(3)]


class Scatter(Transfer):
    def __init__(self, place, src, buffers, out, sends, recvs, chunk, columns):
        super().__init__(place, sends, recvs, chunk, columns, chunk)
        self.src, self.out = src, out
        self.halves, self.line, self.got = buffers[:-2], buffers[-2], buffers[-1]
        self.rows = self.line.shape[1]
        core = len(self.bits) - 1
        self.parts = [(columns, [core] + order) for columns, order in self.parts]

    def make(self, stage, count_only):
        levels = len(self.bits)
        if stage == levels:
            ks = range(1, self.p.narrow)
            if count_only:
                return list(ks)
            return [
                self.copy(self.line.at[lax.rem(self.p.n + k, self.p.narrow), :, self.all],
                          self.got.at[k - 1, :, self.all], self.in_line(k))
                for k in ks
            ]
        parts = self.parts if stage else [(self.all, self.parts[0][1])]
        if count_only:
            return list(parts)
        found = []
        for columns, order in parts:
            source, index, kept = self.level(order, stage, True)
            into = self.halves[stage].at[(*kept, slice(None), columns)]
            found.append(self.copy(source.at[(*index, slice(None), columns)], into, self.along(order[stage])))
        return found

    def level(self, order, stage, theirs):
        source = self.src if stage == 0 else self.halves[stage - 1]
        left = [level for level in range(len(self.bits)) if level not in order[:stage]]
        bit = self.bits[order[stage]]
        bit = 1 - bit if theirs else bit
        index = [bit if level == order[stage] else slice(None) for level in left]
        return source, index, [slice(None)] * (len(left) - 1)

    def wait(self, stage):
        for copy in self.copies(stage):
            copy.wait()
        levels = len(self.bits)
        if stage == levels:
            value = self.line[self.p.n, :, self.all].astype(F32)
            for k in range(1, self.p.narrow):
                value = value + self.got[k - 1, :, self.all].astype(F32)
            self.out[:, self.all] = value
            return
        for columns, order in self.parts:
            source, index, kept = self.level(order, stage, False)
            into = self.halves[stage]
            for j in range(1 << len(kept)):
                digits = [(j >> i) & 1 for i in range(len(kept))]
                mine = [v if not isinstance(v, slice) else None for v in index]
                rest = iter(digits)
                mine = [next(rest) if v is None else v for v in mine]
                self.add(source, tuple(mine), into, tuple(digits), columns, stage == levels - 1)

    def add(self, source, mine, into, arrived, columns, last):
        if last:
            total = source[(*mine, slice(None), columns)].astype(F32) + into[
                (*arrived, slice(None), columns)
            ].astype(F32)
            for m in range(self.p.narrow):
                rows = slice(m * self.rows, (m + 1) * self.rows)
                self.line[m, :, columns] = total[rows].astype(BF16)
            return

        into[(*arrived, slice(None), columns)] = (
            source[(*mine, slice(None), columns)] + into[(*arrived, slice(None), columns)]
        )


def scatter_scratch(wide, narrow, shapes):
    scratch = []
    for *_, height, columns in shapes:
        for stage in range(wide.bit_length() - 1):
            scratch.append(pltpu.VMEM((*bit_sizes(wide)[stage + 1 :], height, columns), BF16))
        scratch.append(pltpu.VMEM((narrow, height // narrow, columns), BF16))
        scratch.append(pltpu.VMEM((narrow - 1, height // narrow, columns), BF16))
    return scratch


def scatter_jobs(place, srcs, outs, buffers, sends, recvs, chunks, plan=None):
    per = len(buffers) // len(srcs)
    jobs = [
        Scatter(place, srcs[i], buffers[i * per : (i + 1) * per], outs[i], sends, recvs, c, columns)
        for c, (i, *columns) in enumerate(chunks)
    ]
    return Waves(jobs, plan)


def owned_shape(shape, narrow):
    return like((shape[-2] // narrow, shape[-1]), F32)


def move_lanes(tiles, moves, count):
    rows = tiles[0].shape[0]
    lane = lax.broadcasted_iota(jnp.int32, (rows, 128), 1)
    out = [jnp.zeros((rows, 128), F32) for _ in range(count)]
    for start, to, length in moves:
        while length:
            size = min(length, 128 - start % 128, 128 - to % 128)
            tile = tiles[start // 128]
            turn = (to - start) % 128
            if turn:
                tile = pltpu.roll(tile, turn, 1)
            inside = (lane >= to % 128) & (lane < to % 128 + size)
            out[to // 128] = jnp.where(inside, tile, out[to // 128])
            start, to, length = start + size, to + size, length - size
    return out


def tiles_of(values):
    return [values[:, i : i + 128] for i in range(0, values.shape[1], 128)]


def front_kernel(wide, narrow, chunks, plan, spans, own, own_ff, *refs):
    count = len(spans)
    (x_ref, cot_ref, mask_ref, cond_ref, ada_ref, bias_ref, small_ref, fc1_ref) = refs[:8]
    srcs, refs = refs[8 : 8 + count], refs[8 + count :]
    srcs = [part_of(ref, span) for ref, span in zip(srcs, spans)]
    (mod_ref, sils_ref, model_ref, hidden_ref, lat_ref, gout_ref, g2_ref, normed_ref, mixed_ref,
     keep_ref, fc2b_ref, fc1b_ref) = refs[:12]
    dsts, refs = refs[12 : 13 + count], refs[13 + count :]
    (order_ref, fc1a_ref, sil_out, got, part, sib, rows_in, smalls, send_a, recv_a, send_b, recv_b, send_c, recv_c,
     sends, recvs, local) = refs
    p = Place(wide, narrow)
    mine = digits_of(p.w, wide)
    model = x_ref.shape[1]
    slabs = model // 128
    own_copies = [
        pltpu.make_async_copy(srcs[i], dsts[1 + i].at[(*mine, p.n)], local.at[i]) for i in range(count)
    ]
    for copy in own_copies:
        copy.start()
    greet_all(p)
    order_ref[...] = order_matrix()
    waves = gather_jobs(p, [small_ref, fc1a_ref, *srcs], [smalls, *dsts], sends, recvs, chunks, plan)
    last = waves.plan[chunks.index((3, 0, model))][-1]
    cond = cond_ref[...].astype(F32)
    sil = (cond * jax.nn.sigmoid(cond)).astype(BF16).astype(F32)
    tiles = tiles_of(sil)
    for sid in range(p.total):
        d = p.order_of(sid)
        sil_out[sid] = move_lanes(tiles, [(own * d, 0, own)], 1)[0]
    got[p.sid] = sil_out[p.sid]
    smalls[(*mine, p.n)] = small_ref[...]

    def arrange(t):
        rows = pl.ds(t * GROUP, GROUP)
        tokens = dot_nn(order_ref[...], x_ref[rows, :])
        unit, _ = unit_rows(tokens)
        mask = mask_ref[:, t * GROUP : (t + 1) * GROUP].astype(F32)
        mask = (order_ref[...].astype(F32) * mask).astype(BF16)
        kept = dot_nn(mask, jnp.ones((GROUP, 128), BF16))
        gout = dot_nn(order_ref[...], cot_ref[rows, :]) * jnp.concatenate([kept] * slabs, axis=1)
        for g in range(4):
            src = slice(64 * g, 64 * g + 64)
            dst = pl.ds(g * GROUP + 64 * t, 64)
            lat_ref[dst, :] = tokens[src].astype(BF16)
            gout_ref[dst, :] = gout[src].astype(BF16)
            keep_ref[dst, :] = (kept[src] - 1.0) * 1e30
            for s in range(slabs):
                tile = unit[src, s * 128 : s * 128 + 128].reshape(8, 8, 128)
                normed_ref[s, g, 2 + 8 * t : 10 + 8 * t] = tile

    met(p.total - 1)
    wait_sil = p.to_all(lambda sid: sil_out.at[sid], got.at[p.sid], send_a, recv_a)
    waves.tick(2)
    arrange(0)
    for copy in own_copies:
        copy.wait()
    waves.tick()
    arrange(1)
    wait_sil()
    sil = got[...].reshape(p.total, 128)
    sils_ref[...] = sil
    product = dot_nn(sil[:, :own].astype(BF16), ada_ref[...]) + bias_ref[...]
    for d in range(p.total):
        part[d // p.half, d % p.half] = product[d : d + 1, :]
    to_sibling = remote(part.at[1 - p.core], sib, send_b, recv_b, p.sibling)
    to_sibling.start()
    waves.tick()
    arrange(2)
    to_sibling.wait()
    part[p.core] = part[p.core] + sib[...]
    rows_in[p.slot] = part[p.core, p.slot]
    wait_rows = p.to_kin(lambda slot: part.at[p.core, slot], rows_in.at[p.slot], send_c, recv_c)
    waves.tick()
    arrange(3)
    clear_edges(normed_ref)
    waves.tick()
    columns = tiles_of(fc1_ref[...].astype(F32))
    for h, ref in enumerate((fc1a_ref, fc1b_ref)):
        moves = [
            (own_ff * d + own_ff // 2 * h, own_ff // 2 * d, own_ff // 2) for d in range(p.total)
        ]
        ref[...] = jnp.concatenate(move_lanes(columns, moves, len(columns) // 2), axis=1).astype(BF16)
    own_fc1 = pltpu.make_async_copy(fc1a_ref, dsts[0].at[(*mine, p.n)], local.at[count])
    own_fc1.start()
    waves.through(waves.plan[0][-1])
    pieces = [smalls[(*static_digits(d // narrow, wide), d % narrow)].astype(F32) for d in range(p.total)]
    moves = [(128 * d, own * d, own) for d in range(p.total)]
    model_ref[...] = jnp.concatenate(move_lanes([q[:16] for q in pieces], moves, slabs), axis=1)
    half, hidden = own_ff // 2, fc1_ref.shape[1]
    moves = [
        (128 * d + half * h, hidden // 2 * h + half * d, half) for d in range(p.total) for h in (0, 1)
    ]
    hidden_ref[...] = jnp.concatenate(
        move_lanes([q[16:] for q in pieces], moves, hidden // 128), axis=1
    )
    own_fc1.wait()
    wait_rows()
    mod = jnp.sum(rows_in[...], axis=0)
    for i in range(6):
        mod_ref[i : i + 1, :] = mod[:, i * model : (i + 1) * model]

    shift, scale, gate = mod_ref[0:1, :], mod_ref[1:2, :], mod_ref[5:6, :]
    total = jnp.zeros((8, model), F32)
    for g in range(4):
        rows = pl.ds(g * GROUP, GROUP)
        two = gout_ref[rows, :].astype(F32) * gate
        total = total + row_sum(two)
        g2_ref[rows, :] = two.astype(BF16)
    fc2b_ref[...] = total
    masks = edge_masks()
    for s in range(slabs):
        lanes = pl.ds(s * 128, 128)
        at_s = slice(s * 128, s * 128 + 128)
        shift8 = jnp.broadcast_to(shift[:, at_s], (8, 128))
        scale8 = jnp.broadcast_to(1.0 + scale[:, at_s], (8, 128))
        normed_ref[s, :, 2:34] = normed_ref[s, :, 2:34] * scale8 + shift8
        k = [jnp.broadcast_to(model_ref[n : n + 1, at_s], (8, 128)) for n in range(9)]
        bias = jnp.broadcast_to(model_ref[9:10, at_s], (8, 128))

        def body(r, carry):
            for gi in (0, 1):
                for gj in (0, 1):
                    pair = conv_cell(normed_ref, s, gi, gj, r, k, bias, masks)
                    mixed_ref[group_rows(gi, gj, r), lanes] = jnp.concatenate(pair, 0).astype(BF16)
            return carry

        lax.fori_loop(0, HALF, body, 0)
        waves.through(min(waves.wave, last))
    waves.end(last)


def front(wide, narrow, x, cot, mask, cond, ada, bias, small, fc1, blocks, spans, chunks, plan):
    total = wide * narrow
    tokens, model = x.shape
    slabs, count, columns = model // 128, len(blocks), ada.shape[1]
    hidden = fc1.shape[1]
    own, own_ff = model // total, hidden // total
    inside = pl.BlockSpec(memory_space=pltpu.VMEM)
    anywhere = pl.BlockSpec(memory_space=pl.ANY)
    all_sems = pltpu.SemaphoreType.DMA((total,))
    one_sem = pltpu.SemaphoreType.DMA
    kin_sems = pltpu.SemaphoreType.DMA((total // 2,))
    return pl.pallas_call(
        functools.partial(front_kernel, wide, narrow, chunks, plan, spans, own, own_ff),
        in_specs=[inside] * 8 + [anywhere] * count,
        out_specs=[inside] * 12 + [anywhere] * (count + 1),
        out_shape=[
            like((8, model), F32), like((total, 128), F32), like((16, model), F32),
            like((16, hidden), F32), like((tokens, model), BF16), like((tokens, model), BF16),
            like((tokens, model), BF16), like((slabs, 4, 36, 8, 128), F32),
            like((tokens, model), BF16), like((tokens, 128), F32), like((8, model), F32),
            like((own, hidden // 2), BF16),
            gathered_shape(wide, narrow, (own, hidden // 2)),
        ] + [gathered_shape(wide, narrow, span_shape(b, s)) for b, s in zip(blocks, spans)],
        scratch_shapes=[
            pltpu.VMEM((GROUP, GROUP), BF16), pltpu.VMEM((own, hidden // 2), BF16), pltpu.VMEM((total, 1, 128), F32),
            pltpu.VMEM((total, 1, 128), F32), pltpu.VMEM((2, total // 2, 1, columns), F32),
            pltpu.VMEM((total // 2, 1, columns), F32), pltpu.VMEM((total // 2, 1, columns), F32),
            pltpu.VMEM((*bit_sizes(wide), narrow, 32, 128), BF16),
            all_sems, all_sems, one_sem, one_sem, kin_sems, kin_sems,
            *job_sems(wide, narrow, chunks), pltpu.SemaphoreType.DMA((count + 1,)),
        ],
        compiler_params=pltpu.CompilerParams(
            vmem_limit_bytes=56 * MIB, collective_id=0, has_side_effects=True
        ),
        name="front",
    )(x, cot, mask, cond, ada, bias, small, fc1, *blocks)


def attend_kernel(wide, narrow, chunks, plan, resume, shift, *refs):
    mixed_ref, lat_ref, keep_ref, mod_ref, small_ref, qkv_ref, proj_ref, fc1_in, fc2_in = refs[:9]
    triple_ref, probs_ref, att_ref, branch_ref, n2_ref, n2t_ref, fc1_ref, fc2_ref = refs[9:17]
    sends, recvs = refs[17:]
    step = pl.program_id(0)
    p = Place(wide, narrow)
    waves = gather_jobs(p, [fc1_in, fc2_in], [fc1_ref, fc2_ref], sends, recvs, chunks, plan, resume,
                        shift)

    def on(when, work):
        pl.when(step == when)(work)

    def hook(position):
        for when in range(4):
            on(when, lambda: waves.at_hook(2 * when + position, 8))

    def first():
        met(len(p.partners()))
        waves.run(resume + 1)
        waves.run(resume + 2)

    on(0, lambda: greet(p.partners()))
    model = lat_ref.shape[1]
    slabs = model // 128
    triple_ref[...] = dot_nn(mixed_ref[...], qkv_ref[...]).astype(BF16)
    on(0, first)
    lane = lax.broadcasted_iota(jnp.int32, (GROUP, 128), 1)
    left = lane < HEAD
    keep = jnp.concatenate([keep_ref[...]] * 2, axis=1)
    for s in range(slabs):
        q = triple_ref[:, s * 128 : s * 128 + 128]
        k = triple_ref[:, model + s * 128 : model + s * 128 + 128] * jnp.asarray(0.125, BF16)
        v = triple_ref[:, 2 * model + s * 128 : 2 * model + s * 128 + 128]
        outs = []
        for h in (0, 1):
            mine = left if h == 0 else jnp.logical_not(left)
            scores = dot_nt(jnp.where(mine, k, jnp.zeros_like(k)), q) + keep
            e = jnp.exp(scores - jnp.max(scores, axis=0, keepdims=True))
            prob = (e * (1.0 / jnp.sum(e, axis=0, keepdims=True))).astype(BF16)
            probs_ref[2 * s + h, 0] = prob
            outs.append(dot_tn(prob, v))
        att_ref[:, s * 128 : s * 128 + 128] = jnp.where(left, outs[0], outs[1]).astype(BF16)
        if s == slabs // 2 - 1:
            hook(0)
    branch = dot_nn(att_ref[...], proj_ref[...]) + small_ref[10:11, :]
    middle = lat_ref[...].astype(F32) + mod_ref[2:3, :] * branch
    unit, _ = unit_rows(middle)
    branch_ref[...] = branch
    n2 = unit * (1.0 + mod_ref[4:5, :]) + mod_ref[3:4, :]
    n2_ref[...] = n2.astype(BF16)
    n2t_ref[...] = n2.T.astype(BF16)
    hook(1)
    on(3, waves.finish)


def attend(wide, narrow, mixed, lat, keep, mod, small, qkv, proj, fc1, fc2, chunks, plan, resume, shift):
    tokens, model = lat.shape
    heads = model // HEAD
    by_group = lambda columns: pl.BlockSpec((GROUP, columns), lambda g: (g, 0))
    anywhere = pl.BlockSpec(memory_space=pl.ANY)
    return pl.pallas_call(
        functools.partial(attend_kernel, wide, narrow, chunks, plan, resume, shift),
        grid=(4,),
        in_specs=[
            by_group(model), by_group(model), by_group(128), whole(mod.shape),
            whole(small.shape), once(qkv.shape), once(proj.shape), anywhere, anywhere,
        ],
        out_specs=[
            by_group(3 * model), pl.BlockSpec((heads, 1, GROUP, GROUP), lambda g: (0, g, 0, 0)),
            by_group(model), by_group(model), by_group(model),
            pl.BlockSpec((model, GROUP), lambda g: (0, g)), anywhere, anywhere,
        ],
        out_shape=[
            like((tokens, 3 * model), BF16), like((heads, 4, GROUP, GROUP), BF16),
            like((tokens, model), BF16), like((tokens, model), F32),
            like((tokens, model), BF16), like((model, tokens), BF16),
            like(fc1.shape, BF16), like(fc2.shape, BF16),
        ],
        input_output_aliases={7: 6, 8: 7},
        scratch_shapes=job_sems(wide, narrow, chunks),
        compiler_params=pltpu.CompilerParams(
            vmem_limit_bytes=56 * MIB, collective_id=1, has_side_effects=True
        ),
        name="attend",
    )(mixed, lat, keep, mod, small, qkv, proj, fc1, fc2)


def back_kernel(wide, narrow, chunks, plan, own, own_ff, *refs):
    (gn2_ref, two_ref, branch_ref, gout_ref, att_ref, mixed_ref,
     q_ref, k_ref, v_ref, probs_ref, mod_ref, small_ref, proj_ref, wq_ref, wk_ref, wv_ref,
     lat_ref, normed_hbm, fc2b_ref, hida_ref, hidb_ref, sils_ref, ada_ref, fc1s_ref,
     fc2s_ref) = refs[:25]
    (rows_ref, xg_ref, wgrad_ref, cond_ref, small_out, qkvg_ref, projg_ref, fc1g_ref,
     fc2g_ref) = refs[25:34]
    (ga, gmid, gmix, gmoved, sums, proj_src, qkv_src, early, late, cuts, cuts_in, hcuts, hcuts_in, part, cond_in,
     gt, normed_ref, held,
     send_a, recv_a, send_b, recv_b, send_c, recv_c, send_d, recv_d, send_e, recv_e, send_f, recv_f,
     send_g, recv_g) = refs[34:66]
    buffers, (sends, recvs) = refs[66:-2], refs[-2:]
    step = pl.program_id(0)
    model = lat_ref.shape[1]
    slabs = model // 128
    last = 3 + slabs
    p = Place(wide, narrow)
    half, hidden = own_ff // 2, 2 * hida_ref.shape[1]
    waves = scatter_jobs(p, [fc1s_ref, fc2s_ref, proj_src, qkv_src],
                         [fc1g_ref, fc2g_ref, projg_ref, qkvg_ref], buffers, sends, recvs, chunks,
                         plan)
    gbl = xg_ref
    mine = lambda ref: ref.at[p.core, p.slot]

    @pl.when(step == 0)
    def _():
        greet_all(p)
        pltpu.make_async_copy(normed_hbm, normed_ref, held).start()
        sums[...] = jnp.zeros_like(sums)
        gmix[...] = jnp.zeros_like(gmix)
        clear_edges(gmoved)
        tiles = tiles_of(hida_ref[...]) + tiles_of(hidb_ref[...])
        for sid in range(p.total):
            d = p.order_of(sid)
            moves = [(half * d, 0, half), (hidden // 2 + half * d, half, half)]
            hcuts[sid] = move_lanes(tiles, moves, 1)[0]
        hcuts_in[p.sid] = hcuts[p.sid]

    @pl.when(step < 4)
    def _():
        rows = pl.ds(pl.multiple_of(step * GROUP, GROUP), GROUP)
        branch = branch_ref[...]
        middle = lat_ref[rows, :].astype(F32) + mod_ref[2:3, :] * branch
        two = two_ref[...] + small_ref[11:12, :]
        gout = gout_ref[...].astype(F32)
        rows_ref[...] = (middle + mod_ref[5:6, :] * two).astype(BF16)
        sums[3] += row_sum(gout * two)
        unit, scale = unit_rows(middle)
        gn2 = gn2_ref[...]
        sums[1] += row_sum(gn2)
        sums[2] += row_sum(gn2 * unit)
        gm = gout + unit_back(gn2 * (1.0 + mod_ref[4:5, :]), unit, scale)
        gmid[rows, :] = gm
        sums[0] += row_sum(gm * branch)
        gb = gm * mod_ref[2:3, :]
        sums[4] += row_sum(gb)
        low = gb.astype(BF16)
        gbl[rows, :] = low
        ga[rows, :] = dot_nt(low, proj_ref[...]).astype(BF16)

    @pl.when(step == 0)
    def _():
        met(p.total - 1)
        waves.run(0)
        waves.run(1)
        p.to_all(lambda sid: hcuts.at[sid], hcuts_in.at[p.sid], send_g, recv_g)

    for when in (1, 2):
        pl.when(step == when)(lambda: waves.run(when + 1))

    @pl.when(step == 3)
    def _():
        proj_src[...] = dot_tn(att_ref[...], gbl[...]).astype(BF16).reshape(proj_src.shape)
        waves.run(4)
        for i in range(4):
            early[p.core, p.slot, :, i * model : (i + 1) * model] = jnp.sum(
                sums[i], axis=0, keepdims=True
            )
        p.to_kin(lambda slot: mine(early), mine(early), send_a, recv_a)

    def attention(groups):
        s = step - 4
        lane = lax.broadcasted_iota(jnp.int32, (GROUP, 128), 1)
        left = lane < HEAD
        eighth = jnp.asarray(0.125, BF16)
        lanes = pl.ds(pl.multiple_of(s * 128, 128), 128)
        weight = jnp.concatenate([wq_ref[...], wk_ref[...], wv_ref[...]], axis=1)
        for g in groups:
            rows = slice(g * GROUP, (g + 1) * GROUP)
            q, k, v = q_ref[rows, :] * eighth, k_ref[rows, :] * eighth, v_ref[rows, :]
            grad = ga[rows, lanes]
            gq = gk = gv = None
            for h in (0, 1):
                keep = left if h == 0 else jnp.logical_not(left)
                only = lambda value: jnp.where(keep, value, jnp.zeros_like(value))
                p_low = probs_ref[h, g]
                prob = p_low.astype(F32)
                gh = only(grad)
                gp = dot_nt(v, gh)
                inner = jnp.sum(prob * gp, axis=0, keepdims=True)
                gs = (prob * (gp - inner)).astype(BF16)
                terms = (dot_tn(gs, only(k)), dot_nn(gs, only(q)), dot_nn(p_low, gh))
                if h == 0:
                    gq, gk, gv = terms
                else:
                    gq, gk, gv = gq + terms[0], gk + terms[1], gv + terms[2]
            found = jnp.concatenate([gq, gk, gv], axis=1).astype(BF16)
            gt[rows, :] = found
            gmixed = dot_nt(found, weight)
            for t in range(slabs):
                gmix[t + 1, g, 2:34] += gmixed[:, t * 128 : t * 128 + 128].reshape(32, 8, 128)

    pl.when(step >= 4)(lambda: attention((0, 1)))
    for s in range(slabs):
        pl.when(step == 4 + s)(lambda: waves.run(5 + 2 * s))

    @pl.when(step >= 4)
    def _():
        attention((2, 3))
        columns = pl.ds(pl.multiple_of((step - 4) * 384, 128), 384)
        found = dot_tn(mixed_ref[...], gt[...]).astype(BF16)
        qkv_src[..., columns] = found.reshape(*qkv_src.shape[:-1], 384)

    for s in range(slabs):
        pl.when(step == 4 + s)(lambda: waves.run(6 + 2 * s))

    @pl.when(step == 6)
    def _():
        p.to_kin_wait(lambda slot: mine(early), mine(early), send_a, recv_a)
        remote(early.at[p.core], early.at[p.core], send_d, recv_d, p.sibling).start()

    @pl.when(step == last)
    def _():
        waves.wave = 5 + 2 * slabs
        pltpu.make_async_copy(normed_hbm, normed_ref, held).wait()
        masks = edge_masks()
        rows_out = []
        for s in range(slabs):
            at_s = slice(s * 128, s * 128 + 128)
            k = [jnp.broadcast_to(small_ref[n : n + 1, at_s], (8, 128)) for n in range(9)]

            def move(r, total):
                for gi in (0, 1):
                    for gj in (0, 1):
                        pair = load_pair(gmix, s + 1, gi, gj, r)
                        total = total + pair[0] + pair[1]
                        store_pair(gmoved, 0, gi, gj, r, shift_pair(pair, 1 - gj, *masks))
                return total

            total = lax.fori_loop(0, HALF, move, jnp.zeros((8, 128), F32))

            def put(gi, gj, r, pair):
                store_pair(gmix, s, gi, gj, r, pair)

            found = conv_back(0, k, normed_ref.at[s : s + 1], gmix.at[s + 1 : s + 2], gmoved, put)
            late[p.core, p.slot, :, at_s] = jnp.sum(found[9], axis=0, keepdims=True)
            column = [jnp.sum(v, axis=0, keepdims=True) for v in (*found[:9], total)]
            column.append(jnp.sum(sums[4, :, at_s], axis=0, keepdims=True))
            column.append(jnp.sum(fc2b_ref[:, at_s], axis=0, keepdims=True))
            rows_out.append(jnp.concatenate(column + [jnp.zeros((4, 128), F32)], axis=0))
            if s % 2:
                waves.tick()
        scale_sum = jnp.zeros((8, model), F32)
        for g in range(4):
            rows = pl.ds(g * GROUP, GROUP)
            unit, scale = unit_rows(lat_ref[rows, :].astype(F32))
            gn = jnp.concatenate(
                [gmix[s, g, 2:34].reshape(GROUP, 128) for s in range(slabs)], axis=1
            )
            scale_sum = scale_sum + row_sum(gn * unit)
            gmid[rows, :] = gmid[rows, :] + unit_back(gn * (1.0 + mod_ref[1:2, :]), unit, scale)
        late[p.core, p.slot, :, model:] = jnp.sum(scale_sum, axis=0, keepdims=True)
        wait_late = p.to_kin(lambda slot: mine(late), mine(late), send_c, recv_c)
        waves.tick()
        p.to_all_wait(lambda sid: hcuts.at[sid], hcuts_in.at[p.sid], send_g, recv_g)
        small_out[8:, :] = jnp.sum(hcuts_in[...], axis=0)
        modulation = tiles_of(late[p.core, p.slot]) + tiles_of(early[p.core, p.slot])
        third = 2 * own
        for sid in range(p.total):
            d = p.order_of(sid)
            piece = move_lanes(rows_out, [(own * d, 0, own)], 1)[0][:8]
            piece = piece + move_lanes(rows_out, [(own * d, 32, own)], 1)[0][8:]
            bias = [
                move_lanes(modulation, [(third * (3 * d + i), 64, third)], 1)[0] for i in range(3)
            ]
            cuts[sid] = piece + jnp.concatenate(bias + [jnp.zeros((5, 128), F32)], axis=0)
        cuts_in[p.sid] = cuts[p.sid]
        wait_cuts = p.to_all(lambda sid: cuts.at[sid], cuts_in.at[p.sid], send_b, recv_b)
        xg_ref[...] = gmid[...].astype(BF16)
        wait_late()
        swap_late = remote(late.at[p.core], late.at[p.core], send_e, recv_e, p.sibling)
        swap_late.start()
        waves.tick()
        remote(early.at[p.core], early.at[p.core], send_d, recv_d, p.sibling).wait()
        swap_late.wait()
        sil = sils_ref[:, :own].astype(BF16)
        cond = None
        for ref, start in ((late, 0), (early, 2 * model)):
            size = ref.shape[-1]
            span = slice(start, start + size)
            found = ref[...].reshape(p.total, size)
            low = found.astype(BF16)
            wgrad_ref[:, span] = dot_tn(sil, low)
            term = dot_nt(low, ada_ref[:, span])
            cond = term if cond is None else cond + term
        cond = jnp.concatenate([cond, jnp.zeros((p.total, 128 - own), F32)], axis=1)
        for sid in range(p.total):
            part[sid] = cond[sid : sid + 1, :]
        cond_in[p.me] = part[p.sid]
        wait_cond = p.to_all(lambda sid: part.at[sid], cond_in.at[p.me], send_f, recv_f)
        waves.end()
        wait_cuts()
        small_out[:8, :] = jnp.sum(cuts_in[...], axis=0)
        wait_cond()
        cond_ref[...] = cond_in[...]


def back(wide, narrow, gn2, two, branch, gout, att, mixed, triple, probs, mod, small, proj, qkv,
         lat, normed, fc2b, hidden_sums, sils, ada, fc1s, fc2s):
    total = wide * narrow
    tokens, model = lat.shape
    slabs, columns = model // 128, ada.shape[1]
    hidden = 2 * hidden_sums[0].shape[1]
    own, own_ff = ada.shape[0], hidden // total
    by_group = pl.BlockSpec((GROUP, model), lambda t: (jnp.minimum(t, 3), 0))
    slab = lambda t: jnp.clip(t - 4, 0, slabs - 1)
    third = lambda rows, i: pl.BlockSpec((rows, 128), lambda t: (0, i * slabs + slab(t)))
    all_sems, kin_sems = (pltpu.SemaphoreType.DMA((n,)) for n in (total, total // 2))
    one_sem = pltpu.SemaphoreType.DMA
    padded = lambda count: pltpu.VMEM((count, 4, 36, 8, 128), F32)
    height = model // wide
    bits = bit_sizes(wide)
    shapes = [fc1s.shape, fc2s.shape, (*bits, height, model), (*bits, height, 3 * model)]
    chunks = thirds(0, hidden // 2) + thirds(1, model) + [(2, 0, model)]
    chunks += [(3, 384 * s, 384) for s in range(slabs)]
    starts = [0, 2, 5, 8, 11, 14, 4] + [6 + 2 * s for s in range(slabs)]
    plan = [steady(c, wide.bit_length()) for c in starts]
    full = lambda a: once(a.shape)
    outs = [
        like((tokens, model), BF16), like((tokens, model), BF16), like((own, columns), F32),
        like((total, 1, 128), F32), like((24, 128), F32), like((own, 3 * model), F32),
        like((own, model), F32), like((own, hidden // 2), F32), like((own_ff // 2, model), F32),
    ]
    return pl.pallas_call(
        functools.partial(back_kernel, wide, narrow, chunks, plan, own, own_ff),
        grid=(4 + slabs,),
        in_specs=[by_group] * 4 + [full(att), full(mixed)] + [third(tokens, i) for i in range(3)] + [
            pl.BlockSpec((2, 4, GROUP, GROUP), lambda t: (slab(t), 0, 0, 0)),
            full(mod), full(small), full(proj), third(model, 0), third(model, 1), third(model, 2),
            full(lat), pl.BlockSpec(memory_space=pl.ANY), full(fc2b), full(hidden_sums[0]), full(hidden_sums[1]),
            full(sils), full(ada), full(fc1s), full(fc2s),
        ],
        out_specs=[by_group] + [once(o.shape) for o in outs[1:]],
        out_shape=outs,
        scratch_shapes=[
            pltpu.VMEM((tokens, model), BF16), pltpu.VMEM((tokens, model), F32),
            padded(slabs + 1), padded(1), pltpu.VMEM((5, 8, model), F32),
            pltpu.VMEM(shapes[2], BF16), pltpu.VMEM(shapes[3], BF16),
            pltpu.VMEM((2, total // 2, 1, 4 * model), F32),
            pltpu.VMEM((2, total // 2, 1, 2 * model), F32),
            pltpu.VMEM((total, 8, 128), F32), pltpu.VMEM((total, 8, 128), F32),
            pltpu.VMEM((total, 16, 128), F32), pltpu.VMEM((total, 16, 128), F32),
            pltpu.VMEM((total, 1, 128), F32), pltpu.VMEM((total, 1, 128), F32),
            pltpu.VMEM((tokens, 384), BF16), padded(slabs), one_sem,
            kin_sems, kin_sems, all_sems, all_sems, kin_sems, kin_sems, one_sem, one_sem,
            one_sem, one_sem, all_sems, all_sems, all_sems, all_sems,
            *scatter_scratch(wide, narrow, shapes), *job_sems(wide, narrow, chunks),
        ],
        compiler_params=pltpu.CompilerParams(
            vmem_limit_bytes=63 * MIB, collective_id=2, has_side_effects=True
        ),
        name="attend_back",
    )(gn2, two, branch, gout, att, mixed, triple, triple, triple, probs, mod,
      small, proj, qkv, qkv, qkv, lat, normed, fc2b, *hidden_sums, sils, ada, fc1s,
      fc2s)


def finish_kernel(own, own_ff, rows_ref, grads_ref, wgrad_ref, qkvg_ref, projg_ref, fc1a_ref,
                  fc1b_ref, fc2a_ref, fc2b_ref, small_ref, cond_ref, pieces_ref,
                  out_ref, xg_ref, wgrad_out, qkv_out, proj_out, fc1_out, fc2_out, condg_out, adab_out,
                  dw1k_out, dw1b_out, projb_out, fc2b_out, dw2k_out, dw2b_out, fc1b_out):
    model = out_ref.shape[1]
    order = order_matrix()
    for src, dst in ((rows_ref, out_ref), (grads_ref, xg_ref)):
        block = src[...].reshape(GROUP, model)
        dst[...] = dot_tn(order, block).astype(BF16)

    @pl.when(pl.program_id(0) == 0)
    def _():
        half, hidden, total = own_ff // 2, fc1_out.shape[1], pieces_ref.shape[0]
        wgrad_out[...] = wgrad_ref[...]
        proj_out[...] = projg_ref[...]
        for s in range(model // 128):
            for i in range(3):
                to = i * model + s * 128
                qkv_out[:, to : to + 128] = qkvg_ref[:, s * 384 + i * 128 : s * 384 + i * 128 + 128]
        moves = [
            (hidden // 2 * h + half * d, own_ff * d + half * h, half)
            for d in range(total) for h in (0, 1)
        ]
        tiles = tiles_of(fc1a_ref[...]) + tiles_of(fc1b_ref[...])
        for i, tile in enumerate(move_lanes(tiles, moves, hidden // 128)):
            fc1_out[:, i * 128 : i * 128 + 128] = tile
        fc2_out[:half, :] = fc2a_ref[...]
        fc2_out[half:, :] = fc2b_ref[...]
        tiles = [pieces_ref[d] for d in range(total)]
        moves = [(128 * d, own * d, own) for d in range(total)]
        grad = jnp.concatenate(move_lanes(tiles, moves, model // 128), axis=1)
        cond = cond_ref[...].astype(F32)
        gate = jax.nn.sigmoid(cond)
        condg_out[...] = grad * (gate + cond * gate * (1.0 - gate))
        dw1k_out[:8, :] = small_ref[:8, :own]
        dw2k_out[...] = small_ref[8:17, :own_ff]
        rows = ((dw1k_out.at[8:9], 0, 32), (dw1b_out, 1, 32), (projb_out, 2, 32), (fc2b_out, 3, 32),
                (dw2b_out, 17, 0), (fc1b_out, 18, 0))
        for ref, row, lane in rows:
            ref[...] = small_ref[row : row + 1, lane : lane + ref.shape[1]]
        for i in range(3):
            adab_out[:, 2 * own * i : 2 * own * (i + 1)] = small_ref[i : i + 1, 64 : 64 + 2 * own]


def finish(rows, grads, wgrad, qkvg, projg, fc1, fc2, small, cond, pieces):
    tokens, model = rows.shape
    own, hidden, own_ff = wgrad.shape[0], 2 * fc1[0].shape[1], 2 * fc2[0].shape[0]
    split = lambda value: value.reshape(4, 4, 64, model)
    block = pl.BlockSpec((4, 1, 64, model), lambda t: (0, t, 0, 0))
    lines = pl.BlockSpec((GROUP, model), lambda t: (t, 0))
    rest = [wgrad, qkvg, projg, *fc1, *fc2, small, cond, pieces]
    outs = [
        like((tokens, model), BF16), like((tokens, model), BF16), like(wgrad.shape, F32),
        like(qkvg.shape, F32), like(projg.shape, F32), like((own, hidden), F32),
        like((own_ff, model), F32), like((1, model), F32), like((1, 6 * own), F32),
        like((9, own), F32), like((1, own), F32), like((1, own), F32), like((1, own), F32),
        like((9, own_ff), F32), like((1, own_ff), F32), like((1, own_ff), F32),
    ]
    return pl.pallas_call(
        functools.partial(finish_kernel, own, own_ff),
        grid=(4,),
        in_specs=[block, block] + [once(a.shape) for a in rest],
        out_specs=[lines, lines] + [once(o.shape) for o in outs[2:]],
        out_shape=outs,
        compiler_params=pltpu.CompilerParams(vmem_limit_bytes=60 * MIB),
        name="finish",
    )(split(rows), split(grads), *rest)


def on_device(wide, narrow, latents, condition, valid_mask, ada_weight, ada_bias, dw1_kernel, dw1_bias,
              qkv_weight, proj_weight, proj_bias, fc1_weight, fc1_bias, dw2_kernel, dw2_bias,
              fc2_weight, fc2_bias, out_cotangent):
    total = wide * narrow
    w, n = lax.axis_index("wide"), lax.axis_index("narrow")
    me = w * narrow + n
    model, hidden = latents.shape[2], fc1_weight.shape[1]
    own, own_ff = model // total, hidden // total

    bias_at = lax.dynamic_update_slice(
        jnp.zeros((1, 6 * model), F32), ada_bias.astype(F32)[None, :], (0, me * ada_bias.shape[0])
    )
    parts = [(0, dw1_kernel), (9, dw1_bias[None]), (10, proj_bias[None]), (11, fc2_bias[None]),
             (16, dw2_kernel), (25, dw2_bias[None]), (26, fc1_bias[None])]
    small = sum(
        jnp.pad(v, ((row, 32 - row - v.shape[0]), (0, 128 - v.shape[1]))) for row, v in parts
    )
    half = own_ff // 2
    if half % 16:
        fc2a, fc2_rows, spans = fc2_weight[:half], fc2_weight[half:], (None, None)
    else:
        fc2a = fc2_rows = fc2_weight
        spans = ((0, half), (half, half))
    chunks = [(0, 0, 128)] + thirds(2, 3 * model) + [(3, 0, model)]
    stages = wide.bit_length()
    plan = [steady(c, stages) for c in range(5)]
    needed = plan[4][-1]
    chunks += thirds(1, hidden // 2) + thirds(4, model)
    plan += [[6 + c] + steady(needed + 1 + c, stages - 1) for c in range(6)]
    (mod, sils, model_small, hidden_small, lat, gout, g2, normed, mixed, keep, fc2b, fc1b, fc1_one, qkv,
     proj, fc2_one) = front(
        wide, narrow, latents[0], out_cotangent[0], valid_mask, condition, ada_weight, bias_at, small,
        fc1_weight, [qkv_weight, proj_weight, fc2a], (None, None, spans[0]), chunks, plan,
    )
    qkv, proj = qkv.reshape(model, 3 * model), proj.reshape(model, model)
    triple, probs, att, branch, n2, n2t, fc1_one, fc2_one = attend(
        wide, narrow, mixed, lat, keep, mod, model_small, qkv, proj, fc1_one, fc2_one,
        thirds(0, hidden // 2) + thirds(1, model), plan[5:], needed, 5,
    )
    chunks = thirds(0, hidden // 2) + thirds(1, model)
    as_fc1 = lambda rows: rows.reshape(model, hidden // 2)
    as_fc2 = lambda rows: rows.reshape(hidden // 2, model)
    as_lines = lambda grad: grad.reshape(*bit_sizes(wide), grad.shape[0] // wide, grad.shape[1])
    two, gn2, fc1g, fc2g, sums_a, fc1_two, fc2_two = feed_forward(
        wide, narrow, n2, n2t, g2, as_fc1(fc1_one), hidden_small, 0, as_fc2(fc2_one),
        [fc1b, fc2_rows], (None, spans[1]), chunks,
    )
    two, gn2, fc1h, fc2h, sums_b, fc1o, fc2o = feed_forward(
        wide, narrow, n2, n2t, g2, as_fc1(fc1_two), hidden_small, 1, as_fc2(fc2_two),
        [as_lines(fc1g), as_lines(fc2g)], (None, None), chunks, (two, gn2),
    )
    rows, grads, ada_wgrad, pieces, small, qkvg, projg, fc1p, fc2p = back(
        wide, narrow, gn2, two, branch, gout, att, mixed, triple, probs,
        mod, model_small, proj, qkv, lat, normed, fc2b, (sums_a, sums_b), sils, ada_weight,
        as_lines(fc1h), as_lines(fc2h),
    )
    (out, xg, ada_wgrad, qkvg, projg, fc1g, fc2g, cond_grad, ada_bgrad, dw1k, dw1b, projb, fc2bg, dw2k,
     dw2b, fc1bg) = finish(
        rows, grads, ada_wgrad, qkvg, projg, (fc1o, fc1p), (fc2o, fc2p), small, condition, pieces
    )
    return (
        out[None], xg[None], cond_grad, ada_wgrad, ada_bgrad[0], dw1k, dw1b[0], qkvg, projg, projb[0],
        fc1g, fc1bg[0], dw2k, dw2b[0], fc2g, fc2bg[0],
    )


def solution(mesh):
    wide, narrow = mesh.shape["wide"], mesh.shape["narrow"]
    rows = lambda rank: P(AXES, *(None,) * (rank - 1))
    lanes = P(None, AXES)
    in_specs = (
        rows(3), rows(2), rows(2), rows(2), rows(1), lanes, rows(1), rows(2), rows(2), rows(1),
        rows(2), rows(1), lanes, rows(1), rows(2), rows(1), rows(3),
    )
    out_specs = (
        rows(3), rows(3), rows(2), rows(2), rows(1), lanes, rows(1), rows(2), rows(2), rows(1),
        rows(2), rows(1), lanes, rows(1), rows(2), rows(1),
    )
    return jax.shard_map(
        functools.partial(on_device, wide, narrow), mesh=mesh, in_specs=in_specs,
        out_specs=out_specs, check_vma=False,
    )
```

```python
import functools

import jax
import jax.numpy as jnp
from jax import lax
from jax.experimental import pallas as pl
from jax.experimental.pallas import tpu as pltpu
from jax.sharding import PartitionSpec as P

HEAD = 64
GRID = 32
HALF = 16
GROUP = 256
TOKENS = 1024
C0 = 0.7978845608028654
C1 = 0.044715
EPS = 1e-06
MIB = 1 << 20
AXES = ("wide", "narrow")
F32, BF16 = jnp.float32, jnp.bfloat16


def dot_nn(a, b):
    return lax.dot_general(a, b, (((1,), (0,)), ((), ())), preferred_element_type=F32)


def dot_nt(a, b):
    return lax.dot_general(a, b, (((1,), (1,)), ((), ())), preferred_element_type=F32)


def dot_tn(a, b):
    return lax.dot_general(a, b, (((0,), (0,)), ((), ())), preferred_element_type=F32)


def whole(shape):
    return pl.BlockSpec(shape, lambda *_: (0,) * len(shape))


def once(shape):
    return pl.BlockSpec(shape, lambda *_: (0,) * len(shape), pipeline_mode=pl.Buffered(1))


def like(shape, dtype):
    return jax.ShapeDtypeStruct(shape, dtype)


def shift_pair(pair, parity, first, last):
    low, high = pair
    zero = jnp.zeros_like(low)
    if parity == 0:
        low, high = pltpu.roll(low, 1, 0), pltpu.roll(high, 1, 0)
        return jnp.where(first, zero, low), jnp.where(first, low, high)
    low, high = pltpu.roll(low, 7, 0), pltpu.roll(high, 7, 0)
    return jnp.where(last, high, low), jnp.where(last, zero, high)


def row_sources(gi, r):
    if gi == 0:
        return ((1, r - 1), (0, r), (1, r))
    return ((0, r), (1, r), (0, r + 1))


def load_pair(ref, slab, gi, gj, r):
    tile = 2 + 2 * r
    group = 2 * gi + gj
    return ref[slab, group, tile], ref[slab, group, tile + 1]


def store_pair(ref, slab, gi, gj, r, pair):
    tile = 2 + 2 * r
    group = 2 * gi + gj
    ref[slab, group, tile] = pair[0]
    ref[slab, group, tile + 1] = pair[1]


def edge_masks():
    sub = lax.broadcasted_iota(jnp.int32, (8, 128), 0)
    return sub == 0, sub == 7


def clear_edges(ref):
    slabs = ref.shape[0]
    ref[:, :, 0:2] = jnp.zeros((slabs, 4, 2, 8, 128), F32)
    ref[:, :, 34:36] = jnp.zeros((slabs, 4, 2, 8, 128), F32)


def conv_cell(src, slab, gi, gj, r, k, bias, masks):
    sources = row_sources(gi, r)
    other = 1 - gj
    near = 2 if gj == 0 else 0
    far = 2 - near
    same = [load_pair(src, slab, p, gj, rr) for p, rr in sources]
    cross = [load_pair(src, slab, p, other, rr) for p, rr in sources]
    straight, moved = [], []
    for h in (0, 1):
        acc, off = bias, None
        for a in range(3):
            acc = acc + k[3 * a + 1] * same[a][h] + k[3 * a + near] * cross[a][h]
            term = k[3 * a + far] * cross[a][h]
            off = term if off is None else off + term
        straight.append(acc)
        moved.append(off)
    moved = shift_pair(moved, gj, *masks)
    return straight[0] + moved[0], straight[1] + moved[1]


def conv_back_row(slab, k, src, grad, grad_moved, put, r, carry):
    kg, total = list(carry[:9]), carry[9]
    for gi in (0, 1):
        sources = row_sources(gi, r)
        for gj in (0, 1):
            other = 1 - gj
            near = 2 if gj == 0 else 0
            here = load_pair(src, slab, gi, gj, r)
            out = [None, None]
            for a in range(3):
                p, rr = sources[2 - a]
                trio = {
                    1: load_pair(grad, slab, p, gj, rr),
                    2 - near: load_pair(grad, slab, p, other, rr),
                    near: load_pair(grad_moved, slab, p, other, rr),
                }
                for b in range(3):
                    n = 3 * a + b
                    for h in (0, 1):
                        term = k[n] * trio[b][h]
                        out[h] = term if out[h] is None else out[h] + term
                        kg[n] = kg[n] + here[h] * trio[b][h]
            total = total + out[0] + out[1]
            put(gi, gj, r, out)
    return tuple(kg) + (total,)


def conv_back(slab, k, src, grad, grad_moved, put):
    body = lambda r, carry: conv_back_row(slab, k, src, grad, grad_moved, put, r, carry)
    return lax.fori_loop(0, HALF, body, (jnp.zeros((8, 128), F32),) * 10)


def group_rows(gi, gj, r):
    return pl.ds(pl.multiple_of((2 * gi + gj) * GROUP + r * HALF, HALF), HALF)


def row_sum(values):
    rows, columns = values.shape
    return jnp.sum(values.reshape(rows // 8, 8, columns), axis=0)


def unit_rows(values):
    model = values.shape[-1]
    centered = values - jnp.sum(values, axis=-1, keepdims=True) * (1.0 / model)
    spread = jnp.sum(centered * centered, axis=-1, keepdims=True) * (1.0 / model)
    scale = lax.rsqrt(spread + EPS)
    return centered * scale, scale


def unit_back(grad, unit, scale):
    model = grad.shape[-1]
    mean = jnp.sum(grad, axis=-1, keepdims=True) * (1.0 / model)
    tilt = jnp.sum(grad * unit, axis=-1, keepdims=True) * (1.0 / model)
    return scale * (grad - mean - unit * tilt)


def order_matrix():
    d = lax.broadcasted_iota(jnp.int32, (GROUP, GROUP), 0)
    column = lax.broadcasted_iota(jnp.int32, (GROUP, GROUP), 1)
    group, position = d >> 6, (d >> 4) & 3
    source = (2 * position + (group >> 1)) * GRID + 2 * (d & 15) + (group & 1)
    return jnp.where(source == column, 1.0, 0.0).astype(BF16)


def part_of(ref, span):
    return ref if span is None else ref.at[pl.ds(*span)]


def span_shape(array, span):
    return array.shape if span is None else (span[1], *array.shape[1:])


def ff_kernel(wide, narrow, chunks, spans, steps, sums_over, *refs):
    count = len(spans)
    n2_ref, n2t_ref, g2_ref, fc1_ref, small_ref, fc2_ref = refs[:6]
    so_far, refs = refs[6 : 6 + 2 * sums_over], refs[6 + 2 * sums_over :]
    srcs = [part_of(ref, span) for ref, span in zip(refs, spans)]
    branch_out, gn2_out, w1g_ref, w2g_ref, sums_ref = refs[count : 5 + count]
    dsts, refs = refs[5 + count : 5 + 2 * count], refs[5 + 2 * count :]
    hid, ga, gc, gcs, act, ghl, branch_ref, gn2_ref, held = refs[:9]
    totals = (branch_ref, gn2_ref)
    step = pl.program_id(0)
    slabs = hid.shape[0]
    p = Place(wide, narrow)
    if sums_over:
        buffers, (sends, recvs) = refs[9:-2], refs[-2:]
        waves = scatter_jobs(p, srcs, dsts, buffers, sends, recvs, chunks)
        own_copies = []
    else:
        sends, recvs, local = refs[9:]
        waves = gather_jobs(p, srcs, dsts, sends, recvs, chunks)
        own_copies = [
            pltpu.make_async_copy(
                srcs[i], dsts[i].at[(*digits_of(p.w, wide), p.n)], local.at[i]
            )
            for i in range(count)
        ]

    def hook(position):
        for when in range(steps):
            pl.when(step == when)(lambda: waves.at_hook(3 * when + position, 3 * steps))

    @pl.when(step == 0)
    def _():
        greet(p.partners())
        for copy in own_copies:
            copy.start()
        for i, ref in enumerate(totals):
            if sums_over:
                pltpu.make_async_copy(so_far[i], ref, held.at[i]).start()
            else:
                ref[...] = jnp.zeros_like(ref)
        for ref in (hid, gc, gcs):
            clear_edges(ref)

    for g in range(4):
        rows = pl.ds(g * GROUP, GROUP)
        full = dot_nn(n2_ref[rows, :], fc1_ref[...]) + small_ref[10:11, :]
        back = dot_nt(g2_ref[rows, :], fc2_ref[...])
        for slab in range(slabs):
            lanes = slice(slab * 128, slab * 128 + 128)
            hid[slab, g, 2:34] = full[:, lanes].reshape(32, 8, 128)
            ga[slab, g] = back[:, lanes].reshape(32, 8, 128)

    @pl.when(step == 0)
    def _():
        met(len(p.partners()))
        waves.run(0)
        waves.run(1)
        for copy in own_copies:
            copy.wait()

    hook(0)
    masks = edge_masks()
    for slab in range(slabs):
        lanes = pl.ds(slab * 128, 128)
        k = [jnp.broadcast_to(small_ref[n : n + 1, lanes], (8, 128)) for n in range(9)]
        bias = jnp.broadcast_to(small_ref[9:10, lanes], (8, 128))

        def forward(r, total):
            for gi in (0, 1):
                for gj in (0, 1):
                    pair = conv_cell(hid, slab, gi, gj, r, k, bias, masks)
                    acts, grads = [], []
                    for h in (0, 1):
                        x = pair[h]
                        x2 = x * x
                        half = 0.5 * jnp.tanh(x * (C0 + (C0 * C1) * x2)) + 0.5
                        value = x * half
                        slope = half + (value - value * half) * (2.0 * C0 + (6.0 * C0 * C1) * x2)
                        acts.append(value)
                        grads.append(ga[slab, 2 * gi + gj, 2 * r + h] * slope)
                        total = total + grads[-1]
                    act[group_rows(gi, gj, r), lanes] = jnp.concatenate(acts, 0).astype(BF16)
                    store_pair(gc, slab, gi, gj, r, grads)
                    store_pair(gcs, slab, gi, gj, r, shift_pair(grads, 1 - gj, *masks))
            return total

        total = lax.fori_loop(0, HALF, forward, jnp.zeros((8, 128), F32))

        def put(gi, gj, r, pair):
            ghl[group_rows(gi, gj, r), lanes] = jnp.concatenate(pair, 0).astype(BF16)

        sums = conv_back(slab, k, hid, gc, gcs, put)
        for n, value in enumerate([*sums[:9], total, sums[9]]):
            sums_ref[n : n + 1, lanes] = jnp.sum(value, axis=0, keepdims=True)
        sums_ref[11:16, lanes] = jnp.zeros((5, 128), F32)
        if slab == 0:
            hook(1)

    if sums_over:
        @pl.when(step == 0)
        def _():
            for i, ref in enumerate(totals):
                pltpu.make_async_copy(so_far[i], ref, held.at[i]).wait()

    branch_ref[...] += dot_nn(act[...], fc2_ref[...])
    gn2_ref[...] += dot_nt(ghl[...], fc1_ref[...])

    @pl.when(step == steps - 1)
    def _():
        for i, out in enumerate((branch_out, gn2_out)):
            pltpu.make_async_copy(totals[i], out, held.at[i]).start()

    w2g_ref[...] = dot_tn(act[...], g2_ref[...]).astype(w2g_ref.dtype)
    w1g_ref[...] = dot_nn(n2t_ref[...], ghl[...]).astype(w1g_ref.dtype)
    hook(2)

    @pl.when(step == steps - 1)
    def _():
        waves.finish()
        for i, out in enumerate((branch_out, gn2_out)):
            pltpu.make_async_copy(totals[i], out, held.at[i]).wait()


def feed_forward(wide, narrow, n2, n2t, g2, fc1, small, part, fc2, arrays, spans, chunks, so_far=(),
                 width=256):
    sums_over = bool(so_far)
    tokens, model = n2.shape
    hidden = fc1.shape[1]
    slabs, steps, count = width // 128, hidden // width, len(arrays)
    padded = pltpu.VMEM((slabs, 4, 36, 8, 128), F32)
    columns = lambda rows: pl.BlockSpec((rows, width), lambda s: (0, s))
    lines = pl.BlockSpec((width, model), lambda s: (s, 0))
    anywhere = pl.BlockSpec(memory_space=pl.ANY)
    if sums_over:
        shapes = [a.shape for a in arrays]
        moved = [owned_shape(s, narrow) for s in shapes]
        extra = scatter_scratch(wide, narrow, shapes) + job_sems(wide, narrow, chunks)
        in_moved, out_moved = [once(s) for s in shapes], [once(m.shape) for m in moved]
    else:
        moved = [gathered_shape(wide, narrow, span_shape(a, s)) for a, s in zip(arrays, spans)]
        extra = job_sems(wide, narrow, chunks) + [pltpu.SemaphoreType.DMA((count,))]
        in_moved = out_moved = [anywhere] * count
    return pl.pallas_call(
        functools.partial(ff_kernel, wide, narrow, chunks, spans, steps, sums_over),
        grid=(steps,),
        in_specs=[
            once((tokens, model)), once((model, tokens)), once((tokens, model)),
            columns(model), pl.BlockSpec((16, width), lambda s: (0, part * steps + s)), lines,
        ] + [anywhere] * len(so_far) + in_moved,
        out_specs=[
            anywhere, anywhere, columns(model), lines, columns(16)
        ] + out_moved,
        out_shape=[
            like((tokens, model), F32), like((tokens, model), F32),
            like((model, hidden), BF16), like((hidden, model), BF16), like((16, hidden), F32),
        ] + moved,
        scratch_shapes=[
            padded, pltpu.VMEM((slabs, 4, 32, 8, 128), F32), padded, padded,
            pltpu.VMEM((tokens, width), BF16), pltpu.VMEM((tokens, width), BF16),
            pltpu.VMEM((tokens, model), F32), pltpu.VMEM((tokens, model), F32),
            pltpu.SemaphoreType.DMA((2,)),
        ] + extra,
        compiler_params=pltpu.CompilerParams(
            vmem_limit_bytes=56 * MIB, collective_id=4 if sums_over else 3, has_side_effects=True
        ),
        name="feed_forward",
    )(n2, n2t, g2, fc1, small, fc2, *so_far, *arrays)


def flip(index, bit):
    return index + bit - 2 * bit * lax.rem(index // bit, 2)


def bits_of(count):
    return [1 << b for b in range(count.bit_length() - 1)]


def digits_of(index, wide):
    levels = wide.bit_length() - 1
    return [lax.rem(index // (1 << (levels - 1 - i)), 2) for i in range(levels)]


def static_digits(index, wide):
    levels = wide.bit_length() - 1
    return [(index >> (levels - 1 - i)) & 1 for i in range(levels)]


def at(w, n):
    return {"wide": w, "narrow": n}


def greet(places):
    barrier = pltpu.get_barrier_semaphore()
    for place in places:
        pl.semaphore_signal(barrier, inc=1, device_id=place, device_id_type=pl.DeviceIdType.MESH)


def met(count):
    pl.semaphore_wait(pltpu.get_barrier_semaphore(), count)


def greet_all(place):
    barrier = pltpu.get_barrier_semaphore()
    total = place.total

    def body(k, carry):
        pl.semaphore_signal(
            barrier, inc=1, device_id=place.device(lax.rem(place.sid + k, total)),
            device_id_type=pl.DeviceIdType.MESH,
        )
        return carry

    lax.fori_loop(1, total, body, 0)


def remote(src, dst, send_sem, recv_sem, place):
    return pltpu.make_async_remote_copy(
        src_ref=src, dst_ref=dst, send_sem=send_sem, recv_sem=recv_sem, device_id=place,
        device_id_type=pl.DeviceIdType.MESH,
    )


class Place:
    def __init__(self, wide, narrow):
        self.wide, self.narrow = wide, narrow
        self.w, self.n = lax.axis_index("wide"), lax.axis_index("narrow")
        self.total, self.half = wide * narrow, wide * narrow // 2
        self.me = self.w * narrow + self.n
        self.core = lax.rem(self.w, 2)
        self.slot = (self.w // 2) * narrow + self.n
        self.sid = self.core * self.half + self.slot
        self.sibling = at(flip(self.w, 1), self.n)

    def device(self, sid):
        core, slot = sid // self.half, lax.rem(sid, self.half)
        return at(2 * (slot // self.narrow) + core, lax.rem(slot, self.narrow))

    def order_of(self, sid):
        core, slot = divmod(sid, self.half)
        return (2 * (slot // self.narrow) + core) * self.narrow + slot % self.narrow

    def partners(self):
        places = [at(self.w, lax.rem(self.n + k, self.narrow)) for k in range(1, self.narrow)]
        return places + [at(flip(self.w, bit), self.n) for bit in bits_of(self.wide)]

    def all_copies(self, src_of, dst, sends, recvs):
        def copy(k):
            sid = lax.rem(self.sid + k, self.total)
            return remote(src_of(sid), dst, sends.at[k], recvs.at[k], self.device(sid))

        return Exchange(copy, self.total)

    def kin_copies(self, src_of, dst, sends, recvs):
        def copy(k):
            slot = lax.rem(self.slot + k, self.half)
            return remote(src_of(slot), dst, sends.at[k], recvs.at[k],
                          self.device(self.core * self.half + slot))

        return Exchange(copy, self.half)

    def to_all(self, *refs):
        return self.all_copies(*refs).start()

    def to_kin(self, *refs):
        return self.kin_copies(*refs).start()

    def to_all_wait(self, *refs):
        self.all_copies(*refs).wait()

    def to_kin_wait(self, *refs):
        self.kin_copies(*refs).wait()


class Exchange:
    def __init__(self, copy, count):
        self.copy, self.count = copy, count

    def start(self):
        def body(k, carry):
            self.copy(k).start()
            return carry

        lax.fori_loop(1, self.count, body, 0)
        return self.wait

    def wait(self):
        def body(k, carry):
            self.copy(k).wait()
            return carry

        lax.fori_loop(1, self.count, body, 0)


def bit_sizes(wide):
    return (2,) * (wide.bit_length() - 1)


class Transfer:
    def __init__(self, place, sends, recvs, chunk, columns, turn):
        self.p, self.sends, self.recvs, self.chunk = place, sends, recvs, chunk
        start, size = columns
        self.all = pl.ds(start, size)
        levels = len(bit_sizes(place.wide))
        far = list(range(levels - 1))
        half = size // 256 * 128
        if turn % 2:
            far = far[::-1]
        self.parts = [(pl.ds(start, size - half), far)]
        if half:
            self.parts.append((pl.ds(start + size - half, half), far[::-1]))
        self.stages = levels + 1
        self.bits = digits_of(place.w, place.wide)
        self.count = 0

    def copy(self, src, dst, place):
        slot = self.count
        self.count += 1
        return remote(src, dst, self.sends.at[self.chunk, slot], self.recvs.at[self.chunk, slot], place)

    def along(self, level):
        return at(flip(self.p.w, 1 << (len(self.bits) - 1 - level)), self.p.n)

    def in_line(self, k):
        return at(self.p.w, lax.rem(self.p.n + k, self.p.narrow))

    def copies(self, stage):
        self.count = 0
        for before in range(stage):
            self.count += len(self.make(before, True))
        return self.make(stage, False)

    def start(self, stage):
        for copy in self.copies(stage):
            copy.start()

    def finish(self, stages):
        pass


class Gather(Transfer):
    def __init__(self, place, src, dst, sends, recvs, chunk, columns, turn):
        super().__init__(place, sends, recvs, chunk, columns, turn)
        self.src, self.dst = src, dst

    def make(self, stage, count_only):
        levels = len(self.bits)
        if stage == 0:
            ks = range(1, self.p.narrow)
            if count_only:
                return list(ks)
            return [
                self.copy(self.src.at[:, self.all],
                          self.dst.at[(*self.bits, self.p.n, slice(None), self.all)], self.in_line(k))
                for k in ks
            ]
        if stage == levels:
            parts = [(self.all, list(range(levels)))]
        else:
            parts = self.parts
        if count_only:
            return list(parts)
        found = []
        for columns, order in parts:
            index = list(self.bits)
            for level in order[: stage - 1]:
                index[level] = slice(None)
            part = self.dst.at[(*index, slice(None), slice(None), columns)]
            found.append(self.copy(part, part, self.along(order[stage - 1])))
        return found

    def wait(self, stage):
        for copy in self.copies(stage):
            copy.wait_recv()

    def finish(self, stages):
        for stage in stages:
            for copy in self.copies(stage):
                copy.wait_send()


def steady(first, stages, lag=2):
    return [first + lag * s for s in range(stages + 1)]


class Waves:
    def __init__(self, jobs, plan, resume=-1):
        self.jobs, self.resume = jobs, resume
        self.stages = jobs[0].stages
        self.plan = plan or [steady(c, self.stages) for c in range(len(jobs))]
        self.wave = resume + 1
        self.last = max(waves[-1] for waves in self.plan)

    def run(self, wave):
        for job, waves in zip(self.jobs, self.plan):
            for stage, when in enumerate(waves):
                if when != wave:
                    continue
                if stage and waves[stage - 1] > self.resume:
                    job.wait(stage - 1)
                if stage < self.stages:
                    job.start(stage)

    def tick(self, times=1):
        for _ in range(times):
            if self.wave <= self.last:
                self.run(self.wave)
                self.wave += 1

    def through(self, wave):
        while self.wave <= min(wave, self.last):
            self.tick()

    def at_hook(self, hook, hooks):
        first = self.resume + 3
        left = self.last + 1 - first
        for wave in range(first + hook * left // hooks, first + (hook + 1) * left // hooks):
            self.run(wave)

    def finish(self, last=None):
        last = self.last if last is None else last
        for job, waves in zip(self.jobs, self.plan):
            here = [s for s in range(self.stages) if self.resume < waves[s] <= last]
            for stage in here:
                if waves[stage + 1] > last:
                    job.wait(stage)
            job.finish(here)

    def end(self, last=None):
        last = self.last if last is None else last
        self.through(last)
        self.finish(last)


def job_sems(wide, narrow, chunks):
    per = narrow - 1 + 2 * (wide.bit_length() - 1)
    return [pltpu.SemaphoreType.DMA((len(chunks), per))] * 2


def gather_jobs(place, srcs, dsts, sends, recvs, chunks, plan=None, resume=-1, shift=0):
    jobs = [
        Gather(place, srcs[i], dsts[i], sends, recvs, c, columns, c + shift)
        for c, (i, *columns) in enumerate(chunks)
    ]
    return Waves(jobs, plan, resume)


def gathered_shape(wide, narrow, shape):
    return like((*bit_sizes(wide), narrow, *shape), BF16)


def thirds(i, size):
    return [(i, t * (size // 3), size // 3) for t in range(3)]


class Scatter(Transfer):
    def __init__(self, place, src, buffers, out, sends, recvs, chunk, columns):
        super().__init__(place, sends, recvs, chunk, columns, chunk)
        self.src, self.out = src, out
        self.halves, self.line, self.got = buffers[:-2], buffers[-2], buffers[-1]
        self.rows = self.line.shape[1]
        core = len(self.bits) - 1
        self.parts = [(columns, [core] + order) for columns, order in self.parts]

    def make(self, stage, count_only):
        levels = len(self.bits)
        if stage == levels:
            ks = range(1, self.p.narrow)
            if count_only:
                return list(ks)
            return [
                self.copy(self.line.at[lax.rem(self.p.n + k, self.p.narrow), :, self.all],
                          self.got.at[k - 1, :, self.all], self.in_line(k))
                for k in ks
            ]
        parts = self.parts if stage else [(self.all, self.parts[0][1])]
        if count_only:
            return list(parts)
        found = []
        for columns, order in parts:
            source, index, kept = self.level(order, stage, True)
            into = self.halves[stage].at[(*kept, slice(None), columns)]
            found.append(self.copy(source.at[(*index, slice(None), columns)], into, self.along(order[stage])))
        return found

    def level(self, order, stage, theirs):
        source = self.src if stage == 0 else self.halves[stage - 1]
        left = [level for level in range(len(self.bits)) if level not in order[:stage]]
        bit = self.bits[order[stage]]
        bit = 1 - bit if theirs else bit
        index = [bit if level == order[stage] else slice(None) for level in left]
        return source, index, [slice(None)] * (len(left) - 1)

    def wait(self, stage):
        for copy in self.copies(stage):
            copy.wait()
        levels = len(self.bits)
        if stage == levels:
            value = self.line[self.p.n, :, self.all].astype(F32)
            for k in range(1, self.p.narrow):
                value = value + self.got[k - 1, :, self.all].astype(F32)
            self.out[:, self.all] = value
            return
        for columns, order in self.parts:
            source, index, kept = self.level(order, stage, False)
            into = self.halves[stage]
            for j in range(1 << len(kept)):
                digits = [(j >> i) & 1 for i in range(len(kept))]
                mine = [v if not isinstance(v, slice) else None for v in index]
                rest = iter(digits)
                mine = [next(rest) if v is None else v for v in mine]
                self.add(source, tuple(mine), into, tuple(digits), columns, stage == levels - 1)

    def add(self, source, mine, into, arrived, columns, last):
        if last:
            total = source[(*mine, slice(None), columns)].astype(F32) + into[
                (*arrived, slice(None), columns)
            ].astype(F32)
            for m in range(self.p.narrow):
                rows = slice(m * self.rows, (m + 1) * self.rows)
                self.line[m, :, columns] = total[rows].astype(BF16)
            return

        into[(*arrived, slice(None), columns)] = (
            source[(*mine, slice(None), columns)] + into[(*arrived, slice(None), columns)]
        )


def scatter_scratch(wide, narrow, shapes):
    scratch = []
    for *_, height, columns in shapes:
        for stage in range(wide.bit_length() - 1):
            scratch.append(pltpu.VMEM((*bit_sizes(wide)[stage + 1 :], height, columns), BF16))
        scratch.append(pltpu.VMEM((narrow, height // narrow, columns), BF16))
        scratch.append(pltpu.VMEM((narrow - 1, height // narrow, columns), BF16))
    return scratch


def scatter_jobs(place, srcs, outs, buffers, sends, recvs, chunks, plan=None):
    per = len(buffers) // len(srcs)
    jobs = [
        Scatter(place, srcs[i], buffers[i * per : (i + 1) * per], outs[i], sends, recvs, c, columns)
        for c, (i, *columns) in enumerate(chunks)
    ]
    return Waves(jobs, plan)


def owned_shape(shape, narrow):
    return like((shape[-2] // narrow, shape[-1]), F32)


def move_lanes(tiles, moves, count):
    rows = tiles[0].shape[0]
    lane = lax.broadcasted_iota(jnp.int32, (rows, 128), 1)
    out = [jnp.zeros((rows, 128), F32) for _ in range(count)]
    for start, to, length in moves:
        while length:
            size = min(length, 128 - start % 128, 128 - to % 128)
            tile = tiles[start // 128]
            turn = (to - start) % 128
            if turn:
                tile = pltpu.roll(tile, turn, 1)
            inside = (lane >= to % 128) & (lane < to % 128 + size)
            out[to // 128] = jnp.where(inside, tile, out[to // 128])
            start, to, length = start + size, to + size, length - size
    return out


def tiles_of(values):
    return [values[:, i : i + 128] for i in range(0, values.shape[1], 128)]


def front_kernel(wide, narrow, chunks, plan, spans, own, own_ff, *refs):
    count = len(spans)
    (x_ref, cot_ref, mask_ref, cond_ref, ada_ref, bias_ref, small_ref, fc1_ref) = refs[:8]
    srcs, refs = refs[8 : 8 + count], refs[8 + count :]
    srcs = [part_of(ref, span) for ref, span in zip(srcs, spans)]
    (mod_ref, sils_ref, model_ref, hidden_ref, lat_ref, gout_ref, g2_ref, normed_ref, mixed_ref,
     keep_ref, fc2b_ref, fc1b_ref) = refs[:12]
    dsts, refs = refs[12 : 13 + count], refs[13 + count :]
    (order_ref, fc1a_ref, sil_out, got, part, sib, rows_in, smalls, send_a, recv_a, send_b, recv_b, send_c, recv_c,
     sends, recvs, local) = refs
    p = Place(wide, narrow)
    mine = digits_of(p.w, wide)
    model = x_ref.shape[1]
    slabs = model // 128
    own_copies = [
        pltpu.make_async_copy(srcs[i], dsts[1 + i].at[(*mine, p.n)], local.at[i]) for i in range(count)
    ]
    for copy in own_copies:
        copy.start()
    greet_all(p)
    order_ref[...] = order_matrix()
    waves = gather_jobs(p, [small_ref, fc1a_ref, *srcs], [smalls, *dsts], sends, recvs, chunks, plan)
    last = waves.plan[chunks.index((3, 0, model))][-1]
    cond = cond_ref[...].astype(F32)
    sil = (cond * jax.nn.sigmoid(cond)).astype(BF16).astype(F32)
    tiles = tiles_of(sil)
    for sid in range(p.total):
        d = p.order_of(sid)
        sil_out[sid] = move_lanes(tiles, [(own * d, 0, own)], 1)[0]
    got[p.sid] = sil_out[p.sid]
    smalls[(*mine, p.n)] = small_ref[...]

    def arrange(t):
        rows = pl.ds(t * GROUP, GROUP)
        tokens = dot_nn(order_ref[...], x_ref[rows, :])
        unit, _ = unit_rows(tokens)
        mask = mask_ref[:, t * GROUP : (t + 1) * GROUP].astype(F32)
        mask = (order_ref[...].astype(F32) * mask).astype(BF16)
        kept = dot_nn(mask, jnp.ones((GROUP, 128), BF16))
        gout = dot_nn(order_ref[...], cot_ref[rows, :]) * jnp.concatenate([kept] * slabs, axis=1)
        for g in range(4):
            src = slice(64 * g, 64 * g + 64)
            dst = pl.ds(g * GROUP + 64 * t, 64)
            lat_ref[dst, :] = tokens[src].astype(BF16)
            gout_ref[dst, :] = gout[src].astype(BF16)
            keep_ref[dst, :] = (kept[src] - 1.0) * 1e30
            for s in range(slabs):
                tile = unit[src, s * 128 : s * 128 + 128].reshape(8, 8, 128)
                normed_ref[s, g, 2 + 8 * t : 10 + 8 * t] = tile

    met(p.total - 1)
    wait_sil = p.to_all(lambda sid: sil_out.at[sid], got.at[p.sid], send_a, recv_a)
    waves.tick(2)
    arrange(0)
    for copy in own_copies:
        copy.wait()
    waves.tick()
    arrange(1)
    wait_sil()
    sil = got[...].reshape(p.total, 128)
    sils_ref[...] = sil
    product = dot_nn(sil[:, :own].astype(BF16), ada_ref[...]) + bias_ref[...]
    for d in range(p.total):
        part[d // p.half, d % p.half] = product[d : d + 1, :]
    to_sibling = remote(part.at[1 - p.core], sib, send_b, recv_b, p.sibling)
    to_sibling.start()
    waves.tick()
    arrange(2)
    to_sibling.wait()
    part[p.core] = part[p.core] + sib[...]
    rows_in[p.slot] = part[p.core, p.slot]
    wait_rows = p.to_kin(lambda slot: part.at[p.core, slot], rows_in.at[p.slot], send_c, recv_c)
    waves.tick()
    arrange(3)
    clear_edges(normed_ref)
    waves.tick()
    columns = tiles_of(fc1_ref[...].astype(F32))
    for h, ref in enumerate((fc1a_ref, fc1b_ref)):
        moves = [
            (own_ff * d + own_ff // 2 * h, own_ff // 2 * d, own_ff // 2) for d in range(p.total)
        ]
        ref[...] = jnp.concatenate(move_lanes(columns, moves, len(columns) // 2), axis=1).astype(BF16)
    own_fc1 = pltpu.make_async_copy(fc1a_ref, dsts[0].at[(*mine, p.n)], local.at[count])
    own_fc1.start()
    waves.through(waves.plan[0][-1])
    pieces = [smalls[(*static_digits(d // narrow, wide), d % narrow)].astype(F32) for d in range(p.total)]
    moves = [(128 * d, own * d, own) for d in range(p.total)]
    model_ref[...] = jnp.concatenate(move_lanes([q[:16] for q in pieces], moves, slabs), axis=1)
    half, hidden = own_ff // 2, fc1_ref.shape[1]
    moves = [
        (128 * d + half * h, hidden // 2 * h + half * d, half) for d in range(p.total) for h in (0, 1)
    ]
    hidden_ref[...] = jnp.concatenate(
        move_lanes([q[16:] for q in pieces], moves, hidden // 128), axis=1
    )
    own_fc1.wait()
    wait_rows()
    mod = jnp.sum(rows_in[...], axis=0)
    for i in range(6):
        mod_ref[i : i + 1, :] = mod[:, i * model : (i + 1) * model]

    shift, scale, gate = mod_ref[0:1, :], mod_ref[1:2, :], mod_ref[5:6, :]
    total = jnp.zeros((8, model), F32)
    for g in range(4):
        rows = pl.ds(g * GROUP, GROUP)
        two = gout_ref[rows, :].astype(F32) * gate
        total = total + row_sum(two)
        g2_ref[rows, :] = two.astype(BF16)
    fc2b_ref[...] = total
    masks = edge_masks()
    for s in range(slabs):
        lanes = pl.ds(s * 128, 128)
        at_s = slice(s * 128, s * 128 + 128)
        shift8 = jnp.broadcast_to(shift[:, at_s], (8, 128))
        scale8 = jnp.broadcast_to(1.0 + scale[:, at_s], (8, 128))
        normed_ref[s, :, 2:34] = normed_ref[s, :, 2:34] * scale8 + shift8
        k = [jnp.broadcast_to(model_ref[n : n + 1, at_s], (8, 128)) for n in range(9)]
        bias = jnp.broadcast_to(model_ref[9:10, at_s], (8, 128))

        def body(r, carry):
            for gi in (0, 1):
                for gj in (0, 1):
                    pair = conv_cell(normed_ref, s, gi, gj, r, k, bias, masks)
                    mixed_ref[group_rows(gi, gj, r), lanes] = jnp.concatenate(pair, 0).astype(BF16)
            return carry

        lax.fori_loop(0, HALF, body, 0)
        waves.through(min(waves.wave, last))
    waves.end(last)


def front(wide, narrow, x, cot, mask, cond, ada, bias, small, fc1, blocks, spans, chunks, plan):
    total = wide * narrow
    tokens, model = x.shape
    slabs, count, columns = model // 128, len(blocks), ada.shape[1]
    hidden = fc1.shape[1]
    own, own_ff = model // total, hidden // total
    inside = pl.BlockSpec(memory_space=pltpu.VMEM)
    anywhere = pl.BlockSpec(memory_space=pl.ANY)
    all_sems = pltpu.SemaphoreType.DMA((total,))
    one_sem = pltpu.SemaphoreType.DMA
    kin_sems = pltpu.SemaphoreType.DMA((total // 2,))
    return pl.pallas_call(
        functools.partial(front_kernel, wide, narrow, chunks, plan, spans, own, own_ff),
        in_specs=[inside] * 8 + [anywhere] * count,
        out_specs=[inside] * 12 + [anywhere] * (count + 1),
        out_shape=[
            like((8, model), F32), like((total, 128), F32), like((16, model), F32),
            like((16, hidden), F32), like((tokens, model), BF16), like((tokens, model), BF16),
            like((tokens, model), BF16), like((slabs, 4, 36, 8, 128), F32),
            like((tokens, model), BF16), like((tokens, 128), F32), like((8, model), F32),
            like((own, hidden // 2), BF16),
            gathered_shape(wide, narrow, (own, hidden // 2)),
        ] + [gathered_shape(wide, narrow, span_shape(b, s)) for b, s in zip(blocks, spans)],
        scratch_shapes=[
            pltpu.VMEM((GROUP, GROUP), BF16), pltpu.VMEM((own, hidden // 2), BF16), pltpu.VMEM((total, 1, 128), F32),
            pltpu.VMEM((total, 1, 128), F32), pltpu.VMEM((2, total // 2, 1, columns), F32),
            pltpu.VMEM((total // 2, 1, columns), F32), pltpu.VMEM((total // 2, 1, columns), F32),
            pltpu.VMEM((*bit_sizes(wide), narrow, 32, 128), BF16),
            all_sems, all_sems, one_sem, one_sem, kin_sems, kin_sems,
            *job_sems(wide, narrow, chunks), pltpu.SemaphoreType.DMA((count + 1,)),
        ],
        compiler_params=pltpu.CompilerParams(
            vmem_limit_bytes=56 * MIB, collective_id=0, has_side_effects=True
        ),
        name="front",
    )(x, cot, mask, cond, ada, bias, small, fc1, *blocks)


def attend_kernel(wide, narrow, chunks, plan, resume, shift, *refs):
    mixed_ref, lat_ref, keep_ref, mod_ref, small_ref, qkv_ref, proj_ref, fc1_in, fc2_in = refs[:9]
    triple_ref, probs_ref, att_ref, branch_ref, n2_ref, n2t_ref, fc1_ref, fc2_ref = refs[9:17]
    sends, recvs = refs[17:]
    step = pl.program_id(0)
    p = Place(wide, narrow)
    waves = gather_jobs(p, [fc1_in, fc2_in], [fc1_ref, fc2_ref], sends, recvs, chunks, plan, resume,
                        shift)

    def on(when, work):
        pl.when(step == when)(work)

    def hook(position):
        for when in range(4):
            on(when, lambda: waves.at_hook(2 * when + position, 8))

    def first():
        met(len(p.partners()))
        waves.run(resume + 1)
        waves.run(resume + 2)

    on(0, lambda: greet(p.partners()))
    model = lat_ref.shape[1]
    slabs = model // 128
    triple_ref[...] = dot_nn(mixed_ref[...], qkv_ref[...]).astype(BF16)
    on(0, first)
    lane = lax.broadcasted_iota(jnp.int32, (GROUP, 128), 1)
    left = lane < HEAD
    keep = jnp.concatenate([keep_ref[...]] * 2, axis=1)
    for s in range(slabs):
        q = triple_ref[:, s * 128 : s * 128 + 128]
        k = triple_ref[:, model + s * 128 : model + s * 128 + 128] * jnp.asarray(0.125, BF16)
        v = triple_ref[:, 2 * model + s * 128 : 2 * model + s * 128 + 128]
        outs = []
        for h in (0, 1):
            mine = left if h == 0 else jnp.logical_not(left)
            scores = dot_nt(jnp.where(mine, k, jnp.zeros_like(k)), q) + keep
            e = jnp.exp(scores - jnp.max(scores, axis=0, keepdims=True))
            prob = (e * (1.0 / jnp.sum(e, axis=0, keepdims=True))).astype(BF16)
            probs_ref[2 * s + h, 0] = prob
            outs.append(dot_tn(prob, v))
        att_ref[:, s * 128 : s * 128 + 128] = jnp.where(left, outs[0], outs[1]).astype(BF16)
        if s == slabs // 2 - 1:
            hook(0)
    branch = dot_nn(att_ref[...], proj_ref[...]) + small_ref[10:11, :]
    middle = lat_ref[...].astype(F32) + mod_ref[2:3, :] * branch
    unit, _ = unit_rows(middle)
    branch_ref[...] = branch
    n2 = unit * (1.0 + mod_ref[4:5, :]) + mod_ref[3:4, :]
    n2_ref[...] = n2.astype(BF16)
    n2t_ref[...] = n2.T.astype(BF16)
    hook(1)
    on(3, waves.finish)


def attend(wide, narrow, mixed, lat, keep, mod, small, qkv, proj, fc1, fc2, chunks, plan, resume, shift):
    tokens, model = lat.shape
    heads = model // HEAD
    by_group = lambda columns: pl.BlockSpec((GROUP, columns), lambda g: (g, 0))
    anywhere = pl.BlockSpec(memory_space=pl.ANY)
    return pl.pallas_call(
        functools.partial(attend_kernel, wide, narrow, chunks, plan, resume, shift),
        grid=(4,),
        in_specs=[
            by_group(model), by_group(model), by_group(128), whole(mod.shape),
            whole(small.shape), once(qkv.shape), once(proj.shape), anywhere, anywhere,
        ],
        out_specs=[
            by_group(3 * model), pl.BlockSpec((heads, 1, GROUP, GROUP), lambda g: (0, g, 0, 0)),
            by_group(model), by_group(model), by_group(model),
            pl.BlockSpec((model, GROUP), lambda g: (0, g)), anywhere, anywhere,
        ],
        out_shape=[
            like((tokens, 3 * model), BF16), like((heads, 4, GROUP, GROUP), BF16),
            like((tokens, model), BF16), like((tokens, model), F32),
            like((tokens, model), BF16), like((model, tokens), BF16),
            like(fc1.shape, BF16), like(fc2.shape, BF16),
        ],
        input_output_aliases={7: 6, 8: 7},
        scratch_shapes=job_sems(wide, narrow, chunks),
        compiler_params=pltpu.CompilerParams(
            vmem_limit_bytes=56 * MIB, collective_id=1, has_side_effects=True
        ),
        name="attend",
    )(mixed, lat, keep, mod, small, qkv, proj, fc1, fc2)


def back_kernel(wide, narrow, chunks, plan, own, own_ff, *refs):
    (gn2_ref, two_ref, branch_ref, gout_ref, att_hbm, mixed_hbm,
     q_ref, k_ref, v_ref, probs_ref, mod_ref, small_ref, proj_ref, wq_ref, wk_ref, wv_ref,
     lat_ref, normed_hbm, fc2b_ref, hida_ref, hidb_ref, sils_ref, ada_ref, fc1s_hbm,
     fc2s_hbm) = refs[:25]
    (rows_ref, xg_ref, wgrad_ref, cond_ref, small_out, qkvg_ref, projg_ref, fc1g_ref,
     fc2g_ref) = refs[25:34]
    (ga, gmid, gmix, gmoved, sums, proj_src, qkv_src, early, late, cuts, cuts_in, hcuts, hcuts_in, part, cond_in,
     gt, normed_ref, att_ref, mixed_ref, fc1s_ref, fc2s_ref, fetched,
     send_a, recv_a, send_b, recv_b, send_c, recv_c, send_d, recv_d, send_e, recv_e, send_f, recv_f,
     send_g, recv_g) = refs[34:70]
    buffers, (sends, recvs) = refs[70:-2], refs[-2:]
    step = pl.program_id(0)
    model = lat_ref.shape[1]
    slabs = model // 128
    last = 3 + slabs
    p = Place(wide, narrow)
    half, hidden = own_ff // 2, 2 * hida_ref.shape[1]
    waves = scatter_jobs(p, [fc1s_ref, fc2s_ref, proj_src, qkv_src],
                         [fc1g_ref, fc2g_ref, projg_ref, qkvg_ref], buffers, sends, recvs, chunks,
                         plan)
    gbl = xg_ref
    later = [(fc1s_hbm, fc1s_ref), (fc2s_hbm, fc2s_ref), (att_hbm, att_ref), (mixed_hbm, mixed_ref),
             (normed_hbm, normed_ref)]
    fetch = [pltpu.make_async_copy(src, dst, fetched.at[i]) for i, (src, dst) in enumerate(later)]
    mine = lambda ref: ref.at[p.core, p.slot]

    @pl.when(step == 0)
    def _():
        greet_all(p)
        for copy in fetch:
            copy.start()
        sums[...] = jnp.zeros_like(sums)
        gmix[...] = jnp.zeros_like(gmix)
        clear_edges(gmoved)
        tiles = tiles_of(hida_ref[...]) + tiles_of(hidb_ref[...])
        for sid in range(p.total):
            d = p.order_of(sid)
            moves = [(half * d, 0, half), (hidden // 2 + half * d, half, half)]
            hcuts[sid] = move_lanes(tiles, moves, 1)[0]
        hcuts_in[p.sid] = hcuts[p.sid]

    @pl.when(step < 4)
    def _():
        rows = pl.ds(pl.multiple_of(step * GROUP, GROUP), GROUP)
        branch = branch_ref[...]
        middle = lat_ref[rows, :].astype(F32) + mod_ref[2:3, :] * branch
        two = two_ref[...] + small_ref[11:12, :]
        gout = gout_ref[...].astype(F32)
        rows_ref[...] = (middle + mod_ref[5:6, :] * two).astype(BF16)
        sums[3] += row_sum(gout * two)
        unit, scale = unit_rows(middle)
        gn2 = gn2_ref[...]
        sums[1] += row_sum(gn2)
        sums[2] += row_sum(gn2 * unit)
        gm = gout + unit_back(gn2 * (1.0 + mod_ref[4:5, :]), unit, scale)
        gmid[rows, :] = gm
        sums[0] += row_sum(gm * branch)
        gb = gm * mod_ref[2:3, :]
        sums[4] += row_sum(gb)
        low = gb.astype(BF16)
        gbl[rows, :] = low
        ga[rows, :] = dot_nt(low, proj_ref[...]).astype(BF16)

    @pl.when(step == 0)
    def _():
        met(p.total - 1)
        fetch[0].wait()
        fetch[1].wait()
        waves.run(0)
        waves.run(1)
        p.to_all(lambda sid: hcuts.at[sid], hcuts_in.at[p.sid], send_g, recv_g)

    for when in (1, 2):
        pl.when(step == when)(lambda: waves.run(when + 1))

    @pl.when(step == 3)
    def _():
        fetch[2].wait()
        fetch[3].wait()
        proj_src[...] = dot_tn(att_ref[...], gbl[...]).astype(BF16).reshape(proj_src.shape)
        waves.run(4)
        for i in range(4):
            early[p.core, p.slot, :, i * model : (i + 1) * model] = jnp.sum(
                sums[i], axis=0, keepdims=True
            )
        p.to_kin(lambda slot: mine(early), mine(early), send_a, recv_a)

    def attention(groups):
        s = step - 4
        lane = lax.broadcasted_iota(jnp.int32, (GROUP, 128), 1)
        left = lane < HEAD
        eighth = jnp.asarray(0.125, BF16)
        lanes = pl.ds(pl.multiple_of(s * 128, 128), 128)
        weight = jnp.concatenate([wq_ref[...], wk_ref[...], wv_ref[...]], axis=1)
        for g in groups:
            rows = slice(g * GROUP, (g + 1) * GROUP)
            q, k, v = q_ref[rows, :] * eighth, k_ref[rows, :] * eighth, v_ref[rows, :]
            grad = ga[rows, lanes]
            gq = gk = gv = None
            for h in (0, 1):
                keep = left if h == 0 else jnp.logical_not(left)
                only = lambda value: jnp.where(keep, value, jnp.zeros_like(value))
                p_low = probs_ref[h, g]
                prob = p_low.astype(F32)
                gh = only(grad)
                gp = dot_nt(v, gh)
                inner = jnp.sum(prob * gp, axis=0, keepdims=True)
                gs = (prob * (gp - inner)).astype(BF16)
                terms = (dot_tn(gs, only(k)), dot_nn(gs, only(q)), dot_nn(p_low, gh))
                if h == 0:
                    gq, gk, gv = terms
                else:
                    gq, gk, gv = gq + terms[0], gk + terms[1], gv + terms[2]
            found = jnp.concatenate([gq, gk, gv], axis=1).astype(BF16)
            gt[rows, :] = found
            gmixed = dot_nt(found, weight)
            for t in range(slabs):
                gmix[t + 1, g, 2:34] += gmixed[:, t * 128 : t * 128 + 128].reshape(32, 8, 128)

    pl.when(step >= 4)(lambda: attention((0, 1)))
    for s in range(slabs):
        pl.when(step == 4 + s)(lambda: waves.run(5 + 2 * s))

    @pl.when(step >= 4)
    def _():
        attention((2, 3))
        columns = pl.ds(pl.multiple_of((step - 4) * 384, 128), 384)
        found = dot_tn(mixed_ref[...], gt[...]).astype(BF16)
        qkv_src[..., columns] = found.reshape(*qkv_src.shape[:-1], 384)

    for s in range(slabs):
        pl.when(step == 4 + s)(lambda: waves.run(6 + 2 * s))

    @pl.when(step == 6)
    def _():
        p.to_kin_wait(lambda slot: mine(early), mine(early), send_a, recv_a)
        remote(early.at[p.core], early.at[p.core], send_d, recv_d, p.sibling).start()

    @pl.when(step == last)
    def _():
        waves.wave = 5 + 2 * slabs
        fetch[4].wait()
        masks = edge_masks()
        rows_out = []
        for s in range(slabs):
            at_s = slice(s * 128, s * 128 + 128)
            k = [jnp.broadcast_to(small_ref[n : n + 1, at_s], (8, 128)) for n in range(9)]

            def move(r, total):
                for gi in (0, 1):
                    for gj in (0, 1):
                        pair = load_pair(gmix, s + 1, gi, gj, r)
                        total = total + pair[0] + pair[1]
                        store_pair(gmoved, 0, gi, gj, r, shift_pair(pair, 1 - gj, *masks))
                return total

            total = lax.fori_loop(0, HALF, move, jnp.zeros((8, 128), F32))

            def put(gi, gj, r, pair):
                store_pair(gmix, s, gi, gj, r, pair)

            found = conv_back(0, k, normed_ref.at[s : s + 1], gmix.at[s + 1 : s + 2], gmoved, put)
            late[p.core, p.slot, :, at_s] = jnp.sum(found[9], axis=0, keepdims=True)
            column = [jnp.sum(v, axis=0, keepdims=True) for v in (*found[:9], total)]
            column.append(jnp.sum(sums[4, :, at_s], axis=0, keepdims=True))
            column.append(jnp.sum(fc2b_ref[:, at_s], axis=0, keepdims=True))
            rows_out.append(jnp.concatenate(column + [jnp.zeros((4, 128), F32)], axis=0))
            if s % 2:
                waves.tick()
        scale_sum = jnp.zeros((8, model), F32)
        for g in range(4):
            rows = pl.ds(g * GROUP, GROUP)
            unit, scale = unit_rows(lat_ref[rows, :].astype(F32))
            gn = jnp.concatenate(
                [gmix[s, g, 2:34].reshape(GROUP, 128) for s in range(slabs)], axis=1
            )
            scale_sum = scale_sum + row_sum(gn * unit)
            gmid[rows, :] = gmid[rows, :] + unit_back(gn * (1.0 + mod_ref[1:2, :]), unit, scale)
        late[p.core, p.slot, :, model:] = jnp.sum(scale_sum, axis=0, keepdims=True)
        wait_late = p.to_kin(lambda slot: mine(late), mine(late), send_c, recv_c)
        waves.tick()
        p.to_all_wait(lambda sid: hcuts.at[sid], hcuts_in.at[p.sid], send_g, recv_g)
        small_out[8:, :] = jnp.sum(hcuts_in[...], axis=0)
        modulation = tiles_of(late[p.core, p.slot]) + tiles_of(early[p.core, p.slot])
        third = 2 * own
        for sid in range(p.total):
            d = p.order_of(sid)
            piece = move_lanes(rows_out, [(own * d, 0, own)], 1)[0][:8]
            piece = piece + move_lanes(rows_out, [(own * d, 32, own)], 1)[0][8:]
            bias = [
                move_lanes(modulation, [(third * (3 * d + i), 64, third)], 1)[0] for i in range(3)
            ]
            cuts[sid] = piece + jnp.concatenate(bias + [jnp.zeros((5, 128), F32)], axis=0)
        cuts_in[p.sid] = cuts[p.sid]
        wait_cuts = p.to_all(lambda sid: cuts.at[sid], cuts_in.at[p.sid], send_b, recv_b)
        xg_ref[...] = gmid[...].astype(BF16)
        wait_late()
        swap_late = remote(late.at[p.core], late.at[p.core], send_e, recv_e, p.sibling)
        swap_late.start()
        waves.tick()
        remote(early.at[p.core], early.at[p.core], send_d, recv_d, p.sibling).wait()
        swap_late.wait()
        sil = sils_ref[:, :own].astype(BF16)
        cond = None
        for ref, start in ((late, 0), (early, 2 * model)):
            size = ref.shape[-1]
            span = slice(start, start + size)
            found = ref[...].reshape(p.total, size)
            low = found.astype(BF16)
            wgrad_ref[:, span] = dot_tn(sil, low)
            term = dot_nt(low, ada_ref[:, span])
            cond = term if cond is None else cond + term
        cond = jnp.concatenate([cond, jnp.zeros((p.total, 128 - own), F32)], axis=1)
        for sid in range(p.total):
            part[sid] = cond[sid : sid + 1, :]
        cond_in[p.me] = part[p.sid]
        wait_cond = p.to_all(lambda sid: part.at[sid], cond_in.at[p.me], send_f, recv_f)
        waves.end()
        wait_cuts()
        small_out[:8, :] = jnp.sum(cuts_in[...], axis=0)
        wait_cond()
        cond_ref[...] = cond_in[...]


def back(wide, narrow, gn2, two, branch, gout, att, mixed, triple, probs, mod, small, proj, qkv,
         lat, normed, fc2b, hidden_sums, sils, ada, fc1s, fc2s):
    total = wide * narrow
    tokens, model = lat.shape
    slabs, columns = model // 128, ada.shape[1]
    hidden = 2 * hidden_sums[0].shape[1]
    own, own_ff = ada.shape[0], hidden // total
    by_group = pl.BlockSpec((GROUP, model), lambda t: (jnp.minimum(t, 3), 0))
    slab = lambda t: jnp.clip(t - 4, 0, slabs - 1)
    third = lambda rows, i: pl.BlockSpec((rows, 128), lambda t: (0, i * slabs + slab(t)))
    all_sems, kin_sems = (pltpu.SemaphoreType.DMA((n,)) for n in (total, total // 2))
    one_sem = pltpu.SemaphoreType.DMA
    padded = lambda count: pltpu.VMEM((count, 4, 36, 8, 128), F32)
    height = model // wide
    bits = bit_sizes(wide)
    shapes = [fc1s.shape, fc2s.shape, (*bits, height, model), (*bits, height, 3 * model)]
    chunks = thirds(0, hidden // 2) + thirds(1, model) + [(2, 0, model)]
    chunks += [(3, 384 * s, 384) for s in range(slabs)]
    starts = [0, 2, 5, 8, 11, 14, 4] + [6 + 2 * s for s in range(slabs)]
    plan = [steady(c, wide.bit_length()) for c in starts]
    full = lambda a: once(a.shape)
    anywhere = pl.BlockSpec(memory_space=pl.ANY)
    outs = [
        like((tokens, model), BF16), like((tokens, model), BF16), like((own, columns), F32),
        like((total, 1, 128), F32), like((24, 128), F32), like((own, 3 * model), F32),
        like((own, model), F32), like((own, hidden // 2), F32), like((own_ff // 2, model), F32),
    ]
    return pl.pallas_call(
        functools.partial(back_kernel, wide, narrow, chunks, plan, own, own_ff),
        grid=(4 + slabs,),
        in_specs=[by_group] * 4 + [anywhere, anywhere] + [third(tokens, i) for i in range(3)] + [
            pl.BlockSpec((2, 4, GROUP, GROUP), lambda t: (slab(t), 0, 0, 0)),
            full(mod), full(small), full(proj), third(model, 0), third(model, 1), third(model, 2),
            full(lat), pl.BlockSpec(memory_space=pl.ANY), full(fc2b), full(hidden_sums[0]), full(hidden_sums[1]),
            full(sils), full(ada), anywhere, anywhere,
        ],
        out_specs=[by_group] + [once(o.shape) for o in outs[1:]],
        out_shape=outs,
        scratch_shapes=[
            pltpu.VMEM((tokens, model), BF16), pltpu.VMEM((tokens, model), F32),
            padded(slabs + 1), padded(1), pltpu.VMEM((5, 8, model), F32),
            pltpu.VMEM(shapes[2], BF16), pltpu.VMEM(shapes[3], BF16),
            pltpu.VMEM((2, total // 2, 1, 4 * model), F32),
            pltpu.VMEM((2, total // 2, 1, 2 * model), F32),
            pltpu.VMEM((total, 8, 128), F32), pltpu.VMEM((total, 8, 128), F32),
            pltpu.VMEM((total, 16, 128), F32), pltpu.VMEM((total, 16, 128), F32),
            pltpu.VMEM((total, 1, 128), F32), pltpu.VMEM((total, 1, 128), F32),
            pltpu.VMEM((tokens, 384), BF16), padded(slabs),
            pltpu.VMEM((tokens, model), BF16), pltpu.VMEM((tokens, model), BF16),
            pltpu.VMEM(shapes[0], BF16), pltpu.VMEM(shapes[1], BF16), pltpu.SemaphoreType.DMA((5,)),
            kin_sems, kin_sems, all_sems, all_sems, kin_sems, kin_sems, one_sem, one_sem,
            one_sem, one_sem, all_sems, all_sems, all_sems, all_sems,
            *scatter_scratch(wide, narrow, shapes), *job_sems(wide, narrow, chunks),
        ],
        compiler_params=pltpu.CompilerParams(
            vmem_limit_bytes=63 * MIB, collective_id=2, has_side_effects=True
        ),
        name="attend_back",
    )(gn2, two, branch, gout, att, mixed, triple, triple, triple, probs, mod,
      small, proj, qkv, qkv, qkv, lat, normed, fc2b, *hidden_sums, sils, ada, fc1s,
      fc2s)


def finish_kernel(own, own_ff, rows_ref, grads_ref, wgrad_ref, qkvg_ref, projg_ref, fc1a_ref,
                  fc1b_ref, fc2a_ref, fc2b_ref, small_ref, cond_ref, pieces_ref,
                  out_ref, xg_ref, wgrad_out, qkv_out, proj_out, fc1_out, fc2_out, condg_out, adab_out,
                  dw1k_out, dw1b_out, projb_out, fc2b_out, dw2k_out, dw2b_out, fc1b_out):
    model = out_ref.shape[1]
    order = order_matrix()
    for src, dst in ((rows_ref, out_ref), (grads_ref, xg_ref)):
        block = src[...].reshape(GROUP, model)
        dst[...] = dot_tn(order, block).astype(BF16)

    @pl.when(pl.program_id(0) == 0)
    def _():
        half, hidden, total = own_ff // 2, fc1_out.shape[1], pieces_ref.shape[0]
        wgrad_out[...] = wgrad_ref[...]
        proj_out[...] = projg_ref[...]
        for s in range(model // 128):
            for i in range(3):
                to = i * model + s * 128
                qkv_out[:, to : to + 128] = qkvg_ref[:, s * 384 + i * 128 : s * 384 + i * 128 + 128]
        moves = [
            (hidden // 2 * h + half * d, own_ff * d + half * h, half)
            for d in range(total) for h in (0, 1)
        ]
        tiles = tiles_of(fc1a_ref[...]) + tiles_of(fc1b_ref[...])
        for i, tile in enumerate(move_lanes(tiles, moves, hidden // 128)):
            fc1_out[:, i * 128 : i * 128 + 128] = tile
        fc2_out[:half, :] = fc2a_ref[...]
        fc2_out[half:, :] = fc2b_ref[...]
        tiles = [pieces_ref[d] for d in range(total)]
        moves = [(128 * d, own * d, own) for d in range(total)]
        grad = jnp.concatenate(move_lanes(tiles, moves, model // 128), axis=1)
        cond = cond_ref[...].astype(F32)
        gate = jax.nn.sigmoid(cond)
        condg_out[...] = grad * (gate + cond * gate * (1.0 - gate))
        dw1k_out[:8, :] = small_ref[:8, :own]
        dw2k_out[...] = small_ref[8:17, :own_ff]
        rows = ((dw1k_out.at[8:9], 0, 32), (dw1b_out, 1, 32), (projb_out, 2, 32), (fc2b_out, 3, 32),
                (dw2b_out, 17, 0), (fc1b_out, 18, 0))
        for ref, row, lane in rows:
            ref[...] = small_ref[row : row + 1, lane : lane + ref.shape[1]]
        for i in range(3):
            adab_out[:, 2 * own * i : 2 * own * (i + 1)] = small_ref[i : i + 1, 64 : 64 + 2 * own]


def finish(rows, grads, wgrad, qkvg, projg, fc1, fc2, small, cond, pieces):
    tokens, model = rows.shape
    own, hidden, own_ff = wgrad.shape[0], 2 * fc1[0].shape[1], 2 * fc2[0].shape[0]
    split = lambda value: value.reshape(4, 4, 64, model)
    block = pl.BlockSpec((4, 1, 64, model), lambda t: (0, t, 0, 0))
    lines = pl.BlockSpec((GROUP, model), lambda t: (t, 0))
    rest = [wgrad, qkvg, projg, *fc1, *fc2, small, cond, pieces]
    outs = [
        like((tokens, model), BF16), like((tokens, model), BF16), like(wgrad.shape, F32),
        like(qkvg.shape, F32), like(projg.shape, F32), like((own, hidden), F32),
        like((own_ff, model), F32), like((1, model), F32), like((1, 6 * own), F32),
        like((9, own), F32), like((1, own), F32), like((1, own), F32), like((1, own), F32),
        like((9, own_ff), F32), like((1, own_ff), F32), like((1, own_ff), F32),
    ]
    return pl.pallas_call(
        functools.partial(finish_kernel, own, own_ff),
        grid=(4,),
        in_specs=[block, block] + [once(a.shape) for a in rest],
        out_specs=[lines, lines] + [once(o.shape) for o in outs[2:]],
        out_shape=outs,
        compiler_params=pltpu.CompilerParams(vmem_limit_bytes=60 * MIB),
        name="finish",
    )(split(rows), split(grads), *rest)


def on_device(wide, narrow, latents, condition, valid_mask, ada_weight, ada_bias, dw1_kernel, dw1_bias,
              qkv_weight, proj_weight, proj_bias, fc1_weight, fc1_bias, dw2_kernel, dw2_bias,
              fc2_weight, fc2_bias, out_cotangent):
    total = wide * narrow
    w, n = lax.axis_index("wide"), lax.axis_index("narrow")
    me = w * narrow + n
    model, hidden = latents.shape[2], fc1_weight.shape[1]
    own, own_ff = model // total, hidden // total

    bias_at = lax.dynamic_update_slice(
        jnp.zeros((1, 6 * model), F32), ada_bias.astype(F32)[None, :], (0, me * ada_bias.shape[0])
    )
    parts = [(0, dw1_kernel), (9, dw1_bias[None]), (10, proj_bias[None]), (11, fc2_bias[None]),
             (16, dw2_kernel), (25, dw2_bias[None]), (26, fc1_bias[None])]
    small = sum(
        jnp.pad(v, ((row, 32 - row - v.shape[0]), (0, 128 - v.shape[1]))) for row, v in parts
    )
    half = own_ff // 2
    if half % 16:
        fc2a, fc2_rows, spans = fc2_weight[:half], fc2_weight[half:], (None, None)
    else:
        fc2a = fc2_rows = fc2_weight
        spans = ((0, half), (half, half))
    chunks = [(0, 0, 128)] + thirds(2, 3 * model) + [(3, 0, model)]
    stages = wide.bit_length()
    plan = [steady(c, stages) for c in range(5)]
    needed = plan[4][-1]
    chunks += thirds(1, hidden // 2) + thirds(4, model)
    plan += [[6 + c] + steady(needed + 1 + c, stages - 1) for c in range(6)]
    (mod, sils, model_small, hidden_small, lat, gout, g2, normed, mixed, keep, fc2b, fc1b, fc1_one, qkv,
     proj, fc2_one) = front(
        wide, narrow, latents[0], out_cotangent[0], valid_mask, condition, ada_weight, bias_at, small,
        fc1_weight, [qkv_weight, proj_weight, fc2a], (None, None, spans[0]), chunks, plan,
    )
    qkv, proj = qkv.reshape(model, 3 * model), proj.reshape(model, model)
    triple, probs, att, branch, n2, n2t, fc1_one, fc2_one = attend(
        wide, narrow, mixed, lat, keep, mod, model_small, qkv, proj, fc1_one, fc2_one,
        thirds(0, hidden // 2) + thirds(1, model), plan[5:], needed, 5,
    )
    chunks = thirds(0, hidden // 2) + thirds(1, model)
    as_fc1 = lambda rows: rows.reshape(model, hidden // 2)
    as_fc2 = lambda rows: rows.reshape(hidden // 2, model)
    as_lines = lambda grad: grad.reshape(*bit_sizes(wide), grad.shape[0] // wide, grad.shape[1])
    two, gn2, fc1g, fc2g, sums_a, fc1_two, fc2_two = feed_forward(
        wide, narrow, n2, n2t, g2, as_fc1(fc1_one), hidden_small, 0, as_fc2(fc2_one),
        [fc1b, fc2_rows], (None, spans[1]), chunks,
    )
    two, gn2, fc1h, fc2h, sums_b, fc1o, fc2o = feed_forward(
        wide, narrow, n2, n2t, g2, as_fc1(fc1_two), hidden_small, 1, as_fc2(fc2_two),
        [as_lines(fc1g), as_lines(fc2g)], (None, None), chunks, (two, gn2),
    )
    rows, grads, ada_wgrad, pieces, small, qkvg, projg, fc1p, fc2p = back(
        wide, narrow, gn2, two, branch, gout, att, mixed, triple, probs,
        mod, model_small, proj, qkv, lat, normed, fc2b, (sums_a, sums_b), sils, ada_weight,
        as_lines(fc1h), as_lines(fc2h),
    )
    (out, xg, ada_wgrad, qkvg, projg, fc1g, fc2g, cond_grad, ada_bgrad, dw1k, dw1b, projb, fc2bg, dw2k,
     dw2b, fc1bg) = finish(
        rows, grads, ada_wgrad, qkvg, projg, (fc1o, fc1p), (fc2o, fc2p), small, condition, pieces
    )
    return (
        out[None], xg[None], cond_grad, ada_wgrad, ada_bgrad[0], dw1k, dw1b[0], qkvg, projg, projb[0],
        fc1g, fc1bg[0], dw2k, dw2b[0], fc2g, fc2bg[0],
    )


def solution(mesh):
    wide, narrow = mesh.shape["wide"], mesh.shape["narrow"]
    rows = lambda rank: P(AXES, *(None,) * (rank - 1))
    lanes = P(None, AXES)
    in_specs = (
        rows(3), rows(2), rows(2), rows(2), rows(1), lanes, rows(1), rows(2), rows(2), rows(1),
        rows(2), rows(1), lanes, rows(1), rows(2), rows(1), rows(3),
    )
    out_specs = (
        rows(3), rows(3), rows(2), rows(2), rows(1), lanes, rows(1), rows(2), rows(2), rows(1),
        rows(2), rows(1), lanes, rows(1), rows(2), rows(1),
    )
    return jax.shard_map(
        functools.partial(on_device, wide, narrow), mesh=mesh, in_specs=in_specs,
        out_specs=out_specs, check_vma=False,
    )
```

```python
import functools

import jax
import jax.numpy as jnp
from jax import lax
from jax.experimental import pallas as pl
from jax.experimental.pallas import tpu as pltpu
from jax.sharding import PartitionSpec as P

HEAD = 64
GRID = 32
HALF = 16
GROUP = 256
TOKENS = 1024
C0 = 0.7978845608028654
C1 = 0.044715
EPS = 1e-06
MIB = 1 << 20
AXES = ("wide", "narrow")
F32, BF16 = jnp.float32, jnp.bfloat16


def dot_nn(a, b):
    return lax.dot_general(a, b, (((1,), (0,)), ((), ())), preferred_element_type=F32)


def dot_nt(a, b):
    return lax.dot_general(a, b, (((1,), (1,)), ((), ())), preferred_element_type=F32)


def dot_tn(a, b):
    return lax.dot_general(a, b, (((0,), (0,)), ((), ())), preferred_element_type=F32)


def whole(shape):
    return pl.BlockSpec(shape, lambda *_: (0,) * len(shape))


def once(shape):
    return pl.BlockSpec(shape, lambda *_: (0,) * len(shape), pipeline_mode=pl.Buffered(1))


def like(shape, dtype):
    return jax.ShapeDtypeStruct(shape, dtype)


def shift_pair(pair, parity, first, last):
    low, high = pair
    zero = jnp.zeros_like(low)
    if parity == 0:
        low, high = pltpu.roll(low, 1, 0), pltpu.roll(high, 1, 0)
        return jnp.where(first, zero, low), jnp.where(first, low, high)
    low, high = pltpu.roll(low, 7, 0), pltpu.roll(high, 7, 0)
    return jnp.where(last, high, low), jnp.where(last, zero, high)


def row_sources(gi, r):
    if gi == 0:
        return ((1, r - 1), (0, r), (1, r))
    return ((0, r), (1, r), (0, r + 1))


def load_pair(ref, slab, gi, gj, r):
    tile = 2 + 2 * r
    group = 2 * gi + gj
    return ref[slab, group, tile], ref[slab, group, tile + 1]


def store_pair(ref, slab, gi, gj, r, pair):
    tile = 2 + 2 * r
    group = 2 * gi + gj
    ref[slab, group, tile] = pair[0]
    ref[slab, group, tile + 1] = pair[1]


def edge_masks():
    sub = lax.broadcasted_iota(jnp.int32, (8, 128), 0)
    return sub == 0, sub == 7


def clear_edges(ref):
    slabs = ref.shape[0]
    ref[:, :, 0:2] = jnp.zeros((slabs, 4, 2, 8, 128), F32)
    ref[:, :, 34:36] = jnp.zeros((slabs, 4, 2, 8, 128), F32)


def conv_cell(src, slab, gi, gj, r, k, bias, masks):
    sources = row_sources(gi, r)
    other = 1 - gj
    near = 2 if gj == 0 else 0
    far = 2 - near
    same = [load_pair(src, slab, p, gj, rr) for p, rr in sources]
    cross = [load_pair(src, slab, p, other, rr) for p, rr in sources]
    straight, moved = [], []
    for h in (0, 1):
        acc, off = bias, None
        for a in range(3):
            acc = acc + k[3 * a + 1] * same[a][h] + k[3 * a + near] * cross[a][h]
            term = k[3 * a + far] * cross[a][h]
            off = term if off is None else off + term
        straight.append(acc)
        moved.append(off)
    moved = shift_pair(moved, gj, *masks)
    return straight[0] + moved[0], straight[1] + moved[1]


def conv_back_row(slab, k, src, grad, grad_moved, put, r, carry):
    kg, total = list(carry[:9]), carry[9]
    for gi in (0, 1):
        sources = row_sources(gi, r)
        for gj in (0, 1):
            other = 1 - gj
            near = 2 if gj == 0 else 0
            here = load_pair(src, slab, gi, gj, r)
            out = [None, None]
            for a in range(3):
                p, rr = sources[2 - a]
                trio = {
                    1: load_pair(grad, slab, p, gj, rr),
                    2 - near: load_pair(grad, slab, p, other, rr),
                    near: load_pair(grad_moved, slab, p, other, rr),
                }
                for b in range(3):
                    n = 3 * a + b
                    for h in (0, 1):
                        term = k[n] * trio[b][h]
                        out[h] = term if out[h] is None else out[h] + term
                        kg[n] = kg[n] + here[h] * trio[b][h]
            total = total + out[0] + out[1]
            put(gi, gj, r, out)
    return tuple(kg) + (total,)


def conv_back(slab, k, src, grad, grad_moved, put):
    body = lambda r, carry: conv_back_row(slab, k, src, grad, grad_moved, put, r, carry)
    return lax.fori_loop(0, HALF, body, (jnp.zeros((8, 128), F32),) * 10)


def group_rows(gi, gj, r):
    return pl.ds(pl.multiple_of((2 * gi + gj) * GROUP + r * HALF, HALF), HALF)


def row_sum(values):
    rows, columns = values.shape
    return jnp.sum(values.reshape(rows // 8, 8, columns), axis=0)


def unit_rows(values):
    model = values.shape[-1]
    centered = values - jnp.sum(values, axis=-1, keepdims=True) * (1.0 / model)
    spread = jnp.sum(centered * centered, axis=-1, keepdims=True) * (1.0 / model)
    scale = lax.rsqrt(spread + EPS)
    return centered * scale, scale


def unit_back(grad, unit, scale):
    model = grad.shape[-1]
    mean = jnp.sum(grad, axis=-1, keepdims=True) * (1.0 / model)
    tilt = jnp.sum(grad * unit, axis=-1, keepdims=True) * (1.0 / model)
    return scale * (grad - mean - unit * tilt)


def order_matrix():
    d = lax.broadcasted_iota(jnp.int32, (GROUP, GROUP), 0)
    column = lax.broadcasted_iota(jnp.int32, (GROUP, GROUP), 1)
    group, position = d >> 6, (d >> 4) & 3
    source = (2 * position + (group >> 1)) * GRID + 2 * (d & 15) + (group & 1)
    return jnp.where(source == column, 1.0, 0.0).astype(BF16)


def part_of(ref, span):
    return ref if span is None else ref.at[pl.ds(*span)]


def span_shape(array, span):
    return array.shape if span is None else (span[1], *array.shape[1:])


def ff_kernel(wide, narrow, chunks, spans, steps, sums_over, *refs):
    count = len(spans)
    n2_ref, n2t_ref, g2_ref, fc1_ref, small_ref, fc2_ref = refs[:6]
    so_far, refs = refs[6 : 6 + 2 * sums_over], refs[6 + 2 * sums_over :]
    srcs = [part_of(ref, span) for ref, span in zip(refs, spans)]
    branch_out, gn2_out, w1g_ref, w2g_ref, sums_ref = refs[count : 5 + count]
    dsts, refs = refs[5 + count : 5 + 2 * count], refs[5 + 2 * count :]
    hid, ga, gc, gcs, act, ghl, branch_ref, gn2_ref, held = refs[:9]
    totals = (branch_ref, gn2_ref)
    step = pl.program_id(0)
    slabs = hid.shape[0]
    p = Place(wide, narrow)
    if sums_over:
        buffers, (sends, recvs) = refs[9:-2], refs[-2:]
        waves = scatter_jobs(p, srcs, dsts, buffers, sends, recvs, chunks)
        own_copies = []
    else:
        sends, recvs, local = refs[9:]
        waves = gather_jobs(p, srcs, dsts, sends, recvs, chunks)
        own_copies = [
            pltpu.make_async_copy(
                srcs[i], dsts[i].at[(*digits_of(p.w, wide), p.n)], local.at[i]
            )
            for i in range(count)
        ]

    def hook(position):
        for when in range(steps):
            pl.when(step == when)(lambda: waves.at_hook(3 * when + position, 3 * steps))

    @pl.when(step == 0)
    def _():
        greet(p.partners())
        for copy in own_copies:
            copy.start()
        for i, ref in enumerate(totals):
            if sums_over:
                pltpu.make_async_copy(so_far[i], ref, held.at[i]).start()
            else:
                ref[...] = jnp.zeros_like(ref)
        for ref in (hid, gc, gcs):
            clear_edges(ref)

    for g in range(4):
        rows = pl.ds(g * GROUP, GROUP)
        full = dot_nn(n2_ref[rows, :], fc1_ref[...]) + small_ref[10:11, :]
        back = dot_nt(g2_ref[rows, :], fc2_ref[...])
        for slab in range(slabs):
            lanes = slice(slab * 128, slab * 128 + 128)
            hid[slab, g, 2:34] = full[:, lanes].reshape(32, 8, 128)
            ga[slab, g] = back[:, lanes].reshape(32, 8, 128)

    @pl.when(step == 0)
    def _():
        met(len(p.partners()))
        waves.run(0)
        waves.run(1)
        for copy in own_copies:
            copy.wait()

    hook(0)
    masks = edge_masks()
    for slab in range(slabs):
        lanes = pl.ds(slab * 128, 128)
        k = [jnp.broadcast_to(small_ref[n : n + 1, lanes], (8, 128)) for n in range(9)]
        bias = jnp.broadcast_to(small_ref[9:10, lanes], (8, 128))

        def forward(r, total):
            for gi in (0, 1):
                for gj in (0, 1):
                    pair = conv_cell(hid, slab, gi, gj, r, k, bias, masks)
                    acts, grads = [], []
                    for h in (0, 1):
                        x = pair[h]
                        x2 = x * x
                        half = 0.5 * jnp.tanh(x * (C0 + (C0 * C1) * x2)) + 0.5
                        value = x * half
                        slope = half + (value - value * half) * (2.0 * C0 + (6.0 * C0 * C1) * x2)
                        acts.append(value)
                        grads.append(ga[slab, 2 * gi + gj, 2 * r + h] * slope)
                        total = total + grads[-1]
                    act[group_rows(gi, gj, r), lanes] = jnp.concatenate(acts, 0).astype(BF16)
                    store_pair(gc, slab, gi, gj, r, grads)
                    store_pair(gcs, slab, gi, gj, r, shift_pair(grads, 1 - gj, *masks))
            return total

        total = lax.fori_loop(0, HALF, forward, jnp.zeros((8, 128), F32))

        def put(gi, gj, r, pair):
            ghl[group_rows(gi, gj, r), lanes] = jnp.concatenate(pair, 0).astype(BF16)

        sums = conv_back(slab, k, hid, gc, gcs, put)
        for n, value in enumerate([*sums[:9], total, sums[9]]):
            sums_ref[n : n + 1, lanes] = jnp.sum(value, axis=0, keepdims=True)
        sums_ref[11:16, lanes] = jnp.zeros((5, 128), F32)
        if slab == 0:
            hook(1)

    if sums_over:
        @pl.when(step == 0)
        def _():
            for i, ref in enumerate(totals):
                pltpu.make_async_copy(so_far[i], ref, held.at[i]).wait()

    branch_ref[...] += dot_nn(act[...], fc2_ref[...])
    gn2_ref[...] += dot_nt(ghl[...], fc1_ref[...])

    @pl.when(step == steps - 1)
    def _():
        for i, out in enumerate((branch_out, gn2_out)):
            pltpu.make_async_copy(totals[i], out, held.at[i]).start()

    w2g_ref[...] = dot_tn(act[...], g2_ref[...]).astype(w2g_ref.dtype)
    w1g_ref[...] = dot_nn(n2t_ref[...], ghl[...]).astype(w1g_ref.dtype)
    hook(2)

    @pl.when(step == steps - 1)
    def _():
        waves.finish()
        for i, out in enumerate((branch_out, gn2_out)):
            pltpu.make_async_copy(totals[i], out, held.at[i]).wait()


def feed_forward(wide, narrow, n2, n2t, g2, fc1, small, part, fc2, arrays, spans, chunks, so_far=(),
                 width=256):
    sums_over = bool(so_far)
    tokens, model = n2.shape
    hidden = fc1.shape[1]
    slabs, steps, count = width // 128, hidden // width, len(arrays)
    padded = pltpu.VMEM((slabs, 4, 36, 8, 128), F32)
    columns = lambda rows: pl.BlockSpec((rows, width), lambda s: (0, s))
    lines = pl.BlockSpec((width, model), lambda s: (s, 0))
    anywhere = pl.BlockSpec(memory_space=pl.ANY)
    if sums_over:
        shapes = [a.shape for a in arrays]
        moved = [owned_shape(s, narrow) for s in shapes]
        extra = scatter_scratch(wide, narrow, shapes) + job_sems(wide, narrow, chunks)
        in_moved, out_moved = [once(s) for s in shapes], [once(m.shape) for m in moved]
    else:
        moved = [gathered_shape(wide, narrow, span_shape(a, s)) for a, s in zip(arrays, spans)]
        extra = job_sems(wide, narrow, chunks) + [pltpu.SemaphoreType.DMA((count,))]
        in_moved = out_moved = [anywhere] * count
    return pl.pallas_call(
        functools.partial(ff_kernel, wide, narrow, chunks, spans, steps, sums_over),
        grid=(steps,),
        in_specs=[
            once((tokens, model)), once((model, tokens)), once((tokens, model)),
            columns(model), pl.BlockSpec((16, width), lambda s: (0, part * steps + s)), lines,
        ] + [anywhere] * len(so_far) + in_moved,
        out_specs=[
            anywhere, anywhere, columns(model), lines, columns(16)
        ] + out_moved,
        out_shape=[
            like((tokens, model), F32), like((tokens, model), F32),
            like((model, hidden), BF16), like((hidden, model), BF16), like((16, hidden), F32),
        ] + moved,
        scratch_shapes=[
            padded, pltpu.VMEM((slabs, 4, 32, 8, 128), F32), padded, padded,
            pltpu.VMEM((tokens, width), BF16), pltpu.VMEM((tokens, width), BF16),
            pltpu.VMEM((tokens, model), F32), pltpu.VMEM((tokens, model), F32),
            pltpu.SemaphoreType.DMA((2,)),
        ] + extra,
        compiler_params=pltpu.CompilerParams(
            vmem_limit_bytes=56 * MIB, collective_id=4 if sums_over else 3, has_side_effects=True
        ),
        name="feed_forward",
    )(n2, n2t, g2, fc1, small, fc2, *so_far, *arrays)


def flip(index, bit):
    return index + bit - 2 * bit * lax.rem(index // bit, 2)


def bits_of(count):
    return [1 << b for b in range(count.bit_length() - 1)]


def digits_of(index, wide):
    levels = wide.bit_length() - 1
    return [lax.rem(index // (1 << (levels - 1 - i)), 2) for i in range(levels)]


def static_digits(index, wide):
    levels = wide.bit_length() - 1
    return [(index >> (levels - 1 - i)) & 1 for i in range(levels)]


def at(w, n):
    return {"wide": w, "narrow": n}


def greet(places):
    barrier = pltpu.get_barrier_semaphore()
    for place in places:
        pl.semaphore_signal(barrier, inc=1, device_id=place, device_id_type=pl.DeviceIdType.MESH)


def met(count):
    pl.semaphore_wait(pltpu.get_barrier_semaphore(), count)


def greet_all(place):
    barrier = pltpu.get_barrier_semaphore()
    total = place.total

    def body(k, carry):
        pl.semaphore_signal(
            barrier, inc=1, device_id=place.device(lax.rem(place.sid + k, total)),
            device_id_type=pl.DeviceIdType.MESH,
        )
        return carry

    lax.fori_loop(1, total, body, 0)


def remote(src, dst, send_sem, recv_sem, place):
    return pltpu.make_async_remote_copy(
        src_ref=src, dst_ref=dst, send_sem=send_sem, recv_sem=recv_sem, device_id=place,
        device_id_type=pl.DeviceIdType.MESH,
    )


class Place:
    def __init__(self, wide, narrow):
        self.wide, self.narrow = wide, narrow
        self.w, self.n = lax.axis_index("wide"), lax.axis_index("narrow")
        self.total, self.half = wide * narrow, wide * narrow // 2
        self.me = self.w * narrow + self.n
        self.core = lax.rem(self.w, 2)
        self.slot = (self.w // 2) * narrow + self.n
        self.sid = self.core * self.half + self.slot
        self.sibling = at(flip(self.w, 1), self.n)

    def device(self, sid):
        core, slot = sid // self.half, lax.rem(sid, self.half)
        return at(2 * (slot // self.narrow) + core, lax.rem(slot, self.narrow))

    def order_of(self, sid):
        core, slot = divmod(sid, self.half)
        return (2 * (slot // self.narrow) + core) * self.narrow + slot % self.narrow

    def partners(self):
        places = [at(self.w, lax.rem(self.n + k, self.narrow)) for k in range(1, self.narrow)]
        return places + [at(flip(self.w, bit), self.n) for bit in bits_of(self.wide)]

    def all_copies(self, src_of, dst, sends, recvs):
        def copy(k):
            sid = lax.rem(self.sid + k, self.total)
            return remote(src_of(sid), dst, sends.at[k], recvs.at[k], self.device(sid))

        return Exchange(copy, self.total)

    def kin_copies(self, src_of, dst, sends, recvs):
        def copy(k):
            slot = lax.rem(self.slot + k, self.half)
            return remote(src_of(slot), dst, sends.at[k], recvs.at[k],
                          self.device(self.core * self.half + slot))

        return Exchange(copy, self.half)

    def to_all(self, *refs):
        return self.all_copies(*refs).start()

    def to_kin(self, *refs):
        return self.kin_copies(*refs).start()

    def to_all_wait(self, *refs):
        self.all_copies(*refs).wait()

    def to_kin_wait(self, *refs):
        self.kin_copies(*refs).wait()


class Exchange:
    def __init__(self, copy, count):
        self.copy, self.count = copy, count

    def start(self):
        def body(k, carry):
            self.copy(k).start()
            return carry

        lax.fori_loop(1, self.count, body, 0)
        return self.wait

    def wait(self):
        def body(k, carry):
            self.copy(k).wait()
            return carry

        lax.fori_loop(1, self.count, body, 0)


def bit_sizes(wide):
    return (2,) * (wide.bit_length() - 1)


class Transfer:
    def __init__(self, place, sends, recvs, chunk, columns, turn):
        self.p, self.sends, self.recvs, self.chunk = place, sends, recvs, chunk
        start, size = columns
        self.all = pl.ds(start, size)
        levels = len(bit_sizes(place.wide))
        far = list(range(levels - 1))
        half = size // 256 * 128
        if turn % 2:
            far = far[::-1]
        self.parts = [(pl.ds(start, size - half), far)]
        if half:
            self.parts.append((pl.ds(start + size - half, half), far[::-1]))
        self.stages = levels + 1
        self.bits = digits_of(place.w, place.wide)
        self.count = 0

    def copy(self, src, dst, place):
        slot = self.count
        self.count += 1
        return remote(src, dst, self.sends.at[self.chunk, slot], self.recvs.at[self.chunk, slot], place)

    def along(self, level):
        return at(flip(self.p.w, 1 << (len(self.bits) - 1 - level)), self.p.n)

    def in_line(self, k):
        return at(self.p.w, lax.rem(self.p.n + k, self.p.narrow))

    def copies(self, stage):
        self.count = 0
        for before in range(stage):
            self.count += len(self.make(before, True))
        return self.make(stage, False)

    def start(self, stage):
        for copy in self.copies(stage):
            copy.start()

    def finish(self, stages):
        pass


class Gather(Transfer):
    def __init__(self, place, src, dst, sends, recvs, chunk, columns, turn):
        super().__init__(place, sends, recvs, chunk, columns, turn)
        self.src, self.dst = src, dst

    def make(self, stage, count_only):
        levels = len(self.bits)
        if stage == 0:
            ks = range(1, self.p.narrow)
            if count_only:
                return list(ks)
            return [
                self.copy(self.src.at[:, self.all],
                          self.dst.at[(*self.bits, self.p.n, slice(None), self.all)], self.in_line(k))
                for k in ks
            ]
        if stage == levels:
            parts = [(self.all, list(range(levels)))]
        else:
            parts = self.parts
        if count_only:
            return list(parts)
        found = []
        for columns, order in parts:
            index = list(self.bits)
            for level in order[: stage - 1]:
                index[level] = slice(None)
            part = self.dst.at[(*index, slice(None), slice(None), columns)]
            found.append(self.copy(part, part, self.along(order[stage - 1])))
        return found

    def wait(self, stage):
        for copy in self.copies(stage):
            copy.wait_recv()

    def finish(self, stages):
        for stage in stages:
            for copy in self.copies(stage):
                copy.wait_send()


def steady(first, stages, lag=2):
    return [first + lag * s for s in range(stages + 1)]


class Waves:
    def __init__(self, jobs, plan, resume=-1):
        self.jobs, self.resume = jobs, resume
        self.stages = jobs[0].stages
        self.plan = plan or [steady(c, self.stages) for c in range(len(jobs))]
        self.wave = resume + 1
        self.last = max(waves[-1] for waves in self.plan)

    def run(self, wave):
        for job, waves in zip(self.jobs, self.plan):
            for stage, when in enumerate(waves):
                if when != wave:
                    continue
                if stage and waves[stage - 1] > self.resume:
                    job.wait(stage - 1)
                if stage < self.stages:
                    job.start(stage)

    def tick(self, times=1):
        for _ in range(times):
            if self.wave <= self.last:
                self.run(self.wave)
                self.wave += 1

    def through(self, wave):
        while self.wave <= min(wave, self.last):
            self.tick()

    def at_hook(self, hook, hooks):
        first = self.resume + 3
        left = self.last + 1 - first
        for wave in range(first + hook * left // hooks, first + (hook + 1) * left // hooks):
            self.run(wave)

    def finish(self, last=None):
        last = self.last if last is None else last
        for job, waves in zip(self.jobs, self.plan):
            here = [s for s in range(self.stages) if self.resume < waves[s] <= last]
            for stage in here:
                if waves[stage + 1] > last:
                    job.wait(stage)
            job.finish(here)

    def end(self, last=None):
        last = self.last if last is None else last
        self.through(last)
        self.finish(last)


def job_sems(wide, narrow, chunks):
    per = narrow - 1 + 2 * (wide.bit_length() - 1)
    return [pltpu.SemaphoreType.DMA((len(chunks), per))] * 2


def gather_jobs(place, srcs, dsts, sends, recvs, chunks, plan=None, resume=-1, shift=0):
    jobs = [
        Gather(place, srcs[i], dsts[i], sends, recvs, c, columns, c + shift)
        for c, (i, *columns) in enumerate(chunks)
    ]
    return Waves(jobs, plan, resume)


def gathered_shape(wide, narrow, shape):
    return like((*bit_sizes(wide), narrow, *shape), BF16)


def thirds(i, size):
    return [(i, t * (size // 3), size // 3) for t in range(3)]


class Scatter(Transfer):
    def __init__(self, place, src, buffers, out, sends, recvs, chunk, columns):
        super().__init__(place, sends, recvs, chunk, columns, chunk)
        self.src, self.out = src, out
        self.halves, self.line, self.got = buffers[:-2], buffers[-2], buffers[-1]
        self.rows = self.line.shape[1]
        core = len(self.bits) - 1
        self.parts = [(columns, [core] + order) for columns, order in self.parts]

    def make(self, stage, count_only):
        levels = len(self.bits)
        if stage == levels:
            ks = range(1, self.p.narrow)
            if count_only:
                return list(ks)
            return [
                self.copy(self.line.at[lax.rem(self.p.n + k, self.p.narrow), :, self.all],
                          self.got.at[k - 1, :, self.all], self.in_line(k))
                for k in ks
            ]
        parts = self.parts if stage else [(self.all, self.parts[0][1])]
        if count_only:
            return list(parts)
        found = []
        for columns, order in parts:
            source, index, kept = self.level(order, stage, True)
            into = self.halves[stage].at[(*kept, slice(None), columns)]
            found.append(self.copy(source.at[(*index, slice(None), columns)], into, self.along(order[stage])))
        return found

    def level(self, order, stage, theirs):
        source = self.src if stage == 0 else self.halves[stage - 1]
        left = [level for level in range(len(self.bits)) if level not in order[:stage]]
        bit = self.bits[order[stage]]
        bit = 1 - bit if theirs else bit
        index = [bit if level == order[stage] else slice(None) for level in left]
        return source, index, [slice(None)] * (len(left) - 1)

    def wait(self, stage):
        for copy in self.copies(stage):
            copy.wait()
        levels = len(self.bits)
        if stage == levels:
            value = self.line[self.p.n, :, self.all].astype(F32)
            for k in range(1, self.p.narrow):
                value = value + self.got[k - 1, :, self.all].astype(F32)
            self.out[:, self.all] = value
            return
        for columns, order in self.parts:
            source, index, kept = self.level(order, stage, False)
            into = self.halves[stage]
            for j in range(1 << len(kept)):
                digits = [(j >> i) & 1 for i in range(len(kept))]
                mine = [v if not isinstance(v, slice) else None for v in index]
                rest = iter(digits)
                mine = [next(rest) if v is None else v for v in mine]
                self.add(source, tuple(mine), into, tuple(digits), columns, stage == levels - 1)

    def add(self, source, mine, into, arrived, columns, last):
        if last:
            total = source[(*mine, slice(None), columns)].astype(F32) + into[
                (*arrived, slice(None), columns)
            ].astype(F32)
            for m in range(self.p.narrow):
                rows = slice(m * self.rows, (m + 1) * self.rows)
                self.line[m, :, columns] = total[rows].astype(BF16)
            return

        into[(*arrived, slice(None), columns)] = (
            source[(*mine, slice(None), columns)] + into[(*arrived, slice(None), columns)]
        )


def scatter_scratch(wide, narrow, shapes):
    scratch = []
    for *_, height, columns in shapes:
        for stage in range(wide.bit_length() - 1):
            scratch.append(pltpu.VMEM((*bit_sizes(wide)[stage + 1 :], height, columns), BF16))
        scratch.append(pltpu.VMEM((narrow, height // narrow, columns), BF16))
        scratch.append(pltpu.VMEM((narrow - 1, height // narrow, columns), BF16))
    return scratch


def scatter_jobs(place, srcs, outs, buffers, sends, recvs, chunks, plan=None):
    per = len(buffers) // len(srcs)
    jobs = [
        Scatter(place, srcs[i], buffers[i * per : (i + 1) * per], outs[i], sends, recvs, c, columns)
        for c, (i, *columns) in enumerate(chunks)
    ]
    return Waves(jobs, plan)


def owned_shape(shape, narrow):
    return like((shape[-2] // narrow, shape[-1]), F32)


def move_lanes(tiles, moves, count):
    rows = tiles[0].shape[0]
    lane = lax.broadcasted_iota(jnp.int32, (rows, 128), 1)
    out = [jnp.zeros((rows, 128), F32) for _ in range(count)]
    for start, to, length in moves:
        while length:
            size = min(length, 128 - start % 128, 128 - to % 128)
            tile = tiles[start // 128]
            turn = (to - start) % 128
            if turn:
                tile = pltpu.roll(tile, turn, 1)
            inside = (lane >= to % 128) & (lane < to % 128 + size)
            out[to // 128] = jnp.where(inside, tile, out[to // 128])
            start, to, length = start + size, to + size, length - size
    return out


def tiles_of(values):
    return [values[:, i : i + 128] for i in range(0, values.shape[1], 128)]


def front_kernel(wide, narrow, chunks, plan, spans, own, own_ff, *refs):
    count = len(spans)
    (x_ref, cot_ref, mask_ref, cond_ref, ada_ref, bias_ref, small_ref, fc1_ref) = refs[:8]
    srcs, refs = refs[8 : 8 + count], refs[8 + count :]
    srcs = [part_of(ref, span) for ref, span in zip(srcs, spans)]
    (mod_ref, sils_ref, model_ref, hidden_ref, lat_ref, gout_ref, g2_ref, normed_ref, mixed_ref,
     keep_ref, fc2b_ref, fc1b_ref) = refs[:12]
    dsts, refs = refs[12 : 13 + count], refs[13 + count :]
    (order_ref, fc1a_ref, sil_out, got, part, sib, rows_in, smalls, send_a, recv_a, send_b, recv_b, send_c, recv_c,
     sends, recvs, local) = refs
    p = Place(wide, narrow)
    mine = digits_of(p.w, wide)
    model = x_ref.shape[1]
    slabs = model // 128
    own_copies = [
        pltpu.make_async_copy(srcs[i], dsts[1 + i].at[(*mine, p.n)], local.at[i]) for i in range(count)
    ]
    for copy in own_copies:
        copy.start()
    greet_all(p)
    order_ref[...] = order_matrix()
    waves = gather_jobs(p, [small_ref, fc1a_ref, *srcs], [smalls, *dsts], sends, recvs, chunks, plan)
    last = waves.plan[chunks.index((3, 0, model))][-1]
    cond = cond_ref[...].astype(F32)
    sil = (cond * jax.nn.sigmoid(cond)).astype(BF16).astype(F32)
    tiles = tiles_of(sil)
    for sid in range(p.total):
        d = p.order_of(sid)
        sil_out[sid] = move_lanes(tiles, [(own * d, 0, own)], 1)[0]
    got[p.sid] = sil_out[p.sid]
    smalls[(*mine, p.n)] = small_ref[...]

    def arrange(t):
        rows = pl.ds(t * GROUP, GROUP)
        tokens = dot_nn(order_ref[...], x_ref[rows, :])
        unit, _ = unit_rows(tokens)
        mask = mask_ref[:, t * GROUP : (t + 1) * GROUP].astype(F32)
        mask = (order_ref[...].astype(F32) * mask).astype(BF16)
        kept = dot_nn(mask, jnp.ones((GROUP, 128), BF16))
        gout = dot_nn(order_ref[...], cot_ref[rows, :]) * jnp.concatenate([kept] * slabs, axis=1)
        for g in range(4):
            src = slice(64 * g, 64 * g + 64)
            dst = pl.ds(g * GROUP + 64 * t, 64)
            lat_ref[dst, :] = tokens[src].astype(BF16)
            gout_ref[dst, :] = gout[src].astype(BF16)
            keep_ref[dst, :] = (kept[src] - 1.0) * 1e30
            for s in range(slabs):
                tile = unit[src, s * 128 : s * 128 + 128].reshape(8, 8, 128)
                normed_ref[s, g, 2 + 8 * t : 10 + 8 * t] = tile

    met(p.total - 1)
    wait_sil = p.to_all(lambda sid: sil_out.at[sid], got.at[p.sid], send_a, recv_a)
    waves.tick(2)
    arrange(0)
    for copy in own_copies:
        copy.wait()
    waves.tick()
    arrange(1)
    wait_sil()
    sil = got[...].reshape(p.total, 128)
    sils_ref[...] = sil
    product = dot_nn(sil[:, :own].astype(BF16), ada_ref[...]) + bias_ref[...]
    for d in range(p.total):
        part[d // p.half, d % p.half] = product[d : d + 1, :]
    to_sibling = remote(part.at[1 - p.core], sib, send_b, recv_b, p.sibling)
    to_sibling.start()
    waves.tick()
    arrange(2)
    to_sibling.wait()
    part[p.core] = part[p.core] + sib[...]
    rows_in[p.slot] = part[p.core, p.slot]
    wait_rows = p.to_kin(lambda slot: part.at[p.core, slot], rows_in.at[p.slot], send_c, recv_c)
    waves.tick()
    arrange(3)
    clear_edges(normed_ref)
    waves.tick()
    columns = tiles_of(fc1_ref[...].astype(F32))
    for h, ref in enumerate((fc1a_ref, fc1b_ref)):
        moves = [
            (own_ff * d + own_ff // 2 * h, own_ff // 2 * d, own_ff // 2) for d in range(p.total)
        ]
        ref[...] = jnp.concatenate(move_lanes(columns, moves, len(columns) // 2), axis=1).astype(BF16)
    own_fc1 = pltpu.make_async_copy(fc1a_ref, dsts[0].at[(*mine, p.n)], local.at[count])
    own_fc1.start()
    waves.through(waves.plan[0][-1])
    pieces = [smalls[(*static_digits(d // narrow, wide), d % narrow)].astype(F32) for d in range(p.total)]
    moves = [(128 * d, own * d, own) for d in range(p.total)]
    model_ref[...] = jnp.concatenate(move_lanes([q[:16] for q in pieces], moves, slabs), axis=1)
    half, hidden = own_ff // 2, fc1_ref.shape[1]
    moves = [
        (128 * d + half * h, hidden // 2 * h + half * d, half) for d in range(p.total) for h in (0, 1)
    ]
    hidden_ref[...] = jnp.concatenate(
        move_lanes([q[16:] for q in pieces], moves, hidden // 128), axis=1
    )
    own_fc1.wait()
    wait_rows()
    mod = jnp.sum(rows_in[...], axis=0)
    for i in range(6):
        mod_ref[i : i + 1, :] = mod[:, i * model : (i + 1) * model]

    shift, scale, gate = mod_ref[0:1, :], mod_ref[1:2, :], mod_ref[5:6, :]
    total = jnp.zeros((8, model), F32)
    for g in range(4):
        rows = pl.ds(g * GROUP, GROUP)
        two = gout_ref[rows, :].astype(F32) * gate
        total = total + row_sum(two)
        g2_ref[rows, :] = two.astype(BF16)
    fc2b_ref[...] = total
    masks = edge_masks()
    for s in range(slabs):
        lanes = pl.ds(s * 128, 128)
        at_s = slice(s * 128, s * 128 + 128)
        shift8 = jnp.broadcast_to(shift[:, at_s], (8, 128))
        scale8 = jnp.broadcast_to(1.0 + scale[:, at_s], (8, 128))
        normed_ref[s, :, 2:34] = normed_ref[s, :, 2:34] * scale8 + shift8
        k = [jnp.broadcast_to(model_ref[n : n + 1, at_s], (8, 128)) for n in range(9)]
        bias = jnp.broadcast_to(model_ref[9:10, at_s], (8, 128))

        def body(r, carry):
            for gi in (0, 1):
                for gj in (0, 1):
                    pair = conv_cell(normed_ref, s, gi, gj, r, k, bias, masks)
                    mixed_ref[group_rows(gi, gj, r), lanes] = jnp.concatenate(pair, 0).astype(BF16)
            return carry

        lax.fori_loop(0, HALF, body, 0)
        waves.through(min(waves.wave, last))
    waves.end(last)


def front(wide, narrow, x, cot, mask, cond, ada, bias, small, fc1, blocks, spans, chunks, plan):
    total = wide * narrow
    tokens, model = x.shape
    slabs, count, columns = model // 128, len(blocks), ada.shape[1]
    hidden = fc1.shape[1]
    own, own_ff = model // total, hidden // total
    inside = pl.BlockSpec(memory_space=pltpu.VMEM)
    anywhere = pl.BlockSpec(memory_space=pl.ANY)
    all_sems = pltpu.SemaphoreType.DMA((total,))
    one_sem = pltpu.SemaphoreType.DMA
    kin_sems = pltpu.SemaphoreType.DMA((total // 2,))
    return pl.pallas_call(
        functools.partial(front_kernel, wide, narrow, chunks, plan, spans, own, own_ff),
        in_specs=[inside] * 8 + [anywhere] * count,
        out_specs=[inside] * 12 + [anywhere] * (count + 1),
        out_shape=[
            like((8, model), F32), like((total, 128), F32), like((16, model), F32),
            like((16, hidden), F32), like((tokens, model), BF16), like((tokens, model), BF16),
            like((tokens, model), BF16), like((slabs, 4, 36, 8, 128), F32),
            like((tokens, model), BF16), like((tokens, 128), F32), like((8, model), F32),
            like((own, hidden // 2), BF16),
            gathered_shape(wide, narrow, (own, hidden // 2)),
        ] + [gathered_shape(wide, narrow, span_shape(b, s)) for b, s in zip(blocks, spans)],
        scratch_shapes=[
            pltpu.VMEM((GROUP, GROUP), BF16), pltpu.VMEM((own, hidden // 2), BF16), pltpu.VMEM((total, 1, 128), F32),
            pltpu.VMEM((total, 1, 128), F32), pltpu.VMEM((2, total // 2, 1, columns), F32),
            pltpu.VMEM((total // 2, 1, columns), F32), pltpu.VMEM((total // 2, 1, columns), F32),
            pltpu.VMEM((*bit_sizes(wide), narrow, 32, 128), BF16),
            all_sems, all_sems, one_sem, one_sem, kin_sems, kin_sems,
            *job_sems(wide, narrow, chunks), pltpu.SemaphoreType.DMA((count + 1,)),
        ],
        compiler_params=pltpu.CompilerParams(
            vmem_limit_bytes=56 * MIB, collective_id=0, has_side_effects=True
        ),
        name="front",
    )(x, cot, mask, cond, ada, bias, small, fc1, *blocks)


def attend_kernel(wide, narrow, chunks, plan, resume, shift, *refs):
    mixed_ref, lat_ref, keep_ref, mod_ref, small_ref, qkv_ref, proj_ref, fc1_in, fc2_in = refs[:9]
    triple_ref, probs_ref, att_ref, branch_ref, n2_ref, n2t_ref, fc1_ref, fc2_ref = refs[9:17]
    sends, recvs = refs[17:]
    step = pl.program_id(0)
    p = Place(wide, narrow)
    waves = gather_jobs(p, [fc1_in, fc2_in], [fc1_ref, fc2_ref], sends, recvs, chunks, plan, resume,
                        shift)

    def on(when, work):
        pl.when(step == when)(work)

    def hook(position):
        for when in range(4):
            on(when, lambda: waves.at_hook(2 * when + position, 8))

    def first():
        met(len(p.partners()))
        waves.run(resume + 1)
        waves.run(resume + 2)

    on(0, lambda: greet(p.partners()))
    model = lat_ref.shape[1]
    slabs = model // 128
    triple_ref[...] = dot_nn(mixed_ref[...], qkv_ref[...]).astype(BF16)
    on(0, first)
    lane = lax.broadcasted_iota(jnp.int32, (GROUP, 128), 1)
    left = lane < HEAD
    keep = jnp.concatenate([keep_ref[...]] * 2, axis=1)
    for s in range(slabs):
        q = triple_ref[:, s * 128 : s * 128 + 128]
        k = triple_ref[:, model + s * 128 : model + s * 128 + 128] * jnp.asarray(0.125, BF16)
        v = triple_ref[:, 2 * model + s * 128 : 2 * model + s * 128 + 128]
        outs = []
        for h in (0, 1):
            mine = left if h == 0 else jnp.logical_not(left)
            scores = dot_nt(jnp.where(mine, k, jnp.zeros_like(k)), q) + keep
            e = jnp.exp(scores - jnp.max(scores, axis=0, keepdims=True))
            prob = (e * (1.0 / jnp.sum(e, axis=0, keepdims=True))).astype(BF16)
            probs_ref[2 * s + h, 0] = prob
            outs.append(dot_tn(prob, v))
        att_ref[:, s * 128 : s * 128 + 128] = jnp.where(left, outs[0], outs[1]).astype(BF16)
        if s == slabs // 2 - 1:
            hook(0)
    branch = dot_nn(att_ref[...], proj_ref[...]) + small_ref[10:11, :]
    middle = lat_ref[...].astype(F32) + mod_ref[2:3, :] * branch
    unit, _ = unit_rows(middle)
    branch_ref[...] = branch
    n2 = unit * (1.0 + mod_ref[4:5, :]) + mod_ref[3:4, :]
    n2_ref[...] = n2.astype(BF16)
    n2t_ref[...] = n2.T.astype(BF16)
    hook(1)
    on(3, waves.finish)


def attend(wide, narrow, mixed, lat, keep, mod, small, qkv, proj, fc1, fc2, chunks, plan, resume, shift):
    tokens, model = lat.shape
    heads = model // HEAD
    by_group = lambda columns: pl.BlockSpec((GROUP, columns), lambda g: (g, 0))
    anywhere = pl.BlockSpec(memory_space=pl.ANY)
    return pl.pallas_call(
        functools.partial(attend_kernel, wide, narrow, chunks, plan, resume, shift),
        grid=(4,),
        in_specs=[
            by_group(model), by_group(model), by_group(128), whole(mod.shape),
            whole(small.shape), once(qkv.shape), once(proj.shape), anywhere, anywhere,
        ],
        out_specs=[
            by_group(3 * model), pl.BlockSpec((heads, 1, GROUP, GROUP), lambda g: (0, g, 0, 0)),
            by_group(model), by_group(model), by_group(model),
            pl.BlockSpec((model, GROUP), lambda g: (0, g)), anywhere, anywhere,
        ],
        out_shape=[
            like((tokens, 3 * model), BF16), like((heads, 4, GROUP, GROUP), BF16),
            like((tokens, model), BF16), like((tokens, model), F32),
            like((tokens, model), BF16), like((model, tokens), BF16),
            like(fc1.shape, BF16), like(fc2.shape, BF16),
        ],
        input_output_aliases={7: 6, 8: 7},
        scratch_shapes=job_sems(wide, narrow, chunks),
        compiler_params=pltpu.CompilerParams(
            vmem_limit_bytes=56 * MIB, collective_id=1, has_side_effects=True
        ),
        name="attend",
    )(mixed, lat, keep, mod, small, qkv, proj, fc1, fc2)


def back_kernel(wide, narrow, chunks, plan, own, own_ff, *refs):
    (gn2_ref, two_ref, branch_ref, gout_ref, att_hbm, mixed_hbm,
     q_ref, k_ref, v_ref, probs_ref, mod_ref, small_ref, proj_ref, wq_ref, wk_ref, wv_ref,
     lat_ref, normed_hbm, fc2b_ref, hida_ref, hidb_ref, sils_ref, ada_ref, fc1s_hbm,
     fc2s_hbm) = refs[:25]
    (rows_ref, xg_ref, wgrad_ref, cond_ref, small_out, qkvg_ref, projg_ref, fc1g_ref,
     fc2g_ref) = refs[25:34]
    (ga, gmid, gmix, gmoved, sums, proj_src, qkv_src, early, late, cuts, cuts_in, hcuts, hcuts_in, part, cond_in,
     gt, normed_ref, att_ref, mixed_ref, fc1s_ref, fc2s_ref, fetched,
     send_a, recv_a, send_b, recv_b, send_c, recv_c, send_d, recv_d, send_e, recv_e, send_f, recv_f,
     send_g, recv_g) = refs[34:70]
    buffers, (sends, recvs) = refs[70:-2], refs[-2:]
    step = pl.program_id(0)
    model = lat_ref.shape[1]
    slabs = model // 128
    last = 3 + slabs
    p = Place(wide, narrow)
    half, hidden = own_ff // 2, 2 * hida_ref.shape[1]
    waves = scatter_jobs(p, [fc1s_ref, fc2s_ref, proj_src, qkv_src],
                         [fc1g_ref, fc2g_ref, projg_ref, qkvg_ref], buffers, sends, recvs, chunks,
                         plan)
    gbl = xg_ref
    later = [(fc1s_hbm, fc1s_ref), (fc2s_hbm, fc2s_ref), (att_hbm, att_ref), (mixed_hbm, mixed_ref),
             (normed_hbm, normed_ref)]
    fetch = [pltpu.make_async_copy(src, dst, fetched.at[i]) for i, (src, dst) in enumerate(later)]
    mine = lambda ref: ref.at[p.core, p.slot]

    @pl.when(step == 0)
    def _():
        greet_all(p)
        for copy in fetch:
            copy.start()
        sums[...] = jnp.zeros_like(sums)
        gmix[...] = jnp.zeros_like(gmix)
        clear_edges(gmoved)
        tiles = tiles_of(hida_ref[...]) + tiles_of(hidb_ref[...])
        for sid in range(p.total):
            d = p.order_of(sid)
            moves = [(half * d, 0, half), (hidden // 2 + half * d, half, half)]
            hcuts[sid] = move_lanes(tiles, moves, 1)[0]
        hcuts_in[p.sid] = hcuts[p.sid]

    @pl.when(step < 4)
    def _():
        rows = pl.ds(pl.multiple_of(step * GROUP, GROUP), GROUP)
        branch = branch_ref[...]
        middle = lat_ref[rows, :].astype(F32) + mod_ref[2:3, :] * branch
        two = two_ref[...] + small_ref[11:12, :]
        gout = gout_ref[...].astype(F32)
        rows_ref[...] = (middle + mod_ref[5:6, :] * two).astype(BF16)
        sums[3] += row_sum(gout * two)
        unit, scale = unit_rows(middle)
        gn2 = gn2_ref[...]
        sums[1] += row_sum(gn2)
        sums[2] += row_sum(gn2 * unit)
        gm = gout + unit_back(gn2 * (1.0 + mod_ref[4:5, :]), unit, scale)
        gmid[rows, :] = gm
        sums[0] += row_sum(gm * branch)
        gb = gm * mod_ref[2:3, :]
        sums[4] += row_sum(gb)
        low = gb.astype(BF16)
        gbl[rows, :] = low
        ga[rows, :] = dot_nt(low, proj_ref[...]).astype(BF16)

    @pl.when(step == 0)
    def _():
        met(p.total - 1)
        fetch[0].wait()
        fetch[1].wait()
        waves.run(0)
        waves.run(1)
        p.to_all(lambda sid: hcuts.at[sid], hcuts_in.at[p.sid], send_g, recv_g)

    for when in (1, 2):
        pl.when(step == when)(lambda: waves.run(when + 1))

    @pl.when(step == 3)
    def _():
        fetch[2].wait()
        fetch[3].wait()
        proj_src[...] = dot_tn(att_ref[...], gbl[...]).astype(BF16).reshape(proj_src.shape)
        waves.run(4)
        for i in range(4):
            early[p.core, p.slot, :, i * model : (i + 1) * model] = jnp.sum(
                sums[i], axis=0, keepdims=True
            )
        p.to_kin(lambda slot: mine(early), mine(early), send_a, recv_a)

    def attention(groups):
        s = step - 4
        lane = lax.broadcasted_iota(jnp.int32, (GROUP, 128), 1)
        left = lane < HEAD
        eighth = jnp.asarray(0.125, BF16)
        lanes = pl.ds(pl.multiple_of(s * 128, 128), 128)
        weight = jnp.concatenate([wq_ref[...], wk_ref[...], wv_ref[...]], axis=1)
        for g in groups:
            rows = slice(g * GROUP, (g + 1) * GROUP)
            q, k, v = q_ref[rows, :] * eighth, k_ref[rows, :] * eighth, v_ref[rows, :]
            grad = ga[rows, lanes]
            gq = gk = gv = None
            for h in (0, 1):
                keep = left if h == 0 else jnp.logical_not(left)
                only = lambda value: jnp.where(keep, value, jnp.zeros_like(value))
                p_low = probs_ref[h, g]
                prob = p_low.astype(F32)
                gh = only(grad)
                gp = dot_nt(v, gh)
                inner = jnp.sum(prob * gp, axis=0, keepdims=True)
                gs = (prob * (gp - inner)).astype(BF16)
                terms = (dot_tn(gs, only(k)), dot_nn(gs, only(q)), dot_nn(p_low, gh))
                if h == 0:
                    gq, gk, gv = terms
                else:
                    gq, gk, gv = gq + terms[0], gk + terms[1], gv + terms[2]
            found = jnp.concatenate([gq, gk, gv], axis=1).astype(BF16)
            gt[rows, :] = found
            gmixed = dot_nt(found, weight)
            for t in range(slabs):
                gmix[t + 1, g, 2:34] += gmixed[:, t * 128 : t * 128 + 128].reshape(32, 8, 128)

    pl.when(step >= 4)(lambda: attention((0, 1)))
    for s in range(slabs):
        pl.when(step == 4 + s)(lambda: waves.run(5 + 2 * s))

    @pl.when(step >= 4)
    def _():
        attention((2, 3))
        columns = pl.ds(pl.multiple_of((step - 4) * 384, 128), 384)
        found = dot_tn(mixed_ref[...], gt[...]).astype(BF16)
        qkv_src[..., columns] = found.reshape(*qkv_src.shape[:-1], 384)

    for s in range(slabs):
        pl.when(step == 4 + s)(lambda: waves.run(6 + 2 * s))

    @pl.when(step == 6)
    def _():
        p.to_kin_wait(lambda slot: mine(early), mine(early), send_a, recv_a)
        remote(early.at[p.core], early.at[p.core], send_d, recv_d, p.sibling).start()

    @pl.when(step == last)
    def _():
        waves.wave = 5 + 2 * slabs
        fetch[4].wait()
        masks = edge_masks()
        rows_out = []
        for s in range(slabs):
            at_s = slice(s * 128, s * 128 + 128)
            k = [jnp.broadcast_to(small_ref[n : n + 1, at_s], (8, 128)) for n in range(9)]

            def move(r, total):
                for gi in (0, 1):
                    for gj in (0, 1):
                        pair = load_pair(gmix, s + 1, gi, gj, r)
                        total = total + pair[0] + pair[1]
                        store_pair(gmoved, 0, gi, gj, r, shift_pair(pair, 1 - gj, *masks))
                return total

            total = lax.fori_loop(0, HALF, move, jnp.zeros((8, 128), F32))

            def put(gi, gj, r, pair):
                store_pair(gmix, s, gi, gj, r, pair)

            found = conv_back(0, k, normed_ref.at[s : s + 1], gmix.at[s + 1 : s + 2], gmoved, put)
            late[p.core, p.slot, :, at_s] = jnp.sum(found[9], axis=0, keepdims=True)
            column = [jnp.sum(v, axis=0, keepdims=True) for v in (*found[:9], total)]
            column.append(jnp.sum(sums[4, :, at_s], axis=0, keepdims=True))
            column.append(jnp.sum(fc2b_ref[:, at_s], axis=0, keepdims=True))
            rows_out.append(jnp.concatenate(column + [jnp.zeros((4, 128), F32)], axis=0))
            if s % 2:
                waves.tick()
        scale_sum = jnp.zeros((8, model), F32)
        for g in range(4):
            rows = pl.ds(g * GROUP, GROUP)
            unit, scale = unit_rows(lat_ref[rows, :].astype(F32))
            gn = jnp.concatenate(
                [gmix[s, g, 2:34].reshape(GROUP, 128) for s in range(slabs)], axis=1
            )
            scale_sum = scale_sum + row_sum(gn * unit)
            gmid[rows, :] = gmid[rows, :] + unit_back(gn * (1.0 + mod_ref[1:2, :]), unit, scale)
        late[p.core, p.slot, :, model:] = jnp.sum(scale_sum, axis=0, keepdims=True)
        wait_late = p.to_kin(lambda slot: mine(late), mine(late), send_c, recv_c)
        waves.tick()
        p.to_all_wait(lambda sid: hcuts.at[sid], hcuts_in.at[p.sid], send_g, recv_g)
        small_out[8:, :] = jnp.sum(hcuts_in[...], axis=0)
        modulation = tiles_of(late[p.core, p.slot]) + tiles_of(early[p.core, p.slot])
        third = 2 * own
        for sid in range(p.total):
            d = p.order_of(sid)
            piece = move_lanes(rows_out, [(own * d, 0, own)], 1)[0][:8]
            piece = piece + move_lanes(rows_out, [(own * d, 32, own)], 1)[0][8:]
            bias = [
                move_lanes(modulation, [(third * (3 * d + i), 64, third)], 1)[0] for i in range(3)
            ]
            cuts[sid] = piece + jnp.concatenate(bias + [jnp.zeros((5, 128), F32)], axis=0)
        cuts_in[p.sid] = cuts[p.sid]
        wait_cuts = p.to_all(lambda sid: cuts.at[sid], cuts_in.at[p.sid], send_b, recv_b)
        xg_ref[...] = gmid[...].astype(BF16)
        wait_late()
        swap_late = remote(late.at[p.core], late.at[p.core], send_e, recv_e, p.sibling)
        swap_late.start()
        waves.tick()
        remote(early.at[p.core], early.at[p.core], send_d, recv_d, p.sibling).wait()
        swap_late.wait()
        sil = sils_ref[:, :own].astype(BF16)
        cond = None
        for ref, start in ((late, 0), (early, 2 * model)):
            size = ref.shape[-1]
            span = slice(start, start + size)
            found = ref[...].reshape(p.total, size)
            low = found.astype(BF16)
            wgrad_ref[:, span] = dot_tn(sil, low)
            term = dot_nt(low, ada_ref[:, span])
            cond = term if cond is None else cond + term
        cond = jnp.concatenate([cond, jnp.zeros((p.total, 128 - own), F32)], axis=1)
        for sid in range(p.total):
            part[sid] = cond[sid : sid + 1, :]
        cond_in[p.me] = part[p.sid]
        wait_cond = p.to_all(lambda sid: part.at[sid], cond_in.at[p.me], send_f, recv_f)
        waves.end()
        wait_cuts()
        small_out[:8, :] = jnp.sum(cuts_in[...], axis=0)
        wait_cond()
        cond_ref[...] = cond_in[...]


def back(wide, narrow, gn2, two, branch, gout, att, mixed, triple, probs, mod, small, proj, qkv,
         lat, normed, fc2b, hidden_sums, sils, ada, fc1s, fc2s):
    total = wide * narrow
    tokens, model = lat.shape
    slabs, columns = model // 128, ada.shape[1]
    hidden = 2 * hidden_sums[0].shape[1]
    own, own_ff = ada.shape[0], hidden // total
    by_group = pl.BlockSpec((GROUP, model), lambda t: (jnp.minimum(t, 3), 0))
    slab = lambda t: jnp.clip(t - 4, 0, slabs - 1)
    third = lambda rows, i: pl.BlockSpec((rows, 128), lambda t: (0, i * slabs + slab(t)))
    all_sems, kin_sems = (pltpu.SemaphoreType.DMA((n,)) for n in (total, total // 2))
    one_sem = pltpu.SemaphoreType.DMA
    padded = lambda count: pltpu.VMEM((count, 4, 36, 8, 128), F32)
    height = model // wide
    bits = bit_sizes(wide)
    shapes = [fc1s.shape, fc2s.shape, (*bits, height, model), (*bits, height, 3 * model)]
    chunks = thirds(0, hidden // 2) + thirds(1, model) + [(2, 0, model)]
    chunks += [(3, 384 * s, 384) for s in range(slabs)]
    starts = [0, 3, 7, 9, 11, 13, 4] + [6 + 2 * s for s in range(slabs)]
    plan = [steady(c, wide.bit_length()) for c in starts]
    full = lambda a: once(a.shape)
    anywhere = pl.BlockSpec(memory_space=pl.ANY)
    outs = [
        like((tokens, model), BF16), like((tokens, model), BF16), like((own, columns), F32),
        like((total, 1, 128), F32), like((24, 128), F32), like((own, 3 * model), F32),
        like((own, model), F32), like((own, hidden // 2), F32), like((own_ff // 2, model), F32),
    ]
    return pl.pallas_call(
        functools.partial(back_kernel, wide, narrow, chunks, plan, own, own_ff),
        grid=(4 + slabs,),
        in_specs=[by_group] * 4 + [anywhere, anywhere] + [third(tokens, i) for i in range(3)] + [
            pl.BlockSpec((2, 4, GROUP, GROUP), lambda t: (slab(t), 0, 0, 0)),
            full(mod), full(small), full(proj), third(model, 0), third(model, 1), third(model, 2),
            full(lat), pl.BlockSpec(memory_space=pl.ANY), full(fc2b), full(hidden_sums[0]), full(hidden_sums[1]),
            full(sils), full(ada), anywhere, anywhere,
        ],
        out_specs=[by_group] + [once(o.shape) for o in outs[1:]],
        out_shape=outs,
        scratch_shapes=[
            pltpu.VMEM((tokens, model), BF16), pltpu.VMEM((tokens, model), F32),
            padded(slabs + 1), padded(1), pltpu.VMEM((5, 8, model), F32),
            pltpu.VMEM(shapes[2], BF16), pltpu.VMEM(shapes[3], BF16),
            pltpu.VMEM((2, total // 2, 1, 4 * model), F32),
            pltpu.VMEM((2, total // 2, 1, 2 * model), F32),
            pltpu.VMEM((total, 8, 128), F32), pltpu.VMEM((total, 8, 128), F32),
            pltpu.VMEM((total, 16, 128), F32), pltpu.VMEM((total, 16, 128), F32),
            pltpu.VMEM((total, 1, 128), F32), pltpu.VMEM((total, 1, 128), F32),
            pltpu.VMEM((tokens, 384), BF16), padded(slabs),
            pltpu.VMEM((tokens, model), BF16), pltpu.VMEM((tokens, model), BF16),
            pltpu.VMEM(shapes[0], BF16), pltpu.VMEM(shapes[1], BF16), pltpu.SemaphoreType.DMA((5,)),
            kin_sems, kin_sems, all_sems, all_sems, kin_sems, kin_sems, one_sem, one_sem,
            one_sem, one_sem, all_sems, all_sems, all_sems, all_sems,
            *scatter_scratch(wide, narrow, shapes), *job_sems(wide, narrow, chunks),
        ],
        compiler_params=pltpu.CompilerParams(
            vmem_limit_bytes=63 * MIB, collective_id=2, has_side_effects=True
        ),
        name="attend_back",
    )(gn2, two, branch, gout, att, mixed, triple, triple, triple, probs, mod,
      small, proj, qkv, qkv, qkv, lat, normed, fc2b, *hidden_sums, sils, ada, fc1s,
      fc2s)


def finish_kernel(own, own_ff, rows_ref, grads_ref, wgrad_ref, qkvg_ref, projg_ref, fc1a_ref,
                  fc1b_ref, fc2a_ref, fc2b_ref, small_ref, cond_ref, pieces_ref,
                  out_ref, xg_ref, wgrad_out, qkv_out, proj_out, fc1_out, fc2_out, condg_out, adab_out,
                  dw1k_out, dw1b_out, projb_out, fc2b_out, dw2k_out, dw2b_out, fc1b_out):
    model = out_ref.shape[1]
    order = order_matrix()
    for src, dst in ((rows_ref, out_ref), (grads_ref, xg_ref)):
        block = src[...].reshape(GROUP, model)
        dst[...] = dot_tn(order, block).astype(BF16)

    @pl.when(pl.program_id(0) == 0)
    def _():
        half, hidden, total = own_ff // 2, fc1_out.shape[1], pieces_ref.shape[0]
        wgrad_out[...] = wgrad_ref[...]
        proj_out[...] = projg_ref[...]
        for s in range(model // 128):
            for i in range(3):
                to = i * model + s * 128
                qkv_out[:, to : to + 128] = qkvg_ref[:, s * 384 + i * 128 : s * 384 + i * 128 + 128]
        moves = [
            (hidden // 2 * h + half * d, own_ff * d + half * h, half)
            for d in range(total) for h in (0, 1)
        ]
        tiles = tiles_of(fc1a_ref[...]) + tiles_of(fc1b_ref[...])
        for i, tile in enumerate(move_lanes(tiles, moves, hidden // 128)):
            fc1_out[:, i * 128 : i * 128 + 128] = tile
        fc2_out[:half, :] = fc2a_ref[...]
        fc2_out[half:, :] = fc2b_ref[...]
        tiles = [pieces_ref[d] for d in range(total)]
        moves = [(128 * d, own * d, own) for d in range(total)]
        grad = jnp.concatenate(move_lanes(tiles, moves, model // 128), axis=1)
        cond = cond_ref[...].astype(F32)
        gate = jax.nn.sigmoid(cond)
        condg_out[...] = grad * (gate + cond * gate * (1.0 - gate))
        dw1k_out[:8, :] = small_ref[:8, :own]
        dw2k_out[...] = small_ref[8:17, :own_ff]
        rows = ((dw1k_out.at[8:9], 0, 32), (dw1b_out, 1, 32), (projb_out, 2, 32), (fc2b_out, 3, 32),
                (dw2b_out, 17, 0), (fc1b_out, 18, 0))
        for ref, row, lane in rows:
            ref[...] = small_ref[row : row + 1, lane : lane + ref.shape[1]]
        for i in range(3):
            adab_out[:, 2 * own * i : 2 * own * (i + 1)] = small_ref[i : i + 1, 64 : 64 + 2 * own]


def finish(rows, grads, wgrad, qkvg, projg, fc1, fc2, small, cond, pieces):
    tokens, model = rows.shape
    own, hidden, own_ff = wgrad.shape[0], 2 * fc1[0].shape[1], 2 * fc2[0].shape[0]
    split = lambda value: value.reshape(4, 4, 64, model)
    block = pl.BlockSpec((4, 1, 64, model), lambda t: (0, t, 0, 0))
    lines = pl.BlockSpec((GROUP, model), lambda t: (t, 0))
    rest = [wgrad, qkvg, projg, *fc1, *fc2, small, cond, pieces]
    outs = [
        like((tokens, model), BF16), like((tokens, model), BF16), like(wgrad.shape, F32),
        like(qkvg.shape, F32), like(projg.shape, F32), like((own, hidden), F32),
        like((own_ff, model), F32), like((1, model), F32), like((1, 6 * own), F32),
        like((9, own), F32), like((1, own), F32), like((1, own), F32), like((1, own), F32),
        like((9, own_ff), F32), like((1, own_ff), F32), like((1, own_ff), F32),
    ]
    return pl.pallas_call(
        functools.partial(finish_kernel, own, own_ff),
        grid=(4,),
        in_specs=[block, block] + [once(a.shape) for a in rest],
        out_specs=[lines, lines] + [once(o.shape) for o in outs[2:]],
        out_shape=outs,
        compiler_params=pltpu.CompilerParams(vmem_limit_bytes=60 * MIB),
        name="finish",
    )(split(rows), split(grads), *rest)


def on_device(wide, narrow, latents, condition, valid_mask, ada_weight, ada_bias, dw1_kernel, dw1_bias,
              qkv_weight, proj_weight, proj_bias, fc1_weight, fc1_bias, dw2_kernel, dw2_bias,
              fc2_weight, fc2_bias, out_cotangent):
    total = wide * narrow
    w, n = lax.axis_index("wide"), lax.axis_index("narrow")
    me = w * narrow + n
    model, hidden = latents.shape[2], fc1_weight.shape[1]
    own, own_ff = model // total, hidden // total

    bias_at = lax.dynamic_update_slice(
        jnp.zeros((1, 6 * model), F32), ada_bias.astype(F32)[None, :], (0, me * ada_bias.shape[0])
    )
    parts = [(0, dw1_kernel), (9, dw1_bias[None]), (10, proj_bias[None]), (11, fc2_bias[None]),
             (16, dw2_kernel), (25, dw2_bias[None]), (26, fc1_bias[None])]
    small = sum(
        jnp.pad(v, ((row, 32 - row - v.shape[0]), (0, 128 - v.shape[1]))) for row, v in parts
    )
    half = own_ff // 2
    if half % 16:
        fc2a, fc2_rows, spans = fc2_weight[:half], fc2_weight[half:], (None, None)
    else:
        fc2a = fc2_rows = fc2_weight
        spans = ((0, half), (half, half))
    chunks = [(0, 0, 128)] + thirds(2, 3 * model) + [(3, 0, model)]
    stages = wide.bit_length()
    plan = [steady(c, stages) for c in range(5)]
    needed = plan[4][-1]
    chunks += thirds(1, hidden // 2) + thirds(4, model)
    plan += [[6 + c] + steady(needed + 1 + c, stages - 1) for c in range(6)]
    (mod, sils, model_small, hidden_small, lat, gout, g2, normed, mixed, keep, fc2b, fc1b, fc1_one, qkv,
     proj, fc2_one) = front(
        wide, narrow, latents[0], out_cotangent[0], valid_mask, condition, ada_weight, bias_at, small,
        fc1_weight, [qkv_weight, proj_weight, fc2a], (None, None, spans[0]), chunks, plan,
    )
    qkv, proj = qkv.reshape(model, 3 * model), proj.reshape(model, model)
    triple, probs, att, branch, n2, n2t, fc1_one, fc2_one = attend(
        wide, narrow, mixed, lat, keep, mod, model_small, qkv, proj, fc1_one, fc2_one,
        thirds(0, hidden // 2) + thirds(1, model), plan[5:], needed, 5,
    )
    chunks = thirds(0, hidden // 2) + thirds(1, model)
    as_fc1 = lambda rows: rows.reshape(model, hidden // 2)
    as_fc2 = lambda rows: rows.reshape(hidden // 2, model)
    as_lines = lambda grad: grad.reshape(*bit_sizes(wide), grad.shape[0] // wide, grad.shape[1])
    two, gn2, fc1g, fc2g, sums_a, fc1_two, fc2_two = feed_forward(
        wide, narrow, n2, n2t, g2, as_fc1(fc1_one), hidden_small, 0, as_fc2(fc2_one),
        [fc1b, fc2_rows], (None, spans[1]), chunks,
    )
    two, gn2, fc1h, fc2h, sums_b, fc1o, fc2o = feed_forward(
        wide, narrow, n2, n2t, g2, as_fc1(fc1_two), hidden_small, 1, as_fc2(fc2_two),
        [as_lines(fc1g), as_lines(fc2g)], (None, None), chunks, (two, gn2),
    )
    rows, grads, ada_wgrad, pieces, small, qkvg, projg, fc1p, fc2p = back(
        wide, narrow, gn2, two, branch, gout, att, mixed, triple, probs,
        mod, model_small, proj, qkv, lat, normed, fc2b, (sums_a, sums_b), sils, ada_weight,
        as_lines(fc1h), as_lines(fc2h),
    )
    (out, xg, ada_wgrad, qkvg, projg, fc1g, fc2g, cond_grad, ada_bgrad, dw1k, dw1b, projb, fc2bg, dw2k,
     dw2b, fc1bg) = finish(
        rows, grads, ada_wgrad, qkvg, projg, (fc1o, fc1p), (fc2o, fc2p), small, condition, pieces
    )
    return (
        out[None], xg[None], cond_grad, ada_wgrad, ada_bgrad[0], dw1k, dw1b[0], qkvg, projg, projb[0],
        fc1g, fc1bg[0], dw2k, dw2b[0], fc2g, fc2bg[0],
    )


def solution(mesh):
    wide, narrow = mesh.shape["wide"], mesh.shape["narrow"]
    rows = lambda rank: P(AXES, *(None,) * (rank - 1))
    lanes = P(None, AXES)
    in_specs = (
        rows(3), rows(2), rows(2), rows(2), rows(1), lanes, rows(1), rows(2), rows(2), rows(1),
        rows(2), rows(1), lanes, rows(1), rows(2), rows(1), rows(3),
    )
    out_specs = (
        rows(3), rows(3), rows(2), rows(2), rows(1), lanes, rows(1), rows(2), rows(2), rows(1),
        rows(2), rows(1), lanes, rows(1), rows(2), rows(1),
    )
    return jax.shard_map(
        functools.partial(on_device, wide, narrow), mesh=mesh, in_specs=in_specs,
        out_specs=out_specs, check_vma=False,
    )
```
